32 devices in a mesh: section: 16 (over z, y, x), rep: 2 (over core).
Axes of the slice: x: 2, y: 2, z: 4, core: 2. Of those that a mesh axis runs over, the one named last changes fastest.
Arguments:
- features: bfloat16 [16384, 512], P('section'), may hold values from -6 to 6
- weight: bfloat16 [512, 512], replicated, may hold values from -0.25 to 0.25
- tile_values: bfloat16 [16, 16, 24, 128, 128], P('section', 'rep'), may hold values from 0 to 0.033691406
- tile_rows: int32 [16, 16, 24], P('section', 'rep'), may hold values from 0 to 7
- tile_cols: int32 [16, 16, 24], P('section', 'rep'), may hold values from 0 to 7
- tile_count: int32 [16, 16], P('section', 'rep'), may hold values from 3 to 24, as said below
- cotangent: bfloat16 [16384, 512], P(('section', 'rep')), may hold values from -6 to 6
Outputs:
- activated: bfloat16 [16384, 512], P(('section', 'rep'))
- feat_grad: bfloat16 [2, 8192, 512], P('rep', 'section')
- weight_grad: float32 [512, 512], replicated
The draws below stay inside these ranges and needn't reach their ends.
Inputs may be any that keep to these rules, and one draw needn't show every extreme that they name: Slots k >= tile_count[s, j] of a row block and panel are ignored; some row block and panel has all 24 slots live.
All inputs are finite; a program needn't handle non-finite values.
Results may differ from the reference program's by a relative error of at most 0.02.
Values may be sent and summed in bfloat16 or wider, within the bound.
No kernel may reach another device: no remote copies, remote signals or barrier semaphores. Data moves between devices by JAX's collectives and lax.ppermute only.
A program may use at most 128 MiB of HBM per device.

```python
import jax
import jax.numpy as jnp
from jax import lax

F = 512
TILE = 128
KT = 24
RB = 1024
NODES = 16384
RT = 8
N_SECTION = 16
N_REP = 2


def draw_tile_count(key, part):
    key = jax.random.fold_in(key, 11)
    first, second, third, fourth = jax.random.split(key, 4)
    lowest = max(KT // 8, 1)
    light = jax.random.randint(first, (N_SECTION, N_SECTION), lowest, KT // 2 + 1)
    heavy = jax.random.randint(second, (N_SECTION, N_SECTION), KT // 2, KT + 1)
    heavy_block = jax.random.randint(third, (N_SECTION, 1), 0, 4) == 0
    counts = jnp.where(heavy_block, heavy, light).reshape(-1)
    full_slot = jax.random.randint(fourth, (), 0, N_SECTION * N_SECTION)
    position = jnp.arange(N_SECTION * N_SECTION, dtype=jnp.int32)
    counts = jnp.where(position == full_slot, KT, counts)
    return counts.reshape(N_SECTION, N_SECTION).astype(jnp.int32)


def set_ends(entries, own_key, low, top_value):
    spot = [jax.random.randint(jax.random.fold_in(own_key, axis), (), 0, length) for axis, length in enumerate(entries.shape)]
    main_axis = entries.shape.index(max(entries.shape))
    beside = spot[:main_axis] + [(spot[main_axis] + 1) % entries.shape[main_axis]] + spot[main_axis + 1:]
    return entries.at[tuple(spot)].set(low).at[tuple(beside)].set(top_value)


def shard_levels(own_key, dims, cuts, least, largest):
    factor_of, own = 1.0, jax.random.fold_in(own_key, 6)
    for dim, parts in cuts:
        steps = jnp.exp(jax.random.uniform(jax.random.fold_in(own, dim), (parts,), jnp.float32, least / len(cuts), largest / len(cuts)))
        factor_of = factor_of * jnp.repeat(steps, dims[dim] // parts).reshape([-1 if axis == dim else 1 for axis in range(len(dims))])
    return factor_of


def scatter_about(key, shape, deviation, reach, cuts=(), kind=jnp.bfloat16):
    values = jax.random.normal(key, shape, jnp.float32) * deviation
    if len(cuts) > 0:
        values = shard_levels(key, shape, cuts, -0.22, 0.18) * values
    return jnp.clip(values, min=-reach, max=reach).astype(kind)


def setup_inputs(seed: int = 0) -> dict:
    key_of = jax.random.split(jax.random.key(seed), 8)
    return {
        "features": scatter_about(key_of[0], (NODES, F), 1.0, 6.0, ((0, 16),)),
        "weight": scatter_about(key_of[1], (F, F), F ** -0.5, 0.25),
        "tile_values": jnp.clip(0.033691406 * jax.random.uniform(key_of[2], (N_SECTION, N_SECTION, KT, TILE, TILE), jnp.float32) ** shard_levels(key_of[2], (N_SECTION, N_SECTION, KT, TILE, TILE), ((0, 16), (1, 2)), -0.2, 0.2), 0.0, 0.033691406).astype(jnp.bfloat16),
        "tile_rows": set_ends(jax.random.randint(key_of[3], (N_SECTION, N_SECTION, KT), 0, RT), jax.random.fold_in(key_of[3], 1), 0, RT - 1).astype(jnp.int32),
        "tile_cols": set_ends(jax.random.randint(key_of[4], (N_SECTION, N_SECTION, KT), 0, RT), jax.random.fold_in(key_of[4], 1), 0, RT - 1).astype(jnp.int32),
        "tile_count": draw_tile_count(jax.random.fold_in(key_of[7], 71), 0),
        "cotangent": scatter_about(key_of[6], (NODES, F), 1.0, 6.0, ((0, 32),)),
    }


def slope_grad(pre, cotangent):
    sigma = jax.nn.sigmoid(pre)
    return (cotangent.astype(jnp.float32) * sigma * (1.0 + pre * (1.0 - sigma))).astype(jnp.bfloat16)

def aggregate(features, tile_values, tile_rows, tile_cols, tile_count):
    blocks = features.reshape(N_SECTION, RT, TILE, F)
    slot_index = jnp.arange(KT, dtype=jnp.int32)
    tile_index = jnp.arange(RT, dtype=jnp.int32)
    panel_index = jnp.arange(N_SECTION, dtype=jnp.int32)

    def one_block(row_block):
        values = tile_values[row_block].astype(jnp.float32)
        picked = blocks[panel_index[:, None], tile_cols[row_block]].astype(jnp.float32)
        product = jnp.einsum('jkab,jkbf->jkaf', values, picked, precision=lax.Precision.HIGHEST)
        is_live = slot_index[None, :] < tile_count[row_block][:, None]
        select = ((tile_rows[row_block][:, :, None] == tile_index) & is_live[:, :, None]).astype(jnp.float32)
        return jnp.einsum('jki,jkaf->iaf', select, product, precision=lax.Precision.HIGHEST).reshape(RB, F)
    return lax.map(one_block, jnp.arange(N_SECTION, dtype=jnp.int32)).reshape(NODES, F)

def spread_back(grad, tile_values, tile_rows, tile_cols, tile_count):
    blocks = grad.reshape(N_SECTION, RT, TILE, F)
    slot_index = jnp.arange(KT, dtype=jnp.int32)
    tile_index = jnp.arange(RT, dtype=jnp.int32)
    block_index = jnp.arange(N_SECTION, dtype=jnp.int32)

    def one_panel(panel_pos):
        values = tile_values[:, panel_pos].astype(jnp.float32)
        picked = blocks[block_index[:, None], tile_rows[:, panel_pos]].astype(jnp.float32)
        product = jnp.einsum('skab,skaf->skbf', values, picked, precision=lax.Precision.HIGHEST)
        is_live = slot_index[None, :] < tile_count[:, panel_pos][:, None]
        select = ((tile_cols[:, panel_pos][:, :, None] == tile_index) & is_live[:, :, None]).astype(jnp.float32)
        per_block = jnp.einsum('ski,skbf->sibf', select, product, precision=lax.Precision.HIGHEST)
        rounded = lax.optimization_barrier(per_block.astype(jnp.bfloat16)).astype(jnp.float32)
        return lax.optimization_barrier(jnp.sum(rounded, axis=0)).reshape(RB, F)
    return lax.map(one_panel, jnp.arange(N_SECTION, dtype=jnp.int32)).reshape(NODES, F)

def reference(features, weight, tile_values, tile_rows, tile_cols, tile_count, cotangent):
    agg = aggregate(features, tile_values, tile_rows, tile_cols, tile_count).astype(jnp.bfloat16)
    pre = jnp.dot(agg, weight, preferred_element_type=jnp.float32)
    activated = jax.nn.silu(pre).astype(jnp.bfloat16)
    pre_grad = slope_grad(pre, cotangent)
    weight_grad = jnp.dot(agg.T, pre_grad, preferred_element_type=jnp.float32)
    agg_grad = jnp.dot(pre_grad, weight.T, preferred_element_type=jnp.float32).astype(jnp.bfloat16)
    grad_full = spread_back(agg_grad, tile_values, tile_rows, tile_cols, tile_count).astype(jnp.bfloat16)
    feat_grad = grad_full.reshape(N_REP, NODES // N_REP, F)
    return (activated, feat_grad, weight_grad)
```

```python
import functools

import jax
import jax.numpy as jnp
import numpy as np
from jax import lax
from jax.experimental import pallas as pl
from jax.experimental.pallas import tpu as pltpu
from jax.sharding import PartitionSpec as P

BF16 = jnp.bfloat16
F32 = jnp.float32
BOTH = ("section", "rep")


def dense_kernel(count_ref, rows_ref, cols_ref, tiles_ref, out_ref):
    panel = pl.program_id(0)
    size = tiles_ref.shape[-1]
    out_ref[...] = jnp.zeros_like(out_ref)

    def add_tile(slot, carry):
        row = pl.multiple_of(rows_ref[panel, slot] * size, size)
        col = pl.multiple_of(cols_ref[panel, slot] * size, size)
        out_ref[0, pl.ds(row, size), pl.ds(col, size)] += tiles_ref[0, slot]
        return carry

    lax.fori_loop(0, count_ref[panel], add_tile, 0)


def make_dense(tiles, rows, cols, count, block_rows):
    panels, slots, size, _ = tiles.shape
    return pl.pallas_call(
        dense_kernel,
        out_shape=jax.ShapeDtypeStruct((panels, block_rows, block_rows), BF16),
        grid_spec=pltpu.PrefetchScalarGridSpec(
            num_scalar_prefetch=3,
            grid=(panels,),
            in_specs=[pl.BlockSpec((1, slots, size, size), lambda p, *_: (p, 0, 0, 0))],
            out_specs=pl.BlockSpec((1, block_rows, block_rows), lambda p, *_: (p, 0, 0)),
        ),
        compiler_params=pltpu.CompilerParams(vmem_limit_bytes=32 * 2**20),
        cost_estimate=pl.CostEstimate(
            flops=0,
            transcendentals=0,
            bytes_accessed=tiles.size * 2 + panels * block_rows * block_rows * 2,
        ),
    )(count, rows, cols, tiles)


def forward_kernel(has_total, place_ref, *refs):
    if has_total:
        total_ref, a_ref, own_ref, x_ref, y_ref, da_ref, db_ref, out_ref = refs
    else:
        a_ref, own_ref, x_ref, y_ref, da_ref, db_ref, out_ref = refs
    step = pl.program_id(0)

    @pl.when(step == 0)
    def _():
        out_ref[...] = total_ref[...] if has_total else jnp.zeros_like(out_ref)

    live = place_ref[0] > 0

    def add(feat, columns):
        out_ref[...] += jnp.dot(a_ref[0, :, columns], feat, preferred_element_type=F32)

    whole = slice(None)
    half = da_ref.shape[0]

    @pl.when(live & (step == 0))
    def _():
        add(own_ref[...], whole)

    @pl.when(live & (step == 1))
    def _():
        add(x_ref[...], whole)

    @pl.when(live & (step == 2))
    def _():
        add(y_ref[...], whole)

    @pl.when(live & (step == 3))
    def _():
        add(da_ref[...], slice(0, half))
        add(db_ref[...], slice(half, 2 * half))


def forward_part(place, total, dense, own, x_side, y_side, diag_a, diag_b):
    rows, width = own.shape
    fixed = lambda shape: pl.BlockSpec(shape, lambda i, place: (0, 0))
    in_specs = [
        pl.BlockSpec((1, rows, rows), lambda i, place: (place[1 + i], 0, 0)),
        fixed((rows, width)),
        fixed((rows, width)),
        fixed((rows, width)),
        fixed((rows // 2, width)),
        fixed((rows // 2, width)),
    ]
    args = [dense, own, x_side, y_side, diag_a, diag_b]
    has_total = total is not None
    if has_total:
        in_specs = [fixed((rows, width))] + in_specs
        args = [total] + args
    return pl.pallas_call(
        functools.partial(forward_kernel, has_total),
        out_shape=jax.ShapeDtypeStruct((rows, width), F32),
        grid_spec=pltpu.PrefetchScalarGridSpec(
            num_scalar_prefetch=1,
            grid=(4,),
            in_specs=in_specs,
            out_specs=fixed((rows, width)),
        ),
        input_output_aliases={1: 0} if has_total else {},
        compiler_params=pltpu.CompilerParams(vmem_limit_bytes=48 * 2**20),
        cost_estimate=pl.CostEstimate(
            flops=8 * rows * rows * width,
            transcendentals=0,
            bytes_accessed=4 * rows * rows * 2 + 8 * rows * width * 2,
        ),
    )(place, *args)


def middle_kernel(place_ref, agg_ref, weight_ref, cot_ref, grad_ref, act_ref, agg_out, pre_out):
    agg = agg_ref[...].astype(BF16)
    pre = jnp.dot(agg, weight_ref[...], preferred_element_type=F32)
    sigma = jax.nn.sigmoid(pre)
    act_ref[...] = (pre * sigma).astype(BF16)
    slope = cot_ref[...].astype(F32) * sigma * (1.0 + pre * (1.0 - sigma))
    pre_grad = slope.astype(BF16)
    grad_ref[...] = lax.dot_general(
        weight_ref[...], pre_grad, (((1,), (1,)), ((), ())), preferred_element_type=F32
    ).astype(BF16)
    agg_out[...] = agg
    pre_out[...] = pre_grad


def middle(place, agg, weight, cotangent, n_rep):
    rows, width = agg.shape
    part = rows // n_rep
    block = lambda i, place: ((place[0] + 1 + i) % n_rep, 0)
    last = pl.BlockSpec((part, width), lambda i, place: (0, 0))
    own = jax.ShapeDtypeStruct((part, width), BF16)
    return pl.pallas_call(
        middle_kernel,
        out_shape=[jax.ShapeDtypeStruct((width, rows), BF16), own, own, own],
        grid_spec=pltpu.PrefetchScalarGridSpec(
            num_scalar_prefetch=1,
            grid=(n_rep,),
            in_specs=[
                pl.BlockSpec((part, width), block),
                pl.BlockSpec((width, width), lambda i, place: (0, 0)),
                pl.BlockSpec((part, width), block),
            ],
            out_specs=[
                pl.BlockSpec((width, part), lambda i, place: (0, block(i, place)[0])),
                last,
                last,
                last,
            ],
        ),
        compiler_params=pltpu.CompilerParams(vmem_limit_bytes=40 * 2**20),
        cost_estimate=pl.CostEstimate(
            flops=4 * rows * width * width,
            transcendentals=rows * width,
            bytes_accessed=rows * width * 10,
        ),
    )(place, agg, weight, cotangent)


def backward_kernel(place_ref, grad_ref, a_ref, x_ref, y_ref, xb_ref, ya_ref, own_ref):
    step = pl.program_id(0)
    half = xb_ref.shape[0]
    chunk = jnp.dot(grad_ref[...], a_ref[0], preferred_element_type=F32).astype(BF16)

    @pl.when(step == 0)
    def _():
        x_ref[0] = chunk[:half]
        y_ref[0] = chunk[half:]

    @pl.when(step == 1)
    def _():
        x_ref[1] = chunk[:half]
        xb_ref[...] = chunk[half:]

    @pl.when(step == 2)
    def _():
        y_ref[1] = chunk[half:]
        ya_ref[...] = chunk[:half]

    @pl.when(step == 3)
    def _():
        own_ref[...] = chunk


def backward_part(place, grad, dense, cols):
    width, rows = grad.shape
    per_panel = dense.shape[2] // cols
    half = width // 2
    pair = pl.BlockSpec((2, half, cols), lambda i, place: (0, 0, 0))
    single = pl.BlockSpec((half, cols), lambda i, place: (0, 0))
    return pl.pallas_call(
        backward_kernel,
        out_shape=[
            jax.ShapeDtypeStruct((2, half, cols), BF16),
            jax.ShapeDtypeStruct((2, half, cols), BF16),
            jax.ShapeDtypeStruct((half, cols), BF16),
            jax.ShapeDtypeStruct((half, cols), BF16),
            jax.ShapeDtypeStruct((width, cols), BF16),
        ],
        grid_spec=pltpu.PrefetchScalarGridSpec(
            num_scalar_prefetch=1,
            grid=(4,),
            in_specs=[
                pl.BlockSpec((width, rows), lambda i, place: (0, 0)),
                pl.BlockSpec(
                    (1, rows, cols),
                    lambda i, place: (place[i] // per_panel, 0, place[i] % per_panel),
                ),
            ],
            out_specs=[
                pair,
                pair,
                single,
                single,
                pl.BlockSpec((width, cols), lambda i, place: (0, 0)),
            ],
        ),
        compiler_params=pltpu.CompilerParams(vmem_limit_bytes=40 * 2**20),
        cost_estimate=pl.CostEstimate(
            flops=8 * rows * width * cols,
            transcendentals=0,
            bytes_accessed=8 * rows * cols + 8 * width * cols + 2 * width * rows,
        ),
    )(place, grad, dense)


class Places:
    def __init__(self, n_section, n_rep):
        self.n_section, self.n_rep = n_section, n_rep
        self.depth = n_section // 4
        self.span = self.depth // n_rep
        self.panels = n_section // n_rep

    def devices(self):
        for section in range(self.n_section):
            for rep in range(self.n_rep):
                yield section // 4, section // 2 % 2, section % 2, rep

    def flat(self, z, y, x, rep):
        return ((z * 2 + y) * 2 + x) * self.n_rep + rep

    def wants(self, z, rep):
        return rep * self.span <= z < (rep + 1) * self.span

    def heading(self, rep):
        return 1 if rep < self.n_rep / 2 else -1

    def flow(self, step, way):
        pairs = []
        for z, y, x, rep in self.devices():
            head = way * self.heading(rep)
            source = z - head * (step - 1)
            if 0 <= z + head < self.depth and self.wants(source, rep):
                pairs.append((self.flat(z, y, x, rep), self.flat(z + head, y, x, rep)))
        return pairs

    def source(self, step, z, rep):
        for source in sorted({z - step, z + step}):
            if 0 <= source < self.depth and self.wants(source, rep):
                return source
        return None

    def across(self, step, axis):
        return [
            (self.flat(z, y, x, rep), self.flat(z, y ^ (axis == "y"), x ^ (axis == "x"), rep))
            for z, y, x, rep in self.devices()
            if step is None or self.source(step, z, rep) is not None
        ]

    def order(self, z):
        near_end = z < self.depth / 2
        return sorted(
            range(self.depth), key=lambda d: (-abs(d - z), (d < z) if near_end else (d > z))
        )

    def up_dest(self, step, z):
        dest = self.depth - step + z
        return dest if z < dest < self.depth else None

    def down_dest(self, step, z):
        dest = z - self.depth + step
        return dest if 0 <= dest < z else None

    def table(self):
        rows = []
        for z, y, x, rep in self.devices():
            row = []
            for step in range(self.depth):
                source = self.source(step, z, rep)
                if source is None:
                    row += [0, 0, 0, 0, 0]
                else:
                    base = (source - rep * self.span) * 4
                    row += [1] + [base + 2 * b + a for b, a in ((y, x), (y, 1 - x), (1 - y, x), (1 - y, 1 - x))]
            for dest in self.order(z):
                row += [dest * 4 + 2 * b + a for b, a in ((1 - y, 1 - x), (y, 1 - x), (1 - y, x), (y, x))]
            rows.append(row)
        return np.array(rows, np.int32)


def shards(sizes, features, weight, tile_values, tile_rows, tile_cols, tile_count, cotangent):
    places = Places(*sizes)
    depth, n_rep = places.depth, places.n_rep
    block_rows, width = features.shape
    cols = block_rows * places.panels // places.n_section
    section, rep = lax.axis_index("section"), lax.axis_index("rep")
    z = section // 4
    table = lax.dynamic_index_in_dim(
        jnp.asarray(places.table()), section * n_rep + rep, keepdims=False
    )
    send = lambda value, pairs: lax.ppermute(value, BOTH, pairs)
    rep_pairs = lambda shift: [
        (places.flat(a, b, c, r), places.flat(a, b, c, (r + shift) % n_rep))
        for a, b, c, r in places.devices()
    ]

    arrivals = []
    major = minor = features
    for step in range(depth):
        if step == 0:
            arrived = features
        else:
            with jax.named_scope("features_along_z"):
                parts = []
                pairs = places.flow(step, 1)
                if pairs:
                    major = send(major, pairs)
                    parts.append(major)
                pairs = places.flow(step, -1)
                if pairs:
                    minor = send(minor, pairs)
                    parts.append(minor)
                arrived = functools.reduce(jnp.add, parts)
        with jax.named_scope("features_across"):
            to_x, to_y = places.across(step, "x"), places.across(step, "y")
            x_side, y_side = send(arrived, to_x), send(arrived, to_y)
            half = block_rows // 2
            diag_a = send(x_side[:half], to_y)
            diag_b = send(y_side[half:], to_x)
        arrivals.append((arrived, x_side, y_side, diag_a, diag_b))

    with jax.named_scope("cotangent_rows"):
        held = [send(cotangent, rep_pairs(-shift)) if shift else cotangent for shift in range(n_rep)]
        cot_rows = jnp.roll(jnp.stack(held), rep, axis=0).reshape(block_rows, width)

    with jax.named_scope("dense_blocks"):
        dense = make_dense(tile_values[0], tile_rows[0], tile_cols[0], tile_count[0], block_rows)

    total = None
    for step, arrival in enumerate(arrivals):
        with jax.named_scope("forward"):
            total = forward_part(table[5 * step : 5 * step + 5], total, dense, *arrival)

    with jax.named_scope("partial_sums"):
        shift = 1
        while shift < n_rep:
            sent = total.astype(BF16)
            pairs = [
                (places.flat(a, b, c, r), places.flat(a, b, c, r ^ shift))
                for a, b, c, r in places.devices()
            ]
            total = sent.astype(F32) + send(sent, pairs).astype(F32)
            shift *= 2

    with jax.named_scope("middle"):
        grad, activated, agg_own, pre_own = middle(rep[None], total, weight, cot_rows, n_rep)

    with jax.named_scope("weight_grad"):
        weight_grad = lax.psum(
            lax.dot_general(
                agg_own, pre_own, (((0,), (0,)), ((), ())), preferred_element_type=F32
            ),
            BOTH,
        )

    to_x, to_y = places.across(None, "x"), places.across(None, "y")
    sums = []
    up = down = None
    for turn in range(depth):
        with jax.named_scope("backward"):
            start = 5 * depth + 4 * turn
            x_pair, y_pair, x_b, y_a, own = backward_part(
                table[start : start + 4], grad, dense, cols
            )
        with jax.named_scope("grads_across"):
            from_x, from_y = send(x_pair, to_x), send(y_pair, to_y)
            x_b = (x_b.astype(F32) + from_y[0].astype(F32)).astype(BF16)
            y_a = (y_a.astype(F32) + from_x[0].astype(F32)).astype(BF16)
            last_x, last_y = send(x_b, to_x), send(y_a, to_y)
            own = own.reshape(2, width // 2, cols).astype(F32)
            summed = jnp.stack(
                [
                    own[0] + from_x[1].astype(F32) + last_y.astype(F32),
                    own[1] + from_y[1].astype(F32) + last_x.astype(F32),
                ]
            )
            sums.append(summed)
        step = turn + 1
        if step == depth:
            break
        with jax.named_scope("grads_along_z"):
            passed = []
            for dest_of, way, carried in (
                (places.up_dest, 1, up),
                (places.down_dest, -1, down),
            ):
                pairs, picks = [], {}
                for a, b, c, r in places.devices():
                    dest = dest_of(step, a)
                    if dest is not None:
                        pairs.append((places.flat(a, b, c, r), places.flat(a + way, b, c, r)))
                        picks[a] = places.order(a).index(dest)
                chosen = None
                for pick in sorted(set(picks.values())):
                    if chosen is None:
                        chosen = sums[pick]
                    else:
                        here = functools.reduce(
                            jnp.logical_or, [z == a for a in picks if picks[a] == pick]
                        )
                        chosen = jnp.where(here, sums[pick], chosen)
                if carried is not None:
                    chosen = chosen + carried.astype(F32)
                passed.append(send(chosen.astype(BF16), pairs))
            up, down = passed
    with jax.named_scope("grads_out"):
        final = sums[-1] + up.astype(F32) + down.astype(F32)
        feat_grad = final.reshape(width, cols).astype(BF16).T
    return (activated, feat_grad[None], weight_grad)


def solution(mesh):
    placed = (
        P("section", None),
        P(),
        P("section", "rep", None, None, None),
        P("section", "rep", None),
        P("section", "rep", None),
        P("section", "rep"),
        P(("section", "rep"), None),
    )
    sizes = (mesh.shape["section"], mesh.shape["rep"])
    return jax.shard_map(
        functools.partial(shards, sizes),
        mesh=mesh,
        in_specs=placed,
        out_specs=(P(("section", "rep"), None), P("rep", "section", None), P()),
        check_vma=False,
    )
```

```python
import functools

import jax
import jax.numpy as jnp
import numpy as np
from jax import lax
from jax.experimental import pallas as pl
from jax.experimental.pallas import tpu as pltpu
from jax.sharding import PartitionSpec as P

BF16 = jnp.bfloat16
F32 = jnp.float32
BOTH = ("section", "rep")


def dense_kernel(count_ref, rows_ref, cols_ref, tiles_ref, out_ref):
    panel = pl.program_id(0)
    size = tiles_ref.shape[-1]
    out_ref[...] = jnp.zeros_like(out_ref)

    def add_tile(slot, carry):
        row = pl.multiple_of(rows_ref[panel, slot] * size, size)
        col = pl.multiple_of(cols_ref[panel, slot] * size, size)
        out_ref[0, pl.ds(row, size), pl.ds(col, size)] += tiles_ref[0, slot]
        return carry

    lax.fori_loop(0, count_ref[panel], add_tile, 0)


def make_dense(tiles, rows, cols, count, block_rows):
    panels, slots, size, _ = tiles.shape
    return pl.pallas_call(
        dense_kernel,
        out_shape=jax.ShapeDtypeStruct((panels, block_rows, block_rows), BF16),
        grid_spec=pltpu.PrefetchScalarGridSpec(
            num_scalar_prefetch=3,
            grid=(panels,),
            in_specs=[pl.BlockSpec((1, slots, size, size), lambda p, *_: (p, 0, 0, 0))],
            out_specs=pl.BlockSpec((1, block_rows, block_rows), lambda p, *_: (p, 0, 0)),
        ),
        compiler_params=pltpu.CompilerParams(vmem_limit_bytes=32 * 2**20),
        cost_estimate=pl.CostEstimate(
            flops=0,
            transcendentals=0,
            bytes_accessed=tiles.size * 2 + panels * block_rows * block_rows * 2,
        ),
    )(count, rows, cols, tiles)


def forward_kernel(has_total, place_ref, *refs):
    if has_total:
        total_ref, a_ref, own_ref, x_ref, y_ref, da_ref, db_ref, out_ref = refs
    else:
        a_ref, own_ref, x_ref, y_ref, da_ref, db_ref, out_ref = refs
    step = pl.program_id(0)

    @pl.when(step == 0)
    def _():
        out_ref[...] = total_ref[...] if has_total else jnp.zeros_like(out_ref)

    live = place_ref[0] > 0

    def add(feat, columns):
        out_ref[...] += jnp.dot(a_ref[0, :, columns], feat, preferred_element_type=F32)

    whole = slice(None)
    half = da_ref.shape[0]

    @pl.when(live & (step == 0))
    def _():
        add(own_ref[...], whole)

    @pl.when(live & (step == 1))
    def _():
        add(x_ref[...], whole)

    @pl.when(live & (step == 2))
    def _():
        add(y_ref[...], whole)

    @pl.when(live & (step == 3))
    def _():
        add(da_ref[...], slice(0, half))
        add(db_ref[...], slice(half, 2 * half))


def forward_part(place, total, dense, own, x_side, y_side, diag_a, diag_b):
    rows, width = own.shape
    fixed = lambda shape: pl.BlockSpec(shape, lambda i, place: (0, 0))
    in_specs = [
        pl.BlockSpec((1, rows, rows), lambda i, place: (place[1 + i], 0, 0)),
        fixed((rows, width)),
        fixed((rows, width)),
        fixed((rows, width)),
        fixed((rows // 2, width)),
        fixed((rows // 2, width)),
    ]
    args = [dense, own, x_side, y_side, diag_a, diag_b]
    has_total = total is not None
    if has_total:
        in_specs = [fixed((rows, width))] + in_specs
        args = [total] + args
    return pl.pallas_call(
        functools.partial(forward_kernel, has_total),
        out_shape=jax.ShapeDtypeStruct((rows, width), F32),
        grid_spec=pltpu.PrefetchScalarGridSpec(
            num_scalar_prefetch=1,
            grid=(4,),
            in_specs=in_specs,
            out_specs=fixed((rows, width)),
        ),
        input_output_aliases={1: 0} if has_total else {},
        compiler_params=pltpu.CompilerParams(vmem_limit_bytes=48 * 2**20),
        cost_estimate=pl.CostEstimate(
            flops=8 * rows * rows * width,
            transcendentals=0,
            bytes_accessed=4 * rows * rows * 2 + 8 * rows * width * 2,
        ),
    )(place, *args)


def middle_kernel(place_ref, agg_ref, weight_ref, cot_ref, grad_ref, act_ref, term_ref, sum_ref):
    agg = agg_ref[...].astype(BF16)
    pre = jnp.dot(agg, weight_ref[...], preferred_element_type=F32)
    sigma = jax.nn.sigmoid(pre)
    act_ref[...] = (pre * sigma).astype(BF16)
    slope = cot_ref[...].astype(F32) * sigma * (1.0 + pre * (1.0 - sigma))
    pre_grad = slope.astype(BF16)
    grad_ref[...] = lax.dot_general(
        weight_ref[...], pre_grad, (((1,), (1,)), ((), ())), preferred_element_type=F32
    ).astype(BF16)
    term = lax.dot_general(
        agg, pre_grad, (((0,), (0,)), ((), ())), preferred_element_type=F32
    )
    step = pl.program_id(0)

    @pl.when(step == 0)
    def _():
        sum_ref[...] = term

    @pl.when(step > 0)
    def _():
        sum_ref[...] += term

    @pl.when(step == pl.num_programs(0) - 1)
    def _():
        size = term_ref.shape[0]
        start = pl.multiple_of(place_ref[0] * size, size)
        term_ref[...] = sum_ref[pl.ds(start, size), :].astype(BF16)


def middle(place, agg, weight, cotangent, n_rep):
    rows, width = agg.shape
    part = rows // n_rep
    block = lambda i, place: ((place[0] + 1 + i) % n_rep, 0)
    last = pl.BlockSpec((part, width), lambda i, place: (0, 0))
    return pl.pallas_call(
        middle_kernel,
        out_shape=[
            jax.ShapeDtypeStruct((width, rows), BF16),
            jax.ShapeDtypeStruct((part, width), BF16),
            jax.ShapeDtypeStruct((width // n_rep, width), BF16),
        ],
        grid_spec=pltpu.PrefetchScalarGridSpec(
            num_scalar_prefetch=1,
            grid=(n_rep,),
            in_specs=[
                pl.BlockSpec((part, width), block),
                pl.BlockSpec((width, width), lambda i, place: (0, 0)),
                pl.BlockSpec((part, width), block),
            ],
            out_specs=[
                pl.BlockSpec((width, part), lambda i, place: (0, block(i, place)[0])),
                last,
                pl.BlockSpec((width // n_rep, width), lambda i, place: (0, 0)),
            ],
            scratch_shapes=[pltpu.VMEM((width, width), F32)],
        ),
        compiler_params=pltpu.CompilerParams(vmem_limit_bytes=40 * 2**20),
        cost_estimate=pl.CostEstimate(
            flops=6 * rows * width * width,
            transcendentals=rows * width,
            bytes_accessed=rows * width * 10,
        ),
    )(place, agg, weight, cotangent)


def backward_kernel(place_ref, grad_ref, a_ref, x_ref, y_ref, xb_ref, ya_ref, own_ref):
    step = pl.program_id(0)
    half = xb_ref.shape[0]
    chunk = jnp.dot(grad_ref[...], a_ref[0], preferred_element_type=F32).astype(BF16)

    @pl.when(step == 0)
    def _():
        x_ref[0] = chunk[:half]
        y_ref[0] = chunk[half:]

    @pl.when(step == 1)
    def _():
        x_ref[1] = chunk[:half]
        xb_ref[...] = chunk[half:]

    @pl.when(step == 2)
    def _():
        y_ref[1] = chunk[half:]
        ya_ref[...] = chunk[:half]

    @pl.when(step == 3)
    def _():
        own_ref[...] = chunk


def backward_part(place, grad, dense, cols):
    width, rows = grad.shape
    per_panel = dense.shape[2] // cols
    half = width // 2
    pair = pl.BlockSpec((2, half, cols), lambda i, place: (0, 0, 0))
    single = pl.BlockSpec((half, cols), lambda i, place: (0, 0))
    return pl.pallas_call(
        backward_kernel,
        out_shape=[
            jax.ShapeDtypeStruct((2, half, cols), BF16),
            jax.ShapeDtypeStruct((2, half, cols), BF16),
            jax.ShapeDtypeStruct((half, cols), BF16),
            jax.ShapeDtypeStruct((half, cols), BF16),
            jax.ShapeDtypeStruct((width, cols), BF16),
        ],
        grid_spec=pltpu.PrefetchScalarGridSpec(
            num_scalar_prefetch=1,
            grid=(4,),
            in_specs=[
                pl.BlockSpec((width, rows), lambda i, place: (0, 0)),
                pl.BlockSpec(
                    (1, rows, cols),
                    lambda i, place: (place[i] // per_panel, 0, place[i] % per_panel),
                ),
            ],
            out_specs=[
                pair,
                pair,
                single,
                single,
                pl.BlockSpec((width, cols), lambda i, place: (0, 0)),
            ],
        ),
        compiler_params=pltpu.CompilerParams(vmem_limit_bytes=40 * 2**20),
        cost_estimate=pl.CostEstimate(
            flops=8 * rows * width * cols,
            transcendentals=0,
            bytes_accessed=8 * rows * cols + 8 * width * cols + 2 * width * rows,
        ),
    )(place, grad, dense)


class Places:
    def __init__(self, n_section, n_rep):
        self.n_section, self.n_rep = n_section, n_rep
        self.depth = n_section // 4
        self.span = self.depth // n_rep
        self.panels = n_section // n_rep

    def devices(self):
        for section in range(self.n_section):
            for rep in range(self.n_rep):
                yield section // 4, section // 2 % 2, section % 2, rep

    def flat(self, z, y, x, rep):
        return ((z * 2 + y) * 2 + x) * self.n_rep + rep

    def wants(self, z, rep):
        return rep * self.span <= z < (rep + 1) * self.span

    def heading(self, rep):
        return 1 if rep < self.n_rep / 2 else -1

    def flow(self, step, way):
        pairs = []
        for z, y, x, rep in self.devices():
            head = way * self.heading(rep)
            source = z - head * (step - 1)
            if 0 <= z + head < self.depth and self.wants(source, rep):
                pairs.append((self.flat(z, y, x, rep), self.flat(z + head, y, x, rep)))
        return pairs

    def source(self, step, z, rep):
        for source in sorted({z - step, z + step}):
            if 0 <= source < self.depth and self.wants(source, rep):
                return source
        return None

    def across(self, step, axis):
        return [
            (self.flat(z, y, x, rep), self.flat(z, y ^ (axis == "y"), x ^ (axis == "x"), rep))
            for z, y, x, rep in self.devices()
            if step is None or self.source(step, z, rep) is not None
        ]

    def order(self, z):
        near_end = z < self.depth / 2
        return sorted(
            range(self.depth), key=lambda d: (-abs(d - z), (d < z) if near_end else (d > z))
        )

    def up_dest(self, step, z):
        dest = self.depth - step + z
        return dest if z < dest < self.depth else None

    def down_dest(self, step, z):
        dest = z - self.depth + step
        return dest if 0 <= dest < z else None

    def table(self):
        rows = []
        for z, y, x, rep in self.devices():
            row = []
            for step in range(self.depth):
                source = self.source(step, z, rep)
                if source is None:
                    row += [0, 0, 0, 0, 0]
                else:
                    base = (source - rep * self.span) * 4
                    row += [1] + [base + 2 * b + a for b, a in ((y, x), (y, 1 - x), (1 - y, x), (1 - y, 1 - x))]
            for dest in self.order(z):
                row += [dest * 4 + 2 * b + a for b, a in ((1 - y, 1 - x), (y, 1 - x), (1 - y, x), (y, x))]
            rows.append(row)
        return np.array(rows, np.int32)


def shards(sizes, features, weight, tile_values, tile_rows, tile_cols, tile_count, cotangent):
    places = Places(*sizes)
    depth, n_rep = places.depth, places.n_rep
    block_rows, width = features.shape
    cols = block_rows * places.panels // places.n_section
    section, rep = lax.axis_index("section"), lax.axis_index("rep")
    z = section // 4
    table = lax.dynamic_index_in_dim(
        jnp.asarray(places.table()), section * n_rep + rep, keepdims=False
    )
    send = lambda value, pairs: lax.ppermute(value, BOTH, pairs)
    rep_pairs = lambda shift: [
        (places.flat(a, b, c, r), places.flat(a, b, c, (r + shift) % n_rep))
        for a, b, c, r in places.devices()
    ]

    half = block_rows // 2
    fence = lax.optimization_barrier

    def forward_step(step, total, dense, arrival):
        with jax.named_scope("forward"):
            return forward_part(table[5 * step : 5 * step + 5], total, dense, *arrival)

    arrived = major = minor = features
    crossed = complete = total = None
    tiles = (tile_values[0], tile_rows[0], tile_cols[0], tile_count[0])
    for phase in range(depth + 1):
        next_arrived = next_crossed = next_complete = None
        if phase + 1 < depth:
            with jax.named_scope("features_along_z"):
                parts = []
                pairs = places.flow(phase + 1, 1)
                if pairs:
                    major = send(major, pairs)
                    parts.append(major)
                pairs = places.flow(phase + 1, -1)
                if pairs:
                    minor = send(minor, pairs)
                    parts.append(minor)
                next_arrived = functools.reduce(jnp.add, parts)
        with jax.named_scope("features_across"):
            if crossed is not None:
                whole, x_side, y_side, x_top, y_bottom = crossed
                to_x, to_y = places.across(phase - 1, "x"), places.across(phase - 1, "y")
                next_complete = (whole, x_side, y_side, send(x_top, to_y), send(y_bottom, to_x))
            if arrived is not None:
                x_side = send(arrived, places.across(phase, "x"))
                y_side = send(arrived, places.across(phase, "y"))
                next_crossed = (arrived, x_side, y_side, x_side[:half], y_side[half:])
        if phase == 0:
            with jax.named_scope("dense_blocks"):
                dense = make_dense(*tiles, block_rows)
        if phase == depth:
            with jax.named_scope("cotangent_rows"):
                held = [
                    send(cotangent, rep_pairs(-shift)) if shift else cotangent
                    for shift in range(n_rep)
                ]
                cot_rows = jnp.roll(jnp.stack(held), rep, axis=0).reshape(block_rows, width)
        if complete is not None:
            total = forward_step(phase - 2, total, dense, complete)
        arrived, crossed, complete, major, minor, total, dense = fence(
            (next_arrived, next_crossed, next_complete, major, minor, total, dense)
        )
    total = forward_step(depth - 1, total, dense, complete)

    with jax.named_scope("partial_sums"):
        shift = 1
        while shift < n_rep:
            sent = total.astype(BF16)
            pairs = [
                (places.flat(a, b, c, r), places.flat(a, b, c, r ^ shift))
                for a, b, c, r in places.devices()
            ]
            total = sent.astype(F32) + send(sent, pairs).astype(F32)
            shift *= 2

    with jax.named_scope("middle"):
        grad, activated, term = middle(rep[None], total, weight, cot_rows, n_rep)

    to_x, to_y = places.across(None, "x"), places.across(None, "y")
    bits = places.n_section.bit_length() - 1

    def backward_step(turn, grad, dense):
        with jax.named_scope("backward"):
            start = 5 * depth + 4 * turn
            return backward_part(table[start : start + 4], grad, dense, cols)

    def chosen_sum(step, way, dest_of, carried):
        pairs, picks = [], {}
        for a, b, c, r in places.devices():
            dest = dest_of(step, a)
            if dest is not None:
                pairs.append((places.flat(a, b, c, r), places.flat(a + way, b, c, r)))
                picks[a] = places.order(a).index(dest)
        chosen = None
        for pick in sorted(set(picks.values())):
            if chosen is None:
                chosen = sums[pick]
            else:
                here = functools.reduce(
                    jnp.logical_or, [z == a for a in picks if picks[a] == pick]
                )
                chosen = jnp.where(here, sums[pick], chosen)
        if carried is not None:
            chosen = chosen + carried.astype(F32)
        return chosen.astype(BF16), pairs

    sums = []
    up = down = waiting = None
    parts = backward_step(0, grad, dense)
    for phase in range(depth + 1):
        next_waiting = next_parts = None
        if phase >= 2:
            to_up = chosen_sum(phase - 1, 1, places.up_dest, up)
            to_down = chosen_sum(phase - 1, -1, places.down_dest, down)
            with jax.named_scope("grads_along_z"):
                up, down = send(*to_up), send(*to_down)
        with jax.named_scope("grads_across"):
            if waiting is not None:
                x_b, y_a, kept = waiting
                last_x, last_y = send(x_b, to_x), send(y_a, to_y)
                sums.append(kept + jnp.stack([last_y, last_x]).astype(F32))
            if parts is not None:
                x_pair, y_pair, x_b, y_a, own = parts
                from_x, from_y = send(x_pair, to_x), send(y_pair, to_y)
                x_b = (x_b.astype(F32) + from_y[0].astype(F32)).astype(BF16)
                y_a = (y_a.astype(F32) + from_x[0].astype(F32)).astype(BF16)
                kept = own.reshape(2, width // 2, cols).astype(F32) + jnp.stack(
                    [from_x[1], from_y[1]]
                ).astype(F32)
                next_waiting = (x_b, y_a, kept)
        if phase < bits:
            with jax.named_scope("weight_grad"):
                flip = 1 << phase
                pairs = [
                    (a * n_rep + r, (a ^ flip) * n_rep + r)
                    for a in range(places.n_section)
                    for r in range(n_rep)
                ]
                term = (term.astype(F32) + send(term, pairs).astype(F32)).astype(BF16)
        if phase + 1 < depth:
            next_parts = backward_step(phase + 1, grad, dense)
        waiting, parts, sums, up, down, term, grad, dense = fence(
            (next_waiting, next_parts, sums, up, down, term, grad, dense)
        )
    with jax.named_scope("grads_out"):
        final = sums[-1] + up.astype(F32) + down.astype(F32)
        feat_grad = final.reshape(width, cols).astype(BF16).T
    with jax.named_scope("weight_grad_out"):
        parts = [send(term, rep_pairs(-shift)) if shift else term for shift in range(n_rep)]
        weight_grad = jnp.roll(jnp.stack(parts), rep, axis=0).reshape(width, width).astype(F32)
    return (activated, feat_grad[None], weight_grad)


def solution(mesh):
    placed = (
        P("section", None),
        P(),
        P("section", "rep", None, None, None),
        P("section", "rep", None),
        P("section", "rep", None),
        P("section", "rep"),
        P(("section", "rep"), None),
    )
    sizes = (mesh.shape["section"], mesh.shape["rep"])
    return jax.shard_map(
        functools.partial(shards, sizes),
        mesh=mesh,
        in_specs=placed,
        out_specs=(P(("section", "rep"), None), P("rep", "section", None), P()),
        check_vma=False,
    )
```

```python
import functools

import jax
import jax.numpy as jnp
from jax import lax
from jax.experimental import pallas as pl
from jax.experimental.pallas import tpu as pltpu
from jax.sharding import PartitionSpec as P

BF16 = jnp.bfloat16
F32 = jnp.float32
BOTH = ("section", "rep")


def dense_kernel(where_ref, count_ref, rows_ref, cols_ref, tiles_ref, out_ref, *send_refs):
    panel = pl.program_id(0)
    size = tiles_ref.shape[-1]
    per_part = out_ref.shape[-1] // size
    out_ref[...] = jnp.zeros_like(out_ref)

    def add_tile(slot, carry):
        row = pl.multiple_of(rows_ref[panel, slot] * size, size)
        tile_col = cols_ref[panel, slot]
        part = tile_col // per_part
        col = pl.multiple_of((tile_col % per_part) * size, size)
        out_ref[part, 0, pl.ds(row, size), pl.ds(col, size)] += tiles_ref[0, slot]
        return carry

    lax.fori_loop(0, count_ref[panel], add_tile, 0)
    for shift, send_ref in enumerate(send_refs, 1):
        send_ref[0] = out_ref[where_ref[0] ^ shift, 0]


def make_dense(where, tiles, rows, cols, count, block_rows, n_rep):
    panels, slots, size, _ = tiles.shape
    part = block_rows // n_rep
    sent = jax.ShapeDtypeStruct((panels, block_rows, part), BF16)
    return pl.pallas_call(
        dense_kernel,
        out_shape=[jax.ShapeDtypeStruct((n_rep, panels, block_rows, part), BF16)]
        + [sent] * (n_rep - 1),
        grid_spec=pltpu.PrefetchScalarGridSpec(
            num_scalar_prefetch=4,
            grid=(panels,),
            in_specs=[pl.BlockSpec((1, slots, size, size), lambda p, *_: (p, 0, 0, 0))],
            out_specs=[pl.BlockSpec((n_rep, 1, block_rows, part), lambda p, *_: (0, p, 0, 0))]
            + [pl.BlockSpec((1, block_rows, part), lambda p, *_: (p, 0, 0))] * (n_rep - 1),
        ),
        compiler_params=pltpu.CompilerParams(vmem_limit_bytes=40 * 2**20),
        cost_estimate=pl.CostEstimate(
            flops=0,
            transcendentals=0,
            bytes_accessed=tiles.size * 2 + panels * block_rows * block_rows * 3,
        ),
    )(where, count, rows, cols, tiles)


def forward_kernel(offset, n_units, has_total, where_ref, *refs):
    dense_ref, others_ref = refs[:2]
    units = refs[2 : 2 + n_units]
    refs = refs[2 + n_units :]
    total_ref, refs = (refs[0], refs[1:]) if has_total else (None, refs)
    out_ref, sum_ref, a_buf, u_buf, sems = refs
    _, panels, _, part = dense_ref.shape
    rep = where_ref[0]

    def a_copy(source, slot, side):
        target = a_buf.at[slot, :, pl.ds(side * part, part)]
        return pltpu.make_async_copy(source, target, sems.at[0, slot, side])

    def u_copy(source, slot, side):
        target = u_buf.at[slot, pl.ds(side * part, part), :]
        return pltpu.make_async_copy(source, target, sems.at[1, slot, side])

    def fetch(pair, slot):
        for side in range(2):
            place = where_ref[offset + 2 * pair + side]
            owner, panel = place // panels, place % panels
            mine = owner == rep
            turn = jnp.maximum((owner ^ rep) - 1, 0)

            @pl.when(mine)
            def _():
                a_copy(dense_ref.at[rep, panel], slot, side).start()

            @pl.when(jnp.logical_not(mine))
            def _():
                a_copy(others_ref.at[turn, panel], slot, side).start()

            for number in range(side, n_units, 2):

                @pl.when(pair == number // 2)
                def _():
                    u_copy(units[number], slot, side).start()

    pairs = n_units // 2
    fetch(0, 0)
    sum_ref[...] = total_ref[...] if has_total else jnp.zeros_like(sum_ref)

    def step(pair, carry):
        slot = pair % 2

        @pl.when(pair + 1 < pairs)
        def _():
            fetch(pair + 1, 1 - slot)

        for side in range(2):
            a_copy(dense_ref.at[0, 0], slot, side).wait()
            u_copy(units[0], slot, side).wait()
        sum_ref[...] += jnp.dot(a_buf[slot], u_buf[slot], preferred_element_type=F32)
        return carry

    lax.fori_loop(0, pairs, step, 0)
    out_ref[...] = sum_ref[...].astype(out_ref.dtype)


def forward_part(where, offset, units, total, dense, others, kind):
    part, width = units[0].shape
    rows = dense.shape[2]
    hbm = pl.BlockSpec(memory_space=pl.ANY)
    whole = pl.BlockSpec((rows, width), lambda i, where: (0, 0))
    has_total = total is not None
    n_units = len(units)
    return pl.pallas_call(
        functools.partial(forward_kernel, offset, n_units, has_total),
        out_shape=jax.ShapeDtypeStruct((rows, width), kind),
        grid_spec=pltpu.PrefetchScalarGridSpec(
            num_scalar_prefetch=1,
            grid=(1,),
            in_specs=[hbm] * (2 + n_units) + [whole] * has_total,
            out_specs=whole,
            scratch_shapes=[
                pltpu.VMEM((rows, width), F32),
                pltpu.VMEM((2, rows, 2 * part), BF16),
                pltpu.VMEM((2, 2 * part, width), BF16),
                pltpu.SemaphoreType.DMA((2, 2, 2)),
            ],
        ),
        compiler_params=pltpu.CompilerParams(vmem_limit_bytes=50 * 2**20),
        cost_estimate=pl.CostEstimate(
            flops=2 * n_units * rows * part * width,
            transcendentals=0,
            bytes_accessed=n_units * rows * part * 2 + 8 * rows * width,
        ),
    )(where, dense, others, *units, *([total] if has_total else []))


def middle_kernel(
    where_ref, mine_ref, other_ref, weight_ref, cot_ref, grad_ref, act_ref, term_ref, sum_ref
):
    agg = (mine_ref[...].astype(F32) + other_ref[...].astype(F32)).astype(BF16)
    pre = jnp.dot(agg, weight_ref[...], preferred_element_type=F32)
    sigma = jax.nn.sigmoid(pre)
    act_ref[...] = (pre * sigma).astype(BF16)
    slope = cot_ref[...].astype(F32) * sigma * (1.0 + pre * (1.0 - sigma))
    pre_grad = slope.astype(BF16)
    grad_ref[...] = lax.dot_general(
        weight_ref[...], pre_grad, (((1,), (1,)), ((), ())), preferred_element_type=F32
    ).astype(BF16)
    term = lax.dot_general(
        agg, pre_grad, (((0,), (0,)), ((), ())), preferred_element_type=F32
    )
    step = pl.program_id(0)

    @pl.when(step == 0)
    def _():
        sum_ref[...] = term

    @pl.when(step > 0)
    def _():
        sum_ref[...] += term

    @pl.when(step == pl.num_programs(0) - 1)
    def _():
        size = term_ref.shape[0]
        start = pl.multiple_of(where_ref[0] * size, size)
        term_ref[...] = sum_ref[pl.ds(start, size), :].astype(BF16)


def middle(where, mine, other, weight, cotangent, n_rep):
    rows, width = mine.shape
    part = rows // n_rep
    block = lambda i, where: ((where[0] + 1 + i) % n_rep, 0)
    last = pl.BlockSpec((part, width), lambda i, where: (0, 0))
    return pl.pallas_call(
        middle_kernel,
        out_shape=[
            jax.ShapeDtypeStruct((width, rows), BF16),
            jax.ShapeDtypeStruct((part, width), BF16),
            jax.ShapeDtypeStruct((width // n_rep, width), BF16),
        ],
        grid_spec=pltpu.PrefetchScalarGridSpec(
            num_scalar_prefetch=1,
            grid=(n_rep,),
            in_specs=[
                pl.BlockSpec((part, width), block),
                pl.BlockSpec((part, width), block),
                pl.BlockSpec((width, width), lambda i, where: (0, 0)),
                pl.BlockSpec((part, width), block),
            ],
            out_specs=[
                pl.BlockSpec((width, part), lambda i, where: (0, block(i, where)[0])),
                last,
                pl.BlockSpec((width // n_rep, width), lambda i, where: (0, 0)),
            ],
            scratch_shapes=[pltpu.VMEM((width, width), F32)],
        ),
        compiler_params=pltpu.CompilerParams(vmem_limit_bytes=40 * 2**20),
        cost_estimate=pl.CostEstimate(
            flops=6 * rows * width * width,
            transcendentals=rows * width,
            bytes_accessed=rows * width * 10,
        ),
    )(where, mine, other, weight, cotangent)


def backward_kernel(where_ref, grad_ref, a_ref, *out_refs):
    chunk = jnp.dot(grad_ref[...], a_ref[0, 0], preferred_element_type=F32).astype(BF16)
    for number, out_ref in enumerate(out_refs):

        @pl.when(pl.program_id(0) == number)
        def _():
            out_ref[...] = chunk


def backward_part(where, offset, count, grad, dense):
    width, rows = grad.shape
    n_rep, _, _, cols = dense.shape

    def a_block(i, where):
        place = where[offset + i]
        return (place % n_rep, place // n_rep, 0, 0)

    return pl.pallas_call(
        backward_kernel,
        out_shape=[jax.ShapeDtypeStruct((width, cols), BF16)] * count,
        grid_spec=pltpu.PrefetchScalarGridSpec(
            num_scalar_prefetch=1,
            grid=(count,),
            in_specs=[
                pl.BlockSpec((width, rows), lambda i, where: (0, 0)),
                pl.BlockSpec((1, 1, rows, cols), a_block),
            ],
            out_specs=[pl.BlockSpec((width, cols), lambda i, where: (0, 0))] * count,
        ),
        compiler_params=pltpu.CompilerParams(vmem_limit_bytes=50 * 2**20),
        cost_estimate=pl.CostEstimate(
            flops=2 * count * rows * width * cols,
            transcendentals=0,
            bytes_accessed=2 * count * rows * cols + 2 * count * width * cols + 2 * width * rows,
        ),
    )(where, grad, dense)


def shards(sizes, features, weight, tile_values, tile_rows, tile_cols, tile_count, cotangent):
    n_section, n_rep = sizes
    block_rows, width = features.shape
    part = block_rows // n_rep
    section, rep = lax.axis_index("section"), lax.axis_index("rep")

    X, Y, Z = 1, 2, 4
    pair_count = n_section // 8
    low_bit = lambda mask: mask & -mask

    def flip(value, mask, rep_mask=0):
        pairs = [
            (s * n_rep + r, (s ^ mask) * n_rep + (r ^ rep_mask))
            for s in range(n_section)
            for r in range(n_rep)
        ]
        return lax.ppermute(value, BOTH, pairs)

    def gather_rep(value):
        held = [value] + [flip(value, 0, other) for other in range(1, n_rep)]
        order = rep ^ jnp.arange(n_rep)
        if n_rep == 2:
            held = [jnp.where(rep == 0, held[0], held[1]), jnp.where(rep == 0, held[1], held[0])]
            return jnp.concatenate(held)
        return jnp.stack(held)[order].reshape(-1, width)

    live = {}

    def close(*open_names):
        names = [name for name in live if name not in open_names]
        live.update(zip(names, lax.optimization_barrier([live[name] for name in names])))

    masks, offsets = [], {}

    def plan(name, wanted):
        offsets[name] = 1 + len(masks)
        masks.extend(wanted)

    for pair in range(pair_count):
        even, odd = 2 * pair * Z, (2 * pair + 1) * Z
        plan(("units", pair), [even, even + X, even + Y, odd, odd + X, odd + Y])
        plan(("crossed", pair), [even + X + Y, odd + X + Y])
        plan(("first", pair), [odd + X + Y, even + X + Y])
        plan(("odd", pair), [odd + X, odd + Y, odd])
        plan(("even", pair), [even + X, even + Y, even])
    where = jnp.concatenate([rep[None], section ^ jnp.array(masks, jnp.int32)]).astype(jnp.int32)

    def forward_step(names, units, total, kind=F32):
        with jax.named_scope("forward"):
            return forward_part(
                where, offsets[names], units, total, live["dense"], live["others"], kind
            )

    live[0] = lax.dynamic_slice_in_dim(features, rep * part, part, axis=0)
    total = None
    for pair in range(pair_count):
        even, odd = 2 * pair * Z, (2 * pair + 1) * Z
        later = even + 2 * Z
        last = pair + 1 == pair_count

        with jax.named_scope("features_across"):
            live["even_x"], live["even_y"] = flip(live[even], X), flip(live[even], Y)
        with jax.named_scope("features_along_z"):
            live[odd] = flip(live[even], Z)
        if pair == 0:
            with jax.named_scope("dense_blocks"):
                live["dense"], *live["sent"] = make_dense(
                    where,
                    tile_values[0],
                    tile_rows[0],
                    tile_cols[0],
                    tile_count[0],
                    block_rows,
                    n_rep,
                )
        else:
            live["total"] = forward_step(*waiting, live.pop("waiting"), live.get("total"))
        close()

        with jax.named_scope("features_across"):
            live["odd_x"], live["odd_y"] = flip(live[odd], X), flip(live[odd], Y)
        if pair == 0:
            with jax.named_scope("dense_exchange"):
                others = [flip(value, 0, n) for n, value in enumerate(live.pop("sent"), 1)]
                live["others"] = others[0][None] if n_rep == 2 else jnp.stack(others)
        if not last:
            with jax.named_scope("features_along_z"):
                live[later] = flip(live[later - low_bit(later)], low_bit(later))
        if last:
            with jax.named_scope("cotangent_rows"):
                live["cotangent"] = gather_rep(cotangent)
        close(*([] if last else [later]), *([] if pair else ["others"]))

        with jax.named_scope("features_across"):
            crossed = [flip(live["even_x"], Y), flip(live["odd_y"], X)]
        units = [live[even], live.pop("even_x"), live.pop("even_y")]
        units += [live[odd], live.pop("odd_x"), live.pop("odd_y")]
        if pair > 0:
            live["total"] = forward_step(("units", pair), units, live["total"])
            live["waiting"] = crossed
            waiting = [("crossed", pair)]
        else:
            live["waiting"] = units + crossed
            waiting = [("units", pair)]
        close()
    partial = forward_step(*waiting, live["waiting"], live.get("total"), BF16)

    with jax.named_scope("partial_sums"):
        other = flip(partial, 0, 1)
        for bit in range(1, n_rep.bit_length() - 1):
            partial = (partial.astype(F32) + other.astype(F32)).astype(BF16)
            other = flip(partial, 0, 1 << bit)

    with jax.named_scope("middle"):
        grad, activated, term = middle(where, partial, other, weight, live["cotangent"], n_rep)

    def backward_step(name, count):
        with jax.named_scope("backward"):
            return backward_part(where, offsets[name], count, live["grad"], live["dense"])

    add = lambda *values: functools.reduce(jnp.add, [value.astype(F32) for value in values])
    term_masks = [*(1 << bit for bit in range(2, n_section.bit_length() - 1)), X, Y]

    def end_phase(*open_names):
        if term_masks:
            with jax.named_scope("weight_grad"):
                mask = term_masks.pop(0)
                live["term"] = add(live["term"], flip(live["term"], mask)).astype(BF16)
        elif "weight_grad" not in live:
            with jax.named_scope("weight_grad"):
                live["weight_grad"] = gather_rep(live.pop("term"))
        close(*open_names)

    live = {"grad": grad, "dense": live["dense"], "term": term}
    live["first"] = backward_step(("first", pair_count - 1), 2)
    for pair in reversed(range(pair_count)):
        even = 2 * pair * Z
        passing = [name for name in live if isinstance(name, tuple)]

        with jax.named_scope("grads_across"):
            odd_diag, even_diag = live.pop("first")
            live["odd_diag"], live["even_diag"] = flip(odd_diag, Y), flip(even_diag, X)
        live["odd"] = backward_step(("odd", pair), 3)
        if "passed" in live:
            with jax.named_scope("grads_along_z"):
                mask = low_bit(even + 2 * Z)
                target = even + 2 * Z - mask
                live["to", target, mask] = flip(live.pop("passed"), mask)
                passing = [("to", target, mask)]
        end_phase(*passing)

        with jax.named_scope("grads_across"):
            to_x, to_y, own = live.pop("odd")
            to_x = add(to_x, live.pop("odd_diag")).astype(BF16)
            live["odd_sum"] = [own, flip(to_x, X), flip(to_y, Y)]
        live["even"] = backward_step(("even", pair), 3)
        end_phase()

        with jax.named_scope("grads_across"):
            to_x, to_y, own = live.pop("even")
            to_y = add(to_y, live.pop("even_diag")).astype(BF16)
            live["even_sum"] = [own, flip(to_x, X), flip(to_y, Y)]
        with jax.named_scope("grads_along_z"):
            odd_sum = add(*live.pop("odd_sum")).astype(BF16)
            live["even_sum"].append(flip(odd_sum, Z))
        if pair > 0:
            live["first"] = backward_step(("first", pair - 1), 2)
        end_phase()
        arrived = [name for name in live if isinstance(name, tuple) and name[1] == even]
        total = add(*live.pop("even_sum"), *(live.pop(name) for name in arrived)).astype(BF16)
        if pair > 0:
            live["passed"] = total
    with jax.named_scope("grads_out"):
        feat_grad = total.T
    return (activated, feat_grad[None], live["weight_grad"].astype(F32))


def solution(mesh):
    placed = (
        P("section", None),
        P(),
        P("section", "rep", None, None, None),
        P("section", "rep", None),
        P("section", "rep", None),
        P("section", "rep"),
        P(("section", "rep"), None),
    )
    sizes = (mesh.shape["section"], mesh.shape["rep"])
    return jax.shard_map(
        functools.partial(shards, sizes),
        mesh=mesh,
        in_specs=placed,
        out_specs=(P(("section", "rep"), None), P("rep", "section", None), P()),
        check_vma=False,
    )
```

```python
import functools

import jax
import jax.numpy as jnp
from jax import lax
from jax.experimental import pallas as pl
from jax.experimental.pallas import tpu as pltpu
from jax.sharding import PartitionSpec as P

BF16 = jnp.bfloat16
F32 = jnp.float32
BOTH = ("section", "rep")


def dense_kernel(first, where_ref, count_ref, rows_ref, cols_ref, tiles_ref, *refs):
    out_ref, *send_refs = refs if first == 0 else refs[1:]
    panel = first + pl.program_id(0)
    size = tiles_ref.shape[-1]
    per_part = out_ref.shape[-1] // size
    out_ref[...] = jnp.zeros_like(out_ref)

    def add_tile(slot, carry):
        row = pl.multiple_of(rows_ref[panel, slot] * size, size)
        tile_col = cols_ref[panel, slot]
        part = tile_col // per_part
        col = pl.multiple_of((tile_col % per_part) * size, size)
        out_ref[part, 0, pl.ds(row, size), pl.ds(col, size)] += tiles_ref[0, slot]
        return carry

    lax.fori_loop(0, count_ref[panel], add_tile, 0)
    for shift, send_ref in enumerate(send_refs, 1):
        send_ref[0] = out_ref[where_ref[0] ^ shift, 0]


def make_dense(first, before, where, tiles, rows, cols, count, block_rows, n_rep):
    panels, slots, size, _ = tiles.shape
    half = panels // 2
    part = block_rows // n_rep
    sent = jax.ShapeDtypeStruct((half, block_rows, part), BF16)
    at = lambda p: first + p
    return pl.pallas_call(
        functools.partial(dense_kernel, first),
        out_shape=[jax.ShapeDtypeStruct((n_rep, panels, block_rows, part), BF16)]
        + [sent] * (n_rep - 1),
        grid_spec=pltpu.PrefetchScalarGridSpec(
            num_scalar_prefetch=4,
            grid=(half,),
            in_specs=[pl.BlockSpec((1, slots, size, size), lambda p, *_: (at(p), 0, 0, 0))]
            + [pl.BlockSpec(memory_space=pl.ANY)] * (first > 0),
            out_specs=[pl.BlockSpec((n_rep, 1, block_rows, part), lambda p, *_: (0, at(p), 0, 0))]
            + [pl.BlockSpec((1, block_rows, part), lambda p, *_: (p, 0, 0))] * (n_rep - 1),
        ),
        input_output_aliases={5: 0} if first else {},
        compiler_params=pltpu.CompilerParams(vmem_limit_bytes=36 * 2**20),
        cost_estimate=pl.CostEstimate(
            flops=0,
            transcendentals=0,
            bytes_accessed=tiles.size + half * block_rows * block_rows * 3,
        ),
    )(where, count, rows, cols, tiles, *([before] if first else []))


def forward_kernel(offset, n_units, n_others, has_total, where_ref, dense_ref, *refs):
    others, refs = refs[:n_others], refs[n_others:]
    units, refs = refs[:n_units], refs[n_units:]
    total_ref, refs = (refs[0], refs[1:]) if has_total else (None, refs)
    out_ref, sum_ref, a_buf, u_buf, sems, sum_sem = refs
    _, panels, _, part = dense_ref.shape
    some = others[0].shape[0]
    rep = where_ref[0]

    def a_copy(source, slot, side):
        target = a_buf.at[slot, :, pl.ds(side * part, part)]
        return pltpu.make_async_copy(source, target, sems.at[0, slot, side])

    def u_copy(source, slot, side):
        target = u_buf.at[slot, pl.ds(side * part, part), :]
        return pltpu.make_async_copy(source, target, sems.at[1, slot, side])

    def fetch(pair, slot):
        for side in range(2):
            place = where_ref[offset + 2 * pair + side]
            owner, panel = place // panels, place % panels
            turn = ((owner ^ rep) - 1) * (panels // some) + panel // some

            @pl.when(owner == rep)
            def _():
                a_copy(dense_ref.at[rep, panel], slot, side).start()

            for number, other_ref in enumerate(others):

                @pl.when((owner != rep) & (turn == number))
                def _():
                    a_copy(other_ref.at[panel % some], slot, side).start()

            for number in range(side, n_units, 2):

                @pl.when(pair == number // 2)
                def _():
                    u_copy(units[number], slot, side).start()

    pairs = n_units // 2
    fetch(0, 0)
    if has_total:
        load = pltpu.make_async_copy(total_ref, sum_ref, sum_sem)
        load.start()
        load.wait()
    else:
        sum_ref[...] = jnp.zeros_like(sum_ref)

    def step(pair, carry):
        slot = pair % 2

        @pl.when(pair + 1 < pairs)
        def _():
            fetch(pair + 1, 1 - slot)

        for side in range(2):
            a_copy(dense_ref.at[0, 0], slot, side).wait()
            u_copy(units[0], slot, side).wait()
        sum_ref[...] += jnp.dot(a_buf[slot], u_buf[slot], preferred_element_type=F32)
        return carry

    lax.fori_loop(0, pairs, step, 0)
    if out_ref.dtype == F32:
        store = pltpu.make_async_copy(sum_ref, out_ref, sum_sem)
        store.start()
        store.wait()
    else:
        out_ref[...] = sum_ref[...].astype(out_ref.dtype)


def forward_part(where, offset, units, total, dense, others, kind):
    part, width = units[0].shape
    rows = dense.shape[2]
    hbm = pl.BlockSpec(memory_space=pl.ANY)
    has_total = total is not None
    n_units, n_others = len(units), len(others)
    return pl.pallas_call(
        functools.partial(forward_kernel, offset, n_units, n_others, has_total),
        out_shape=jax.ShapeDtypeStruct((rows, width), kind),
        grid_spec=pltpu.PrefetchScalarGridSpec(
            num_scalar_prefetch=1,
            grid=(1,),
            in_specs=[hbm] * (1 + n_others + n_units + has_total),
            out_specs=hbm if kind == F32 else pl.BlockSpec((rows, width), lambda i, where: (0, 0)),
            scratch_shapes=[
                pltpu.VMEM((rows, width), F32),
                pltpu.VMEM((2, rows, 2 * part), BF16),
                pltpu.VMEM((2, 2 * part, width), BF16),
                pltpu.SemaphoreType.DMA((2, 2, 2)),
                pltpu.SemaphoreType.DMA,
            ],
        ),
        compiler_params=pltpu.CompilerParams(vmem_limit_bytes=36 * 2**20),
        cost_estimate=pl.CostEstimate(
            flops=2 * n_units * rows * part * width,
            transcendentals=0,
            bytes_accessed=n_units * rows * part * 2 + 8 * rows * width,
        ),
    )(where, dense, *others, *units, *([total] if has_total else []))


def middle_kernel(
    n_rep, where_ref, mine_ref, other_ref, weight_ref, cot_ref, a_ref, grad_ref, act_ref, *refs
):
    term_refs, (odd_ref, even_ref, sum_ref) = refs[:-3], refs[-3:]
    step = pl.program_id(0)
    part = mine_ref.shape[0]

    @pl.when(step < n_rep)
    def _():
        agg = (mine_ref[...].astype(F32) + other_ref[...].astype(F32)).astype(BF16)
        pre = jnp.dot(agg, weight_ref[...], preferred_element_type=F32)
        sigma = jax.nn.sigmoid(pre)
        act_ref[...] = (pre * sigma).astype(BF16)
        slope = cot_ref[...].astype(F32) * sigma * (1.0 + pre * (1.0 - sigma))
        pre_grad = slope.astype(BF16)
        block = (where_ref[0] + 1 + step) % n_rep
        grad_ref[:, pl.ds(pl.multiple_of(block * part, part), part)] = lax.dot_general(
            weight_ref[...], pre_grad, (((1,), (1,)), ((), ())), preferred_element_type=F32
        ).astype(BF16)
        term = lax.dot_general(
            agg, pre_grad, (((0,), (0,)), ((), ())), preferred_element_type=F32
        )

        @pl.when(step == 0)
        def _():
            sum_ref[...] = term

        @pl.when(step > 0)
        def _():
            sum_ref[...] += term

    @pl.when(step >= n_rep)
    def _():
        chunk = jnp.dot(grad_ref[...], a_ref[0, 0], preferred_element_type=F32).astype(BF16)

        @pl.when(step == n_rep)
        def _():
            odd_ref[...] = chunk
            z = where_ref[1] // 4
            size = term_refs[0].shape[0]
            for number, term_ref in enumerate(term_refs):
                start = (where_ref[0] * len(term_refs) + (z ^ number)) * size
                term_ref[...] = sum_ref[pl.ds(pl.multiple_of(start, size), size), :].astype(BF16)

        @pl.when(step > n_rep)
        def _():
            even_ref[...] = chunk


def middle(where, offset, mine, other, weight, cotangent, dense, n_rep, depth):
    rows, width = mine.shape
    part = rows // n_rep
    size = width // n_rep // depth
    block = lambda i, where: ((where[0] + 1 + jnp.minimum(i, n_rep - 1)) % n_rep, 0)
    fixed = lambda *shape: pl.BlockSpec(shape, lambda i, where: (0, 0))
    kept = lambda *shape: jax.ShapeDtypeStruct(shape, BF16)

    def a_block(i, where):
        place = where[offset + jnp.maximum(i - n_rep, 0)]
        return (place % n_rep, place // n_rep, 0, 0)

    return pl.pallas_call(
        functools.partial(middle_kernel, n_rep),
        out_shape=[kept(width, rows), kept(part, width)]
        + [kept(size, width)] * depth
        + [kept(width, part)] * 2,
        grid_spec=pltpu.PrefetchScalarGridSpec(
            num_scalar_prefetch=1,
            grid=(n_rep + 2,),
            in_specs=[
                pl.BlockSpec((part, width), block),
                pl.BlockSpec((part, width), block),
                fixed(width, width),
                pl.BlockSpec((part, width), block),
                pl.BlockSpec((1, 1, rows, part), a_block),
            ],
            out_specs=[fixed(width, rows), fixed(part, width)]
            + [fixed(size, width)] * depth
            + [fixed(width, part)] * 2,
            scratch_shapes=[pltpu.VMEM((width, width), F32)],
        ),
        compiler_params=pltpu.CompilerParams(vmem_limit_bytes=36 * 2**20),
        cost_estimate=pl.CostEstimate(
            flops=6 * rows * width * width + 4 * rows * width * part,
            transcendentals=rows * width,
            bytes_accessed=rows * width * 12,
        ),
    )(where, mine, other, weight, cotangent, dense)


def backward_kernel(where_ref, grad_ref, a_ref, *out_refs):
    chunk = jnp.dot(grad_ref[...], a_ref[0, 0], preferred_element_type=F32).astype(BF16)
    for number, out_ref in enumerate(out_refs):

        @pl.when(pl.program_id(0) == number)
        def _():
            out_ref[...] = chunk


def backward_part(where, offset, count, grad, dense):
    width, rows = grad.shape
    n_rep, _, _, cols = dense.shape

    def a_block(i, where):
        place = where[offset + i]
        return (place % n_rep, place // n_rep, 0, 0)

    return pl.pallas_call(
        backward_kernel,
        out_shape=[jax.ShapeDtypeStruct((width, cols), BF16)] * count,
        grid_spec=pltpu.PrefetchScalarGridSpec(
            num_scalar_prefetch=1,
            grid=(count,),
            in_specs=[
                pl.BlockSpec((width, rows), lambda i, where: (0, 0)),
                pl.BlockSpec((1, 1, rows, cols), a_block),
            ],
            out_specs=[pl.BlockSpec((width, cols), lambda i, where: (0, 0))] * count,
        ),
        compiler_params=pltpu.CompilerParams(vmem_limit_bytes=36 * 2**20),
        cost_estimate=pl.CostEstimate(
            flops=2 * count * rows * width * cols,
            transcendentals=0,
            bytes_accessed=2 * count * rows * cols + 2 * count * width * cols + 2 * width * rows,
        ),
    )(where, grad, dense)


def final_kernel(*refs):
    *parts, out_ref = refs
    total = functools.reduce(jnp.add, [part[...].astype(F32) for part in parts])
    out_ref[0] = total.T.astype(BF16)


def final_sum(parts):
    width, cols = parts[0].shape
    return pl.pallas_call(
        final_kernel,
        out_shape=jax.ShapeDtypeStruct((1, cols, width), BF16),
        compiler_params=pltpu.CompilerParams(vmem_limit_bytes=36 * 2**20),
        cost_estimate=pl.CostEstimate(
            flops=len(parts) * width * cols,
            transcendentals=0,
            bytes_accessed=2 * (len(parts) + 1) * width * cols,
        ),
    )(*parts)


def shards(sizes, features, weight, tile_values, tile_rows, tile_cols, tile_count, cotangent):
    n_section, n_rep = sizes
    block_rows, width = features.shape
    part = block_rows // n_rep
    section, rep = lax.axis_index("section"), lax.axis_index("rep")

    X, Y, Z = 1, 2, 4
    pair_count = n_section // 8
    low_bit = lambda mask: mask & -mask

    def flip(value, mask, rep_mask=0):
        pairs = [
            (s * n_rep + r, (s ^ mask) * n_rep + (r ^ rep_mask))
            for s in range(n_section)
            for r in range(n_rep)
        ]
        return lax.ppermute(value, BOTH, pairs)

    def gather_rep(value):
        held = [value] + [flip(value, 0, other) for other in range(1, n_rep)]
        order = rep ^ jnp.arange(n_rep)
        if n_rep == 2:
            held = [jnp.where(rep == 0, held[0], held[1]), jnp.where(rep == 0, held[1], held[0])]
            return jnp.concatenate(held)
        return jnp.stack(held)[order].reshape(-1, width)

    live = {}

    def close(*open_names):
        names = [name for name in live if name not in open_names]
        live.update(zip(names, lax.optimization_barrier([live[name] for name in names])))

    masks, offsets = [], {}

    def plan(name, wanted):
        offsets[name] = 2 + len(masks)
        masks.extend(wanted)

    for pair in range(pair_count):
        even, odd = 2 * pair * Z, (2 * pair + 1) * Z
        plan(("units", pair), [even, even + X, even + Y, odd, odd + X, odd + Y])
        plan(("crossed", pair), [even + X + Y, odd + X + Y])
        plan(("first", pair), [odd + X + Y, even + X + Y])
        plan(("odd", pair), [odd + X, odd + Y, odd])
        plan(("even", pair), [even + X, even + Y, even])
    where = jnp.concatenate(
        [rep[None], section[None], section ^ jnp.array(masks, jnp.int32)]
    ).astype(jnp.int32)

    def forward_step(names, units, total, kind=F32):
        with jax.named_scope("forward"):
            return forward_part(
                where, offsets[names], units, total, live["dense"], live["others"], kind
            )

    panels = tile_values.shape[1]
    tiles = (where, tile_values[0], tile_rows[0], tile_cols[0], tile_count[0], block_rows, n_rep)
    live[0] = lax.dynamic_slice_in_dim(features, rep * part, part, axis=0)
    total = None
    for pair in range(pair_count):
        even, odd = 2 * pair * Z, (2 * pair + 1) * Z
        later = even + 2 * Z
        last = pair + 1 == pair_count

        with jax.named_scope("features_across"):
            live["even_x"], live["even_y"] = flip(live[even], X), flip(live[even], Y)
        with jax.named_scope("features_along_z"):
            live[odd] = flip(live[even], Z)
        if pair == 0:
            with jax.named_scope("dense_blocks"):
                live["dense"], *live["sent"] = make_dense(0, None, *tiles)
        else:
            live["total"] = forward_step(*waiting, live.pop("waiting"), live.get("total"))
        close()

        with jax.named_scope("features_across"):
            live["odd_x"], live["odd_y"] = flip(live[odd], X), flip(live[odd], Y)
        if pair == 0:
            with jax.named_scope("dense_exchange"):
                one = [flip(value, 0, n) for n, value in enumerate(live.pop("sent"), 1)]
            with jax.named_scope("dense_blocks"):
                first = panels // 2
                live["dense"], *live["sent"] = make_dense(first, live["dense"], *tiles)
        if not last:
            with jax.named_scope("features_along_z"):
                live[later] = flip(live[later - low_bit(later)], low_bit(later))
        if last:
            with jax.named_scope("cotangent_rows"):
                live["cotangent"] = gather_rep(cotangent)
        close(*([] if last else [later]))

        with jax.named_scope("features_across"):
            crossed = [flip(live["even_x"], Y), flip(live["odd_y"], X)]
        if pair == 0:
            with jax.named_scope("dense_exchange"):
                two = [flip(value, 0, n) for n, value in enumerate(live.pop("sent"), 1)]
                live["others"] = [half for halves in zip(one, two) for half in halves]
        units = [live[even], live.pop("even_x"), live.pop("even_y")]
        units += [live[odd], live.pop("odd_x"), live.pop("odd_y")]
        if pair > 0:
            live["total"] = forward_step(("units", pair), units, live["total"])
            live["waiting"] = crossed
            waiting = [("crossed", pair)]
        else:
            live["waiting"] = units + crossed
            waiting = [("units", pair)]
        close()
    partial = forward_step(*waiting, live["waiting"], live.get("total"), BF16)

    with jax.named_scope("partial_sums"):
        other = flip(partial, 0, 1)
        for bit in range(1, n_rep.bit_length() - 1):
            partial = (partial.astype(F32) + other.astype(F32)).astype(BF16)
            other = flip(partial, 0, 1 << bit)

    depth = n_section // 4
    with jax.named_scope("middle"):
        grad, activated, *terms, odd_diag, even_diag = middle(
            where,
            offsets["first", pair_count - 1],
            partial,
            other,
            weight,
            live["cotangent"],
            live["dense"],
            n_rep,
            depth,
        )

    def backward_step(name, count):
        with jax.named_scope("backward"):
            return backward_part(where, offsets[name], count, live["grad"], live["dense"])

    add = lambda *values: functools.reduce(jnp.add, [value.astype(F32) for value in values])

    def weight_step(phase):
        terms = live["terms"]
        if phase == 0:
            sums = [terms[0]] + [flip(term, Z * n) for n, term in enumerate(terms[1:], 1)]
            live["terms"] = [add(*sums).astype(BF16)]
        elif phase == 1:
            sums = [terms[0]] + [flip(terms[0], mask) for mask in (X, Y, X + Y)]
            live["terms"] = [(add(*sums[:2]) + add(*sums[2:])).astype(BF16)]
        elif 1 << phase - 2 < depth:
            live["terms"] = terms + [flip(term, Z << phase - 2) for term in terms]
        elif "weight_grad" not in live:
            z = section // 4
            rows = jnp.stack(terms)[z ^ jnp.arange(depth)].reshape(-1, width)
            live["weight_grad"] = gather_rep(rows).astype(F32)

    phases = iter(range(3 * pair_count))

    def end_phase(*open_names):
        with jax.named_scope("weight_grad"):
            weight_step(next(phases))
        close(*open_names)

    live = {"grad": grad, "dense": live["dense"], "terms": terms}
    live["first"] = [odd_diag, even_diag]
    for pair in reversed(range(pair_count)):
        even = 2 * pair * Z
        passing = [name for name in live if isinstance(name, tuple)]

        with jax.named_scope("grads_across"):
            odd_diag, even_diag = live.pop("first")
            live["odd_diag"], live["even_diag"] = flip(odd_diag, Y), flip(even_diag, X)
        live["odd"] = backward_step(("odd", pair), 3)
        if "passed" in live:
            with jax.named_scope("grads_along_z"):
                mask = low_bit(even + 2 * Z)
                target = even + 2 * Z - mask
                live["to", target, mask] = flip(live.pop("passed"), mask)
                passing = [("to", target, mask)]
        end_phase(*passing)

        with jax.named_scope("grads_across"):
            to_x, to_y, own = live.pop("odd")
            to_x = add(to_x, live.pop("odd_diag")).astype(BF16)
            live["odd_sum"] = [own, flip(to_x, X), flip(to_y, Y)]
        live["even"] = backward_step(("even", pair), 3)
        end_phase()

        with jax.named_scope("grads_across"):
            to_x, to_y, own = live.pop("even")
            to_y = add(to_y, live.pop("even_diag")).astype(BF16)
            live["even_sum"] = [own, flip(to_x, X), flip(to_y, Y)]
        with jax.named_scope("grads_along_z"):
            odd_sum = add(*live.pop("odd_sum")).astype(BF16)
            live["even_sum"].append(flip(odd_sum, Z))
        if pair > 0:
            live["first"] = backward_step(("first", pair - 1), 2)
        end_phase()
        arrived = [name for name in live if isinstance(name, tuple) and name[1] == even]
        sums = [*live.pop("even_sum"), *(live.pop(name) for name in arrived)]
        if pair > 0:
            live["passed"] = add(*sums).astype(BF16)
    with jax.named_scope("grads_out"):
        feat_grad = final_sum(sums)
    return (activated, feat_grad, live["weight_grad"])


def solution(mesh):
    placed = (
        P("section", None),
        P(),
        P("section", "rep", None, None, None),
        P("section", "rep", None),
        P("section", "rep", None),
        P("section", "rep"),
        P(("section", "rep"), None),
    )
    sizes = (mesh.shape["section"], mesh.shape["rep"])
    return jax.shard_map(
        functools.partial(shards, sizes),
        mesh=mesh,
        in_specs=placed,
        out_specs=(P(("section", "rep"), None), P("rep", "section", None), P()),
        check_vma=False,
    )
```

```python
import functools

import jax
import jax.numpy as jnp
from jax import lax
from jax.experimental import pallas as pl
from jax.experimental.pallas import tpu as pltpu
from jax.sharding import PartitionSpec as P

BF16 = jnp.bfloat16
F32 = jnp.float32
BOTH = ("section", "rep")


def dense_kernel(first, where_ref, packed_ref, tiles_ref, *refs):
    out_ref = refs[-1]
    panel = first + pl.program_id(0)
    size, slots = tiles_ref.shape[-1], tiles_ref.shape[1]
    row_tiles, per_part = out_ref.shape[2] // size, out_ref.shape[3] // size
    out_ref[...] = jnp.zeros_like(out_ref)

    def add_tile(slot, carry):
        place = packed_ref[panel, slot]
        row = pl.multiple_of(place // row_tiles * size, size)
        tile_col = place % row_tiles
        col = pl.multiple_of(tile_col % per_part * size, size)
        out_ref[tile_col // per_part, 0, pl.ds(row, size), pl.ds(col, size)] += tiles_ref[0, slot]
        return carry

    lax.fori_loop(0, packed_ref[panel, slots], add_tile, 0)


def make_dense(first, before, where, tiles, packed, block_rows, n_rep):
    panels, slots, size, _ = tiles.shape
    half = panels // 2
    part = block_rows // n_rep
    at = lambda p: first + p
    return pl.pallas_call(
        functools.partial(dense_kernel, first),
        out_shape=jax.ShapeDtypeStruct((n_rep, panels, block_rows, part), BF16),
        grid_spec=pltpu.PrefetchScalarGridSpec(
            num_scalar_prefetch=2,
            grid=(half,),
            in_specs=[pl.BlockSpec((1, slots, size, size), lambda p, *_: (at(p), 0, 0, 0))]
            + [pl.BlockSpec(memory_space=pl.ANY)] * (first > 0),
            out_specs=pl.BlockSpec((n_rep, 1, block_rows, part), lambda p, *_: (0, at(p), 0, 0)),
        ),
        input_output_aliases={3: 0} if first else {},
        compiler_params=pltpu.CompilerParams(vmem_limit_bytes=36 * 2**20),
        cost_estimate=pl.CostEstimate(
            flops=0,
            transcendentals=0,
            bytes_accessed=tiles.size // 8,
        ),
    )(where, packed, tiles, *([before] if first else []))


def other_kernel(where_ref, packed_ref, tiles_ref, out_ref):
    panel = pl.program_id(0)
    size, slots = tiles_ref.shape[-1], tiles_ref.shape[1]
    row_tiles, per_part = out_ref.shape[1] // size, out_ref.shape[2] // size
    out_ref[...] = jnp.zeros_like(out_ref)

    def add_tile(slot, carry):
        place = packed_ref[panel, slot]
        row = pl.multiple_of(place // row_tiles * size, size)
        tile_col = place % row_tiles
        col = pl.multiple_of(tile_col % per_part * size, size)

        @pl.when(tile_col // per_part == where_ref[0])
        def _():
            out_ref[0, pl.ds(row, size), pl.ds(col, size)] += tiles_ref[0, slot]

        return carry

    lax.fori_loop(0, packed_ref[panel, slots], add_tile, 0)


def make_other(where, tiles, packed, block_rows, n_rep):
    panels, slots, size, _ = tiles.shape
    part = block_rows // n_rep
    return pl.pallas_call(
        other_kernel,
        out_shape=jax.ShapeDtypeStruct((panels, block_rows, part), BF16),
        grid_spec=pltpu.PrefetchScalarGridSpec(
            num_scalar_prefetch=2,
            grid=(panels,),
            in_specs=[pl.BlockSpec((1, slots, size, size), lambda p, *_: (p, 0, 0, 0))],
            out_specs=pl.BlockSpec((1, block_rows, part), lambda p, *_: (p, 0, 0)),
        ),
        compiler_params=pltpu.CompilerParams(vmem_limit_bytes=36 * 2**20),
        cost_estimate=pl.CostEstimate(
            flops=0,
            transcendentals=0,
            bytes_accessed=tiles.size // 8,
        ),
    )(where, packed, tiles)


def forward_kernel(offset, n_units, n_others, has_total, where_ref, dense_ref, *refs):
    others, refs = refs[:n_others], refs[n_others:]
    units, refs = refs[:n_units], refs[n_units:]
    total_ref, refs = (refs[0], refs[1:]) if has_total else (None, refs)
    out_ref, sum_ref, a_buf, u_buf, sems, sum_sem = refs
    _, panels, _, part = dense_ref.shape
    rep = where_ref[0]

    def a_copy(source, slot, side):
        target = a_buf.at[slot, :, pl.ds(side * part, part)]
        return pltpu.make_async_copy(source, target, sems.at[0, slot, side])

    def u_copy(source, slot, side):
        target = u_buf.at[slot, pl.ds(side * part, part), :]
        return pltpu.make_async_copy(source, target, sems.at[1, slot, side])

    def fetch(pair, slot):
        for side in range(2):
            place = where_ref[offset + 2 * pair + side]
            owner, panel = place // panels, place % panels
            turn = (owner ^ rep) - 1

            @pl.when(owner == rep)
            def _():
                a_copy(dense_ref.at[rep, panel], slot, side).start()

            for number, other_ref in enumerate(others):

                @pl.when((owner != rep) & (turn == number))
                def _():
                    a_copy(other_ref.at[panel], slot, side).start()

            for number in range(side, n_units, 2):

                @pl.when(pair == number // 2)
                def _():
                    u_copy(units[number], slot, side).start()

    pairs = n_units // 2
    fetch(0, 0)
    if has_total:
        load = pltpu.make_async_copy(total_ref, sum_ref, sum_sem)
        load.start()
        load.wait()
    else:
        sum_ref[...] = jnp.zeros_like(sum_ref)

    def step(pair, carry):
        slot = pair % 2

        @pl.when(pair + 1 < pairs)
        def _():
            fetch(pair + 1, 1 - slot)

        for side in range(2):
            a_copy(dense_ref.at[0, 0], slot, side).wait()
            u_copy(units[0], slot, side).wait()
        sum_ref[...] += jnp.dot(a_buf[slot], u_buf[slot], preferred_element_type=F32)
        return carry

    lax.fori_loop(0, pairs, step, 0)
    if out_ref.dtype == F32:
        store = pltpu.make_async_copy(sum_ref, out_ref, sum_sem)
        store.start()
        store.wait()
    else:
        out_ref[...] = sum_ref[...].astype(out_ref.dtype)


def forward_part(where, offset, units, total, dense, others, kind):
    part, width = units[0].shape
    rows = dense.shape[2]
    hbm = pl.BlockSpec(memory_space=pl.ANY)
    has_total = total is not None
    n_units, n_others = len(units), len(others)
    return pl.pallas_call(
        functools.partial(forward_kernel, offset, n_units, n_others, has_total),
        out_shape=jax.ShapeDtypeStruct((rows, width), kind),
        grid_spec=pltpu.PrefetchScalarGridSpec(
            num_scalar_prefetch=1,
            grid=(1,),
            in_specs=[hbm] * (1 + n_others + n_units + has_total),
            out_specs=hbm if kind == F32 else pl.BlockSpec((rows, width), lambda i, where: (0, 0)),
            scratch_shapes=[
                pltpu.VMEM((rows, width), F32),
                pltpu.VMEM((2, rows, 2 * part), BF16),
                pltpu.VMEM((2, 2 * part, width), BF16),
                pltpu.SemaphoreType.DMA((2, 2, 2)),
                pltpu.SemaphoreType.DMA,
            ],
        ),
        compiler_params=pltpu.CompilerParams(vmem_limit_bytes=36 * 2**20),
        cost_estimate=pl.CostEstimate(
            flops=2 * n_units * rows * part * width,
            transcendentals=0,
            bytes_accessed=n_units * rows * part * 2 + 8 * rows * width,
        ),
    )(where, dense, *others, *units, *([total] if has_total else []))


def slopes(mine_ref, other_ref, weight_ref, cot_ref):
    agg = (mine_ref[...].astype(F32) + other_ref[...].astype(F32)).astype(BF16)
    pre = jnp.dot(agg, weight_ref[...], preferred_element_type=F32)
    sigma = jax.nn.sigmoid(pre)
    slope = cot_ref[...].astype(F32) * sigma * (1.0 + pre * (1.0 - sigma))
    return agg, (pre * sigma).astype(BF16), slope.astype(BF16)


def middle_kernel(
    blocks, where_ref, mine_ref, other_ref, weight_ref, cot_ref, a_ref, grad_ref, odd_ref, even_ref
):
    step = pl.program_id(0)
    part = mine_ref.shape[0]

    @pl.when(step < blocks)
    def _():
        _, _, pre_grad = slopes(mine_ref, other_ref, weight_ref, cot_ref)
        grad_ref[:, pl.ds(pl.multiple_of(step * part, part), part)] = lax.dot_general(
            weight_ref[...], pre_grad, (((1,), (1,)), ((), ())), preferred_element_type=F32
        ).astype(BF16)

    @pl.when(step >= blocks)
    def _():
        chunk = jnp.dot(grad_ref[...], a_ref[0, 0], preferred_element_type=F32).astype(BF16)

        @pl.when(step == blocks)
        def _():
            odd_ref[...] = chunk

        @pl.when(step > blocks)
        def _():
            even_ref[...] = chunk


def middle(where, offset, mine, other, weight, cotangent, dense):
    rows, width = mine.shape
    n_rep, _, _, cols = dense.shape
    blocks = 4
    part = rows // blocks
    block = pl.BlockSpec((part, width), lambda i, where: (jnp.minimum(i, blocks - 1), 0))
    fixed = lambda *shape: pl.BlockSpec(shape, lambda i, where: (0, 0))
    kept = lambda *shape: jax.ShapeDtypeStruct(shape, BF16)

    def a_block(i, where):
        place = where[offset + jnp.maximum(i - blocks, 0)]
        return (place % n_rep, place // n_rep, 0, 0)

    return pl.pallas_call(
        functools.partial(middle_kernel, blocks),
        out_shape=[kept(width, rows), kept(width, cols), kept(width, cols)],
        grid_spec=pltpu.PrefetchScalarGridSpec(
            num_scalar_prefetch=1,
            grid=(blocks + 2,),
            in_specs=[
                block,
                block,
                fixed(width, width),
                block,
                pl.BlockSpec((1, 1, rows, cols), a_block),
            ],
            out_specs=[fixed(width, rows), fixed(width, cols), fixed(width, cols)],
        ),
        compiler_params=pltpu.CompilerParams(vmem_limit_bytes=36 * 2**20),
        cost_estimate=pl.CostEstimate(
            flops=4 * rows * width * width + 4 * rows * width * cols,
            transcendentals=rows * width,
            bytes_accessed=rows * width * 12,
        ),
    )(where, mine, other, weight, cotangent, dense)


def term_kernel(n_rep, where_ref, mine_ref, other_ref, weight_ref, cot_ref, act_ref, *refs):
    term_refs, sum_ref = refs[:-1], refs[-1]
    step = pl.program_id(0)
    agg, activated, pre_grad = slopes(mine_ref, other_ref, weight_ref, cot_ref)
    act_ref[...] = activated
    term = lax.dot_general(agg, pre_grad, (((0,), (0,)), ((), ())), preferred_element_type=F32)

    @pl.when(step == 0)
    def _():
        sum_ref[...] = term

    @pl.when(step > 0)
    def _():
        sum_ref[...] += term

    @pl.when(step == n_rep - 1)
    def _():
        z = where_ref[1] // 4
        size = term_refs[0].shape[0]
        for number, term_ref in enumerate(term_refs):
            start = (where_ref[0] * len(term_refs) + (z ^ number)) * size
            term_ref[...] = sum_ref[pl.ds(pl.multiple_of(start, size), size), :].astype(BF16)


def weight_terms(where, mine, other, weight, cotangent, n_rep, depth):
    rows, width = mine.shape
    part = rows // n_rep
    size = width // n_rep // depth
    block = pl.BlockSpec((part, width), lambda i, where: ((where[0] + 1 + i) % n_rep, 0))
    fixed = lambda *shape: pl.BlockSpec(shape, lambda i, where: (0, 0))
    return pl.pallas_call(
        functools.partial(term_kernel, n_rep),
        out_shape=[jax.ShapeDtypeStruct((part, width), BF16)]
        + [jax.ShapeDtypeStruct((size, width), BF16)] * depth,
        grid_spec=pltpu.PrefetchScalarGridSpec(
            num_scalar_prefetch=1,
            grid=(n_rep,),
            in_specs=[block, block, fixed(width, width), block],
            out_specs=[fixed(part, width)] + [fixed(size, width)] * depth,
            scratch_shapes=[pltpu.VMEM((width, width), F32)],
        ),
        compiler_params=pltpu.CompilerParams(vmem_limit_bytes=36 * 2**20),
        cost_estimate=pl.CostEstimate(
            flops=4 * rows * width * width,
            transcendentals=rows * width,
            bytes_accessed=rows * width * 8,
        ),
    )(where, mine, other, weight, cotangent)


def backward_kernel(where_ref, grad_ref, a_ref, *out_refs):
    chunk = jnp.dot(grad_ref[...], a_ref[0, 0], preferred_element_type=F32).astype(BF16)
    for number, out_ref in enumerate(out_refs):

        @pl.when(pl.program_id(0) == number)
        def _():
            out_ref[...] = chunk


def backward_part(where, offset, count, grad, dense):
    width, rows = grad.shape
    n_rep, _, _, cols = dense.shape

    def a_block(i, where):
        place = where[offset + i]
        return (place % n_rep, place // n_rep, 0, 0)

    return pl.pallas_call(
        backward_kernel,
        out_shape=[jax.ShapeDtypeStruct((width, cols), BF16)] * count,
        grid_spec=pltpu.PrefetchScalarGridSpec(
            num_scalar_prefetch=1,
            grid=(count,),
            in_specs=[
                pl.BlockSpec((width, rows), lambda i, where: (0, 0)),
                pl.BlockSpec((1, 1, rows, cols), a_block),
            ],
            out_specs=[pl.BlockSpec((width, cols), lambda i, where: (0, 0))] * count,
        ),
        compiler_params=pltpu.CompilerParams(vmem_limit_bytes=36 * 2**20),
        cost_estimate=pl.CostEstimate(
            flops=2 * count * rows * width * cols,
            transcendentals=0,
            bytes_accessed=2 * count * rows * cols + 2 * count * width * cols + 2 * width * rows,
        ),
    )(where, grad, dense)


def final_kernel(*refs):
    *parts, out_ref = refs
    total = functools.reduce(jnp.add, [part[...].astype(F32) for part in parts])
    out_ref[0] = total.T.astype(BF16)


def final_sum(parts):
    width, cols = parts[0].shape
    return pl.pallas_call(
        final_kernel,
        out_shape=jax.ShapeDtypeStruct((1, cols, width), BF16),
        compiler_params=pltpu.CompilerParams(vmem_limit_bytes=36 * 2**20),
        cost_estimate=pl.CostEstimate(
            flops=len(parts) * width * cols,
            transcendentals=0,
            bytes_accessed=2 * (len(parts) + 1) * width * cols,
        ),
    )(*parts)


def shards(sizes, features, weight, tile_values, tile_rows, tile_cols, tile_count, cotangent):
    n_section, n_rep = sizes
    block_rows, width = features.shape
    part = block_rows // n_rep
    section, rep = lax.axis_index("section"), lax.axis_index("rep")

    X, Y, Z = 1, 2, 4
    pair_count = n_section // 8
    low_bit = lambda mask: mask & -mask

    def flip(value, mask, rep_mask=0):
        pairs = [
            (s * n_rep + r, (s ^ mask) * n_rep + (r ^ rep_mask))
            for s in range(n_section)
            for r in range(n_rep)
        ]
        return lax.ppermute(value, BOTH, pairs)

    def gather_rep(value):
        held = [value] + [flip(value, 0, other) for other in range(1, n_rep)]
        order = rep ^ jnp.arange(n_rep)
        if n_rep == 2:
            held = [jnp.where(rep == 0, held[0], held[1]), jnp.where(rep == 0, held[1], held[0])]
            return jnp.concatenate(held)
        return jnp.stack(held)[order].reshape(-1, width)

    live = {}

    def close(*open_names):
        names = [name for name in live if name not in open_names]
        live.update(zip(names, lax.optimization_barrier([live[name] for name in names])))

    masks, offsets = [], {}

    def plan(name, wanted):
        offsets[name] = 2 + len(masks)
        masks.extend(wanted)

    for pair in range(pair_count):
        even, odd = 2 * pair * Z, (2 * pair + 1) * Z
        plan(("units", pair), [even, even + X, even + Y, odd, odd + X, odd + Y])
        plan(("crossed", pair), [even + X + Y, odd + X + Y])
        plan(("first", pair), [odd + X + Y, even + X + Y])
        plan(("odd", pair), [odd + X, odd + Y, odd])
        plan(("even", pair), [even + X, even + Y, even])
    where = jnp.concatenate(
        [rep[None], section[None], section ^ jnp.array(masks, jnp.int32)]
    ).astype(jnp.int32)

    def forward_step(names, units, total, kind=F32):
        with jax.named_scope("forward"):
            return forward_part(
                where, offsets[names], units, total, live["dense"], live["others"], kind
            )

    row_tiles = block_rows // tile_values.shape[3]
    packed = jnp.concatenate(
        [tile_rows[0] * row_tiles + tile_cols[0], tile_count[0][:, None]], axis=1
    )
    panels = tile_values.shape[1]
    live[0] = lax.dynamic_slice_in_dim(features, rep * part, part, axis=0)
    total = None
    for pair in range(pair_count):
        even, odd = 2 * pair * Z, (2 * pair + 1) * Z
        later = even + 2 * Z
        last = pair + 1 == pair_count

        with jax.named_scope("features_across"):
            live["even_x"], live["even_y"] = flip(live[even], X), flip(live[even], Y)
        with jax.named_scope("features_along_z"):
            live[odd] = flip(live[even], Z)
        if pair == 0:
            with jax.named_scope("dense_blocks"):
                live["dense"] = make_dense(
                    0, None, where, tile_values[0], packed, block_rows, n_rep
                )
            with jax.named_scope("tiles_exchange"):
                live["tiles"] = [
                    (flip(tile_values[0], 0, n), flip(packed, 0, n)) for n in range(1, n_rep)
                ]
        else:
            live["total"] = forward_step(*waiting, live.pop("waiting"), live.get("total"))
        close()

        with jax.named_scope("features_across"):
            live["odd_x"], live["odd_y"] = flip(live[odd], X), flip(live[odd], Y)
        if not last:
            with jax.named_scope("features_along_z"):
                live[later] = flip(live[later - low_bit(later)], low_bit(later))
        if last:
            with jax.named_scope("cotangent_rows"):
                live["cotangent"] = gather_rep(cotangent)
        close(*([] if last else [later]))

        with jax.named_scope("features_across"):
            crossed = [flip(live["even_x"], Y), flip(live["odd_y"], X)]
        if pair == 0:
            with jax.named_scope("dense_blocks"):
                live["dense"] = make_dense(
                    panels // 2, live["dense"], where, tile_values[0], packed, block_rows, n_rep
                )
            with jax.named_scope("other_blocks"):
                live["others"] = [
                    make_other(where, *sent, block_rows, n_rep) for sent in live.pop("tiles")
                ]
        units = [live[even], live.pop("even_x"), live.pop("even_y")]
        units += [live[odd], live.pop("odd_x"), live.pop("odd_y")]
        if pair > 0:
            live["total"] = forward_step(("units", pair), units, live["total"])
            live["waiting"] = crossed
            waiting = [("crossed", pair)]
        else:
            live["waiting"] = units + crossed
            waiting = [("units", pair)]
        close()
    partial = forward_step(*waiting, live["waiting"], live.get("total"), BF16)

    with jax.named_scope("partial_sums"):
        other = flip(partial, 0, 1)
        for bit in range(1, n_rep.bit_length() - 1):
            partial = (partial.astype(F32) + other.astype(F32)).astype(BF16)
            other = flip(partial, 0, 1 << bit)

    depth = n_section // 4
    with jax.named_scope("middle"):
        rows = (partial, other, weight, live["cotangent"])
        grad, odd_diag, even_diag = middle(
            where, offsets["first", pair_count - 1], *rows, live["dense"]
        )

    def backward_step(name, count):
        with jax.named_scope("backward"):
            return backward_part(where, offsets[name], count, live["grad"], live["dense"])

    add = lambda *values: functools.reduce(jnp.add, [value.astype(F32) for value in values])

    def weight_step(phase):
        if phase == 0:
            live["activated"], *live["terms"] = weight_terms(where, *rows, n_rep, depth)
            return
        name = next((name for name in ("odd", "even", "first") if name in live), None)
        if name:
            live[name], live["terms"] = lax.optimization_barrier((live[name], live["terms"]))
        terms = live["terms"]
        if phase == 1:
            sums = [terms[0]] + [flip(term, Z * n) for n, term in enumerate(terms[1:], 1)]
            live["terms"] = [add(*sums).astype(BF16)]
        elif phase == 2:
            sums = [terms[0]] + [flip(terms[0], mask) for mask in (X, Y, X + Y)]
            live["terms"] = [(add(*sums[:2]) + add(*sums[2:])).astype(BF16)]
        elif 1 << phase - 3 < depth:
            live["terms"] = terms + [flip(term, Z << phase - 3) for term in terms]
        elif "weight_grad" not in live:
            z = section // 4
            rows_of = jnp.stack(terms)[z ^ jnp.arange(depth)].reshape(-1, width)
            live["weight_grad"] = gather_rep(rows_of).astype(F32)

    phases = iter(range(3 * pair_count))

    def end_phase(*open_names):
        with jax.named_scope("weight_grad"):
            weight_step(next(phases))
        close(*open_names)

    live = {"grad": grad, "dense": live["dense"]}
    live["first"] = [odd_diag, even_diag]
    for pair in reversed(range(pair_count)):
        even = 2 * pair * Z
        passing = [name for name in live if isinstance(name, tuple)]

        with jax.named_scope("grads_across"):
            odd_diag, even_diag = live.pop("first")
            live["odd_diag"], live["even_diag"] = flip(odd_diag, Y), flip(even_diag, X)
        live["odd"] = backward_step(("odd", pair), 3)
        if "passed" in live:
            with jax.named_scope("grads_along_z"):
                mask = low_bit(even + 2 * Z)
                target = even + 2 * Z - mask
                live["to", target, mask] = flip(live.pop("passed"), mask)
                passing = [("to", target, mask)]
        end_phase(*passing)

        with jax.named_scope("grads_across"):
            to_x, to_y, own = live.pop("odd")
            to_x = add(to_x, live.pop("odd_diag")).astype(BF16)
            live["odd_sum"] = [own, flip(to_x, X), flip(to_y, Y)]
        live["even"] = backward_step(("even", pair), 3)
        end_phase()

        with jax.named_scope("grads_across"):
            to_x, to_y, own = live.pop("even")
            to_y = add(to_y, live.pop("even_diag")).astype(BF16)
            live["even_sum"] = [own, flip(to_x, X), flip(to_y, Y)]
        with jax.named_scope("grads_along_z"):
            odd_sum = add(*live.pop("odd_sum")).astype(BF16)
            live["even_sum"].append(flip(odd_sum, Z))
        if pair > 0:
            live["first"] = backward_step(("first", pair - 1), 2)
        end_phase()
        arrived = [name for name in live if isinstance(name, tuple) and name[1] == even]
        sums = [*live.pop("even_sum"), *(live.pop(name) for name in arrived)]
        if pair > 0:
            live["passed"] = add(*sums).astype(BF16)
    with jax.named_scope("grads_out"):
        feat_grad = final_sum(sums)
    return (live["activated"], feat_grad, live["weight_grad"])


def solution(mesh):
    placed = (
        P("section", None),
        P(),
        P("section", "rep", None, None, None),
        P("section", "rep", None),
        P("section", "rep", None),
        P("section", "rep"),
        P(("section", "rep"), None),
    )
    sizes = (mesh.shape["section"], mesh.shape["rep"])
    return jax.shard_map(
        functools.partial(shards, sizes),
        mesh=mesh,
        in_specs=placed,
        out_specs=(P(("section", "rep"), None), P("rep", "section", None), P()),
        check_vma=False,
    )
```

```python
import functools

import jax
import jax.numpy as jnp
from jax import lax
from jax.experimental import pallas as pl
from jax.experimental.pallas import tpu as pltpu
from jax.sharding import PartitionSpec as P

BF16 = jnp.bfloat16
F32 = jnp.float32
BOTH = ("section", "rep")


def dense_kernel(first, where_ref, packed_ref, tiles_ref, *refs):
    out_ref = refs[-1]
    panel = first + pl.program_id(0)
    size, slots = tiles_ref.shape[-1], tiles_ref.shape[1]
    row_tiles, per_part = out_ref.shape[2] // size, out_ref.shape[3] // size
    out_ref[...] = jnp.zeros_like(out_ref)

    def add_tile(slot, carry):
        place = packed_ref[panel, slot]
        row = pl.multiple_of(place // row_tiles * size, size)
        tile_col = place % row_tiles
        col = pl.multiple_of(tile_col % per_part * size, size)
        out_ref[tile_col // per_part, 0, pl.ds(row, size), pl.ds(col, size)] += tiles_ref[0, slot]
        return carry

    lax.fori_loop(0, packed_ref[panel, slots], add_tile, 0)


def make_dense(first, before, where, tiles, packed, block_rows, n_rep):
    panels, slots, size, _ = tiles.shape
    half = panels // 2
    part = block_rows // n_rep
    at = lambda p: first + p
    return pl.pallas_call(
        functools.partial(dense_kernel, first),
        out_shape=jax.ShapeDtypeStruct((n_rep, panels, block_rows, part), BF16),
        grid_spec=pltpu.PrefetchScalarGridSpec(
            num_scalar_prefetch=2,
            grid=(half,),
            in_specs=[pl.BlockSpec((1, slots, size, size), lambda p, *_: (at(p), 0, 0, 0))]
            + [pl.BlockSpec(memory_space=pl.ANY)] * (first > 0),
            out_specs=pl.BlockSpec((n_rep, 1, block_rows, part), lambda p, *_: (0, at(p), 0, 0)),
        ),
        input_output_aliases={3: 0} if first else {},
        compiler_params=pltpu.CompilerParams(vmem_limit_bytes=36 * 2**20),
        cost_estimate=pl.CostEstimate(
            flops=0,
            transcendentals=0,
            bytes_accessed=tiles.size // 8,
        ),
    )(where, packed, tiles, *([before] if first else []))


def other_kernel(first, where_ref, packed_ref, tiles_ref, out_ref):
    panel = first + pl.program_id(0)
    size, slots = tiles_ref.shape[-1], tiles_ref.shape[1]
    row_tiles, per_part = out_ref.shape[1] // size, out_ref.shape[2] // size
    out_ref[...] = jnp.zeros_like(out_ref)

    def add_tile(slot, carry):
        place = packed_ref[panel, slot]
        row = pl.multiple_of(place // row_tiles * size, size)
        tile_col = place % row_tiles
        col = pl.multiple_of(tile_col % per_part * size, size)

        @pl.when(tile_col // per_part == where_ref[0])
        def _():
            out_ref[0, pl.ds(row, size), pl.ds(col, size)] += tiles_ref[0, slot]

        return carry

    lax.fori_loop(0, packed_ref[panel, slots], add_tile, 0)


def make_other(first, where, tiles, packed, block_rows, n_rep):
    panels, slots, size, _ = tiles.shape
    half = panels // 2
    part = block_rows // n_rep
    return pl.pallas_call(
        functools.partial(other_kernel, first),
        out_shape=jax.ShapeDtypeStruct((half, block_rows, part), BF16),
        grid_spec=pltpu.PrefetchScalarGridSpec(
            num_scalar_prefetch=2,
            grid=(half,),
            in_specs=[pl.BlockSpec((1, slots, size, size), lambda p, *_: (first + p, 0, 0, 0))],
            out_specs=pl.BlockSpec((1, block_rows, part), lambda p, *_: (p, 0, 0)),
        ),
        compiler_params=pltpu.CompilerParams(vmem_limit_bytes=36 * 2**20),
        cost_estimate=pl.CostEstimate(
            flops=0, transcendentals=0, bytes_accessed=tiles.size // 8
        ),
    )(where, packed, tiles)


def forward_kernel(offset, n_units, n_others, has_total, where_ref, dense_ref, *refs):
    others, refs = refs[:n_others], refs[n_others:]
    units, refs = refs[:n_units], refs[n_units:]
    total_ref, refs = (refs[0], refs[1:]) if has_total else (None, refs)
    out_ref, sum_ref, a_buf, u_buf, sems, sum_sem = refs
    _, panels, _, part = dense_ref.shape
    some = others[0].shape[0]
    rep = where_ref[0]

    def a_copy(source, slot, side):
        target = a_buf.at[slot, :, pl.ds(side * part, part)]
        return pltpu.make_async_copy(source, target, sems.at[0, slot, side])

    def u_copy(source, slot, side):
        target = u_buf.at[slot, pl.ds(side * part, part), :]
        return pltpu.make_async_copy(source, target, sems.at[1, slot, side])

    def fetch(pair, slot):
        for side in range(2):
            place = where_ref[offset + 2 * pair + side]
            owner, panel = place // panels, place % panels
            turn = ((owner ^ rep) - 1) * (panels // some) + panel // some

            @pl.when(owner == rep)
            def _():
                a_copy(dense_ref.at[rep, panel], slot, side).start()

            for number, other_ref in enumerate(others):

                @pl.when((owner != rep) & (turn == number))
                def _():
                    a_copy(other_ref.at[panel % some], slot, side).start()

            for number in range(side, n_units, 2):

                @pl.when(pair == number // 2)
                def _():
                    u_copy(units[number], slot, side).start()

    pairs = n_units // 2
    fetch(0, 0)
    if has_total:
        load = pltpu.make_async_copy(total_ref, sum_ref, sum_sem)
        load.start()
        load.wait()
    else:
        sum_ref[...] = jnp.zeros_like(sum_ref)

    def step(pair, carry):
        slot = pair % 2

        @pl.when(pair + 1 < pairs)
        def _():
            fetch(pair + 1, 1 - slot)

        for side in range(2):
            a_copy(dense_ref.at[0, 0], slot, side).wait()
            u_copy(units[0], slot, side).wait()
        sum_ref[...] += jnp.dot(a_buf[slot], u_buf[slot], preferred_element_type=F32)
        return carry

    lax.fori_loop(0, pairs, step, 0)
    if out_ref.dtype == F32:
        store = pltpu.make_async_copy(sum_ref, out_ref, sum_sem)
        store.start()
        store.wait()
    else:
        out_ref[...] = sum_ref[...].astype(out_ref.dtype)


def forward_part(where, offset, units, total, dense, others, kind):
    part, width = units[0].shape
    rows = dense.shape[2]
    near = pl.BlockSpec(memory_space=pl.ANY)
    hbm = pl.BlockSpec(memory_space=pltpu.HBM)
    has_total = total is not None
    n_units, n_others = len(units), len(others)
    return pl.pallas_call(
        functools.partial(forward_kernel, offset, n_units, n_others, has_total),
        out_shape=jax.ShapeDtypeStruct((rows, width), kind),
        grid_spec=pltpu.PrefetchScalarGridSpec(
            num_scalar_prefetch=1,
            grid=(1,),
            in_specs=[hbm] * (1 + n_others) + [near] * (n_units + has_total),
            out_specs=near if kind == F32 else pl.BlockSpec((rows, width), lambda i, where: (0, 0)),
            scratch_shapes=[
                pltpu.VMEM((rows, width), F32),
                pltpu.VMEM((2, rows, 2 * part), BF16),
                pltpu.VMEM((2, 2 * part, width), BF16),
                pltpu.SemaphoreType.DMA((2, 2, 2)),
                pltpu.SemaphoreType.DMA,
            ],
        ),
        compiler_params=pltpu.CompilerParams(vmem_limit_bytes=36 * 2**20),
        cost_estimate=pl.CostEstimate(
            flops=2 * n_units * rows * part * width,
            transcendentals=0,
            bytes_accessed=n_units * rows * part * 2 + 8 * rows * width,
        ),
    )(where, dense, *others, *units, *([total] if has_total else []))


def slopes(mine_ref, other_ref, weight_ref, cot_ref):
    agg = (mine_ref[...].astype(F32) + other_ref[...].astype(F32)).astype(BF16)
    pre = jnp.dot(agg, weight_ref[...], preferred_element_type=F32)
    sigma = jax.nn.sigmoid(pre)
    slope = cot_ref[...].astype(F32) * sigma * (1.0 + pre * (1.0 - sigma))
    return agg, (pre * sigma).astype(BF16), slope.astype(BF16)


def middle_kernel(blocks, where_ref, mine_ref, other_ref, weight_ref, cot_ref, a_ref, *refs):
    grad_ref, odd_ref, even_ref, term_ref, sum_ref = refs
    step = pl.program_id(0)
    part = mine_ref.shape[0]
    width = sum_ref.shape[0]

    @pl.when(step < blocks)
    def _():
        agg, _, pre_grad = slopes(mine_ref, other_ref, weight_ref, cot_ref)
        grad_ref[:, pl.ds(pl.multiple_of(step * part, part), part)] = lax.dot_general(
            weight_ref[...], pre_grad, (((1,), (1,)), ((), ())), preferred_element_type=F32
        ).astype(BF16)
        term = lax.dot_general(agg, pre_grad, (((0,), (0,)), ((), ())), preferred_element_type=F32)

        @pl.when(step == 0)
        def _():
            sum_ref[...] = term

        @pl.when(step > 0)
        def _():
            sum_ref[...] += term

    @pl.when(step >= blocks)
    def _():
        chunk = jnp.dot(grad_ref[...], a_ref[0, 0], preferred_element_type=F32).astype(BF16)

        @pl.when(step == blocks)
        def _():
            _, extra, cols = term_ref.shape
            quarter = extra * cols // width
            for number in range(4):
                start = pl.multiple_of((where_ref[0] * 4 + number) * quarter, quarter)
                rows = sum_ref[pl.ds(start, quarter), :].astype(BF16)
                for turn in range(width // cols):
                    term_ref[number, turn * quarter : (turn + 1) * quarter] = rows[
                        :, turn * cols : (turn + 1) * cols
                    ]
            odd_ref[:width] = chunk
            odd_ref[width:] = term_ref[(where_ref[1] % 4) ^ 3]

        @pl.when(step > blocks)
        def _():
            even_ref[...] = chunk


def middle(where, offset, mine, other, weight, cotangent, dense):
    rows, width = mine.shape
    n_rep, _, _, cols = dense.shape
    blocks = 4
    part = rows // blocks
    extra = width // n_rep // 4 * (width // cols)
    block = pl.BlockSpec((part, width), lambda i, where: (jnp.minimum(i, blocks - 1), 0))
    fixed = lambda *shape: pl.BlockSpec(shape, lambda i, where: (0,) * len(shape))
    shapes = [(width, rows), (width + extra, cols), (width, cols), (4, extra, cols)]

    def a_block(i, where):
        place = where[offset + jnp.maximum(i - blocks, 0)]
        return (place % n_rep, place // n_rep, 0, 0)

    return pl.pallas_call(
        functools.partial(middle_kernel, blocks),
        out_shape=[jax.ShapeDtypeStruct(shape, BF16) for shape in shapes],
        grid_spec=pltpu.PrefetchScalarGridSpec(
            num_scalar_prefetch=1,
            grid=(blocks + 2,),
            in_specs=[
                block,
                block,
                fixed(width, width),
                block,
                pl.BlockSpec((1, 1, rows, cols), a_block),
            ],
            out_specs=[fixed(*shape) for shape in shapes],
            scratch_shapes=[pltpu.VMEM((width, width), F32)],
        ),
        compiler_params=pltpu.CompilerParams(vmem_limit_bytes=36 * 2**20),
        cost_estimate=pl.CostEstimate(
            flops=6 * rows * width * width + 4 * rows * width * cols,
            transcendentals=rows * width,
            bytes_accessed=rows * width * 12,
        ),
    )(where, mine, other, weight, cotangent, dense)


def activated_kernel(where_ref, mine_ref, other_ref, weight_ref, cot_ref, act_ref):
    act_ref[...] = slopes(mine_ref, other_ref, weight_ref, cot_ref)[1]


def activated_rows(where, mine, other, weight, cotangent, n_rep):
    rows, width = mine.shape
    part = rows // n_rep
    block = pl.BlockSpec((part, width), lambda i, where: (where[0], 0))
    fixed = lambda *shape: pl.BlockSpec(shape, lambda i, where: (0, 0))
    return pl.pallas_call(
        activated_kernel,
        out_shape=jax.ShapeDtypeStruct((part, width), BF16),
        grid_spec=pltpu.PrefetchScalarGridSpec(
            num_scalar_prefetch=1,
            grid=(1,),
            in_specs=[block, block, fixed(width, width), block],
            out_specs=fixed(part, width),
        ),
        compiler_params=pltpu.CompilerParams(vmem_limit_bytes=36 * 2**20),
        cost_estimate=pl.CostEstimate(
            flops=2 * part * width * width,
            transcendentals=part * width,
            bytes_accessed=part * width * 8,
        ),
    )(where, mine, other, weight, cotangent)


def backward_kernel(masks, where_ref, grad_ref, a_ref, *refs):
    term_ref, out_refs = (refs[0], refs[1:]) if masks else (None, refs)
    width = grad_ref.shape[0]
    chunk = jnp.dot(grad_ref[...], a_ref[0, 0], preferred_element_type=F32).astype(BF16)
    for number, out_ref in enumerate(out_refs):

        @pl.when(pl.program_id(0) == number)
        def _():
            out_ref[:width] = chunk
            if number < len(masks):
                out_ref[width:] = term_ref[(where_ref[1] % 4) ^ masks[number]]


def backward_part(where, offset, count, grad, dense, masks=(), term=None):
    width, rows = grad.shape
    n_rep, _, _, cols = dense.shape
    fixed = lambda *shape: pl.BlockSpec(shape, lambda i, where: (0,) * len(shape))
    extra = term.shape[1] if masks else 0
    shapes = [(width + extra * (number < len(masks)), cols) for number in range(count)]

    def a_block(i, where):
        place = where[offset + i]
        return (place % n_rep, place // n_rep, 0, 0)

    return pl.pallas_call(
        functools.partial(backward_kernel, masks),
        out_shape=[jax.ShapeDtypeStruct(shape, BF16) for shape in shapes],
        grid_spec=pltpu.PrefetchScalarGridSpec(
            num_scalar_prefetch=1,
            grid=(count,),
            in_specs=[fixed(width, rows), pl.BlockSpec((1, 1, rows, cols), a_block)]
            + ([fixed(*term.shape)] if masks else []),
            out_specs=[fixed(*shape) for shape in shapes],
        ),
        compiler_params=pltpu.CompilerParams(vmem_limit_bytes=36 * 2**20),
        cost_estimate=pl.CostEstimate(
            flops=2 * count * rows * width * cols,
            transcendentals=0,
            bytes_accessed=2 * count * rows * cols + 2 * count * width * cols + 2 * width * rows,
        ),
    )(where, grad, dense, *([term] if masks else []))


def final_kernel(n_parts, where_ref, *refs):
    parts, terms = refs[:n_parts], refs[n_parts:-2]
    out_ref, weight_out = refs[-2:]
    width = out_ref.shape[2]
    total = functools.reduce(jnp.add, [part[:width].astype(F32) for part in parts])
    out_ref[0] = total.T.astype(BF16)
    _, extra, cols = terms[0].shape
    quarter = extra * cols // width
    for other, term_ref in enumerate(terms):
        for number in range(4):
            place = (where_ref[0] ^ other) * 4 + ((where_ref[1] % 4) ^ number)
            rows = pl.ds(pl.multiple_of(place * quarter, quarter), quarter)
            for turn in range(width // cols):
                weight_out[rows, turn * cols : (turn + 1) * cols] = term_ref[
                    number, turn * quarter : (turn + 1) * quarter
                ].astype(F32)


def final_sum(where, parts, terms):
    width, cols = parts[0].shape
    whole = lambda value: pl.BlockSpec(value.shape, lambda i, where: (0,) * value.ndim)
    outs = [
        jax.ShapeDtypeStruct((1, cols, width), BF16),
        jax.ShapeDtypeStruct((width, width), F32),
    ]
    return pl.pallas_call(
        functools.partial(final_kernel, len(parts)),
        out_shape=outs,
        grid_spec=pltpu.PrefetchScalarGridSpec(
            num_scalar_prefetch=1,
            grid=(1,),
            in_specs=[whole(value) for value in [*parts, *terms]],
            out_specs=[whole(value) for value in outs],
        ),
        compiler_params=pltpu.CompilerParams(vmem_limit_bytes=36 * 2**20),
        cost_estimate=pl.CostEstimate(
            flops=len(parts) * width * cols,
            transcendentals=0,
            bytes_accessed=2 * (len(parts) + 1) * width * cols,
        ),
    )(where, *parts, *terms)


def shards(sizes, features, weight, tile_values, tile_rows, tile_cols, tile_count, cotangent):
    n_section, n_rep = sizes
    block_rows, width = features.shape
    part = block_rows // n_rep
    section, rep = lax.axis_index("section"), lax.axis_index("rep")

    X, Y, Z = 1, 2, 4
    pair_count = n_section // 8
    low_bit = lambda mask: mask & -mask

    def flip(value, mask, rep_mask=0):
        pairs = [
            (s * n_rep + r, (s ^ mask) * n_rep + (r ^ rep_mask))
            for s in range(n_section)
            for r in range(n_rep)
        ]
        return lax.ppermute(value, BOTH, pairs)

    def gather_rep(value):
        held = [value] + [flip(value, 0, other) for other in range(1, n_rep)]
        order = rep ^ jnp.arange(n_rep)
        if n_rep == 2:
            held = [jnp.where(rep == 0, held[0], held[1]), jnp.where(rep == 0, held[1], held[0])]
            return jnp.concatenate(held)
        return jnp.stack(held)[order].reshape(-1, width)

    live = {}

    def close(*open_names):
        names = [name for name in live if name not in open_names]
        live.update(zip(names, lax.optimization_barrier([live[name] for name in names])))

    masks, offsets = [], {}

    def plan(name, wanted):
        offsets[name] = 2 + len(masks)
        masks.extend(wanted)

    for pair in range(pair_count):
        even, odd = 2 * pair * Z, (2 * pair + 1) * Z
        plan(("units", pair), [even, even + X, even + Y, odd, odd + X, odd + Y])
        plan(("crossed", pair), [even + X + Y, odd + X + Y])
        plan(("first", pair), [odd + X + Y, even + X + Y])
        plan(("odd", pair), [odd + X, odd + Y, odd])
        plan(("even", pair), [even + X, even + Y, even])
    where = jnp.concatenate(
        [rep[None], section[None], section ^ jnp.array(masks, jnp.int32)]
    ).astype(jnp.int32)

    def forward_step(names, units, total, kind=F32):
        with jax.named_scope("forward"):
            return forward_part(
                where, offsets[names], units, total, live["dense"], live["others"], kind
            )

    row_tiles = block_rows // tile_values.shape[3]
    packed = jnp.concatenate(
        [tile_rows[0] * row_tiles + tile_cols[0], tile_count[0][:, None]], axis=1
    )
    panels = tile_values.shape[1]
    def build(first):
        with jax.named_scope("dense_blocks"):
            live["dense"] = make_dense(
                first, live.get("dense"), where, tile_values[0], packed, block_rows, n_rep
            )
        with jax.named_scope("other_blocks"):
            return [make_other(first, where, *sent, block_rows, n_rep) for sent in live["tiles"]]

    live[0] = lax.dynamic_slice_in_dim(features, rep * part, part, axis=0)
    with jax.named_scope("tiles_exchange"):
        live["tiles"] = [
            (flip(tile_values[0], 0, n), flip(packed, 0, n)) for n in range(1, n_rep)
        ]
    waiting = []
    for pair in range(pair_count):
        even, odd = 2 * pair * Z, (2 * pair + 1) * Z
        later = even + 2 * Z
        last = pair + 1 == pair_count

        with jax.named_scope("features_across"):
            live["even_x"], live["even_y"] = flip(live[even], X), flip(live[even], Y)
        with jax.named_scope("features_along_z"):
            live[odd] = flip(live[even], Z)
        if pair == 1:
            two = build(panels // 2)
            live["others"] = [half for halves in zip(live.pop("one"), two) for half in halves]
            del live["tiles"]
        close()

        with jax.named_scope("features_across"):
            live["odd_x"], live["odd_y"] = flip(live[odd], X), flip(live[odd], Y)
        if not last:
            with jax.named_scope("features_along_z"):
                live[later] = flip(live[later - low_bit(later)], low_bit(later))
        if pair > 0:
            live["total"] = forward_step(*waiting, live.pop("waiting"), live.get("total"))
        close(*([] if last else [later]))

        with jax.named_scope("features_across"):
            crossed = [flip(live["even_x"], Y), flip(live["odd_y"], X)]
        units = [live[even], live.pop("even_x"), live.pop("even_y")]
        units += [live[odd], live.pop("odd_x"), live.pop("odd_y")]
        if pair == 0:
            live["one"] = build(0)
            with jax.named_scope("cotangent_rows"):
                live["cotangent"] = gather_rep(cotangent)
            live["waiting"] = units + crossed
            waiting = [("units", pair)]
        else:
            live["total"] = forward_step(("units", pair), units, live["total"])
            live["waiting"] = crossed
            waiting = [("crossed", pair)]
        close()
    partial = forward_step(*waiting, live["waiting"], live.get("total"), BF16)

    with jax.named_scope("partial_sums"):
        other = flip(partial, 0, 1)
        for bit in range(1, n_rep.bit_length() - 1):
            partial = (partial.astype(F32) + other.astype(F32)).astype(BF16)
            other = flip(partial, 0, 1 << bit)

    with jax.named_scope("middle"):
        rows = (partial, other, weight, live["cotangent"])
        grad, odd_diag, even_diag, term = middle(
            where, offsets["first", pair_count - 1], *rows, live["dense"]
        )

    live = {"grad": grad, "dense": live["dense"], "term": term}
    add = lambda *values: functools.reduce(jnp.add, [value.astype(F32) for value in values])

    def backward_step(names, *carried):
        with jax.named_scope("backward"):
            count = sum(2 if name[0] == "first" else 3 for name in names)
            chunks = backward_part(
                where, offsets[names[0]], count, live["grad"], live["dense"], *carried
            )
            for name in names:
                size = 2 if name[0] == "first" else 3
                live[name[0]], chunks = chunks[:size], chunks[size:]

    z_masks = [1 << bit for bit in range(3, n_section.bit_length() - 1)]

    def weight_step():
        with jax.named_scope("weight_grad"):
            if z_masks:
                flipped = flip(live["weight"], z_masks.pop(0))
                live["weight"] = add(live["weight"], flipped).astype(BF16)
            elif "weight" in live:
                own = live.pop("weight")
                live["quarters"] = [own, *(flip(own, mask) for mask in (X, Y, X + Y))]
            elif "quarters" in live:
                own = jnp.stack(live.pop("quarters"))
                live["terms"] = [own, *(flip(own, 0, n) for n in range(1, n_rep))]

    live["first"] = [odd_diag, even_diag]
    for pair in reversed(range(pair_count)):
        even = 2 * pair * Z
        top = pair + 1 == pair_count
        passing = [name for name in live if isinstance(name, tuple)]

        with jax.named_scope("grads_across"):
            odd_diag, even_diag = live.pop("first")
            live["odd_diag"], live["even_diag"] = flip(odd_diag, Y), flip(even_diag, X)
        if top:
            backward_step([("odd", pair), ("even", pair)], (X, Y, 0), live.pop("term"))
        else:
            with jax.named_scope("grads_along_z"):
                mask = low_bit(even + 2 * Z)
                target = even + 2 * Z - mask
                live["to", target, mask] = flip(live.pop("passed"), mask)
                passing = [("to", target, mask)]
            if "activated" not in live:
                with jax.named_scope("activated"):
                    live["activated"] = activated_rows(where, *rows, n_rep)
                live["activated"], live["weight"] = lax.optimization_barrier(
                    (live["activated"], live["weight"])
                )
            weight_step()
        close(*passing)

        with jax.named_scope("grads_across"):
            to_x, to_y, own = live.pop("odd")
            to_x = add(to_x, live.pop("odd_diag")).astype(BF16)
            live["odd_sum"] = [own, flip(to_x, X), flip(to_y, Y)]
            to_x, to_y, own = live.pop("even")
            live["even"] = [to_x, add(to_y, live.pop("even_diag")).astype(BF16), own]
        if pair > 0:
            following = live.pop("even")
            backward_step([("first", pair - 1), ("odd", pair - 1)])
            live["following"], live["even"] = live.pop("odd"), following
        if not top:
            weight_step()
        close()

        with jax.named_scope("grads_across"):
            to_x, to_y, own = live.pop("even")
            live["even_sum"] = [own, flip(to_x, X), flip(to_y, Y)]
        with jax.named_scope("grads_along_z"):
            odd_sum = add(*live.pop("odd_sum")).astype(BF16)
            from_odd = flip(odd_sum, Z)
            live["even_sum"].append(from_odd[:width] if top and pair else from_odd)
        if pair > 0:
            backward_step([("even", pair - 1)])
            live["odd"] = live.pop("following")
        if top:
            with jax.named_scope("weight_grad"):
                live["weight"] = add(odd_sum[width:], from_odd[width:]).astype(BF16)
        else:
            weight_step()
        close()
        arrived = [name for name in live if isinstance(name, tuple) and name[1] == even]
        sums = [*live.pop("even_sum"), *(live.pop(name) for name in arrived)]
        if pair > 0:
            live["passed"] = add(*sums).astype(BF16)
    with jax.named_scope("grads_out"):
        feat_grad, weight_grad = final_sum(where, sums, live["terms"])
    return (live["activated"], feat_grad, weight_grad)


def solution(mesh):
    placed = (
        P("section", None),
        P(),
        P("section", "rep", None, None, None),
        P("section", "rep", None),
        P("section", "rep", None),
        P("section", "rep"),
        P(("section", "rep"), None),
    )
    sizes = (mesh.shape["section"], mesh.shape["rep"])
    return jax.shard_map(
        functools.partial(shards, sizes),
        mesh=mesh,
        in_specs=placed,
        out_specs=(P(("section", "rep"), None), P("rep", "section", None), P()),
        check_vma=False,
    )
```

```python
import functools

import jax
import jax.numpy as jnp
from jax import lax
from jax.experimental import pallas as pl
from jax.experimental.pallas import tpu as pltpu
from jax.sharding import PartitionSpec as P

BF16 = jnp.bfloat16
F32 = jnp.float32
BOTH = ("section", "rep")


def in_hbm(value):
    return pltpu.with_memory_space_constraint(value, pltpu.HBM)


def dense_kernel(first, where_ref, packed_ref, tiles_ref, *refs):
    out_ref = refs[-1]
    panel = first + pl.program_id(0)
    size, slots = tiles_ref.shape[-1], tiles_ref.shape[1]
    row_tiles, per_part = out_ref.shape[2] // size, out_ref.shape[3] // size
    out_ref[...] = jnp.zeros_like(out_ref)

    def add_tile(slot, carry):
        place = packed_ref[panel, slot]
        row = pl.multiple_of(place // row_tiles * size, size)
        tile_col = place % row_tiles
        col = pl.multiple_of(tile_col % per_part * size, size)
        out_ref[tile_col // per_part, 0, pl.ds(row, size), pl.ds(col, size)] += tiles_ref[0, slot]
        return carry

    lax.fori_loop(0, packed_ref[panel, slots], add_tile, 0)


def make_dense(first, before, where, tiles, packed, block_rows, n_rep):
    panels, slots, size, _ = tiles.shape
    half = panels // 2
    part = block_rows // n_rep
    at = lambda p: first + p
    return pl.pallas_call(
        functools.partial(dense_kernel, first),
        out_shape=pltpu.HBM((n_rep, panels, block_rows, part), BF16),
        grid_spec=pltpu.PrefetchScalarGridSpec(
            num_scalar_prefetch=2,
            grid=(half,),
            in_specs=[pl.BlockSpec((1, slots, size, size), lambda p, *_: (at(p), 0, 0, 0))]
            + [pl.BlockSpec(memory_space=pl.ANY)] * (first > 0),
            out_specs=pl.BlockSpec((n_rep, 1, block_rows, part), lambda p, *_: (0, at(p), 0, 0)),
        ),
        input_output_aliases={3: 0} if first else {},
        compiler_params=pltpu.CompilerParams(vmem_limit_bytes=36 * 2**20),
        cost_estimate=pl.CostEstimate(
            flops=0,
            transcendentals=0,
            bytes_accessed=tiles.size // 8,
        ),
    )(where, packed, in_hbm(tiles), *([in_hbm(before)] if first else []))


def other_kernel(first, where_ref, packed_ref, tiles_ref, out_ref):
    panel = first + pl.program_id(0)
    size, slots = tiles_ref.shape[-1], tiles_ref.shape[1]
    row_tiles, per_part = out_ref.shape[1] // size, out_ref.shape[2] // size
    out_ref[...] = jnp.zeros_like(out_ref)

    def add_tile(slot, carry):
        place = packed_ref[panel, slot]
        row = pl.multiple_of(place // row_tiles * size, size)
        tile_col = place % row_tiles
        col = pl.multiple_of(tile_col % per_part * size, size)

        @pl.when(tile_col // per_part == where_ref[0])
        def _():
            out_ref[0, pl.ds(row, size), pl.ds(col, size)] += tiles_ref[0, slot]

        return carry

    lax.fori_loop(0, packed_ref[panel, slots], add_tile, 0)


def make_other(first, where, tiles, packed, block_rows, n_rep):
    panels, slots, size, _ = tiles.shape
    half = panels // 2
    part = block_rows // n_rep
    return pl.pallas_call(
        functools.partial(other_kernel, first),
        out_shape=pltpu.HBM((half, block_rows, part), BF16),
        grid_spec=pltpu.PrefetchScalarGridSpec(
            num_scalar_prefetch=2,
            grid=(half,),
            in_specs=[pl.BlockSpec((1, slots, size, size), lambda p, *_: (first + p, 0, 0, 0))],
            out_specs=pl.BlockSpec((1, block_rows, part), lambda p, *_: (p, 0, 0)),
        ),
        compiler_params=pltpu.CompilerParams(vmem_limit_bytes=36 * 2**20),
        cost_estimate=pl.CostEstimate(
            flops=0, transcendentals=0, bytes_accessed=tiles.size // 8
        ),
    )(where, packed, tiles)


def forward_kernel(offset, n_units, n_others, has_total, where_ref, dense_ref, *refs):
    others, refs = refs[:n_others], refs[n_others:]
    units, refs = refs[:n_units], refs[n_units:]
    total_ref, refs = (refs[0], refs[1:]) if has_total else (None, refs)
    out_ref, sum_ref, a_buf, u_buf, sems, sum_sem = refs
    _, panels, _, part = dense_ref.shape
    some = others[0].shape[0]
    rep = where_ref[0]

    def a_copy(source, slot, side):
        target = a_buf.at[slot, :, pl.ds(side * part, part)]
        return pltpu.make_async_copy(source, target, sems.at[0, slot, side])

    def u_copy(source, slot, side):
        target = u_buf.at[slot, pl.ds(side * part, part), :]
        return pltpu.make_async_copy(source, target, sems.at[1, slot, side])

    def fetch(pair, slot):
        for side in range(2):
            place = where_ref[offset + 2 * pair + side]
            owner, panel = place // panels, place % panels
            turn = ((owner ^ rep) - 1) * (panels // some) + panel // some

            @pl.when(owner == rep)
            def _():
                a_copy(dense_ref.at[rep, panel], slot, side).start()

            for number, other_ref in enumerate(others):

                @pl.when((owner != rep) & (turn == number))
                def _():
                    a_copy(other_ref.at[panel % some], slot, side).start()

            for number in range(side, n_units, 2):

                @pl.when(pair == number // 2)
                def _():
                    u_copy(units[number], slot, side).start()

    pairs = n_units // 2
    fetch(0, 0)
    if has_total:
        load = pltpu.make_async_copy(total_ref, sum_ref, sum_sem)
        load.start()
        load.wait()
    else:
        sum_ref[...] = jnp.zeros_like(sum_ref)

    def step(pair, carry):
        slot = pair % 2

        @pl.when(pair + 1 < pairs)
        def _():
            fetch(pair + 1, 1 - slot)

        for side in range(2):
            a_copy(dense_ref.at[0, 0], slot, side).wait()
            u_copy(units[0], slot, side).wait()
        sum_ref[...] += jnp.dot(a_buf[slot], u_buf[slot], preferred_element_type=F32)
        return carry

    lax.fori_loop(0, pairs, step, 0)
    if out_ref.dtype == F32:
        store = pltpu.make_async_copy(sum_ref, out_ref, sum_sem)
        store.start()
        store.wait()
    else:
        out_ref[...] = sum_ref[...].astype(out_ref.dtype)


def forward_part(where, offset, units, total, dense, others, kind):
    part, width = units[0].shape
    rows = dense.shape[2]
    near = pl.BlockSpec(memory_space=pl.ANY)
    hbm = pl.BlockSpec(memory_space=pltpu.HBM)
    has_total = total is not None
    n_units, n_others = len(units), len(others)
    return pl.pallas_call(
        functools.partial(forward_kernel, offset, n_units, n_others, has_total),
        out_shape=jax.ShapeDtypeStruct((rows, width), kind),
        grid_spec=pltpu.PrefetchScalarGridSpec(
            num_scalar_prefetch=1,
            grid=(1,),
            in_specs=[hbm] * (1 + n_others) + [near] * (n_units + has_total),
            out_specs=near if kind == F32 else pl.BlockSpec((rows, width), lambda i, where: (0, 0)),
            scratch_shapes=[
                pltpu.VMEM((rows, width), F32),
                pltpu.VMEM((2, rows, 2 * part), BF16),
                pltpu.VMEM((2, 2 * part, width), BF16),
                pltpu.SemaphoreType.DMA((2, 2, 2)),
                pltpu.SemaphoreType.DMA,
            ],
        ),
        compiler_params=pltpu.CompilerParams(vmem_limit_bytes=36 * 2**20),
        cost_estimate=pl.CostEstimate(
            flops=2 * n_units * rows * part * width,
            transcendentals=0,
            bytes_accessed=n_units * rows * part * 2 + 8 * rows * width,
        ),
    )(where, in_hbm(dense), *map(in_hbm, others), *units, *([total] if has_total else []))


def slopes(mine_ref, other_ref, weight_ref, cot_ref):
    agg = (mine_ref[...].astype(F32) + other_ref[...].astype(F32)).astype(BF16)
    pre = jnp.dot(agg, weight_ref[...], preferred_element_type=F32)
    sigma = 0.5 * jnp.tanh(0.5 * pre) + 0.5
    slope = cot_ref[...].astype(F32) * sigma * (1.0 + pre * (1.0 - sigma))
    return agg, (pre * sigma).astype(BF16), slope.astype(BF16)


def middle_kernel(blocks, where_ref, mine_ref, other_ref, weight_ref, cot_ref, a_ref, *refs):
    grad_ref, odd_ref, even_ref, term_ref, sum_ref, full_ref = refs
    step = pl.program_id(0)
    part = mine_ref.shape[0]
    width = sum_ref.shape[0]

    @pl.when(step < blocks)
    def _():
        agg, _, pre_grad = slopes(mine_ref, other_ref, weight_ref, cot_ref)
        grad = lax.dot_general(
            weight_ref[...], pre_grad, (((1,), (1,)), ((), ())), preferred_element_type=F32
        ).astype(BF16)
        grad_ref[...] = grad
        full_ref[:, pl.ds(pl.multiple_of(step * part, part), part)] = grad
        term = lax.dot_general(agg, pre_grad, (((0,), (0,)), ((), ())), preferred_element_type=F32)

        @pl.when(step == 0)
        def _():
            sum_ref[...] = term

        @pl.when(step > 0)
        def _():
            sum_ref[...] += term

    @pl.when(step >= blocks)
    def _():
        chunk = jnp.dot(full_ref[...], a_ref[0, 0], preferred_element_type=F32).astype(BF16)

        @pl.when(step == blocks)
        def _():
            _, extra, cols = term_ref.shape
            quarter = extra * cols // width
            for number in range(4):
                start = pl.multiple_of((where_ref[0] * 4 + number) * quarter, quarter)
                rows = sum_ref[pl.ds(start, quarter), :].astype(BF16)
                for turn in range(width // cols):
                    term_ref[number, turn * quarter : (turn + 1) * quarter] = rows[
                        :, turn * cols : (turn + 1) * cols
                    ]
            odd_ref[:width] = chunk
            odd_ref[width:] = term_ref[(where_ref[1] % 4) ^ 3]

        @pl.when(step > blocks)
        def _():
            even_ref[...] = chunk


def middle(where, offset, mine, other, weight, cotangent, dense):
    rows, width = mine.shape
    n_rep, _, _, cols = dense.shape
    blocks = 4
    part = rows // blocks
    extra = width // n_rep // 4 * (width // cols)
    block = pl.BlockSpec((part, width), lambda i, where: (jnp.minimum(i, blocks - 1), 0))
    fixed = lambda *shape: pl.BlockSpec(shape, lambda i, where: (0,) * len(shape))
    shapes = [(width, rows), (width + extra, cols), (width, cols), (4, extra, cols)]

    def a_block(i, where):
        place = where[offset + jnp.maximum(i - blocks, 0)]
        return (place % n_rep, place // n_rep, 0, 0)

    return pl.pallas_call(
        functools.partial(middle_kernel, blocks),
        out_shape=[jax.ShapeDtypeStruct(shape, BF16) for shape in shapes],
        grid_spec=pltpu.PrefetchScalarGridSpec(
            num_scalar_prefetch=1,
            grid=(blocks + 2,),
            in_specs=[
                block,
                block,
                fixed(width, width),
                block,
                pl.BlockSpec((1, 1, rows, cols), a_block),
            ],
            out_specs=[
                pl.BlockSpec((width, part), lambda i, where: (0, jnp.minimum(i, blocks - 1))),
                *(fixed(*shape) for shape in shapes[1:]),
            ],
            scratch_shapes=[pltpu.VMEM((width, width), F32), pltpu.VMEM((width, rows), BF16)],
        ),
        compiler_params=pltpu.CompilerParams(vmem_limit_bytes=36 * 2**20),
        cost_estimate=pl.CostEstimate(
            flops=6 * rows * width * width + 4 * rows * width * cols,
            transcendentals=rows * width,
            bytes_accessed=rows * width * 12,
        ),
    )(where, mine, other, weight, cotangent, in_hbm(dense))


def activated_kernel(where_ref, mine_ref, other_ref, weight_ref, cot_ref, act_ref):
    act_ref[...] = slopes(mine_ref, other_ref, weight_ref, cot_ref)[1]


def activated_rows(where, mine, other, weight, cotangent, n_rep):
    rows, width = mine.shape
    part = rows // n_rep
    block = pl.BlockSpec((part, width), lambda i, where: (where[0], 0))
    fixed = lambda *shape: pl.BlockSpec(shape, lambda i, where: (0, 0))
    return pl.pallas_call(
        activated_kernel,
        out_shape=jax.ShapeDtypeStruct((part, width), BF16),
        grid_spec=pltpu.PrefetchScalarGridSpec(
            num_scalar_prefetch=1,
            grid=(1,),
            in_specs=[block, block, fixed(width, width), block],
            out_specs=fixed(part, width),
        ),
        compiler_params=pltpu.CompilerParams(vmem_limit_bytes=36 * 2**20),
        cost_estimate=pl.CostEstimate(
            flops=2 * part * width * width,
            transcendentals=part * width,
            bytes_accessed=part * width * 8,
        ),
    )(where, mine, other, weight, cotangent)


def backward_kernel(masks, where_ref, grad_ref, a_ref, *refs):
    term_ref, out_refs = (refs[0], refs[1:]) if masks else (None, refs)
    width = grad_ref.shape[0]
    chunk = jnp.dot(grad_ref[...], a_ref[0, 0], preferred_element_type=F32).astype(BF16)
    for number, out_ref in enumerate(out_refs):

        @pl.when(pl.program_id(0) == number)
        def _():
            out_ref[:width] = chunk
            if number < len(masks):
                out_ref[width:] = term_ref[(where_ref[1] % 4) ^ masks[number]]


def backward_part(where, offset, count, grad, dense, masks=(), term=None):
    width, rows = grad.shape
    n_rep, _, _, cols = dense.shape
    fixed = lambda *shape: pl.BlockSpec(shape, lambda i, where: (0,) * len(shape))
    extra = term.shape[1] if masks else 0
    shapes = [(width + extra * (number < len(masks)), cols) for number in range(count)]

    def a_block(i, where):
        place = where[offset + i]
        return (place % n_rep, place // n_rep, 0, 0)

    return pl.pallas_call(
        functools.partial(backward_kernel, masks),
        out_shape=[jax.ShapeDtypeStruct(shape, BF16) for shape in shapes],
        grid_spec=pltpu.PrefetchScalarGridSpec(
            num_scalar_prefetch=1,
            grid=(count,),
            in_specs=[fixed(width, rows), pl.BlockSpec((1, 1, rows, cols), a_block)]
            + ([fixed(*term.shape)] if masks else []),
            out_specs=[fixed(*shape) for shape in shapes],
        ),
        compiler_params=pltpu.CompilerParams(vmem_limit_bytes=36 * 2**20),
        cost_estimate=pl.CostEstimate(
            flops=2 * count * rows * width * cols,
            transcendentals=0,
            bytes_accessed=2 * count * rows * cols + 2 * count * width * cols + 2 * width * rows,
        ),
    )(where, grad, in_hbm(dense), *([term] if masks else []))


def final_kernel(n_parts, where_ref, *refs):
    parts, terms = refs[:n_parts], refs[n_parts:-2]
    out_ref, weight_out = refs[-2:]
    width = out_ref.shape[2]
    total = functools.reduce(jnp.add, [part[:width].astype(F32) for part in parts])
    out_ref[0] = total.T.astype(BF16)
    _, extra, cols = terms[0].shape
    quarter = extra * cols // width
    for number, term_ref in enumerate(terms):
        for other in range(term_ref.shape[0]):
            place = (where_ref[0] ^ other) * 4 + ((where_ref[1] % 4) ^ number)
            rows = pl.ds(pl.multiple_of(place * quarter, quarter), quarter)
            for turn in range(width // cols):
                weight_out[rows, turn * cols : (turn + 1) * cols] = term_ref[
                    other, turn * quarter : (turn + 1) * quarter
                ].astype(F32)


def final_sum(where, parts, terms):
    width, cols = parts[0].shape
    whole = lambda value: pl.BlockSpec(value.shape, lambda i, where: (0,) * value.ndim)
    outs = [
        jax.ShapeDtypeStruct((1, cols, width), BF16),
        jax.ShapeDtypeStruct((width, width), F32),
    ]
    return pl.pallas_call(
        functools.partial(final_kernel, len(parts)),
        out_shape=outs,
        grid_spec=pltpu.PrefetchScalarGridSpec(
            num_scalar_prefetch=1,
            grid=(1,),
            in_specs=[whole(value) for value in [*parts, *terms]],
            out_specs=[whole(value) for value in outs],
        ),
        compiler_params=pltpu.CompilerParams(vmem_limit_bytes=36 * 2**20),
        cost_estimate=pl.CostEstimate(
            flops=len(parts) * width * cols,
            transcendentals=0,
            bytes_accessed=2 * (len(parts) + 1) * width * cols,
        ),
    )(where, *parts, *terms)


def shards(sizes, features, weight, tile_values, tile_rows, tile_cols, tile_count, cotangent):
    n_section, n_rep = sizes
    block_rows, width = features.shape
    part = block_rows // n_rep
    section, rep = lax.axis_index("section"), lax.axis_index("rep")

    X, Y, Z = 1, 2, 4
    pair_count = n_section // 8
    low_bit = lambda mask: mask & -mask

    def flip(value, mask, rep_mask=0):
        pairs = [
            (s * n_rep + r, (s ^ mask) * n_rep + (r ^ rep_mask))
            for s in range(n_section)
            for r in range(n_rep)
        ]
        return lax.ppermute(value, BOTH, pairs)

    def gather_rep(value):
        held = [value] + [flip(value, 0, other) for other in range(1, n_rep)]
        order = rep ^ jnp.arange(n_rep)
        if n_rep == 2:
            held = [jnp.where(rep == 0, held[0], held[1]), jnp.where(rep == 0, held[1], held[0])]
            return jnp.concatenate(held)
        return jnp.stack(held)[order].reshape(-1, width)

    live = {}

    def close(*open_names):
        names = [name for name in live if name not in open_names]
        live.update(zip(names, lax.optimization_barrier([live[name] for name in names])))

    masks, offsets = [], {}

    def plan(name, wanted):
        offsets[name] = 2 + len(masks)
        masks.extend(wanted)

    for pair in range(pair_count):
        even, odd = 2 * pair * Z, (2 * pair + 1) * Z
        plan(("units", pair), [even, even + X, even + Y, odd, odd + X, odd + Y])
        plan(("crossed", pair), [even + X + Y, odd + X + Y])
        plan(("first", pair), [odd + X + Y, even + X + Y])
        plan(("odd", pair), [odd + X, odd + Y, odd])
        plan(("even", pair), [even + X, even + Y, even])
    where = jnp.concatenate(
        [rep[None], section[None], section ^ jnp.array(masks, jnp.int32)]
    ).astype(jnp.int32)

    def forward_step(names, units, total, kind=F32):
        with jax.named_scope("forward"):
            return forward_part(
                where, offsets[names], units, total, live["dense"], live["others"], kind
            )

    row_tiles = block_rows // tile_values.shape[3]
    packed = jnp.concatenate(
        [tile_rows[0] * row_tiles + tile_cols[0], tile_count[0][:, None]], axis=1
    )
    panels = tile_values.shape[1]
    def build_own(first):
        with jax.named_scope("dense_blocks"):
            live["dense"] = make_dense(
                first, live.get("dense"), where, tile_values[0], packed, block_rows, n_rep
            )

    def build_others(first):
        with jax.named_scope("other_blocks"):
            return [make_other(first, where, *sent, block_rows, n_rep) for sent in live["tiles"]]

    live[0] = lax.dynamic_slice_in_dim(features, rep * part, part, axis=0)
    with jax.named_scope("tiles_exchange"):
        live["tiles"] = [
            (flip(tile_values[0], 0, n), flip(packed, 0, n)) for n in range(1, n_rep)
        ]
    waiting = []
    for pair in range(pair_count):
        even, odd = 2 * pair * Z, (2 * pair + 1) * Z
        later = even + 2 * Z
        last = pair + 1 == pair_count

        with jax.named_scope("features_across"):
            live["even_x"], live["even_y"] = flip(live[even], X), flip(live[even], Y)
        with jax.named_scope("features_along_z"):
            live[odd] = flip(live[even], Z)
        if pair == 0:
            build_own(0)
        if pair == 1:
            two = build_others(panels // 2)
            live["others"] = [half for halves in zip(live.pop("one"), two) for half in halves]
            del live["tiles"]
        close()

        with jax.named_scope("features_across"):
            live["odd_x"], live["odd_y"] = flip(live[odd], X), flip(live[odd], Y)
        if not last:
            with jax.named_scope("features_along_z"):
                live[later] = flip(live[later - low_bit(later)], low_bit(later))
        if pair > 0:
            live["total"] = forward_step(*waiting, live.pop("waiting"), live.get("total"))
        if pair == 1:
            with jax.named_scope("cotangent_rows"):
                live["cotangent"] = gather_rep(cotangent)
        close(*([] if last else [later]))

        with jax.named_scope("features_across"):
            crossed = [flip(live["even_x"], Y), flip(live["odd_y"], X)]
        units = [live[even], live.pop("even_x"), live.pop("even_y")]
        units += [live[odd], live.pop("odd_x"), live.pop("odd_y")]
        if pair == 0:
            build_own(panels // 2)
            live["one"] = build_others(0)
            live["waiting"] = units + crossed
            waiting = [("units", pair)]
        else:
            live["total"] = forward_step(("units", pair), units, live["total"])
            live["waiting"] = crossed
            waiting = [("crossed", pair)]
        close()
    partial = forward_step(*waiting, live["waiting"], live.get("total"), BF16)

    with jax.named_scope("partial_sums"):
        other = flip(partial, 0, 1)
        for bit in range(1, n_rep.bit_length() - 1):
            partial = (partial.astype(F32) + other.astype(F32)).astype(BF16)
            other = flip(partial, 0, 1 << bit)

    with jax.named_scope("middle"):
        rows = (partial, other, weight, live["cotangent"])
        grad, odd_diag, even_diag, term = middle(
            where, offsets["first", pair_count - 1], *rows, live["dense"]
        )

    live = {"grad": grad, "dense": live["dense"], "term": term}
    add = lambda *values: functools.reduce(jnp.add, [value.astype(F32) for value in values])

    def backward_step(names, *carried):
        with jax.named_scope("backward"):
            count = sum(2 if name[0] == "first" else 3 for name in names)
            chunks = backward_part(
                where, offsets[names[0]], count, live["grad"], live["dense"], *carried
            )
            for name in names:
                size = 2 if name[0] == "first" else 3
                live[name[0]], chunks = chunks[:size], chunks[size:]

    z_masks = [1 << bit for bit in range(3, n_section.bit_length() - 1)]

    live["first"] = [odd_diag, even_diag]
    for pair in reversed(range(pair_count)):
        even = 2 * pair * Z
        top = pair + 1 == pair_count
        passing = [name for name in live if isinstance(name, tuple)]

        with jax.named_scope("grads_across"):
            odd_diag, even_diag = live.pop("first")
            live["odd_diag"], live["even_diag"] = flip(odd_diag, Y), flip(even_diag, X)
        if top:
            backward_step([("odd", pair), ("even", pair)], (X, Y, 0), live.pop("term"))
        else:
            with jax.named_scope("grads_along_z"):
                mask = low_bit(even + 2 * Z)
                target = even + 2 * Z - mask
                live["to", target, mask] = flip(live.pop("passed"), mask)
                passing = [("to", target, mask)]
            if "activated" not in live:
                with jax.named_scope("activated"):
                    live["activated"] = activated_rows(where, *rows, n_rep)
        close(*passing)

        with jax.named_scope("grads_across"):
            to_x, to_y, own = live.pop("odd")
            to_x = add(to_x, live.pop("odd_diag")).astype(BF16)
            live["odd_sum"] = [own, flip(to_x, X), flip(to_y, Y)]
            to_x, to_y, own = live.pop("even")
            live["even"] = [to_x, add(to_y, live.pop("even_diag")).astype(BF16), own]
        if pair > 0:
            following = live.pop("even")
            backward_step([("first", pair - 1), ("odd", pair - 1)])
            live["following"], live["even"] = live.pop("odd"), following
        close()

        with jax.named_scope("weight_grad"):
            if not top and z_masks and mask == z_masks[0]:
                z_masks.pop(0)
                arrived = live["to", target, mask][width:]
                live["weight"] = add(live["weight"], arrived).astype(BF16)
            if pair == 0:
                own = live.pop("weight")
                own = jnp.stack([own, *(flip(own, 0, n) for n in range(1, n_rep))])
                live["terms"] = [own, *(flip(own, m) for m in (X, Y, X + Y))]
        with jax.named_scope("grads_across"):
            to_x, to_y, own = live.pop("even")
            live["even_sum"] = [own, flip(to_x, X), flip(to_y, Y)]
        with jax.named_scope("grads_along_z"):
            odd_sum = add(*live.pop("odd_sum")).astype(BF16)
            from_odd = flip(odd_sum, Z)
            live["even_sum"].append(from_odd)
        if pair > 0:
            backward_step([("even", pair - 1)])
            live["odd"] = live.pop("following")
        if top:
            with jax.named_scope("weight_grad"):
                live["weight"] = add(odd_sum[width:], from_odd[width:]).astype(BF16)
        close()
        arrived = [name for name in live if isinstance(name, tuple) and name[1] == even]
        sums = [*live.pop("even_sum"), *(live.pop(name) for name in arrived)]
        if pair > 0:
            live["passed"] = add(*(value[:width] for value in sums)).astype(BF16)
            if z_masks and low_bit(even) == z_masks[0]:
                live["passed"] = jnp.concatenate([live["passed"], live["weight"]])
    with jax.named_scope("grads_out"):
        feat_grad, weight_grad = final_sum(where, sums, live["terms"])
    return (live["activated"], feat_grad, weight_grad)


def solution(mesh):
    placed = (
        P("section", None),
        P(),
        P("section", "rep", None, None, None),
        P("section", "rep", None),
        P("section", "rep", None),
        P("section", "rep"),
        P(("section", "rep"), None),
    )
    sizes = (mesh.shape["section"], mesh.shape["rep"])
    return jax.shard_map(
        functools.partial(shards, sizes),
        mesh=mesh,
        in_specs=placed,
        out_specs=(P(("section", "rep"), None), P("rep", "section", None), P()),
        check_vma=False,
    )
```

```python
import functools

import jax
import jax.numpy as jnp
from jax import lax
from jax.experimental import pallas as pl
from jax.experimental.pallas import tpu as pltpu
from jax.sharding import PartitionSpec as P

BF16 = jnp.bfloat16
F32 = jnp.float32
BOTH = ("section", "rep")


def in_hbm(value):
    return pltpu.with_memory_space_constraint(value, pltpu.HBM)


def dense_kernel(first, where_ref, packed_ref, tiles_ref, *refs):
    out_ref = refs[-1]
    panel = first + pl.program_id(0)
    size, slots = tiles_ref.shape[-1], tiles_ref.shape[1]
    row_tiles, per_part = out_ref.shape[2] // size, out_ref.shape[3] // size
    out_ref[...] = jnp.zeros_like(out_ref)

    def add_tile(slot, carry):
        place = packed_ref[panel, slot]
        row = pl.multiple_of(place // row_tiles * size, size)
        tile_col = place % row_tiles
        col = pl.multiple_of(tile_col % per_part * size, size)
        out_ref[tile_col // per_part, 0, pl.ds(row, size), pl.ds(col, size)] += tiles_ref[0, slot]
        return carry

    lax.fori_loop(0, packed_ref[panel, slots], add_tile, 0)


def make_dense(first, before, where, tiles, packed, block_rows, n_rep):
    panels, slots, size, _ = tiles.shape
    half = panels // 2
    part = block_rows // n_rep
    at = lambda p: first + p
    return pl.pallas_call(
        functools.partial(dense_kernel, first),
        out_shape=pltpu.HBM((n_rep, panels, block_rows, part), BF16),
        grid_spec=pltpu.PrefetchScalarGridSpec(
            num_scalar_prefetch=2,
            grid=(half,),
            in_specs=[pl.BlockSpec((1, slots, size, size), lambda p, *_: (at(p), 0, 0, 0))]
            + [pl.BlockSpec(memory_space=pl.ANY)] * (first > 0),
            out_specs=pl.BlockSpec((n_rep, 1, block_rows, part), lambda p, *_: (0, at(p), 0, 0)),
        ),
        input_output_aliases={3: 0} if first else {},
        compiler_params=pltpu.CompilerParams(vmem_limit_bytes=36 * 2**20),
        cost_estimate=pl.CostEstimate(
            flops=0,
            transcendentals=0,
            bytes_accessed=tiles.size // 8,
        ),
    )(where, packed, in_hbm(tiles), *([in_hbm(before)] if first else []))


def other_kernel(where_ref, packed_ref, tiles_ref, out_ref):
    panel = pl.program_id(0)
    size, slots = tiles_ref.shape[-1], tiles_ref.shape[1]
    row_tiles, per_part = out_ref.shape[1] // size, out_ref.shape[2] // size
    out_ref[...] = jnp.zeros_like(out_ref)

    def add_tile(slot, carry):
        place = packed_ref[panel, slot]
        row = pl.multiple_of(place // row_tiles * size, size)
        tile_col = place % row_tiles
        col = pl.multiple_of(tile_col % per_part * size, size)

        @pl.when(tile_col // per_part == where_ref[0])
        def _():
            out_ref[0, pl.ds(row, size), pl.ds(col, size)] += tiles_ref[0, slot]

        return carry

    lax.fori_loop(0, packed_ref[panel, slots], add_tile, 0)


def make_other(where, tiles, packed, block_rows, n_rep):
    panels, slots, size, _ = tiles.shape
    part = block_rows // n_rep
    return pl.pallas_call(
        other_kernel,
        out_shape=pltpu.HBM((panels, block_rows, part), BF16),
        grid_spec=pltpu.PrefetchScalarGridSpec(
            num_scalar_prefetch=2,
            grid=(panels,),
            in_specs=[pl.BlockSpec((1, slots, size, size), lambda p, *_: (p, 0, 0, 0))],
            out_specs=pl.BlockSpec((1, block_rows, part), lambda p, *_: (p, 0, 0)),
        ),
        compiler_params=pltpu.CompilerParams(vmem_limit_bytes=36 * 2**20),
        cost_estimate=pl.CostEstimate(
            flops=0, transcendentals=0, bytes_accessed=tiles.size // 8
        ),
    )(where, packed, tiles)


def forward_kernel(offset, n_units, n_others, has_total, where_ref, dense_ref, *refs):
    others, refs = refs[:n_others], refs[n_others:]
    units, refs = refs[:n_units], refs[n_units:]
    total_ref, refs = (refs[0], refs[1:]) if has_total else (None, refs)
    out_ref, sum_ref, a_buf, u_buf, sems, sum_sem = refs
    _, panels, _, part = dense_ref.shape
    rep = where_ref[0]

    def a_copy(source, slot, side):
        target = a_buf.at[slot, :, pl.ds(side * part, part)]
        return pltpu.make_async_copy(source, target, sems.at[0, slot, side])

    def u_copy(source, slot, side):
        target = u_buf.at[slot, pl.ds(side * part, part), :]
        return pltpu.make_async_copy(source, target, sems.at[1, slot, side])

    def fetch(pair, slot):
        for side in range(2):
            place = where_ref[offset + 2 * pair + side]
            owner, panel = place // panels, place % panels
            turn = (owner ^ rep) - 1

            @pl.when(owner == rep)
            def _():
                a_copy(dense_ref.at[rep, panel], slot, side).start()

            for number, other_ref in enumerate(others):

                @pl.when((owner != rep) & (turn == number))
                def _():
                    a_copy(other_ref.at[panel], slot, side).start()

            for number in range(side, n_units, 2):

                @pl.when(pair == number // 2)
                def _():
                    u_copy(units[number], slot, side).start()

    pairs = n_units // 2
    fetch(0, 0)
    if has_total:
        load = pltpu.make_async_copy(total_ref, sum_ref, sum_sem)
        load.start()
        load.wait()
    else:
        sum_ref[...] = jnp.zeros_like(sum_ref)

    def step(pair, carry):
        slot = pair % 2

        @pl.when(pair + 1 < pairs)
        def _():
            fetch(pair + 1, 1 - slot)

        for side in range(2):
            a_copy(dense_ref.at[0, 0], slot, side).wait()
            u_copy(units[0], slot, side).wait()
        sum_ref[...] += jnp.dot(a_buf[slot], u_buf[slot], preferred_element_type=F32)
        return carry

    lax.fori_loop(0, pairs, step, 0)
    if out_ref.dtype == F32:
        store = pltpu.make_async_copy(sum_ref, out_ref, sum_sem)
        store.start()
        store.wait()
    else:
        out_ref[...] = sum_ref[...].astype(out_ref.dtype)


def forward_part(where, offset, units, total, dense, others, kind):
    part, width = units[0].shape
    rows = dense.shape[2]
    near = pl.BlockSpec(memory_space=pl.ANY)
    hbm = pl.BlockSpec(memory_space=pltpu.HBM)
    has_total = total is not None
    n_units, n_others = len(units), len(others)
    return pl.pallas_call(
        functools.partial(forward_kernel, offset, n_units, n_others, has_total),
        out_shape=jax.ShapeDtypeStruct((rows, width), kind),
        grid_spec=pltpu.PrefetchScalarGridSpec(
            num_scalar_prefetch=1,
            grid=(1,),
            in_specs=[hbm] * (1 + n_others) + [near] * (n_units + has_total),
            out_specs=near if kind == F32 else pl.BlockSpec((rows, width), lambda i, where: (0, 0)),
            scratch_shapes=[
                pltpu.VMEM((rows, width), F32),
                pltpu.VMEM((2, rows, 2 * part), BF16),
                pltpu.VMEM((2, 2 * part, width), BF16),
                pltpu.SemaphoreType.DMA((2, 2, 2)),
                pltpu.SemaphoreType.DMA,
            ],
        ),
        compiler_params=pltpu.CompilerParams(vmem_limit_bytes=36 * 2**20),
        cost_estimate=pl.CostEstimate(
            flops=2 * n_units * rows * part * width,
            transcendentals=0,
            bytes_accessed=n_units * rows * part * 2 + 8 * rows * width,
        ),
    )(where, in_hbm(dense), *map(in_hbm, others), *units, *([total] if has_total else []))


def slopes(mine_ref, other_ref, weight_ref, cot_ref):
    agg = (mine_ref[...].astype(F32) + other_ref[...].astype(F32)).astype(BF16)
    pre = jnp.dot(agg, weight_ref[...], preferred_element_type=F32)
    sigma = 0.5 * jnp.tanh(0.5 * pre) + 0.5
    slope = cot_ref[...].astype(F32) * sigma * (1.0 + pre * (1.0 - sigma))
    return agg, (pre * sigma).astype(BF16), slope.astype(BF16)


def middle_kernel(blocks, where_ref, mine_ref, other_ref, weight_ref, cot_ref, a_ref, *refs):
    grad_ref, odd_ref, even_ref, term_ref, sum_ref, full_ref = refs
    step = pl.program_id(0)
    part = mine_ref.shape[0]

    @pl.when(step < blocks)
    def _():
        agg, _, pre_grad = slopes(mine_ref, other_ref, weight_ref, cot_ref)
        grad = lax.dot_general(
            weight_ref[...], pre_grad, (((1,), (1,)), ((), ())), preferred_element_type=F32
        ).astype(BF16)
        grad_ref[...] = grad
        full_ref[:, pl.ds(pl.multiple_of(step * part, part), part)] = grad
        term = lax.dot_general(agg, pre_grad, (((0,), (0,)), ((), ())), preferred_element_type=F32)

        @pl.when(step == 0)
        def _():
            sum_ref[...] = term

        @pl.when(step > 0)
        def _():
            sum_ref[...] += term

    @pl.when(step >= blocks)
    def _():
        chunk = jnp.dot(full_ref[...], a_ref[0, 0], preferred_element_type=F32).astype(BF16)

        @pl.when(step == blocks)
        def _():
            odd_ref[...] = chunk
            depth, size, _ = term_ref.shape
            z = where_ref[1] // 4
            for number in range(depth):
                start = (where_ref[0] * depth + (z ^ number)) * size
                rows = sum_ref[pl.ds(pl.multiple_of(start, size), size), :]
                term_ref[number] = rows.astype(BF16)

        @pl.when(step > blocks)
        def _():
            even_ref[...] = chunk


def middle(where, offset, mine, other, weight, cotangent, dense, depth):
    rows, width = mine.shape
    n_rep, _, _, cols = dense.shape
    blocks = 4
    part = rows // blocks
    size = width // n_rep // depth
    block = pl.BlockSpec((part, width), lambda i, where: (jnp.minimum(i, blocks - 1), 0))
    fixed = lambda *shape: pl.BlockSpec(shape, lambda i, where: (0,) * len(shape))
    shapes = [(width, rows), (width, cols), (width, cols), (depth, size, width)]

    def a_block(i, where):
        place = where[offset + jnp.maximum(i - blocks, 0)]
        return (place % n_rep, place // n_rep, 0, 0)

    return pl.pallas_call(
        functools.partial(middle_kernel, blocks),
        out_shape=[jax.ShapeDtypeStruct(shape, BF16) for shape in shapes],
        grid_spec=pltpu.PrefetchScalarGridSpec(
            num_scalar_prefetch=1,
            grid=(blocks + 2,),
            in_specs=[
                block,
                block,
                fixed(width, width),
                block,
                pl.BlockSpec((1, 1, rows, cols), a_block),
            ],
            out_specs=[
                pl.BlockSpec((width, part), lambda i, where: (0, jnp.minimum(i, blocks - 1))),
                *(fixed(*shape) for shape in shapes[1:]),
            ],
            scratch_shapes=[pltpu.VMEM((width, width), F32), pltpu.VMEM((width, rows), BF16)],
        ),
        compiler_params=pltpu.CompilerParams(vmem_limit_bytes=36 * 2**20),
        cost_estimate=pl.CostEstimate(
            flops=6 * rows * width * width + 4 * rows * width * cols,
            transcendentals=rows * width,
            bytes_accessed=rows * width * 12,
        ),
    )(where, mine, other, weight, cotangent, in_hbm(dense))


def activated_kernel(where_ref, mine_ref, other_ref, weight_ref, cot_ref, act_ref):
    act_ref[...] = slopes(mine_ref, other_ref, weight_ref, cot_ref)[1]


def activated_rows(where, mine, other, weight, cotangent, n_rep):
    rows, width = mine.shape
    part = rows // n_rep
    block = pl.BlockSpec((part, width), lambda i, where: (where[0], 0))
    fixed = lambda *shape: pl.BlockSpec(shape, lambda i, where: (0, 0))
    return pl.pallas_call(
        activated_kernel,
        out_shape=jax.ShapeDtypeStruct((part, width), BF16),
        grid_spec=pltpu.PrefetchScalarGridSpec(
            num_scalar_prefetch=1,
            grid=(1,),
            in_specs=[block, block, fixed(width, width), block],
            out_specs=fixed(part, width),
        ),
        compiler_params=pltpu.CompilerParams(vmem_limit_bytes=36 * 2**20),
        cost_estimate=pl.CostEstimate(
            flops=2 * part * width * width,
            transcendentals=part * width,
            bytes_accessed=part * width * 8,
        ),
    )(where, mine, other, weight, cotangent)


def backward_kernel(where_ref, grad_ref, a_ref, *out_refs):
    chunk = jnp.dot(grad_ref[...], a_ref[0, 0], preferred_element_type=F32).astype(BF16)
    for number, out_ref in enumerate(out_refs):

        @pl.when(pl.program_id(0) == number)
        def _():
            out_ref[...] = chunk


def backward_part(where, offset, count, grad, dense):
    width, rows = grad.shape
    n_rep, _, _, cols = dense.shape
    fixed = lambda *shape: pl.BlockSpec(shape, lambda i, where: (0, 0))

    def a_block(i, where):
        place = where[offset + i]
        return (place % n_rep, place // n_rep, 0, 0)

    return pl.pallas_call(
        backward_kernel,
        out_shape=[jax.ShapeDtypeStruct((width, cols), BF16)] * count,
        grid_spec=pltpu.PrefetchScalarGridSpec(
            num_scalar_prefetch=1,
            grid=(count,),
            in_specs=[fixed(width, rows), pl.BlockSpec((1, 1, rows, cols), a_block)],
            out_specs=[fixed(width, cols)] * count,
        ),
        compiler_params=pltpu.CompilerParams(vmem_limit_bytes=36 * 2**20),
        cost_estimate=pl.CostEstimate(
            flops=2 * count * rows * width * cols,
            transcendentals=0,
            bytes_accessed=2 * count * rows * cols + 2 * count * width * cols + 2 * width * rows,
        ),
    )(where, grad, in_hbm(dense))


def final_kernel(n_parts, where_ref, *refs):
    parts, terms = refs[:n_parts], refs[n_parts:-2]
    out_ref, weight_out = refs[-2:]
    total = functools.reduce(jnp.add, [part[...].astype(F32) for part in parts])
    out_ref[0] = total.T.astype(BF16)
    depth, size, _ = terms[0].shape
    for other, term_ref in enumerate(terms):
        for number in range(depth):
            place = (where_ref[0] ^ other) * depth + ((where_ref[1] // 4) ^ number)
            rows = pl.ds(pl.multiple_of(place * size, size), size)
            weight_out[rows, :] = term_ref[number].astype(F32)


def final_sum(where, parts, terms):
    width, cols = parts[0].shape
    whole = lambda value: pl.BlockSpec(value.shape, lambda i, where: (0,) * value.ndim)
    outs = [
        jax.ShapeDtypeStruct((1, cols, width), BF16),
        jax.ShapeDtypeStruct((width, width), F32),
    ]
    return pl.pallas_call(
        functools.partial(final_kernel, len(parts)),
        out_shape=outs,
        grid_spec=pltpu.PrefetchScalarGridSpec(
            num_scalar_prefetch=1,
            grid=(1,),
            in_specs=[whole(value) for value in [*parts, *terms]],
            out_specs=[whole(value) for value in outs],
        ),
        compiler_params=pltpu.CompilerParams(vmem_limit_bytes=36 * 2**20),
        cost_estimate=pl.CostEstimate(
            flops=len(parts) * width * cols,
            transcendentals=0,
            bytes_accessed=2 * (len(parts) + 1) * width * cols,
        ),
    )(where, *parts, *terms)


def shards(sizes, features, weight, tile_values, tile_rows, tile_cols, tile_count, cotangent):
    n_section, n_rep = sizes
    block_rows, width = features.shape
    part = block_rows // n_rep
    section, rep = lax.axis_index("section"), lax.axis_index("rep")

    X, Y, Z = 1, 2, 4
    pair_count = n_section // 8
    low_bit = lambda mask: mask & -mask

    def flip(value, mask, rep_mask=0):
        pairs = [
            (s * n_rep + r, (s ^ mask) * n_rep + (r ^ rep_mask))
            for s in range(n_section)
            for r in range(n_rep)
        ]
        return lax.ppermute(value, BOTH, pairs)

    def gather_rep(value):
        held = [value] + [flip(value, 0, other) for other in range(1, n_rep)]
        order = rep ^ jnp.arange(n_rep)
        if n_rep == 2:
            held = [jnp.where(rep == 0, held[0], held[1]), jnp.where(rep == 0, held[1], held[0])]
            return jnp.concatenate(held)
        return jnp.stack(held)[order].reshape(-1, width)

    live = {}

    def close(*open_names):
        names = [name for name in live if name not in open_names]
        live.update(zip(names, lax.optimization_barrier([live[name] for name in names])))

    masks, offsets = [], {}

    def plan(name, wanted):
        offsets[name] = 2 + len(masks)
        masks.extend(wanted)

    for pair in range(pair_count):
        even, odd = 2 * pair * Z, (2 * pair + 1) * Z
        plan(("units", pair), [even, even + X, even + Y, odd, odd + X, odd + Y])
        plan(("crossed", pair), [even + X + Y, odd + X + Y])
        plan(("first", pair), [odd + X + Y, even + X + Y])
        plan(("odd", pair), [odd + X, odd + Y, odd])
        plan(("even", pair), [even + X, even + Y, even])
    where = jnp.concatenate(
        [rep[None], section[None], section ^ jnp.array(masks, jnp.int32)]
    ).astype(jnp.int32)

    def forward_step(names, units, total, kind=F32):
        with jax.named_scope("forward"):
            return forward_part(
                where, offsets[names], units, total, live["dense"], live["others"], kind
            )

    row_tiles = block_rows // tile_values.shape[3]
    packed = jnp.concatenate(
        [tile_rows[0] * row_tiles + tile_cols[0], tile_count[0][:, None]], axis=1
    )
    panels = tile_values.shape[1]
    def build_own(first):
        with jax.named_scope("dense_blocks"):
            live["dense"] = make_dense(
                first, live.get("dense"), where, tile_values[0], packed, block_rows, n_rep
            )

    live[0] = lax.dynamic_slice_in_dim(features, rep * part, part, axis=0)
    with jax.named_scope("tiles_exchange"):
        live["tiles"] = [
            (flip(tile_values[0], 0, n), flip(packed, 0, n)) for n in range(1, n_rep)
        ]
    waiting = []
    for pair in range(pair_count):
        even, odd = 2 * pair * Z, (2 * pair + 1) * Z
        later = even + 2 * Z
        last = pair + 1 == pair_count

        with jax.named_scope("features_across"):
            live["even_x"], live["even_y"] = flip(live[even], X), flip(live[even], Y)
        with jax.named_scope("features_along_z"):
            live[odd] = flip(live[even], Z)
        if pair == 0:
            build_own(0)
        if pair == 1:
            with jax.named_scope("other_blocks"):
                live["others"] = [
                    make_other(where, *sent, block_rows, n_rep) for sent in live.pop("tiles")
                ]
        close()

        with jax.named_scope("features_across"):
            live["odd_x"], live["odd_y"] = flip(live[odd], X), flip(live[odd], Y)
        if not last:
            with jax.named_scope("features_along_z"):
                live[later] = flip(live[later - low_bit(later)], low_bit(later))
        if pair > 0:
            live["total"] = forward_step(*waiting, live.pop("waiting"), live.get("total"))
        if pair == 1:
            with jax.named_scope("cotangent_rows"):
                live["cotangent"] = gather_rep(cotangent)
        close(*([] if last else [later]))

        with jax.named_scope("features_across"):
            crossed = [flip(live["even_x"], Y), flip(live["odd_y"], X)]
        units = [live[even], live.pop("even_x"), live.pop("even_y")]
        units += [live[odd], live.pop("odd_x"), live.pop("odd_y")]
        if pair == 0:
            build_own(panels // 2)
            live["waiting"] = units + crossed
            waiting = [("units", pair)]
        else:
            live["total"] = forward_step(("units", pair), units, live["total"])
            live["waiting"] = crossed
            waiting = [("crossed", pair)]
        close()
    partial = forward_step(*waiting, live["waiting"], live.get("total"), BF16)

    with jax.named_scope("partial_sums"):
        other = flip(partial, 0, 1)
        for bit in range(1, n_rep.bit_length() - 1):
            partial = (partial.astype(F32) + other.astype(F32)).astype(BF16)
            other = flip(partial, 0, 1 << bit)

    with jax.named_scope("middle"):
        depth = n_section // 4
        rows = (partial, other, weight, live["cotangent"])
        grad, odd_diag, even_diag, term = middle(
            where, offsets["first", pair_count - 1], *rows, live["dense"], depth
        )

    live = {"grad": grad, "dense": live["dense"], "term": term}
    add = lambda *values: functools.reduce(jnp.add, [value.astype(F32) for value in values])

    def backward_step(names):
        with jax.named_scope("backward"):
            count = sum(2 if name[0] == "first" else 3 for name in names)
            chunks = backward_part(where, offsets[names[0]], count, live["grad"], live["dense"])
            for name in names:
                size = 2 if name[0] == "first" else 3
                live[name[0]], chunks = chunks[:size], chunks[size:]

    def weight_step(phase, after=None):
        if after:
            live[after], live["term"] = lax.optimization_barrier((live[after], live["term"]))
        term = live["term"]
        with jax.named_scope("weight_grad"):
            if phase == 0:
                parts = [term[0], *(flip(term[n], Z * n) for n in range(1, depth))]
                live["term"] = add(*parts).astype(BF16)
            elif phase == 1:
                parts = [term, *(flip(term, mask) for mask in (X, Y, X + Y))]
                live["term"] = (add(*parts[:2]) + add(*parts[2:])).astype(BF16)
            elif phase == 2:
                live["term"] = [term, *(flip(term, Z * n) for n in range(1, depth))]
            else:
                term = jnp.stack(term)
                live["terms"] = [term, *(flip(term, 0, n) for n in range(1, n_rep))]
                del live["term"]

    live["first"] = [odd_diag, even_diag]
    for pair in reversed(range(pair_count)):
        even = 2 * pair * Z
        top = pair + 1 == pair_count
        passing = [name for name in live if isinstance(name, tuple)]

        with jax.named_scope("grads_across"):
            odd_diag, even_diag = live.pop("first")
            live["odd_diag"], live["even_diag"] = flip(odd_diag, Y), flip(even_diag, X)
        if top:
            backward_step([("odd", pair), ("even", pair)])
            weight_step(0)
        else:
            with jax.named_scope("grads_along_z"):
                mask = low_bit(even + 2 * Z)
                target = even + 2 * Z - mask
                live["to", target, mask] = flip(live.pop("passed"), mask)
                passing = [("to", target, mask)]
            if "term" in live:
                weight_step(3)
        close(*passing)

        with jax.named_scope("grads_across"):
            to_x, to_y, own = live.pop("odd")
            to_x = add(to_x, live.pop("odd_diag")).astype(BF16)
            live["odd_sum"] = [own, flip(to_x, X), flip(to_y, Y)]
            to_x, to_y, own = live.pop("even")
            live["even"] = [to_x, add(to_y, live.pop("even_diag")).astype(BF16), own]
        if pair > 0:
            following = live.pop("even")
            backward_step([("first", pair - 1), ("odd", pair - 1)])
            live["following"], live["even"] = live.pop("odd"), following
            if top:
                weight_step(1, "following")
        close()

        with jax.named_scope("grads_across"):
            to_x, to_y, own = live.pop("even")
            live["even_sum"] = [own, flip(to_x, X), flip(to_y, Y)]
        with jax.named_scope("grads_along_z"):
            odd_sum = add(*live.pop("odd_sum")).astype(BF16)
            live["even_sum"].append(flip(odd_sum, Z))
        if top:
            weight_step(2)
        if pair > 0:
            backward_step([("even", pair - 1)])
            live["odd"] = live.pop("following")
        else:
            with jax.named_scope("activated"):
                live["activated"] = activated_rows(where, *rows, n_rep)
        close()
        arrived = [name for name in live if isinstance(name, tuple) and name[1] == even]
        sums = [*live.pop("even_sum"), *(live.pop(name) for name in arrived)]
        if pair > 0:
            live["passed"] = add(*sums).astype(BF16)
    with jax.named_scope("grads_out"):
        feat_grad, weight_grad = final_sum(where, sums, live["terms"])
    return (live["activated"], feat_grad, weight_grad)


def solution(mesh):
    placed = (
        P("section", None),
        P(),
        P("section", "rep", None, None, None),
        P("section", "rep", None),
        P("section", "rep", None),
        P("section", "rep"),
        P(("section", "rep"), None),
    )
    sizes = (mesh.shape["section"], mesh.shape["rep"])
    return jax.shard_map(
        functools.partial(shards, sizes),
        mesh=mesh,
        in_specs=placed,
        out_specs=(P(("section", "rep"), None), P("rep", "section", None), P()),
        check_vma=False,
    )
```

```python
import functools

import jax
import jax.numpy as jnp
from jax import lax
from jax.experimental import pallas as pl
from jax.experimental.pallas import tpu as pltpu
from jax.sharding import PartitionSpec as P

BF16 = jnp.bfloat16
F32 = jnp.float32
BOTH = ("section", "rep")


def in_hbm(value):
    return pltpu.with_memory_space_constraint(value, pltpu.HBM)


def dense_kernel(first, where_ref, packed_ref, tiles_ref, *refs):
    out_ref = refs[-1]
    panel = first + pl.program_id(0)
    size, slots = tiles_ref.shape[-1], tiles_ref.shape[1]
    row_tiles, per_part = out_ref.shape[2] // size, out_ref.shape[3] // size
    out_ref[...] = jnp.zeros_like(out_ref)

    def add_tile(slot, carry):
        place = packed_ref[panel, slot]
        row = pl.multiple_of(place // row_tiles * size, size)
        tile_col = place % row_tiles
        col = pl.multiple_of(tile_col % per_part * size, size)
        out_ref[tile_col // per_part, 0, pl.ds(row, size), pl.ds(col, size)] += tiles_ref[0, slot]
        return carry

    lax.fori_loop(0, packed_ref[panel, slots], add_tile, 0)


def make_dense(first, before, where, tiles, packed, block_rows, n_rep):
    panels, slots, size, _ = tiles.shape
    half = panels // 2
    part = block_rows // n_rep
    at = lambda p: first + p
    return pl.pallas_call(
        functools.partial(dense_kernel, first),
        out_shape=pltpu.HBM((n_rep, panels, block_rows, part), BF16),
        grid_spec=pltpu.PrefetchScalarGridSpec(
            num_scalar_prefetch=2,
            grid=(half,),
            in_specs=[pl.BlockSpec((1, slots, size, size), lambda p, *_: (at(p), 0, 0, 0))]
            + [pl.BlockSpec(memory_space=pl.ANY)] * (first > 0),
            out_specs=pl.BlockSpec((n_rep, 1, block_rows, part), lambda p, *_: (0, at(p), 0, 0)),
        ),
        input_output_aliases={3: 0} if first else {},
        compiler_params=pltpu.CompilerParams(vmem_limit_bytes=36 * 2**20),
        cost_estimate=pl.CostEstimate(
            flops=0,
            transcendentals=0,
            bytes_accessed=tiles.size // 8,
        ),
    )(where, packed, in_hbm(tiles), *([in_hbm(before)] if first else []))


def other_kernel(where_ref, packed_ref, tiles_ref, out_ref):
    panel = pl.program_id(0)
    size, slots = tiles_ref.shape[-1], tiles_ref.shape[1]
    row_tiles, per_part = out_ref.shape[1] // size, out_ref.shape[2] // size
    out_ref[...] = jnp.zeros_like(out_ref)

    def add_tile(slot, carry):
        place = packed_ref[panel, slot]
        row = pl.multiple_of(place // row_tiles * size, size)
        tile_col = place % row_tiles
        col = pl.multiple_of(tile_col % per_part * size, size)

        @pl.when(tile_col // per_part == where_ref[0])
        def _():
            out_ref[0, pl.ds(row, size), pl.ds(col, size)] += tiles_ref[0, slot]

        return carry

    lax.fori_loop(0, packed_ref[panel, slots], add_tile, 0)


def make_other(where, tiles, packed, block_rows, n_rep):
    panels, slots, size, _ = tiles.shape
    part = block_rows // n_rep
    return pl.pallas_call(
        other_kernel,
        out_shape=pltpu.HBM((panels, block_rows, part), BF16),
        grid_spec=pltpu.PrefetchScalarGridSpec(
            num_scalar_prefetch=2,
            grid=(panels,),
            in_specs=[pl.BlockSpec((1, slots, size, size), lambda p, *_: (p, 0, 0, 0))],
            out_specs=pl.BlockSpec((1, block_rows, part), lambda p, *_: (p, 0, 0)),
        ),
        compiler_params=pltpu.CompilerParams(vmem_limit_bytes=36 * 2**20),
        cost_estimate=pl.CostEstimate(
            flops=0, transcendentals=0, bytes_accessed=tiles.size // 8
        ),
    )(where, packed, tiles)


def forward_kernel(offset, n_units, n_others, has_total, where_ref, dense_ref, *refs):
    others, refs = refs[:n_others], refs[n_others:]
    units, refs = refs[:n_units], refs[n_units:]
    total_ref, refs = (refs[0], refs[1:]) if has_total else (None, refs)
    out_ref, sum_ref, a_buf, u_buf, sems, sum_sem = refs
    _, panels, _, part = dense_ref.shape
    rep = where_ref[0]

    def a_copy(source, slot, side):
        target = a_buf.at[slot, :, pl.ds(side * part, part)]
        return pltpu.make_async_copy(source, target, sems.at[0, slot, side])

    def u_copy(source, slot, side):
        target = u_buf.at[slot, pl.ds(side * part, part), :]
        return pltpu.make_async_copy(source, target, sems.at[1, slot, side])

    def fetch(pair, slot):
        for side in range(2):
            place = where_ref[offset + 2 * pair + side]
            owner, panel = place // panels, place % panels
            turn = (owner ^ rep) - 1

            @pl.when(owner == rep)
            def _():
                a_copy(dense_ref.at[rep, panel], slot, side).start()

            for number, other_ref in enumerate(others):

                @pl.when((owner != rep) & (turn == number))
                def _():
                    a_copy(other_ref.at[panel], slot, side).start()

            for number in range(side, n_units, 2):

                @pl.when(pair == number // 2)
                def _():
                    u_copy(units[number], slot, side).start()

    pairs = n_units // 2
    fetch(0, 0)
    if has_total:
        load = pltpu.make_async_copy(total_ref, sum_ref, sum_sem)
        load.start()
        load.wait()
    else:
        sum_ref[...] = jnp.zeros_like(sum_ref)

    def step(pair, carry):
        slot = pair % 2

        @pl.when(pair + 1 < pairs)
        def _():
            fetch(pair + 1, 1 - slot)

        for side in range(2):
            a_copy(dense_ref.at[0, 0], slot, side).wait()
            u_copy(units[0], slot, side).wait()
        sum_ref[...] += jnp.dot(a_buf[slot], u_buf[slot], preferred_element_type=F32)
        return carry

    lax.fori_loop(0, pairs, step, 0)
    if out_ref.dtype == F32:
        store = pltpu.make_async_copy(sum_ref, out_ref, sum_sem)
        store.start()
        store.wait()
    else:
        out_ref[...] = sum_ref[...].astype(out_ref.dtype)


def forward_part(where, offset, units, total, dense, others, kind):
    part, width = units[0].shape
    rows = dense.shape[2]
    near = pl.BlockSpec(memory_space=pl.ANY)
    hbm = pl.BlockSpec(memory_space=pltpu.HBM)
    has_total = total is not None
    n_units, n_others = len(units), len(others)
    return pl.pallas_call(
        functools.partial(forward_kernel, offset, n_units, n_others, has_total),
        out_shape=jax.ShapeDtypeStruct((rows, width), kind),
        grid_spec=pltpu.PrefetchScalarGridSpec(
            num_scalar_prefetch=1,
            grid=(1,),
            in_specs=[hbm] * (1 + n_others) + [near] * (n_units + has_total),
            out_specs=near if kind == F32 else pl.BlockSpec((rows, width), lambda i, where: (0, 0)),
            scratch_shapes=[
                pltpu.VMEM((rows, width), F32),
                pltpu.VMEM((2, rows, 2 * part), BF16),
                pltpu.VMEM((2, 2 * part, width), BF16),
                pltpu.SemaphoreType.DMA((2, 2, 2)),
                pltpu.SemaphoreType.DMA,
            ],
        ),
        compiler_params=pltpu.CompilerParams(vmem_limit_bytes=36 * 2**20),
        cost_estimate=pl.CostEstimate(
            flops=2 * n_units * rows * part * width,
            transcendentals=0,
            bytes_accessed=n_units * rows * part * 2 + 8 * rows * width,
        ),
    )(where, in_hbm(dense), *map(in_hbm, others), *units, *([total] if has_total else []))


def slopes(mine_ref, other_ref, weight_ref, cot_ref):
    agg = (mine_ref[...].astype(F32) + other_ref[...].astype(F32)).astype(BF16)
    pre = jnp.dot(agg, weight_ref[...], preferred_element_type=F32)
    sigma = 0.5 * jnp.tanh(0.5 * pre) + 0.5
    slope = cot_ref[...].astype(F32) * sigma * (1.0 + pre * (1.0 - sigma))
    return agg, (pre * sigma).astype(BF16), slope.astype(BF16)


def middle_kernel(blocks, where_ref, mine_ref, other_ref, weight_ref, cot_ref, a_ref, *refs):
    grad_ref, odd_ref, even_ref, term_ref, sum_ref, full_ref = refs
    step = pl.program_id(0)
    part = mine_ref.shape[0]

    @pl.when(step < blocks)
    def _():
        agg, _, pre_grad = slopes(mine_ref, other_ref, weight_ref, cot_ref)
        grad = lax.dot_general(
            weight_ref[...], pre_grad, (((1,), (1,)), ((), ())), preferred_element_type=F32
        ).astype(BF16)
        grad_ref[...] = grad
        full_ref[:, pl.ds(pl.multiple_of(step * part, part), part)] = grad
        term = lax.dot_general(agg, pre_grad, (((0,), (0,)), ((), ())), preferred_element_type=F32)

        @pl.when(step == 0)
        def _():
            sum_ref[...] = term

        @pl.when(step > 0)
        def _():
            sum_ref[...] += term

    @pl.when(step >= blocks)
    def _():
        chunk = jnp.dot(full_ref[...], a_ref[0, 0], preferred_element_type=F32).astype(BF16)

        @pl.when(step == blocks)
        def _():
            odd_ref[...] = chunk
            depth, size, _ = term_ref.shape
            z = where_ref[1] // 4
            for number in range(depth):
                start = (where_ref[0] * depth + (z ^ number)) * size
                rows = sum_ref[pl.ds(pl.multiple_of(start, size), size), :]
                term_ref[number] = rows.astype(BF16)

        @pl.when(step > blocks)
        def _():
            even_ref[...] = chunk


def middle(where, offset, mine, other, weight, cotangent, dense, depth):
    rows, width = mine.shape
    n_rep, _, _, cols = dense.shape
    blocks = 4
    part = rows // blocks
    size = width // n_rep // depth
    block = pl.BlockSpec((part, width), lambda i, where: (jnp.minimum(i, blocks - 1), 0))
    fixed = lambda *shape: pl.BlockSpec(shape, lambda i, where: (0,) * len(shape))
    shapes = [(width, rows), (width, cols), (width, cols), (depth, size, width)]

    def a_block(i, where):
        place = where[offset + jnp.maximum(i - blocks, 0)]
        return (place % n_rep, place // n_rep, 0, 0)

    return pl.pallas_call(
        functools.partial(middle_kernel, blocks),
        out_shape=[jax.ShapeDtypeStruct(shape, BF16) for shape in shapes],
        grid_spec=pltpu.PrefetchScalarGridSpec(
            num_scalar_prefetch=1,
            grid=(blocks + 2,),
            in_specs=[
                block,
                block,
                fixed(width, width),
                block,
                pl.BlockSpec((1, 1, rows, cols), a_block),
            ],
            out_specs=[
                pl.BlockSpec((width, part), lambda i, where: (0, jnp.minimum(i, blocks - 1))),
                *(fixed(*shape) for shape in shapes[1:]),
            ],
            scratch_shapes=[pltpu.VMEM((width, width), F32), pltpu.VMEM((width, rows), BF16)],
        ),
        compiler_params=pltpu.CompilerParams(vmem_limit_bytes=36 * 2**20),
        cost_estimate=pl.CostEstimate(
            flops=6 * rows * width * width + 4 * rows * width * cols,
            transcendentals=rows * width,
            bytes_accessed=rows * width * 12,
        ),
    )(where, mine, other, weight, cotangent, in_hbm(dense))


def activated_kernel(where_ref, mine_ref, other_ref, weight_ref, cot_ref, act_ref):
    act_ref[...] = slopes(mine_ref, other_ref, weight_ref, cot_ref)[1]


def activated_rows(where, mine, other, weight, cotangent, n_rep):
    rows, width = mine.shape
    part = rows // n_rep
    block = pl.BlockSpec((part, width), lambda i, where: (where[0], 0))
    fixed = lambda *shape: pl.BlockSpec(shape, lambda i, where: (0, 0))
    return pl.pallas_call(
        activated_kernel,
        out_shape=jax.ShapeDtypeStruct((part, width), BF16),
        grid_spec=pltpu.PrefetchScalarGridSpec(
            num_scalar_prefetch=1,
            grid=(1,),
            in_specs=[block, block, fixed(width, width), block],
            out_specs=fixed(part, width),
        ),
        compiler_params=pltpu.CompilerParams(vmem_limit_bytes=36 * 2**20),
        cost_estimate=pl.CostEstimate(
            flops=2 * part * width * width,
            transcendentals=part * width,
            bytes_accessed=part * width * 8,
        ),
    )(where, mine, other, weight, cotangent)


def backward_kernel(where_ref, grad_ref, a_ref, *out_refs):
    chunk = jnp.dot(grad_ref[...], a_ref[0, 0], preferred_element_type=F32).astype(BF16)
    for number, out_ref in enumerate(out_refs):

        @pl.when(pl.program_id(0) == number)
        def _():
            out_ref[...] = chunk


def backward_part(where, offset, count, grad, dense):
    width, rows = grad.shape
    n_rep, _, _, cols = dense.shape
    fixed = lambda *shape: pl.BlockSpec(shape, lambda i, where: (0, 0))

    def a_block(i, where):
        place = where[offset + i]
        return (place % n_rep, place // n_rep, 0, 0)

    return pl.pallas_call(
        backward_kernel,
        out_shape=[jax.ShapeDtypeStruct((width, cols), BF16)] * count,
        grid_spec=pltpu.PrefetchScalarGridSpec(
            num_scalar_prefetch=1,
            grid=(count,),
            in_specs=[fixed(width, rows), pl.BlockSpec((1, 1, rows, cols), a_block)],
            out_specs=[fixed(width, cols)] * count,
        ),
        compiler_params=pltpu.CompilerParams(vmem_limit_bytes=36 * 2**20),
        cost_estimate=pl.CostEstimate(
            flops=2 * count * rows * width * cols,
            transcendentals=0,
            bytes_accessed=2 * count * rows * cols + 2 * count * width * cols + 2 * width * rows,
        ),
    )(where, grad, in_hbm(dense))


def final_kernel(n_parts, n_halves, z_order, where_ref, *refs):
    parts, terms = refs[:n_parts], refs[n_parts + n_halves : -2]
    halves = refs[n_parts : n_parts + n_halves]
    out_ref, weight_out = refs[-2:]
    values = [part[...].astype(F32) for part in parts]
    for top, end in zip(halves[::2], halves[1::2]):
        values.append(jnp.concatenate([top[...].astype(F32), end[...].astype(F32)]))
    total = functools.reduce(jnp.add, values)
    out_ref[0] = total.T.astype(BF16)
    depth, size, _ = terms[0].shape
    for other, term_ref in enumerate(terms):
        for number, offset in enumerate(z_order):
            place = (where_ref[0] ^ other) * depth + ((where_ref[1] // 4) ^ offset)
            rows = pl.ds(pl.multiple_of(place * size, size), size)
            weight_out[rows, :] = term_ref[number].astype(F32)


def final_sum(where, parts, halves, terms, z_order):
    width, cols = parts[0].shape
    halves = [half for pair in halves for half in pair]
    whole = lambda value: pl.BlockSpec(value.shape, lambda i, where: (0,) * value.ndim)
    outs = [
        jax.ShapeDtypeStruct((1, cols, width), BF16),
        jax.ShapeDtypeStruct((width, width), F32),
    ]
    return pl.pallas_call(
        functools.partial(final_kernel, len(parts), len(halves), z_order),
        out_shape=outs,
        grid_spec=pltpu.PrefetchScalarGridSpec(
            num_scalar_prefetch=1,
            grid=(1,),
            in_specs=[whole(value) for value in [*parts, *halves, *terms]],
            out_specs=[whole(value) for value in outs],
        ),
        compiler_params=pltpu.CompilerParams(vmem_limit_bytes=36 * 2**20),
        cost_estimate=pl.CostEstimate(
            flops=len(parts) * width * cols,
            transcendentals=0,
            bytes_accessed=2 * (len(parts) + 1) * width * cols,
        ),
    )(where, *parts, *halves, *terms)


def shards(sizes, features, weight, tile_values, tile_rows, tile_cols, tile_count, cotangent):
    n_section, n_rep = sizes
    block_rows, width = features.shape
    part = block_rows // n_rep
    section, rep = lax.axis_index("section"), lax.axis_index("rep")

    X, Y, Z = 1, 2, 4
    pair_count = n_section // 8
    low_bit = lambda mask: mask & -mask

    def flip(value, mask, rep_mask=0):
        pairs = [
            (s * n_rep + r, (s ^ mask) * n_rep + (r ^ rep_mask))
            for s in range(n_section)
            for r in range(n_rep)
        ]
        return lax.ppermute(value, BOTH, pairs)

    def gather_rep(value):
        held = [value] + [flip(value, 0, other) for other in range(1, n_rep)]
        order = rep ^ jnp.arange(n_rep)
        if n_rep == 2:
            held = [jnp.where(rep == 0, held[0], held[1]), jnp.where(rep == 0, held[1], held[0])]
            return jnp.concatenate(held)
        return jnp.stack(held)[order].reshape(-1, width)

    live = {}

    def close(*open_names):
        names = [name for name in live if name not in open_names]
        live.update(zip(names, lax.optimization_barrier([live[name] for name in names])))

    masks, offsets = [], {}

    def plan(name, wanted):
        offsets[name] = 2 + len(masks)
        masks.extend(wanted)

    for pair in range(pair_count):
        even, odd = 2 * pair * Z, (2 * pair + 1) * Z
        plan(("units", pair), [even, even + X, even + Y, odd, odd + X, odd + Y])
        plan(("crossed", pair), [even + X + Y, odd + X + Y])
        plan(("first", pair), [odd + X + Y, even + X + Y])
        plan(("odd", pair), [odd + X, odd + Y, odd])
        plan(("even", pair), [even + X, even + Y, even])
    where = jnp.concatenate(
        [rep[None], section[None], section ^ jnp.array(masks, jnp.int32)]
    ).astype(jnp.int32)

    def forward_step(names, units, total, kind=F32):
        with jax.named_scope("forward"):
            return forward_part(
                where, offsets[names], units, total, live["dense"], live["others"], kind
            )

    row_tiles = block_rows // tile_values.shape[3]
    packed = jnp.concatenate(
        [tile_rows[0] * row_tiles + tile_cols[0], tile_count[0][:, None]], axis=1
    )
    panels = tile_values.shape[1]
    def build_own(first):
        with jax.named_scope("dense_blocks"):
            live["dense"] = make_dense(
                first, live.get("dense"), where, tile_values[0], packed, block_rows, n_rep
            )

    live[0] = lax.dynamic_slice_in_dim(features, rep * part, part, axis=0)
    with jax.named_scope("tiles_exchange"):
        live["tiles"] = [
            (flip(tile_values[0], 0, n), flip(packed, 0, n)) for n in range(1, n_rep)
        ]
    waiting = []
    for pair in range(pair_count):
        even, odd = 2 * pair * Z, (2 * pair + 1) * Z
        later = even + 2 * Z
        last = pair + 1 == pair_count

        with jax.named_scope("features_across"):
            live["even_x"], live["even_y"] = flip(live[even], X), flip(live[even], Y)
        with jax.named_scope("features_along_z"):
            live[odd] = flip(live[even], Z)
        if pair == 0:
            build_own(0)
        if pair == 1:
            with jax.named_scope("other_blocks"):
                live["others"] = [
                    make_other(where, *sent, block_rows, n_rep) for sent in live.pop("tiles")
                ]
        close()

        with jax.named_scope("features_across"):
            live["odd_x"], live["odd_y"] = flip(live[odd], X), flip(live[odd], Y)
        if not last:
            with jax.named_scope("features_along_z"):
                live[later] = flip(live[later - low_bit(later)], low_bit(later))
        if pair > 0:
            live["total"] = forward_step(*waiting, live.pop("waiting"), live.get("total"))
        close(*([] if last else [later]))

        with jax.named_scope("features_across"):
            crossed = [flip(live["even_x"], Y), flip(live["odd_y"], X)]
        units = [live[even], live.pop("even_x"), live.pop("even_y")]
        units += [live[odd], live.pop("odd_x"), live.pop("odd_y")]
        if pair == 0:
            build_own(panels // 2)
            live["waiting"] = units + crossed
            waiting = [("units", pair)]
        else:
            live["total"] = forward_step(("units", pair), units, live["total"])
            live["waiting"] = crossed
            waiting = [("crossed", pair)]
        if last:
            with jax.named_scope("cotangent_rows"):
                live["cotangent"] = gather_rep(cotangent)
        close()
    partial = forward_step(*waiting, live["waiting"], live.get("total"), BF16)

    with jax.named_scope("partial_sums"):
        other = flip(partial, 0, 1)
        for bit in range(1, n_rep.bit_length() - 1):
            partial = (partial.astype(F32) + other.astype(F32)).astype(BF16)
            other = flip(partial, 0, 1 << bit)

    with jax.named_scope("middle"):
        depth = n_section // 4
        rows = (partial, other, weight, live["cotangent"])
        grad, odd_diag, even_diag, term = middle(
            where, offsets["first", pair_count - 1], *rows, live["dense"], depth
        )

    live = {"grad": grad, "dense": live["dense"], "term": term}
    add = lambda *values: functools.reduce(jnp.add, [value.astype(F32) for value in values])

    def backward_step(names):
        with jax.named_scope("backward"):
            count = sum(2 if name[0] == "first" else 3 for name in names)
            chunks = backward_part(where, offsets[names[0]], count, live["grad"], live["dense"])
            for name in names:
                size = 2 if name[0] == "first" else 3
                live[name[0]], chunks = chunks[:size], chunks[size:]

    gather_masks = [Z << bit for bit in reversed(range(depth.bit_length() - 1))]
    z_order = [0]

    def weight_step(phase, after=None):
        if after:
            live[after], live["term"] = lax.optimization_barrier((live[after], live["term"]))
        term = live["term"]
        with jax.named_scope("weight_grad"):
            if phase == 0:
                parts = [term[0], *(flip(term[n], Z * n) for n in range(1, depth))]
                live["term"] = add(*parts).astype(BF16)
            elif phase == 1:
                parts = [term, *(flip(term, mask) for mask in (X, Y, X + Y))]
                live["term"] = (add(*parts[:2]) + add(*parts[2:])).astype(BF16)
            elif gather_masks:
                if term.ndim == 2:
                    term = term[None]
                mask = gather_masks.pop(0)
                live["term"] = jnp.concatenate([term, flip(term, mask)])
                z_order.extend([mask // Z ^ other for other in z_order])
            else:
                live["terms"] = [term, *(flip(term, 0, n) for n in range(1, n_rep))]
                del live["term"]

    live["first"] = [odd_diag, even_diag]
    for pair in reversed(range(pair_count)):
        even = 2 * pair * Z
        top = pair + 1 == pair_count
        with jax.named_scope("grads_across"):
            odd_diag, even_diag = live.pop("first")
            live["odd_diag"], live["even_diag"] = flip(odd_diag, Y), flip(even_diag, X)
        if top:
            backward_step([("odd", pair), ("even", pair)])
            weight_step(0)
        else:
            with jax.named_scope("grads_along_z"):
                mask = low_bit(even + 2 * Z)
                target = even + 2 * Z - mask
                live["to", target, mask] = [flip(live["passed"][0], mask)]
            if "term" in live:
                weight_step(3)
        close()

        with jax.named_scope("grads_across"):
            to_x, to_y, own = live.pop("odd")
            to_x = add(to_x, live.pop("odd_diag")).astype(BF16)
            live["odd_sum"] = [own, flip(to_x, X), flip(to_y, Y)]
            to_x, to_y, own = live.pop("even")
            live["even"] = [to_x, add(to_y, live.pop("even_diag")).astype(BF16), own]
        if pair > 0:
            following = live.pop("even")
            backward_step([("first", pair - 1), ("odd", pair - 1)])
            live["following"], live["even"] = live.pop("odd"), following
            if top:
                weight_step(1, "following")
        if not top:
            with jax.named_scope("grads_along_z"):
                live["to", target, mask].append(flip(live.pop("passed")[1], mask))
            if "term" in live:
                weight_step(4)
        close()

        with jax.named_scope("grads_across"):
            to_x, to_y, own = live.pop("even")
            live["even_sum"] = [own, flip(to_x, X), flip(to_y, Y)]
        with jax.named_scope("grads_along_z"):
            odd_sum = add(*live.pop("odd_sum")).astype(BF16)
            live["even_sum"].append(flip(odd_sum, Z))
        if top:
            weight_step(2)
        if pair > 0:
            backward_step([("even", pair - 1)])
            live["odd"] = live.pop("following")
        else:
            with jax.named_scope("activated"):
                live["activated"] = activated_rows(where, *rows, n_rep)
        close()
        arrived = [name for name in live if isinstance(name, tuple) and name[1] == even]
        sums = live.pop("even_sum")
        halves = [live.pop(name) for name in arrived]
        if pair > 0:
            half = width // 2
            tops = [value[:half] for value in sums] + [value[0] for value in halves]
            ends = [value[half:] for value in sums] + [value[1] for value in halves]
            live["passed"] = [add(*tops).astype(BF16), add(*ends).astype(BF16)]
    with jax.named_scope("grads_out"):
        feat_grad, weight_grad = final_sum(where, sums, halves, live["terms"], tuple(z_order))
    return (live["activated"], feat_grad, weight_grad)


def solution(mesh):
    placed = (
        P("section", None),
        P(),
        P("section", "rep", None, None, None),
        P("section", "rep", None),
        P("section", "rep", None),
        P("section", "rep"),
        P(("section", "rep"), None),
    )
    sizes = (mesh.shape["section"], mesh.shape["rep"])
    return jax.shard_map(
        functools.partial(shards, sizes),
        mesh=mesh,
        in_specs=placed,
        out_specs=(P(("section", "rep"), None), P("rep", "section", None), P()),
        check_vma=False,
    )
```

```python
import functools

import jax
import jax.numpy as jnp
from jax import lax
from jax.experimental import pallas as pl
from jax.experimental.pallas import tpu as pltpu
from jax.sharding import PartitionSpec as P

BF16 = jnp.bfloat16
F32 = jnp.float32
BOTH = ("section", "rep")


def in_hbm(value):
    return pltpu.with_memory_space_constraint(value, pltpu.HBM)


def dense_kernel(first, where_ref, packed_ref, tiles_ref, *refs):
    out_ref = refs[-1]
    panel = first + pl.program_id(0)
    size, slots = tiles_ref.shape[-1], tiles_ref.shape[1]
    row_tiles, per_part = out_ref.shape[2] // size, out_ref.shape[3] // size
    out_ref[...] = jnp.zeros_like(out_ref)

    def add_tile(slot, carry):
        place = packed_ref[panel, slot]
        row = pl.multiple_of(place // row_tiles * size, size)
        tile_col = place % row_tiles
        col = pl.multiple_of(tile_col % per_part * size, size)
        out_ref[tile_col // per_part, 0, pl.ds(row, size), pl.ds(col, size)] += tiles_ref[0, slot]
        return carry

    lax.fori_loop(0, packed_ref[panel, slots], add_tile, 0)


def make_dense(first, before, where, tiles, packed, block_rows, n_rep):
    panels, slots, size, _ = tiles.shape
    half = panels // 2
    part = block_rows // n_rep
    at = lambda p: first + p
    return pl.pallas_call(
        functools.partial(dense_kernel, first),
        out_shape=pltpu.HBM((n_rep, panels, block_rows, part), BF16),
        grid_spec=pltpu.PrefetchScalarGridSpec(
            num_scalar_prefetch=2,
            grid=(half,),
            in_specs=[pl.BlockSpec((1, slots, size, size), lambda p, *_: (at(p), 0, 0, 0))]
            + [pl.BlockSpec(memory_space=pl.ANY)] * (first > 0),
            out_specs=pl.BlockSpec((n_rep, 1, block_rows, part), lambda p, *_: (0, at(p), 0, 0)),
        ),
        input_output_aliases={3: 0} if first else {},
        compiler_params=pltpu.CompilerParams(vmem_limit_bytes=36 * 2**20),
        cost_estimate=pl.CostEstimate(
            flops=0,
            transcendentals=0,
            bytes_accessed=tiles.size // 8,
        ),
    )(where, packed, in_hbm(tiles), *([in_hbm(before)] if first else []))


def other_kernel(first, where_ref, packed_ref, tiles_ref, out_ref):
    panel = first + pl.program_id(0)
    size, slots = tiles_ref.shape[-1], tiles_ref.shape[1]
    row_tiles, per_part = out_ref.shape[1] // size, out_ref.shape[2] // size
    out_ref[...] = jnp.zeros_like(out_ref)

    def add_tile(slot, carry):
        place = packed_ref[panel, slot]
        row = pl.multiple_of(place // row_tiles * size, size)
        tile_col = place % row_tiles
        col = pl.multiple_of(tile_col % per_part * size, size)

        @pl.when(tile_col // per_part == where_ref[0])
        def _():
            out_ref[0, pl.ds(row, size), pl.ds(col, size)] += tiles_ref[0, slot]

        return carry

    lax.fori_loop(0, packed_ref[panel, slots], add_tile, 0)


def make_other(first, where, tiles, packed, block_rows, n_rep):
    panels, slots, size, _ = tiles.shape
    half = panels // 2
    part = block_rows // n_rep
    return pl.pallas_call(
        functools.partial(other_kernel, first),
        out_shape=pltpu.HBM((half, block_rows, part), BF16),
        grid_spec=pltpu.PrefetchScalarGridSpec(
            num_scalar_prefetch=2,
            grid=(half,),
            in_specs=[pl.BlockSpec((1, slots, size, size), lambda p, *_: (first + p, 0, 0, 0))],
            out_specs=pl.BlockSpec((1, block_rows, part), lambda p, *_: (p, 0, 0)),
        ),
        compiler_params=pltpu.CompilerParams(vmem_limit_bytes=36 * 2**20),
        cost_estimate=pl.CostEstimate(
            flops=0, transcendentals=0, bytes_accessed=tiles.size // 8
        ),
    )(where, packed, tiles)


def forward_kernel(offset, n_pieces, n_others, has_total, where_ref, dense_ref, *refs):
    others, refs = refs[:n_others], refs[n_others:]
    units = []
    for pieces in n_pieces:
        tops, refs = refs[:pieces], refs[pieces:]
        half = tops[0].shape[0] // (2 if pieces == 1 else 1)
        units.append([tops[0].at[pl.ds(0, half)], tops[-1].at[pl.ds(half * (2 - pieces), half)]])
    n_units = len(units)
    total_ref, refs = (refs[0], refs[1:]) if has_total else (None, refs)
    out_ref, sum_ref, a_buf, u_buf, sems, sum_sem = refs
    _, panels, _, part = dense_ref.shape
    some = others[0].shape[0]
    rep = where_ref[0]

    def a_copy(source, slot, side):
        target = a_buf.at[slot, :, pl.ds(side * part, part)]
        return pltpu.make_async_copy(source, target, sems.at[0, slot, side])

    def u_copy(source, slot, side, piece):
        half = part // 2
        target = u_buf.at[slot, pl.ds(side * part + piece * half, half), :]
        return pltpu.make_async_copy(source, target, sems.at[1 + piece, slot, side])

    def fetch(pair, slot):
        for side in range(2):
            place = where_ref[offset + 2 * pair + side]
            owner, panel = place // panels, place % panels
            turn = ((owner ^ rep) - 1) * (panels // some) + panel // some

            @pl.when(owner == rep)
            def _():
                a_copy(dense_ref.at[rep, panel], slot, side).start()

            for number, other_ref in enumerate(others):

                @pl.when((owner != rep) & (turn == number))
                def _():
                    a_copy(other_ref.at[panel % some], slot, side).start()

            for number in range(side, n_units, 2):

                @pl.when(pair == number // 2)
                def _():
                    for piece in range(2):
                        u_copy(units[number][piece], slot, side, piece).start()

    pairs = n_units // 2
    fetch(0, 0)
    if has_total:
        load = pltpu.make_async_copy(total_ref, sum_ref, sum_sem)
        load.start()
        load.wait()
    else:
        sum_ref[...] = jnp.zeros_like(sum_ref)

    def step(pair, carry):
        slot = pair % 2

        @pl.when(pair + 1 < pairs)
        def _():
            fetch(pair + 1, 1 - slot)

        for side in range(2):
            a_copy(dense_ref.at[0, 0], slot, side).wait()
            for piece in range(2):
                u_copy(units[0][piece], slot, side, piece).wait()
        sum_ref[...] += jnp.dot(a_buf[slot], u_buf[slot], preferred_element_type=F32)
        return carry

    lax.fori_loop(0, pairs, step, 0)
    if out_ref.dtype == F32:
        store = pltpu.make_async_copy(sum_ref, out_ref, sum_sem)
        store.start()
        store.wait()
    else:
        out_ref[...] = sum_ref[...].astype(out_ref.dtype)


def forward_part(where, offset, units, total, dense, others, kind):
    _, _, rows, part = dense.shape
    width = units[0].shape[1]
    n_pieces = [len(unit) if isinstance(unit, list) else 1 for unit in units]
    pieces = [piece for unit in units for piece in (unit if isinstance(unit, list) else [unit])]
    near = pl.BlockSpec(memory_space=pl.ANY)
    hbm = pl.BlockSpec(memory_space=pltpu.HBM)
    has_total = total is not None
    n_units, n_others = len(units), len(others)
    return pl.pallas_call(
        functools.partial(forward_kernel, offset, n_pieces, n_others, has_total),
        out_shape=jax.ShapeDtypeStruct((rows, width), kind),
        grid_spec=pltpu.PrefetchScalarGridSpec(
            num_scalar_prefetch=1,
            grid=(1,),
            in_specs=[hbm] * (1 + n_others) + [near] * (len(pieces) + has_total),
            out_specs=near if kind == F32 else pl.BlockSpec((rows, width), lambda i, where: (0, 0)),
            scratch_shapes=[
                pltpu.VMEM((rows, width), F32),
                pltpu.VMEM((2, rows, 2 * part), BF16),
                pltpu.VMEM((2, 2 * part, width), BF16),
                pltpu.SemaphoreType.DMA((3, 2, 2)),
                pltpu.SemaphoreType.DMA,
            ],
        ),
        compiler_params=pltpu.CompilerParams(vmem_limit_bytes=36 * 2**20),
        cost_estimate=pl.CostEstimate(
            flops=2 * n_units * rows * part * width,
            transcendentals=0,
            bytes_accessed=n_units * rows * part * 2 + 8 * rows * width,
        ),
    )(where, in_hbm(dense), *map(in_hbm, others), *pieces, *([total] if has_total else []))


def slopes(mine_ref, other_ref, weight_ref, cot_ref):
    agg = (mine_ref[...].astype(F32) + other_ref[...].astype(F32)).astype(BF16)
    pre = jnp.dot(agg, weight_ref[...], preferred_element_type=F32)
    sigma = 0.5 * jnp.tanh(0.5 * pre) + 0.5
    slope = cot_ref[...].astype(F32) * sigma * (1.0 + pre * (1.0 - sigma))
    return agg, (pre * sigma).astype(BF16), slope.astype(BF16)


def middle_kernel(blocks, where_ref, mine_ref, other_ref, weight_ref, cot_ref, a_ref, *refs):
    grad_ref, top_ref, end_ref, term_ref, sum_ref, full_ref = refs
    step = pl.program_id(0)
    part = mine_ref.shape[0]

    @pl.when(step < blocks)
    def _():
        agg, _, pre_grad = slopes(mine_ref, other_ref, weight_ref, cot_ref)
        grad = lax.dot_general(
            weight_ref[...], pre_grad, (((1,), (1,)), ((), ())), preferred_element_type=F32
        ).astype(BF16)
        grad_ref[...] = grad
        full_ref[:, pl.ds(pl.multiple_of(step * part, part), part)] = grad
        term = lax.dot_general(agg, pre_grad, (((0,), (0,)), ((), ())), preferred_element_type=F32)

        @pl.when(step == 0)
        def _():
            sum_ref[...] = term

        @pl.when(step > 0)
        def _():
            sum_ref[...] += term

    @pl.when(step == blocks)
    def _():
        chunk = jnp.dot(full_ref[...], a_ref[0, 0], preferred_element_type=F32).astype(BF16)
        half = top_ref.shape[0]
        top_ref[...] = chunk[:half]
        end_ref[...] = chunk[half:]
        depth, size, _ = term_ref.shape
        z = where_ref[1] // 4
        for number in range(depth):
            start = (where_ref[0] * depth + (z ^ number)) * size
            rows = sum_ref[pl.ds(pl.multiple_of(start, size), size), :]
            term_ref[number] = rows.astype(BF16)


def middle(where, offset, mine, other, weight, cotangent, dense, depth):
    rows, width = mine.shape
    n_rep, _, _, cols = dense.shape
    blocks = 4
    part = rows // blocks
    size = width // n_rep // depth
    block = pl.BlockSpec((part, width), lambda i, where: (jnp.minimum(i, blocks - 1), 0))
    fixed = lambda *shape: pl.BlockSpec(shape, lambda i, where: (0,) * len(shape))
    half = width // 2
    shapes = [(width, rows), (half, cols), (half, cols), (depth, size, width)]

    def a_block(i, where):
        place = where[offset]
        return (place % n_rep, place // n_rep, 0, 0)

    return pl.pallas_call(
        functools.partial(middle_kernel, blocks),
        out_shape=[jax.ShapeDtypeStruct(shape, BF16) for shape in shapes],
        grid_spec=pltpu.PrefetchScalarGridSpec(
            num_scalar_prefetch=1,
            grid=(blocks + 1,),
            in_specs=[
                block,
                block,
                fixed(width, width),
                block,
                pl.BlockSpec((1, 1, rows, cols), a_block),
            ],
            out_specs=[
                pl.BlockSpec((width, part), lambda i, where: (0, jnp.minimum(i, blocks - 1))),
                *(fixed(*shape) for shape in shapes[1:]),
            ],
            scratch_shapes=[pltpu.VMEM((width, width), F32), pltpu.VMEM((width, rows), BF16)],
        ),
        compiler_params=pltpu.CompilerParams(vmem_limit_bytes=36 * 2**20),
        cost_estimate=pl.CostEstimate(
            flops=6 * rows * width * width + 4 * rows * width * cols,
            transcendentals=rows * width,
            bytes_accessed=rows * width * 12,
        ),
    )(where, mine, other, weight, cotangent, in_hbm(dense))


def activated_kernel(where_ref, mine_ref, other_ref, weight_ref, cot_ref, act_ref):
    act_ref[...] = slopes(mine_ref, other_ref, weight_ref, cot_ref)[1]


def activated_rows(where, mine, other, weight, cotangent, n_rep):
    rows, width = mine.shape
    part = rows // n_rep
    block = pl.BlockSpec((part, width), lambda i, where: (where[0], 0))
    fixed = lambda *shape: pl.BlockSpec(shape, lambda i, where: (0, 0))
    return pl.pallas_call(
        activated_kernel,
        out_shape=jax.ShapeDtypeStruct((part, width), BF16),
        grid_spec=pltpu.PrefetchScalarGridSpec(
            num_scalar_prefetch=1,
            grid=(1,),
            in_specs=[block, block, fixed(width, width), block],
            out_specs=fixed(part, width),
        ),
        compiler_params=pltpu.CompilerParams(vmem_limit_bytes=36 * 2**20),
        cost_estimate=pl.CostEstimate(
            flops=2 * part * width * width,
            transcendentals=part * width,
            bytes_accessed=part * width * 8,
        ),
    )(where, mine, other, weight, cotangent)


def backward_kernel(where_ref, grad_ref, a_ref, *out_refs):
    chunk = jnp.dot(grad_ref[...], a_ref[0, 0], preferred_element_type=F32).astype(BF16)
    for number, out_ref in enumerate(out_refs):

        @pl.when(pl.program_id(0) == number)
        def _():
            out_ref[...] = chunk


def backward_part(where, offset, count, grad, dense):
    width, rows = grad.shape
    n_rep, _, _, cols = dense.shape
    fixed = lambda *shape: pl.BlockSpec(shape, lambda i, where: (0, 0))

    def a_block(i, where):
        place = where[offset + i]
        return (place % n_rep, place // n_rep, 0, 0)

    return pl.pallas_call(
        backward_kernel,
        out_shape=[jax.ShapeDtypeStruct((width, cols), BF16)] * count,
        grid_spec=pltpu.PrefetchScalarGridSpec(
            num_scalar_prefetch=1,
            grid=(count,),
            in_specs=[fixed(width, rows), pl.BlockSpec((1, 1, rows, cols), a_block)],
            out_specs=[fixed(width, cols)] * count,
        ),
        compiler_params=pltpu.CompilerParams(vmem_limit_bytes=36 * 2**20),
        cost_estimate=pl.CostEstimate(
            flops=2 * count * rows * width * cols,
            transcendentals=0,
            bytes_accessed=2 * count * rows * cols + 2 * count * width * cols + 2 * width * rows,
        ),
    )(where, grad, in_hbm(dense))


def diagonals_kernel(y_ref, x_ref, top_ref, end_ref, y_out, x_out):
    half = top_ref.shape[0]
    y_out[:half] = (y_ref[:half].astype(F32) + top_ref[...].astype(F32)).astype(BF16)
    y_out[half:] = y_ref[half:]
    x_out[:half] = x_ref[:half]
    x_out[half:] = (x_ref[half:].astype(F32) + end_ref[...].astype(F32)).astype(BF16)


def add_diagonals(odd_y, odd_x, top, end):
    return pl.pallas_call(
        diagonals_kernel,
        out_shape=[jax.ShapeDtypeStruct(odd_y.shape, BF16)] * 2,
        compiler_params=pltpu.CompilerParams(vmem_limit_bytes=36 * 2**20),
        cost_estimate=pl.CostEstimate(
            flops=odd_y.size, transcendentals=0, bytes_accessed=10 * odd_y.size
        ),
    )(odd_y, odd_x, top, end)


def final_kernel(n_parts, n_halves, z_order, where_ref, *refs):
    parts, terms = refs[:n_parts], refs[n_parts + n_halves : -2]
    halves = refs[n_parts : n_parts + n_halves]
    out_ref, weight_out = refs[-2:]
    values = [part[...].astype(F32) for part in parts]
    for top, end in zip(halves[::2], halves[1::2]):
        values.append(jnp.concatenate([top[...].astype(F32), end[...].astype(F32)]))
    total = functools.reduce(jnp.add, values)
    out_ref[0] = total.T.astype(BF16)
    depth, size, _ = terms[0].shape
    for other, term_ref in enumerate(terms):
        for number, offset in enumerate(z_order):
            place = (where_ref[0] ^ other) * depth + ((where_ref[1] // 4) ^ offset)
            rows = pl.ds(pl.multiple_of(place * size, size), size)
            weight_out[rows, :] = term_ref[number].astype(F32)


def final_sum(where, parts, halves, terms, z_order):
    width, cols = parts[0].shape
    halves = [half for pair in halves for half in pair]
    whole = lambda value: pl.BlockSpec(value.shape, lambda i, where: (0,) * value.ndim)
    outs = [
        jax.ShapeDtypeStruct((1, cols, width), BF16),
        jax.ShapeDtypeStruct((width, width), F32),
    ]
    return pl.pallas_call(
        functools.partial(final_kernel, len(parts), len(halves), z_order),
        out_shape=outs,
        grid_spec=pltpu.PrefetchScalarGridSpec(
            num_scalar_prefetch=1,
            grid=(1,),
            in_specs=[whole(value) for value in [*parts, *halves, *terms]],
            out_specs=[whole(value) for value in outs],
        ),
        compiler_params=pltpu.CompilerParams(vmem_limit_bytes=36 * 2**20),
        cost_estimate=pl.CostEstimate(
            flops=len(parts) * width * cols,
            transcendentals=0,
            bytes_accessed=2 * (len(parts) + 1) * width * cols,
        ),
    )(where, *parts, *halves, *terms)


def shards(sizes, features, weight, tile_values, tile_rows, tile_cols, tile_count, cotangent):
    n_section, n_rep = sizes
    block_rows, width = features.shape
    part = block_rows // n_rep
    section, rep = lax.axis_index("section"), lax.axis_index("rep")

    X, Y, Z = 1, 2, 4
    pair_count = n_section // 8
    low_bit = lambda mask: mask & -mask

    def flip(value, mask, rep_mask=0):
        pairs = [
            (s * n_rep + r, (s ^ mask) * n_rep + (r ^ rep_mask))
            for s in range(n_section)
            for r in range(n_rep)
        ]
        return lax.ppermute(value, BOTH, pairs)

    def gather_rep(value):
        held = [value] + [flip(value, 0, other) for other in range(1, n_rep)]
        order = rep ^ jnp.arange(n_rep)
        if n_rep == 2:
            held = [jnp.where(rep == 0, held[0], held[1]), jnp.where(rep == 0, held[1], held[0])]
            return jnp.concatenate(held)
        return jnp.stack(held)[order].reshape(-1, width)

    live = {}

    def close(*open_names):
        names = [name for name in live if name not in open_names]
        live.update(zip(names, lax.optimization_barrier([live[name] for name in names])))

    masks, offsets = [], {}

    def plan(name, wanted):
        offsets[name] = 2 + len(masks)
        masks.extend(wanted)

    for pair in range(pair_count):
        even, odd = 2 * pair * Z, (2 * pair + 1) * Z
        plan(("early", pair), [even, even + X, even + Y, odd])
        plan(("more", pair), [even + X + Y, odd + Y])
        plan(("late", pair), [odd + X, odd + X + Y])
        if pair == 0:
            plan(("first", pair), [odd + X + Y, even + X + Y])
            plan(("odd", pair), [odd + X, odd + Y, odd])
            plan(("even", pair), [even + X, even + Y, even])
        else:
            plan(("first", pair), [odd + X + Y])
            plan(("mid", pair), [even + X + Y, odd + Y, odd + X])
            plan(("last", pair), [even + X, even + Y, odd, even])
    offsets["joined"] = 2 + len(masks)
    masks += [0, X, Y, Z, Z + X, Z + Y, X + Y, Z + X + Y, 2 * Z, 2 * Z + X, 2 * Z + Y, 3 * Z]
    where = jnp.concatenate(
        [rep[None], section[None], section ^ jnp.array(masks, jnp.int32)]
    ).astype(jnp.int32)

    def forward_step(names, units, total, kind=F32):
        with jax.named_scope("forward"):
            return forward_part(
                where, offsets[names], units, total, live["dense"], live["others"], kind
            )

    row_tiles = block_rows // tile_values.shape[3]
    packed = jnp.concatenate(
        [tile_rows[0] * row_tiles + tile_cols[0], tile_count[0][:, None]], axis=1
    )
    panels = tile_values.shape[1]
    def build_own(first):
        with jax.named_scope("dense_blocks"):
            live["dense"] = make_dense(
                first, live.get("dense"), where, tile_values[0], packed, block_rows, n_rep
            )

    def build_others(first):
        with jax.named_scope("other_blocks"):
            return [make_other(first, where, *sent, block_rows, n_rep) for sent in live["tiles"]]

    live[0] = lax.dynamic_slice_in_dim(features, rep * part, part, axis=0)
    with jax.named_scope("tiles_exchange"):
        live["tiles"] = [
            (flip(tile_values[0], 0, n), flip(packed, 0, n)) for n in range(1, n_rep)
        ]
    half = part // 2
    for pair in range(pair_count):
        even, odd = 2 * pair * Z, (2 * pair + 1) * Z
        later = even + 2 * Z
        last = pair + 1 == pair_count

        with jax.named_scope("features_across"):
            live["even_x"], live["even_y"] = flip(live[even], X), flip(live[even], Y)
        with jax.named_scope("features_along_z"):
            live[odd] = flip(live[even], Z)
        if pair == 0:
            build_own(0)
        if pair == 1:
            two = build_others(panels // 2)
            live["others"] = [side for sides in zip(live.pop("one"), two) for side in sides]
            del live["tiles"]
        if pair > 1:
            live["total"] = forward_step(("late", pair - 1), live.pop("waiting"), live["total"])
        close()

        if pair == 0:
            with jax.named_scope("features_across"):
                live["odd_x"], live["odd_y"] = flip(live[odd], X), flip(live[odd], Y)
            build_own(panels // 2)
        else:
            with jax.named_scope("features_across"):
                live["even_xy"], live["odd_y"] = flip(live["even_y"], X), flip(live[odd], Y)
            with jax.named_scope("features_along_z"):
                live["odd_x"] = flip(live["even_x"], Z)
            units = [live[even], live["even_x"], live["even_y"], live[odd]]
            if pair == 1:
                live["total"] = forward_step("joined", live.pop("waiting") + units, None)
            else:
                live["total"] = forward_step(("early", pair), units, live["total"])
        if not last:
            with jax.named_scope("features_along_z"):
                source, mask = live[later - low_bit(later)], low_bit(later)
                live["coming"] = [flip(source[:half], mask)]
        close()

        if pair == 0:
            units = [live[even], live["even_x"], live["even_y"]]
            units += [live[odd], live["odd_x"], live["odd_y"]]
            with jax.named_scope("features_across"):
                units += [flip(live["even_x"], Y), flip(live["odd_y"], X)]
            live["waiting"] = units
            live["one"] = build_others(0)
        else:
            with jax.named_scope("features_across"):
                odd_xy = [flip(live["odd_y"][:half], X), flip(live["odd_x"][half:], Y)]
            live["waiting"] = [live["odd_x"], odd_xy]
            units = [live.pop("even_xy"), live["odd_y"]]
            live["total"] = forward_step(("more", pair), units, live["total"])
        if not last:
            with jax.named_scope("features_along_z"):
                live["coming"].append(flip(source[half:], mask))
        else:
            with jax.named_scope("cotangent_rows"):
                live["cotangent"] = gather_rep(cotangent)
        for name in ("even_x", "even_y", "odd_x", "odd_y"):
            del live[name]
        close()
        if not last:
            live[later] = jnp.concatenate(live.pop("coming"))
    partial = forward_step(
        ("late", pair_count - 1), live.pop("waiting"), live.get("total"), BF16
    )

    with jax.named_scope("partial_sums"):
        other = flip(partial, 0, 1)
        for bit in range(1, n_rep.bit_length() - 1):
            partial = (partial.astype(F32) + other.astype(F32)).astype(BF16)
            other = flip(partial, 0, 1 << bit)

    with jax.named_scope("middle"):
        depth = n_section // 4
        rows = (partial, other, weight, live["cotangent"])
        grad, top_diag, end_diag, term = middle(
            where, offsets["first", pair_count - 1], *rows, live["dense"], depth
        )

    live = {"grad": grad, "dense": live["dense"], "term": term}
    add = lambda *values: functools.reduce(jnp.add, [value.astype(F32) for value in values])

    sizes_of = {"mid": 3, "last": 4, "odd": 3, "even": 3}

    def backward_step(pair, *names):
        with jax.named_scope("backward"):
            counts = [sizes_of.get(name, 1 if pair else 2) for name in names]
            chunks = backward_part(
                where, offsets[names[0], pair], sum(counts), live["grad"], live["dense"]
            )
            for name, count in zip(names, counts):
                live[name], chunks = chunks[:count], chunks[count:]

    steps = ["along_z", X, Y, *(-(Z << bit) for bit in reversed(range(depth.bit_length() - 1)))]
    steps.append("between_cores")
    z_order = [0]

    def weight_step(after=None):
        if not steps:
            return
        step = steps.pop(0)
        if after:
            live[after], live["term"] = lax.optimization_barrier((live[after], live["term"]))
        term = live["term"]
        with jax.named_scope("weight_grad"):
            if step == "along_z":
                parts = [term[0], *(flip(term[n], Z * n) for n in range(1, depth))]
                live["term"] = add(*parts).astype(BF16)
            elif step == "between_cores":
                live["terms"] = [term, *(flip(term, 0, n) for n in range(1, n_rep))]
                del live["term"]
            elif step > 0:
                live["term"] = add(term, flip(term, step)).astype(BF16)
            else:
                term = term[None] if term.ndim == 2 else term
                live["term"] = jnp.concatenate([term, flip(term, -step)])
                z_order.extend([-step // Z ^ other for other in z_order])

    half = width // 2
    tops = lambda values: [value[:half] for value in values]
    ends = lambda values: [value[half:] for value in values]
    live["first"] = [top_diag, end_diag]
    for pair in reversed(range(pair_count)):
        even = 2 * pair * Z
        top = pair + 1 == pair_count
        if not top:
            mask = low_bit(even + 2 * Z)
            name = ("to", even + 2 * Z - mask, mask)

        with jax.named_scope("grads_across"):
            if pair == 0:
                odd_diag, even_diag = live.pop("first")
                live["odd_diag"], live["even_diag"] = flip(odd_diag, Y), flip(even_diag, X)
            else:
                top_diag, end_diag = live.pop("first")
                live["top_diag"], live["end_diag"] = flip(top_diag, X), flip(end_diag, Y)
        if not top:
            with jax.named_scope("grads_along_z"):
                live[name] = [flip(live["passed"][0], mask)]
        backward_step(pair, "even" if pair == 0 else "mid")
        weight_step(None if top else "even" if pair == 0 else "mid")
        close()

        if pair == 0:
            with jax.named_scope("grads_across"):
                to_x, to_y, own = live.pop("odd")
                to_x = add(to_x, live.pop("odd_diag")).astype(BF16)
                live["odd_sum"] = [own, flip(to_x, X), flip(to_y, Y)]
                to_x, to_y, own = live.pop("even")
                live["even"] = [to_x, add(to_y, live.pop("even_diag")).astype(BF16), own]
        else:
            with jax.named_scope("grads_across"):
                even_xy, odd_y, odd_x = live.pop("mid")
                live["to_even_y"] = flip(even_xy, X)
                odd_y, odd_x = add_diagonals(
                    odd_y, odd_x, live.pop("top_diag"), live.pop("end_diag")
                )
                live["to_odd"] = flip(odd_y, Y)
            with jax.named_scope("grads_along_z"):
                live["to_even_x"] = flip(odd_x, Z)
            backward_step(pair, "last")
        if not top:
            with jax.named_scope("grads_along_z"):
                live[name].append(flip(live.pop("passed")[1], mask))
        weight_step("last" if pair else None)
        close()

        if pair == 0:
            with jax.named_scope("grads_across"):
                to_x, to_y, own = live.pop("even")
                sums = [own, flip(to_x, X), flip(to_y, Y)]
            with jax.named_scope("grads_along_z"):
                sums.append(flip(add(*live.pop("odd_sum")).astype(BF16), Z))
            with jax.named_scope("activated"):
                live["activated"] = activated_rows(where, *rows, n_rep)
        else:
            to_x, to_y, odd, own = live.pop("last")
            with jax.named_scope("grads_across"):
                to_x = add(to_x, live.pop("to_even_x")).astype(BF16)
                to_y = add(to_y, live.pop("to_even_y")).astype(BF16)
                sums = [own, flip(to_x, X), flip(to_y, Y)]
            with jax.named_scope("grads_along_z"):
                sums.append(flip(add(odd, live.pop("to_odd")).astype(BF16), Z))
            backward_step(pair - 1, "first", *([] if pair > 1 else ["odd"]))
        live["sums"] = sums
        weight_step("first" if pair else None)
        close()
        sums = live.pop("sums")
        halves = [live.pop(key) for key in list(live) if isinstance(key, tuple) and key[1] == even]
        if pair > 0:
            live["passed"] = [
                add(*tops(sums), *(value[0] for value in halves)).astype(BF16),
                add(*ends(sums), *(value[1] for value in halves)).astype(BF16),
            ]
        if pair > 1:
            (chunk,) = live["first"]
            live["first"] = [chunk[:half], chunk[half:]]
    with jax.named_scope("grads_out"):
        feat_grad, weight_grad = final_sum(where, sums, halves, live["terms"], tuple(z_order))
    return (live["activated"], feat_grad, weight_grad)


def solution(mesh):
    placed = (
        P("section", None),
        P(),
        P("section", "rep", None, None, None),
        P("section", "rep", None),
        P("section", "rep", None),
        P("section", "rep"),
        P(("section", "rep"), None),
    )
    sizes = (mesh.shape["section"], mesh.shape["rep"])
    return jax.shard_map(
        functools.partial(shards, sizes),
        mesh=mesh,
        in_specs=placed,
        out_specs=(P(("section", "rep"), None), P("rep", "section", None), P()),
        check_vma=False,
    )
```

```python
import functools

import jax
import jax.numpy as jnp
from jax import lax
from jax.experimental import pallas as pl
from jax.experimental.pallas import tpu as pltpu
from jax.sharding import PartitionSpec as P

BF16 = jnp.bfloat16
F32 = jnp.float32
BOTH = ("section", "rep")
FEATURES_ACROSS, FEATURES_ALONG = "features_xy", "features_z"
GRADS_ACROSS, GRADS_ALONG = "grads_xy", "grads_z"


def in_hbm(value):
    return pltpu.with_memory_space_constraint(value, pltpu.HBM)


def dense_kernel(first, where_ref, packed_ref, tiles_ref, *refs):
    out_ref = refs[-1]
    panel = first + pl.program_id(0)
    size, slots = tiles_ref.shape[-1], tiles_ref.shape[1]
    row_tiles, per_part = out_ref.shape[2] // size, out_ref.shape[3] // size
    out_ref[...] = jnp.zeros_like(out_ref)

    def add_tile(slot, carry):
        place = packed_ref[panel, slot]
        row = pl.multiple_of(place // row_tiles * size, size)
        tile_col = place % row_tiles
        col = pl.multiple_of(tile_col % per_part * size, size)
        out_ref[tile_col // per_part, 0, pl.ds(row, size), pl.ds(col, size)] += tiles_ref[0, slot]
        return carry

    lax.fori_loop(0, packed_ref[panel, slots], add_tile, 0)


def make_dense(first, before, where, tiles, packed, block_rows, n_rep):
    panels, slots, size, _ = tiles.shape
    half = panels // 2
    part = block_rows // n_rep
    at = lambda p: first + p
    return pl.pallas_call(
        functools.partial(dense_kernel, first),
        out_shape=pltpu.HBM((n_rep, panels, block_rows, part), BF16),
        grid_spec=pltpu.PrefetchScalarGridSpec(
            num_scalar_prefetch=2,
            grid=(half,),
            in_specs=[pl.BlockSpec((1, slots, size, size), lambda p, *_: (at(p), 0, 0, 0))]
            + [pl.BlockSpec(memory_space=pl.ANY)] * (first > 0),
            out_specs=pl.BlockSpec((n_rep, 1, block_rows, part), lambda p, *_: (0, at(p), 0, 0)),
        ),
        input_output_aliases={3: 0} if first else {},
        compiler_params=pltpu.CompilerParams(vmem_limit_bytes=36 * 2**20),
        cost_estimate=pl.CostEstimate(
            flops=0,
            transcendentals=0,
            bytes_accessed=tiles.size // 8,
        ),
    )(where, packed, in_hbm(tiles), *([in_hbm(before)] if first else []))


def other_kernel(first, where_ref, packed_ref, tiles_ref, out_ref):
    panel = first + pl.program_id(0)
    size, slots = tiles_ref.shape[-1], tiles_ref.shape[1]
    row_tiles, per_part = out_ref.shape[1] // size, out_ref.shape[2] // size
    out_ref[...] = jnp.zeros_like(out_ref)

    def add_tile(slot, carry):
        place = packed_ref[panel, slot]
        row = pl.multiple_of(place // row_tiles * size, size)
        tile_col = place % row_tiles
        col = pl.multiple_of(tile_col % per_part * size, size)

        @pl.when(tile_col // per_part == where_ref[0])
        def _():
            out_ref[0, pl.ds(row, size), pl.ds(col, size)] += tiles_ref[0, slot]

        return carry

    lax.fori_loop(0, packed_ref[panel, slots], add_tile, 0)


def make_other(first, where, tiles, packed, block_rows, n_rep):
    panels, slots, size, _ = tiles.shape
    half = panels // 2
    part = block_rows // n_rep
    return pl.pallas_call(
        functools.partial(other_kernel, first),
        out_shape=pltpu.HBM((half, block_rows, part), BF16),
        grid_spec=pltpu.PrefetchScalarGridSpec(
            num_scalar_prefetch=2,
            grid=(half,),
            in_specs=[pl.BlockSpec((1, slots, size, size), lambda p, *_: (first + p, 0, 0, 0))],
            out_specs=pl.BlockSpec((1, block_rows, part), lambda p, *_: (p, 0, 0)),
        ),
        compiler_params=pltpu.CompilerParams(vmem_limit_bytes=36 * 2**20),
        cost_estimate=pl.CostEstimate(
            flops=0, transcendentals=0, bytes_accessed=tiles.size // 8
        ),
    )(where, packed, tiles)


def forward_kernel(offset, n_pieces, n_others, has_total, where_ref, dense_ref, *refs):
    others, refs = refs[:n_others], refs[n_others:]
    units = []
    for pieces in n_pieces:
        tops, refs = refs[:pieces], refs[pieces:]
        half = tops[0].shape[0] // (2 if pieces == 1 else 1)
        units.append([tops[0].at[pl.ds(0, half)], tops[-1].at[pl.ds(half * (2 - pieces), half)]])
    n_units = len(units)
    total_ref, refs = (refs[0], refs[1:]) if has_total else (None, refs)
    out_ref, sum_ref, a_buf, u_buf, sems, sum_sem = refs
    _, panels, _, part = dense_ref.shape
    some = others[0].shape[0]
    rep = where_ref[0]

    def a_copy(source, slot, side):
        target = a_buf.at[slot, :, pl.ds(side * part, part)]
        return pltpu.make_async_copy(source, target, sems.at[0, slot, side])

    def u_copy(source, slot, side, piece):
        half = part // 2
        target = u_buf.at[slot, pl.ds(side * part + piece * half, half), :]
        return pltpu.make_async_copy(source, target, sems.at[1 + piece, slot, side])

    def fetch(pair, slot):
        for side in range(2):
            place = where_ref[offset + 2 * pair + side]
            owner, panel = place // panels, place % panels
            turn = ((owner ^ rep) - 1) * (panels // some) + panel // some

            @pl.when(owner == rep)
            def _():
                a_copy(dense_ref.at[rep, panel], slot, side).start()

            for number, other_ref in enumerate(others):

                @pl.when((owner != rep) & (turn == number))
                def _():
                    a_copy(other_ref.at[panel % some], slot, side).start()

            for number in range(side, n_units, 2):

                @pl.when(pair == number // 2)
                def _():
                    for piece in range(2):
                        u_copy(units[number][piece], slot, side, piece).start()

    pairs = n_units // 2
    fetch(0, 0)
    if has_total:
        load = pltpu.make_async_copy(total_ref, sum_ref, sum_sem)
        load.start()
        load.wait()
    else:
        sum_ref[...] = jnp.zeros_like(sum_ref)

    def step(pair, carry):
        slot = pair % 2

        @pl.when(pair + 1 < pairs)
        def _():
            fetch(pair + 1, 1 - slot)

        for side in range(2):
            a_copy(dense_ref.at[0, 0], slot, side).wait()
            for piece in range(2):
                u_copy(units[0][piece], slot, side, piece).wait()
        sum_ref[...] += jnp.dot(a_buf[slot], u_buf[slot], preferred_element_type=F32)
        return carry

    lax.fori_loop(0, pairs, step, 0)
    if out_ref.dtype == F32:
        store = pltpu.make_async_copy(sum_ref, out_ref, sum_sem)
        store.start()
        store.wait()
    else:
        out_ref[...] = sum_ref[...].astype(out_ref.dtype)


def forward_part(where, offset, units, total, dense, others, kind):
    _, _, rows, part = dense.shape
    width = units[0].shape[1]
    n_pieces = [len(unit) if isinstance(unit, list) else 1 for unit in units]
    pieces = [piece for unit in units for piece in (unit if isinstance(unit, list) else [unit])]
    near = pl.BlockSpec(memory_space=pl.ANY)
    hbm = pl.BlockSpec(memory_space=pltpu.HBM)
    has_total = total is not None
    n_units, n_others = len(units), len(others)
    return pl.pallas_call(
        functools.partial(forward_kernel, offset, n_pieces, n_others, has_total),
        out_shape=jax.ShapeDtypeStruct((rows, width), kind),
        grid_spec=pltpu.PrefetchScalarGridSpec(
            num_scalar_prefetch=1,
            grid=(1,),
            in_specs=[hbm] * (1 + n_others) + [near] * (len(pieces) + has_total),
            out_specs=near if kind == F32 else pl.BlockSpec((rows, width), lambda i, where: (0, 0)),
            scratch_shapes=[
                pltpu.VMEM((rows, width), F32),
                pltpu.VMEM((2, rows, 2 * part), BF16),
                pltpu.VMEM((2, 2 * part, width), BF16),
                pltpu.SemaphoreType.DMA((3, 2, 2)),
                pltpu.SemaphoreType.DMA,
            ],
        ),
        compiler_params=pltpu.CompilerParams(vmem_limit_bytes=36 * 2**20),
        cost_estimate=pl.CostEstimate(
            flops=2 * n_units * rows * part * width,
            transcendentals=0,
            bytes_accessed=n_units * rows * part * 2 + 8 * rows * width,
        ),
    )(where, in_hbm(dense), *map(in_hbm, others), *pieces, *([total] if has_total else []))


def slopes(mine_ref, other_ref, weight_ref, cot_ref):
    agg = (mine_ref[...].astype(F32) + other_ref[...].astype(F32)).astype(BF16)
    pre = jnp.dot(agg, weight_ref[...], preferred_element_type=F32)
    sigma = 0.5 * jnp.tanh(0.5 * pre) + 0.5
    slope = cot_ref[...].astype(F32) * sigma * (1.0 + pre * (1.0 - sigma))
    return agg, (pre * sigma).astype(BF16), slope.astype(BF16)


def middle_kernel(blocks, where_ref, mine_ref, other_ref, weight_ref, cot_ref, a_ref, *refs):
    grad_ref, top_ref, end_ref, term_ref, sum_ref, full_ref = refs
    step = pl.program_id(0)
    part = mine_ref.shape[0]

    @pl.when(step < blocks)
    def _():
        agg, _, pre_grad = slopes(mine_ref, other_ref, weight_ref, cot_ref)
        grad = lax.dot_general(
            weight_ref[...], pre_grad, (((1,), (1,)), ((), ())), preferred_element_type=F32
        ).astype(BF16)
        grad_ref[...] = grad
        full_ref[:, pl.ds(pl.multiple_of(step * part, part), part)] = grad
        term = lax.dot_general(agg, pre_grad, (((0,), (0,)), ((), ())), preferred_element_type=F32)

        @pl.when(step == 0)
        def _():
            sum_ref[...] = term

        @pl.when(step > 0)
        def _():
            sum_ref[...] += term

    @pl.when(step == blocks)
    def _():
        chunk = jnp.dot(full_ref[...], a_ref[0, 0], preferred_element_type=F32).astype(BF16)
        half = top_ref.shape[0]
        top_ref[...] = chunk[:half]
        end_ref[...] = chunk[half:]
        depth, size, _ = term_ref.shape
        z = where_ref[1] // 4
        for number in range(depth):
            start = (where_ref[0] * depth + (z ^ number)) * size
            rows = sum_ref[pl.ds(pl.multiple_of(start, size), size), :]
            term_ref[number] = rows.astype(BF16)


def middle(where, offset, mine, other, weight, cotangent, dense, depth):
    rows, width = mine.shape
    n_rep, _, _, cols = dense.shape
    blocks = 4
    part = rows // blocks
    size = width // n_rep // depth
    block = pl.BlockSpec((part, width), lambda i, where: (jnp.minimum(i, blocks - 1), 0))
    fixed = lambda *shape: pl.BlockSpec(shape, lambda i, where: (0,) * len(shape))
    half = width // 2
    shapes = [(width, rows), (half, cols), (half, cols), (depth, size, width)]

    def a_block(i, where):
        place = where[offset]
        return (place % n_rep, place // n_rep, 0, 0)

    return pl.pallas_call(
        functools.partial(middle_kernel, blocks),
        out_shape=[jax.ShapeDtypeStruct(shape, BF16) for shape in shapes],
        grid_spec=pltpu.PrefetchScalarGridSpec(
            num_scalar_prefetch=1,
            grid=(blocks + 1,),
            in_specs=[
                block,
                block,
                fixed(width, width),
                block,
                pl.BlockSpec((1, 1, rows, cols), a_block),
            ],
            out_specs=[
                pl.BlockSpec((width, part), lambda i, where: (0, jnp.minimum(i, blocks - 1))),
                *(fixed(*shape) for shape in shapes[1:]),
            ],
            scratch_shapes=[pltpu.VMEM((width, width), F32), pltpu.VMEM((width, rows), BF16)],
        ),
        compiler_params=pltpu.CompilerParams(vmem_limit_bytes=36 * 2**20),
        cost_estimate=pl.CostEstimate(
            flops=6 * rows * width * width + 4 * rows * width * cols,
            transcendentals=rows * width,
            bytes_accessed=rows * width * 12,
        ),
    )(where, mine, other, weight, cotangent, in_hbm(dense))


def activated_kernel(where_ref, mine_ref, other_ref, weight_ref, cot_ref, act_ref):
    act_ref[...] = slopes(mine_ref, other_ref, weight_ref, cot_ref)[1]


def activated_rows(where, mine, other, weight, cotangent, n_rep):
    rows, width = mine.shape
    part = rows // n_rep
    block = pl.BlockSpec((part, width), lambda i, where: (where[0], 0))
    fixed = lambda *shape: pl.BlockSpec(shape, lambda i, where: (0, 0))
    return pl.pallas_call(
        activated_kernel,
        out_shape=jax.ShapeDtypeStruct((part, width), BF16),
        grid_spec=pltpu.PrefetchScalarGridSpec(
            num_scalar_prefetch=1,
            grid=(1,),
            in_specs=[block, block, fixed(width, width), block],
            out_specs=fixed(part, width),
        ),
        compiler_params=pltpu.CompilerParams(vmem_limit_bytes=36 * 2**20),
        cost_estimate=pl.CostEstimate(
            flops=2 * part * width * width,
            transcendentals=part * width,
            bytes_accessed=part * width * 8,
        ),
    )(where, mine, other, weight, cotangent)


def backward_kernel(where_ref, grad_ref, a_ref, *out_refs):
    chunk = jnp.dot(grad_ref[...], a_ref[0, 0], preferred_element_type=F32).astype(BF16)
    for number, out_ref in enumerate(out_refs):

        @pl.when(pl.program_id(0) == number)
        def _():
            out_ref[...] = chunk


def backward_part(where, offset, count, grad, dense):
    width, rows = grad.shape
    n_rep, _, _, cols = dense.shape
    fixed = lambda *shape: pl.BlockSpec(shape, lambda i, where: (0, 0))

    def a_block(i, where):
        place = where[offset + i]
        return (place % n_rep, place // n_rep, 0, 0)

    return pl.pallas_call(
        backward_kernel,
        out_shape=[jax.ShapeDtypeStruct((width, cols), BF16)] * count,
        grid_spec=pltpu.PrefetchScalarGridSpec(
            num_scalar_prefetch=1,
            grid=(count,),
            in_specs=[fixed(width, rows), pl.BlockSpec((1, 1, rows, cols), a_block)],
            out_specs=[fixed(width, cols)] * count,
        ),
        compiler_params=pltpu.CompilerParams(vmem_limit_bytes=36 * 2**20),
        cost_estimate=pl.CostEstimate(
            flops=2 * count * rows * width * cols,
            transcendentals=0,
            bytes_accessed=2 * count * rows * cols + 2 * count * width * cols + 2 * width * rows,
        ),
    )(where, grad, in_hbm(dense))


def diagonals_kernel(y_ref, x_ref, top_ref, end_ref, y_out, x_out):
    half = top_ref.shape[0]
    y_out[:half] = (y_ref[:half].astype(F32) + top_ref[...].astype(F32)).astype(BF16)
    y_out[half:] = y_ref[half:]
    x_out[:half] = x_ref[:half]
    x_out[half:] = (x_ref[half:].astype(F32) + end_ref[...].astype(F32)).astype(BF16)


def add_diagonals(odd_y, odd_x, top, end):
    return pl.pallas_call(
        diagonals_kernel,
        out_shape=[jax.ShapeDtypeStruct(odd_y.shape, BF16)] * 2,
        compiler_params=pltpu.CompilerParams(vmem_limit_bytes=36 * 2**20),
        cost_estimate=pl.CostEstimate(
            flops=odd_y.size, transcendentals=0, bytes_accessed=10 * odd_y.size
        ),
    )(odd_y, odd_x, top, end)


def final_kernel(n_parts, n_halves, z_order, where_ref, *refs):
    parts, terms = refs[:n_parts], refs[n_parts + n_halves : -2]
    halves = refs[n_parts : n_parts + n_halves]
    out_ref, weight_out = refs[-2:]
    values = [part[...].astype(F32) for part in parts]
    for top, end in zip(halves[::2], halves[1::2]):
        values.append(jnp.concatenate([top[...].astype(F32), end[...].astype(F32)]))
    total = functools.reduce(jnp.add, values)
    out_ref[0] = total.T.astype(BF16)
    depth, size, _ = terms[0].shape
    for other, term_ref in enumerate(terms):
        for number, offset in enumerate(z_order):
            place = (where_ref[0] ^ other) * depth + ((where_ref[1] // 4) ^ offset)
            rows = pl.ds(pl.multiple_of(place * size, size), size)
            weight_out[rows, :] = term_ref[number].astype(F32)


def final_sum(where, parts, halves, terms, z_order):
    width, cols = parts[0].shape
    halves = [half for pair in halves for half in pair]
    whole = lambda value: pl.BlockSpec(value.shape, lambda i, where: (0,) * value.ndim)
    outs = [
        jax.ShapeDtypeStruct((1, cols, width), BF16),
        jax.ShapeDtypeStruct((width, width), F32),
    ]
    return pl.pallas_call(
        functools.partial(final_kernel, len(parts), len(halves), z_order),
        out_shape=outs,
        grid_spec=pltpu.PrefetchScalarGridSpec(
            num_scalar_prefetch=1,
            grid=(1,),
            in_specs=[whole(value) for value in [*parts, *halves, *terms]],
            out_specs=[whole(value) for value in outs],
        ),
        compiler_params=pltpu.CompilerParams(vmem_limit_bytes=36 * 2**20),
        cost_estimate=pl.CostEstimate(
            flops=len(parts) * width * cols,
            transcendentals=0,
            bytes_accessed=2 * (len(parts) + 1) * width * cols,
        ),
    )(where, *parts, *halves, *terms)


def shards(sizes, features, weight, tile_values, tile_rows, tile_cols, tile_count, cotangent):
    n_section, n_rep = sizes
    block_rows, width = features.shape
    part = block_rows // n_rep
    section, rep = lax.axis_index("section"), lax.axis_index("rep")

    X, Y, Z = 1, 2, 4
    pair_count = n_section // 8
    low_bit = lambda mask: mask & -mask

    def flip(value, mask, rep_mask=0):
        pairs = [
            (s * n_rep + r, (s ^ mask) * n_rep + (r ^ rep_mask))
            for s in range(n_section)
            for r in range(n_rep)
        ]
        return lax.ppermute(value, BOTH, pairs)

    def gather_rep(value):
        held = [value] + [flip(value, 0, other) for other in range(1, n_rep)]
        order = rep ^ jnp.arange(n_rep)
        if n_rep == 2:
            held = [jnp.where(rep == 0, held[0], held[1]), jnp.where(rep == 0, held[1], held[0])]
            return jnp.concatenate(held)
        return jnp.stack(held)[order].reshape(-1, width)

    live = {}

    def close(*open_names):
        names = [name for name in live if name not in open_names]
        live.update(zip(names, lax.optimization_barrier([live[name] for name in names])))

    masks, offsets = [], {}

    def plan(name, wanted):
        offsets[name] = 2 + len(masks)
        masks.extend(wanted)

    for pair in range(pair_count):
        even, odd = 2 * pair * Z, (2 * pair + 1) * Z
        plan(("early", pair), [even, even + X])
        plan(("more", pair), [even + Y, odd, even + X + Y, odd + Y])
        plan(("late", pair), [odd + X, odd + X + Y])
        if pair == 0:
            plan(("first", pair), [odd + X + Y, even + X + Y])
            plan(("odd", pair), [odd + X, odd + Y, odd])
            plan(("even", pair), [even + X, even + Y, even])
        else:
            plan(("first", pair), [odd + X + Y])
            plan(("mid", pair), [even + X + Y, odd + Y, odd + X])
            plan(("last", pair), [even + X, even + Y, odd, even])
    offsets["joined"] = 2 + len(masks)
    masks += [0, X, Y, Z, Z + X, Z + Y, X + Y, Z + X + Y, 2 * Z, 2 * Z + X]
    where = jnp.concatenate(
        [rep[None], section[None], section ^ jnp.array(masks, jnp.int32)]
    ).astype(jnp.int32)

    def forward_step(names, units, total, kind=F32):
        with jax.named_scope("forward"):
            return forward_part(
                where, offsets[names], units, total, live["dense"], live["others"], kind
            )

    row_tiles = block_rows // tile_values.shape[3]
    packed = jnp.concatenate(
        [tile_rows[0] * row_tiles + tile_cols[0], tile_count[0][:, None]], axis=1
    )
    panels = tile_values.shape[1]
    def build_own(first):
        with jax.named_scope("dense_blocks"):
            live["dense"] = make_dense(
                first, live.get("dense"), where, tile_values[0], packed, block_rows, n_rep
            )

    def build_others(first):
        with jax.named_scope("other_blocks"):
            return [make_other(first, where, *sent, block_rows, n_rep) for sent in live["tiles"]]

    live[0] = lax.dynamic_slice_in_dim(features, rep * part, part, axis=0)
    with jax.named_scope("tiles_exchange"):
        live["tiles"] = [
            (flip(tile_values[0], 0, n), flip(packed, 0, n)) for n in range(1, n_rep)
        ]
    half = part // 2
    for pair in range(pair_count):
        even, odd = 2 * pair * Z, (2 * pair + 1) * Z
        later = even + 2 * Z
        last = pair + 1 == pair_count

        with jax.named_scope(FEATURES_ACROSS):
            live["even_x"], live["even_y"] = flip(live[even], X), flip(live[even], Y)
        with jax.named_scope(FEATURES_ALONG):
            live[odd] = flip(live[even], Z)
        if pair == 0:
            build_own(0)
        if pair == 1:
            two = build_others(panels // 2)
            live["others"] = [side for sides in zip(live.pop("one"), two) for side in sides]
            del live["tiles"]
            with jax.named_scope("cotangents"):
                live["cot"] = gather_rep(cotangent)
        if pair > 1:
            live["total"] = forward_step(("late", pair - 1), live.pop("units"), live["total"])
        close(*(["even_x", "even_y"] if pair == 0 else []))

        if pair == 0:
            with jax.named_scope(FEATURES_ACROSS):
                live["odd_x"], live["odd_y"] = flip(live[odd], X), flip(live[odd], Y)
            build_own(panels // 2)
        else:
            with jax.named_scope(FEATURES_ACROSS):
                live["even_xy"], live["odd_y"] = flip(live["even_y"], X), flip(live[odd], Y)
            with jax.named_scope(FEATURES_ALONG):
                live["odd_x"] = flip(live["even_x"], Z)
            units = [live[even], live["even_x"]]
            if pair == 1:
                live["total"] = forward_step("joined", live.pop("units") + units, None)
            else:
                live["total"] = forward_step(("early", pair), units, live["total"])
        if not last:
            with jax.named_scope(FEATURES_ALONG):
                source, mask = live[later - low_bit(later)], low_bit(later)
                live["coming"] = [flip(source[:half], mask)]
        close()

        if pair == 0:
            units = [live[even], live["even_x"], live["even_y"]]
            units += [live[odd], live["odd_x"], live["odd_y"]]
            with jax.named_scope(FEATURES_ACROSS):
                units += [flip(live["even_x"], Y), flip(live["odd_y"], X)]
            live["units"] = units
            live["one"] = build_others(0)
        else:
            with jax.named_scope(FEATURES_ACROSS):
                odd_xy = [flip(live["odd_y"][:half], X), flip(live["odd_x"][half:], Y)]
            live["units"] = [live["odd_x"], odd_xy]
            units = [live["even_y"], live[odd], live.pop("even_xy"), live["odd_y"]]
            live["total"] = forward_step(("more", pair), units, live["total"])
        if not last:
            with jax.named_scope(FEATURES_ALONG):
                live["coming"].append(flip(source[half:], mask))
        for name in ("even_x", "even_y", "odd_x", "odd_y"):
            del live[name]
        close()
        if not last:
            live[later] = jnp.concatenate(live.pop("coming"))
    partial = forward_step(
        ("late", pair_count - 1), live.pop("units"), live.get("total"), BF16
    )

    with jax.named_scope("partial_sums"):
        other = flip(partial, 0, 1)
        for bit in range(1, n_rep.bit_length() - 1):
            partial = (partial.astype(F32) + other.astype(F32)).astype(BF16)
            other = flip(partial, 0, 1 << bit)

    with jax.named_scope("middle"):
        depth = n_section // 4
        rows = (partial, other, weight, live["cot"])
        grad, top_diag, end_diag, term = middle(
            where, offsets["first", pair_count - 1], *rows, live["dense"], depth
        )

    live = {"grad": grad, "dense": live["dense"], "term": term}
    add = lambda *values: functools.reduce(jnp.add, [value.astype(F32) for value in values])

    sizes_of = {"mid": 3, "last": 4, "odd": 3, "even": 3}

    def backward_step(pair, *names):
        with jax.named_scope("backward"):
            counts = [sizes_of.get(name, 1 if pair else 2) for name in names]
            chunks = backward_part(
                where, offsets[names[0], pair], sum(counts), live["grad"], live["dense"]
            )
            for name, count in zip(names, counts):
                live[name], chunks = chunks[:count], chunks[count:]

    steps = ["z", X, Y, *(-(Z << bit) for bit in reversed(range(depth.bit_length() - 1)))]
    steps.append("cores")
    z_order = [0]

    def weight_step(after=None):
        if not steps:
            return
        step = steps.pop(0)
        if after:
            live[after], live["term"] = lax.optimization_barrier((live[after], live["term"]))
        term = live["term"]
        with jax.named_scope("weight_grad"):
            if step == "z":
                parts = [term[0], *(flip(term[n], Z * n) for n in range(1, depth))]
                live["term"] = add(*parts).astype(BF16)
            elif step == "cores":
                live["terms"] = [term, *(flip(term, 0, n) for n in range(1, n_rep))]
                del live["term"]
            elif step > 0:
                live["term"] = add(term, flip(term, step)).astype(BF16)
            else:
                term = term[None] if term.ndim == 2 else term
                live["term"] = jnp.concatenate([term, flip(term, -step)])
                z_order.extend([-step // Z ^ other for other in z_order])

    half = width // 2
    tops = lambda values: [value[:half] for value in values]
    ends = lambda values: [value[half:] for value in values]
    live["first"] = [top_diag, end_diag]
    for pair in reversed(range(pair_count)):
        even = 2 * pair * Z
        top = pair + 1 == pair_count
        if not top:
            mask = low_bit(even + 2 * Z)
            name = ("to", even + 2 * Z - mask, mask)

        with jax.named_scope(GRADS_ACROSS):
            if pair > 0:
                top_diag, end_diag = live.pop("first")
                live["top"], live["end"] = flip(top_diag, X), flip(end_diag, Y)
        if not top:
            with jax.named_scope(GRADS_ALONG):
                live[name] = [flip(live["passed"][0], mask)]
        backward_step(pair, "even" if pair == 0 else "mid")
        weight_step(None if top else "even" if pair == 0 else "mid")
        with jax.named_scope(GRADS_ACROSS):
            if pair == 0:
                to_x, to_y, own = live.pop("odd")
                live["odd"], live["ahead"] = [to_x, own], flip(to_y, Y)
            else:
                even_xy, *live["mid"] = live["mid"]
                live["ahead"] = flip(even_xy, X)
        close("ahead")

        if pair == 0:
            with jax.named_scope(GRADS_ACROSS):
                to_x, own = live.pop("odd")
                to_x = add(to_x, live.pop("o_diag")).astype(BF16)
                live["odd_sum"] = [own, flip(to_x, X), live.pop("ahead")]
                to_x, to_y, own = live.pop("even")
                to_y = add(to_y, live.pop("e_diag")).astype(BF16)
                live["sums"] = [own, flip(to_x, X), flip(to_y, Y)]
        else:
            with jax.named_scope(GRADS_ACROSS):
                odd_y, odd_x = live.pop("mid")
                live["to_y"] = live.pop("ahead")
                odd_y, odd_x = add_diagonals(
                    odd_y, odd_x, live.pop("top"), live.pop("end")
                )
                live["to_odd"] = flip(odd_y, Y)
            with jax.named_scope(GRADS_ALONG):
                live["to_x"] = flip(odd_x, Z)
            backward_step(pair, "last")
        if not top:
            with jax.named_scope(GRADS_ALONG):
                live[name].append(flip(live.pop("passed")[1], mask))
        weight_step("last" if pair else None)
        close(*([] if pair else ["sums"]))

        if pair == 0:
            sums = live["sums"]
            with jax.named_scope(GRADS_ALONG):
                sums.append(flip(add(*live.pop("odd_sum")).astype(BF16), Z))
            with jax.named_scope("activated"):
                live["activated"] = activated_rows(where, *rows, n_rep)
        else:
            to_x, to_y, odd, own = live.pop("last")
            with jax.named_scope(GRADS_ACROSS):
                to_x = add(to_x, live.pop("to_x")).astype(BF16)
                to_y = add(to_y, live.pop("to_y")).astype(BF16)
                sums = [own, flip(to_x, X), flip(to_y, Y)]
            with jax.named_scope(GRADS_ALONG):
                sums.append(flip(add(odd, live.pop("to_odd")).astype(BF16), Z))
            backward_step(pair - 1, "first", *([] if pair > 1 else ["odd"]))
        live["sums"] = sums
        weight_step("first" if pair else None)
        if pair == 1:
            with jax.named_scope(GRADS_ACROSS):
                odd_diag, even_diag = live.pop("first")
                live["o_diag"], live["e_diag"] = flip(odd_diag, Y), flip(even_diag, X)
        close("o_diag", "e_diag")
        sums = live.pop("sums")
        halves = [live.pop(key) for key in list(live) if isinstance(key, tuple) and key[1] == even]
        if pair > 0:
            live["passed"] = [
                add(*tops(sums), *(value[0] for value in halves)).astype(BF16),
                add(*ends(sums), *(value[1] for value in halves)).astype(BF16),
            ]
        if pair > 1:
            (chunk,) = live["first"]
            live["first"] = [chunk[:half], chunk[half:]]
    with jax.named_scope("grads_out"):
        feat_grad, weight_grad = final_sum(where, sums, halves, live["terms"], tuple(z_order))
    return (live["activated"], feat_grad, weight_grad)


def solution(mesh):
    placed = (
        P("section", None),
        P(),
        P("section", "rep", None, None, None),
        P("section", "rep", None),
        P("section", "rep", None),
        P("section", "rep"),
        P(("section", "rep"), None),
    )
    sizes = (mesh.shape["section"], mesh.shape["rep"])
    return jax.shard_map(
        functools.partial(shards, sizes),
        mesh=mesh,
        in_specs=placed,
        out_specs=(P(("section", "rep"), None), P("rep", "section", None), P()),
        check_vma=False,
    )
```

```python
import functools

import jax
import jax.numpy as jnp
from jax import lax
from jax.experimental import pallas as pl
from jax.experimental.pallas import tpu as pltpu
from jax.sharding import PartitionSpec as P

BF16 = jnp.bfloat16
F32 = jnp.float32
BOTH = ("section", "rep")
FEATURES_ACROSS, FEATURES_ALONG = "features_xy", "features_z"
GRADS_ACROSS, GRADS_ALONG = "grads_xy", "grads_z"


def in_hbm(value):
    return pltpu.with_memory_space_constraint(value, pltpu.HBM)


def dense_kernel(first, where_ref, packed_ref, tiles_ref, *refs):
    out_ref = refs[-1]
    panel = first + pl.program_id(0)
    size, slots = tiles_ref.shape[-1], tiles_ref.shape[1]
    row_tiles, per_part = out_ref.shape[2] // size, out_ref.shape[3] // size
    out_ref[...] = jnp.zeros_like(out_ref)

    def add_tile(slot, carry):
        place = packed_ref[panel, slot]
        row = pl.multiple_of(place // row_tiles * size, size)
        tile_col = place % row_tiles
        col = pl.multiple_of(tile_col % per_part * size, size)
        out_ref[tile_col // per_part, 0, pl.ds(row, size), pl.ds(col, size)] += tiles_ref[0, slot]
        return carry

    lax.fori_loop(0, packed_ref[panel, slots], add_tile, 0)


def make_dense(first, before, where, tiles, packed, block_rows, n_rep):
    panels, slots, size, _ = tiles.shape
    half = panels // 2
    part = block_rows // n_rep
    at = lambda p: first + p
    return pl.pallas_call(
        functools.partial(dense_kernel, first),
        out_shape=pltpu.HBM((n_rep, panels, block_rows, part), BF16),
        grid_spec=pltpu.PrefetchScalarGridSpec(
            num_scalar_prefetch=2,
            grid=(half,),
            in_specs=[pl.BlockSpec((1, slots, size, size), lambda p, *_: (at(p), 0, 0, 0))]
            + [pl.BlockSpec(memory_space=pl.ANY)] * (first > 0),
            out_specs=pl.BlockSpec((n_rep, 1, block_rows, part), lambda p, *_: (0, at(p), 0, 0)),
        ),
        input_output_aliases={3: 0} if first else {},
        compiler_params=pltpu.CompilerParams(vmem_limit_bytes=36 * 2**20),
        cost_estimate=pl.CostEstimate(
            flops=0,
            transcendentals=0,
            bytes_accessed=tiles.size // 8,
        ),
    )(where, packed, in_hbm(tiles), *([in_hbm(before)] if first else []))


def other_kernel(first, where_ref, packed_ref, tiles_ref, out_ref):
    panel = first + pl.program_id(0)
    size, slots = tiles_ref.shape[-1], tiles_ref.shape[1]
    row_tiles, per_part = out_ref.shape[1] // size, out_ref.shape[2] // size
    out_ref[...] = jnp.zeros_like(out_ref)

    def add_tile(slot, carry):
        place = packed_ref[panel, slot]
        row = pl.multiple_of(place // row_tiles * size, size)
        tile_col = place % row_tiles
        col = pl.multiple_of(tile_col % per_part * size, size)

        @pl.when(tile_col // per_part == where_ref[0])
        def _():
            out_ref[0, pl.ds(row, size), pl.ds(col, size)] += tiles_ref[0, slot]

        return carry

    lax.fori_loop(0, packed_ref[panel, slots], add_tile, 0)


def make_other(first, where, tiles, packed, block_rows, n_rep):
    panels, slots, size, _ = tiles.shape
    half = panels // 2
    part = block_rows // n_rep
    return pl.pallas_call(
        functools.partial(other_kernel, first),
        out_shape=pltpu.HBM((half, block_rows, part), BF16),
        grid_spec=pltpu.PrefetchScalarGridSpec(
            num_scalar_prefetch=2,
            grid=(half,),
            in_specs=[pl.BlockSpec((1, slots, size, size), lambda p, *_: (first + p, 0, 0, 0))],
            out_specs=pl.BlockSpec((1, block_rows, part), lambda p, *_: (p, 0, 0)),
        ),
        compiler_params=pltpu.CompilerParams(vmem_limit_bytes=36 * 2**20),
        cost_estimate=pl.CostEstimate(
            flops=0, transcendentals=0, bytes_accessed=tiles.size // 8
        ),
    )(where, packed, tiles)


def forward_kernel(offset, n_pieces, n_others, has_total, where_ref, dense_ref, *refs):
    others, refs = refs[:n_others], refs[n_others:]
    units = []
    for pieces in n_pieces:
        tops, refs = refs[:pieces], refs[pieces:]
        half = tops[0].shape[0] // (2 if pieces == 1 else 1)
        units.append([tops[0].at[pl.ds(0, half)], tops[-1].at[pl.ds(half * (2 - pieces), half)]])
    n_units = len(units)
    total_ref, refs = (refs[0], refs[1:]) if has_total else (None, refs)
    out_ref, sum_ref, a_buf, u_buf, sems, sum_sem = refs
    _, panels, _, part = dense_ref.shape
    some = others[0].shape[0]
    rep = where_ref[0]

    def a_copy(source, slot, side):
        target = a_buf.at[slot, :, pl.ds(side * part, part)]
        return pltpu.make_async_copy(source, target, sems.at[0, slot, side])

    def u_copy(source, slot, side, piece):
        half = part // 2
        target = u_buf.at[slot, pl.ds(side * part + piece * half, half), :]
        return pltpu.make_async_copy(source, target, sems.at[1 + piece, slot, side])

    def fetch(pair, slot):
        for side in range(2):
            place = where_ref[offset + 2 * pair + side]
            owner, panel = place // panels, place % panels
            turn = ((owner ^ rep) - 1) * (panels // some) + panel // some

            @pl.when(owner == rep)
            def _():
                a_copy(dense_ref.at[rep, panel], slot, side).start()

            for number, other_ref in enumerate(others):

                @pl.when((owner != rep) & (turn == number))
                def _():
                    a_copy(other_ref.at[panel % some], slot, side).start()

            for number in range(side, n_units, 2):

                @pl.when(pair == number // 2)
                def _():
                    for piece in range(2):
                        u_copy(units[number][piece], slot, side, piece).start()

    pairs = n_units // 2
    fetch(0, 0)
    if has_total:
        load = pltpu.make_async_copy(total_ref, sum_ref, sum_sem)
        load.start()
        load.wait()
    else:
        sum_ref[...] = jnp.zeros_like(sum_ref)

    def step(pair, carry):
        slot = pair % 2

        @pl.when(pair + 1 < pairs)
        def _():
            fetch(pair + 1, 1 - slot)

        for side in range(2):
            a_copy(dense_ref.at[0, 0], slot, side).wait()
            for piece in range(2):
                u_copy(units[0][piece], slot, side, piece).wait()
        sum_ref[...] += jnp.dot(a_buf[slot], u_buf[slot], preferred_element_type=F32)
        return carry

    lax.fori_loop(0, pairs, step, 0)
    if out_ref.dtype == F32:
        store = pltpu.make_async_copy(sum_ref, out_ref, sum_sem)
        store.start()
        store.wait()
    else:
        out_ref[...] = sum_ref[...].astype(out_ref.dtype)


def forward_part(where, offset, units, total, dense, others, kind):
    _, _, rows, part = dense.shape
    width = units[0].shape[1]
    n_pieces = [len(unit) if isinstance(unit, list) else 1 for unit in units]
    pieces = [piece for unit in units for piece in (unit if isinstance(unit, list) else [unit])]
    near = pl.BlockSpec(memory_space=pl.ANY)
    hbm = pl.BlockSpec(memory_space=pltpu.HBM)
    has_total = total is not None
    n_units, n_others = len(units), len(others)
    return pl.pallas_call(
        functools.partial(forward_kernel, offset, n_pieces, n_others, has_total),
        out_shape=jax.ShapeDtypeStruct((rows, width), kind),
        grid_spec=pltpu.PrefetchScalarGridSpec(
            num_scalar_prefetch=1,
            grid=(1,),
            in_specs=[hbm] * (1 + n_others) + [near] * (len(pieces) + has_total),
            out_specs=near if kind == F32 else pl.BlockSpec((rows, width), lambda i, where: (0, 0)),
            scratch_shapes=[
                pltpu.VMEM((rows, width), F32),
                pltpu.VMEM((2, rows, 2 * part), BF16),
                pltpu.VMEM((2, 2 * part, width), BF16),
                pltpu.SemaphoreType.DMA((3, 2, 2)),
                pltpu.SemaphoreType.DMA,
            ],
        ),
        compiler_params=pltpu.CompilerParams(vmem_limit_bytes=36 * 2**20),
        cost_estimate=pl.CostEstimate(
            flops=2 * n_units * rows * part * width,
            transcendentals=0,
            bytes_accessed=n_units * rows * part * 2 + 8 * rows * width,
        ),
    )(where, in_hbm(dense), *map(in_hbm, others), *pieces, *([total] if has_total else []))


def slopes(mine_ref, other_ref, weight_ref, cot_ref):
    agg = (mine_ref[...].astype(F32) + other_ref[...].astype(F32)).astype(BF16)
    pre = jnp.dot(agg, weight_ref[...], preferred_element_type=F32)
    sigma = 0.5 * jnp.tanh(0.5 * pre) + 0.5
    slope = cot_ref[...].astype(F32) * sigma * (1.0 + pre * (1.0 - sigma))
    return agg, (pre * sigma).astype(BF16), slope.astype(BF16)


def middle_kernel(blocks, where_ref, mine_ref, other_ref, weight_ref, cot_ref, a_ref, *refs):
    grad_ref, top_ref, end_ref, term_ref, sum_ref, full_ref = refs
    step = pl.program_id(0)
    part = mine_ref.shape[0]

    @pl.when(step < blocks)
    def _():
        agg, _, pre_grad = slopes(mine_ref, other_ref, weight_ref, cot_ref)
        grad = lax.dot_general(
            weight_ref[...], pre_grad, (((1,), (1,)), ((), ())), preferred_element_type=F32
        ).astype(BF16)
        grad_ref[...] = grad
        full_ref[:, pl.ds(pl.multiple_of(step * part, part), part)] = grad
        term = lax.dot_general(agg, pre_grad, (((0,), (0,)), ((), ())), preferred_element_type=F32)

        @pl.when(step == 0)
        def _():
            sum_ref[...] = term

        @pl.when(step > 0)
        def _():
            sum_ref[...] += term

    @pl.when(step == blocks)
    def _():
        chunk = jnp.dot(full_ref[...], a_ref[0, 0], preferred_element_type=F32).astype(BF16)
        half = top_ref.shape[0]
        top_ref[...] = chunk[:half]
        end_ref[...] = chunk[half:]
        depth, size, _ = term_ref.shape
        z = where_ref[1] // 4
        for number in range(depth):
            start = (where_ref[0] * depth + (z ^ number)) * size
            rows = sum_ref[pl.ds(pl.multiple_of(start, size), size), :]
            term_ref[number] = rows.astype(BF16)


def middle(where, offset, mine, other, weight, cotangent, dense, depth):
    rows, width = mine.shape
    n_rep, _, _, cols = dense.shape
    blocks = 4
    part = rows // blocks
    size = width // n_rep // depth
    block = pl.BlockSpec((part, width), lambda i, where: (jnp.minimum(i, blocks - 1), 0))
    fixed = lambda *shape: pl.BlockSpec(shape, lambda i, where: (0,) * len(shape))
    half = width // 2
    shapes = [(width, rows), (half, cols), (half, cols), (depth, size, width)]

    def a_block(i, where):
        place = where[offset]
        return (place % n_rep, place // n_rep, 0, 0)

    return pl.pallas_call(
        functools.partial(middle_kernel, blocks),
        out_shape=[jax.ShapeDtypeStruct(shape, BF16) for shape in shapes],
        grid_spec=pltpu.PrefetchScalarGridSpec(
            num_scalar_prefetch=1,
            grid=(blocks + 1,),
            in_specs=[
                block,
                block,
                fixed(width, width),
                block,
                pl.BlockSpec((1, 1, rows, cols), a_block),
            ],
            out_specs=[
                pl.BlockSpec((width, part), lambda i, where: (0, jnp.minimum(i, blocks - 1))),
                *(fixed(*shape) for shape in shapes[1:]),
            ],
            scratch_shapes=[pltpu.VMEM((width, width), F32), pltpu.VMEM((width, rows), BF16)],
        ),
        compiler_params=pltpu.CompilerParams(vmem_limit_bytes=36 * 2**20),
        cost_estimate=pl.CostEstimate(
            flops=6 * rows * width * width + 4 * rows * width * cols,
            transcendentals=rows * width,
            bytes_accessed=rows * width * 12,
        ),
    )(where, mine, other, weight, cotangent, in_hbm(dense))


def activated_kernel(where_ref, mine_ref, other_ref, weight_ref, cot_ref, act_ref):
    act_ref[...] = slopes(mine_ref, other_ref, weight_ref, cot_ref)[1]


def activated_rows(where, mine, other, weight, cotangent, n_rep):
    rows, width = mine.shape
    part = rows // n_rep
    block = pl.BlockSpec((part, width), lambda i, where: (where[0], 0))
    fixed = lambda *shape: pl.BlockSpec(shape, lambda i, where: (0, 0))
    return pl.pallas_call(
        activated_kernel,
        out_shape=jax.ShapeDtypeStruct((part, width), BF16),
        grid_spec=pltpu.PrefetchScalarGridSpec(
            num_scalar_prefetch=1,
            grid=(1,),
            in_specs=[block, block, fixed(width, width), block],
            out_specs=fixed(part, width),
        ),
        compiler_params=pltpu.CompilerParams(vmem_limit_bytes=36 * 2**20),
        cost_estimate=pl.CostEstimate(
            flops=2 * part * width * width,
            transcendentals=part * width,
            bytes_accessed=part * width * 8,
        ),
    )(where, mine, other, weight, cotangent)


def backward_kernel(where_ref, grad_ref, a_ref, *out_refs):
    chunk = jnp.dot(grad_ref[...], a_ref[0, 0], preferred_element_type=F32).astype(BF16)
    for number, out_ref in enumerate(out_refs):

        @pl.when(pl.program_id(0) == number)
        def _():
            out_ref[...] = chunk


def backward_part(where, offset, count, grad, dense):
    width, rows = grad.shape
    n_rep, _, _, cols = dense.shape
    fixed = lambda *shape: pl.BlockSpec(shape, lambda i, where: (0, 0))

    def a_block(i, where):
        place = where[offset + i]
        return (place % n_rep, place // n_rep, 0, 0)

    return pl.pallas_call(
        backward_kernel,
        out_shape=[jax.ShapeDtypeStruct((width, cols), BF16)] * count,
        grid_spec=pltpu.PrefetchScalarGridSpec(
            num_scalar_prefetch=1,
            grid=(count,),
            in_specs=[fixed(width, rows), pl.BlockSpec((1, 1, rows, cols), a_block)],
            out_specs=[fixed(width, cols)] * count,
        ),
        compiler_params=pltpu.CompilerParams(vmem_limit_bytes=36 * 2**20),
        cost_estimate=pl.CostEstimate(
            flops=2 * count * rows * width * cols,
            transcendentals=0,
            bytes_accessed=2 * count * rows * cols + 2 * count * width * cols + 2 * width * rows,
        ),
    )(where, grad, in_hbm(dense))


def diagonals_kernel(y_ref, x_ref, top_ref, end_ref, y_out, x_out):
    half = top_ref.shape[0]
    y_out[:half] = (y_ref[:half].astype(F32) + top_ref[...].astype(F32)).astype(BF16)
    y_out[half:] = y_ref[half:]
    x_out[:half] = x_ref[:half]
    x_out[half:] = (x_ref[half:].astype(F32) + end_ref[...].astype(F32)).astype(BF16)


def add_diagonals(odd_y, odd_x, top, end):
    return pl.pallas_call(
        diagonals_kernel,
        out_shape=[jax.ShapeDtypeStruct(odd_y.shape, BF16)] * 2,
        compiler_params=pltpu.CompilerParams(vmem_limit_bytes=36 * 2**20),
        cost_estimate=pl.CostEstimate(
            flops=odd_y.size, transcendentals=0, bytes_accessed=10 * odd_y.size
        ),
    )(odd_y, odd_x, top, end)


def final_kernel(n_parts, n_halves, z_order, where_ref, *refs):
    parts, terms = refs[:n_parts], refs[n_parts + n_halves : -2]
    halves = refs[n_parts : n_parts + n_halves]
    out_ref, weight_out = refs[-2:]
    values = [part[...].astype(F32) for part in parts]
    for top, end in zip(halves[::2], halves[1::2]):
        values.append(jnp.concatenate([top[...].astype(F32), end[...].astype(F32)]))
    total = functools.reduce(jnp.add, values)
    out_ref[0] = total.T.astype(BF16)
    depth, size, _ = terms[0].shape
    for other, term_ref in enumerate(terms):
        for number, offset in enumerate(z_order):
            place = (where_ref[0] ^ other) * depth + ((where_ref[1] // 4) ^ offset)
            rows = pl.ds(pl.multiple_of(place * size, size), size)
            weight_out[rows, :] = term_ref[number].astype(F32)


def final_sum(where, parts, halves, terms, z_order):
    width, cols = parts[0].shape
    halves = [half for pair in halves for half in pair]
    whole = lambda value: pl.BlockSpec(value.shape, lambda i, where: (0,) * value.ndim)
    outs = [
        jax.ShapeDtypeStruct((1, cols, width), BF16),
        jax.ShapeDtypeStruct((width, width), F32),
    ]
    return pl.pallas_call(
        functools.partial(final_kernel, len(parts), len(halves), z_order),
        out_shape=outs,
        grid_spec=pltpu.PrefetchScalarGridSpec(
            num_scalar_prefetch=1,
            grid=(1,),
            in_specs=[whole(value) for value in [*parts, *halves, *terms]],
            out_specs=[whole(value) for value in outs],
        ),
        compiler_params=pltpu.CompilerParams(vmem_limit_bytes=36 * 2**20),
        cost_estimate=pl.CostEstimate(
            flops=len(parts) * width * cols,
            transcendentals=0,
            bytes_accessed=2 * (len(parts) + 1) * width * cols,
        ),
    )(where, *parts, *halves, *terms)


def shards(sizes, features, weight, tile_values, tile_rows, tile_cols, tile_count, cotangent):
    n_section, n_rep = sizes
    block_rows, width = features.shape
    part = block_rows // n_rep
    section, rep = lax.axis_index("section"), lax.axis_index("rep")

    X, Y, Z = 1, 2, 4
    pair_count = n_section // 8
    low_bit = lambda mask: mask & -mask

    def flip(value, mask, rep_mask=0):
        pairs = [
            (s * n_rep + r, (s ^ mask) * n_rep + (r ^ rep_mask))
            for s in range(n_section)
            for r in range(n_rep)
        ]
        return lax.ppermute(value, BOTH, pairs)

    def gather_rep(value):
        held = [value] + [flip(value, 0, other) for other in range(1, n_rep)]
        order = rep ^ jnp.arange(n_rep)
        if n_rep == 2:
            held = [jnp.where(rep == 0, held[0], held[1]), jnp.where(rep == 0, held[1], held[0])]
            return jnp.concatenate(held)
        return jnp.stack(held)[order].reshape(-1, width)

    live = {}

    def close(*open_names):
        names = [name for name in live if name not in open_names]
        live.update(zip(names, lax.optimization_barrier([live[name] for name in names])))

    masks, offsets = [], {}

    def plan(name, wanted):
        offsets[name] = 2 + len(masks)
        masks.extend(wanted)

    for pair in range(pair_count):
        even, odd = 2 * pair * Z, (2 * pair + 1) * Z
        plan(("early", pair), [even, even + X])
        plan(("more", pair), [even + Y, odd, even + X + Y, odd + Y])
        plan(("late", pair), [odd + X, odd + X + Y])
        if pair == 0:
            plan(("first", pair), [odd + X + Y, even + X + Y])
            plan(("odd", pair), [odd + X, odd + Y, odd])
            plan(("even", pair), [even + X, even + Y, even])
        else:
            plan(("first", pair), [odd + X + Y])
            plan(("mid", pair), [even + X + Y, odd + Y, odd + X])
            plan(("last", pair), [even + X, even + Y, odd, even])
    offsets["joined"] = 2 + len(masks)
    masks += [0, X, Y, Z, Z + X, Z + Y, X + Y, Z + X + Y, 2 * Z, 2 * Z + X]
    where = jnp.concatenate(
        [rep[None], section[None], section ^ jnp.array(masks, jnp.int32)]
    ).astype(jnp.int32)

    def forward_step(names, units, total, kind=F32):
        with jax.named_scope("forward"):
            return forward_part(
                where, offsets[names], units, total, live["dense"], live["others"], kind
            )

    row_tiles = block_rows // tile_values.shape[3]
    packed = jnp.concatenate(
        [tile_rows[0] * row_tiles + tile_cols[0], tile_count[0][:, None]], axis=1
    )
    panels = tile_values.shape[1]
    def build_own(first):
        with jax.named_scope("dense_blocks"):
            live["dense"] = make_dense(
                first, live.get("dense"), where, tile_values[0], packed, block_rows, n_rep
            )

    def build_others(first):
        with jax.named_scope("other_blocks"):
            return [make_other(first, where, *sent, block_rows, n_rep) for sent in live["tiles"]]

    live[0] = lax.dynamic_slice_in_dim(features, rep * part, part, axis=0)
    with jax.named_scope("tiles_exchange"):
        live["tiles"] = [
            (flip(tile_values[0], 0, n), flip(packed, 0, n)) for n in range(1, n_rep)
        ]
    half = part // 2
    for pair in range(pair_count):
        even, odd = 2 * pair * Z, (2 * pair + 1) * Z
        later = even + 2 * Z
        last = pair + 1 == pair_count

        with jax.named_scope(FEATURES_ACROSS):
            live["even_x"], live["even_y"] = flip(live[even], X), flip(live[even], Y)
        with jax.named_scope(FEATURES_ALONG):
            live[odd] = flip(live[even], Z)
        if pair == 0:
            build_own(0)
        if pair == 1:
            two = build_others(panels // 2)
            live["others"] = [side for sides in zip(live.pop("one"), two) for side in sides]
            del live["tiles"]
            with jax.named_scope("cotangents"):
                live["cot"] = gather_rep(cotangent)
        if pair > 1:
            live["total"] = forward_step(("late", pair - 1), live.pop("units"), live["total"])
        close(*(["even_x", "even_y"] if pair == 0 else []))

        if pair == 0:
            with jax.named_scope(FEATURES_ACROSS):
                live["odd_x"], live["odd_y"] = flip(live[odd], X), flip(live[odd], Y)
        else:
            with jax.named_scope(FEATURES_ACROSS):
                live["even_xy"], live["odd_y"] = flip(live["even_y"], X), flip(live[odd], Y)
            with jax.named_scope(FEATURES_ALONG):
                live["odd_x"] = flip(live["even_x"], Z)
            units = [live[even], live["even_x"]]
            if pair == 1:
                live["total"] = forward_step("joined", live.pop("units") + units, None)
            else:
                live["total"] = forward_step(("early", pair), units, live["total"])
        if not last:
            with jax.named_scope(FEATURES_ALONG):
                live[later] = flip(live[later - low_bit(later)], low_bit(later))
        close(*([] if last else [later]))

        if pair == 0:
            units = [live[even], live["even_x"], live["even_y"]]
            units += [live[odd], live["odd_x"], live["odd_y"]]
            with jax.named_scope(FEATURES_ACROSS):
                units += [flip(live["even_x"], Y), flip(live["odd_y"], X)]
            live["units"] = units
            build_own(panels // 2)
            live["one"] = build_others(0)
        else:
            with jax.named_scope(FEATURES_ACROSS):
                odd_xy = [flip(live["odd_y"][:half], X), flip(live["odd_x"][half:], Y)]
            live["units"] = [live["odd_x"], odd_xy]
            units = [live["even_y"], live[odd], live.pop("even_xy"), live["odd_y"]]
            live["total"] = forward_step(("more", pair), units, live["total"])
        for name in ("even_x", "even_y", "odd_x", "odd_y"):
            del live[name]
        close()
    partial = forward_step(
        ("late", pair_count - 1), live.pop("units"), live.get("total"), BF16
    )

    with jax.named_scope("partial_sums"):
        other = flip(partial, 0, 1)
        for bit in range(1, n_rep.bit_length() - 1):
            partial = (partial.astype(F32) + other.astype(F32)).astype(BF16)
            other = flip(partial, 0, 1 << bit)

    with jax.named_scope("middle"):
        depth = n_section // 4
        rows = (partial, other, weight, live["cot"])
        grad, top_diag, end_diag, term = middle(
            where, offsets["first", pair_count - 1], *rows, live["dense"], depth
        )

    live = {"grad": grad, "dense": live["dense"], "term": term}
    add = lambda *values: functools.reduce(jnp.add, [value.astype(F32) for value in values])

    sizes_of = {"mid": 3, "last": 4, "odd": 3, "even": 3}

    def backward_step(pair, *names):
        with jax.named_scope("backward"):
            counts = [sizes_of.get(name, 1 if pair else 2) for name in names]
            chunks = backward_part(
                where, offsets[names[0], pair], sum(counts), live["grad"], live["dense"]
            )
            for name, count in zip(names, counts):
                live[name], chunks = chunks[:count], chunks[count:]

    steps = ["z", X, Y, *(-(Z << bit) for bit in reversed(range(depth.bit_length() - 1)))]
    steps.append("cores")
    z_order = [0]

    def weight_step(after=None):
        if not steps:
            return
        step = steps.pop(0)
        if after:
            live[after], live["term"] = lax.optimization_barrier((live[after], live["term"]))
        term = live["term"]
        with jax.named_scope("weight_grad"):
            if step == "z":
                parts = [term[0], *(flip(term[n], Z * n) for n in range(1, depth))]
                live["term"] = add(*parts).astype(BF16)
            elif step == "cores":
                live["terms"] = [term, *(flip(term, 0, n) for n in range(1, n_rep))]
                del live["term"]
            elif step > 0:
                live["term"] = add(term, flip(term, step)).astype(BF16)
            else:
                term = term[None] if term.ndim == 2 else term
                live["term"] = jnp.concatenate([term, flip(term, -step)])
                z_order.extend([-step // Z ^ other for other in z_order])

    half = width // 2
    tops = lambda values: [value[:half] for value in values]
    ends = lambda values: [value[half:] for value in values]
    live["first"] = [top_diag, end_diag]
    for pair in reversed(range(pair_count)):
        even = 2 * pair * Z
        top = pair + 1 == pair_count
        if not top:
            mask = low_bit(even + 2 * Z)
            name = ("to", even + 2 * Z - mask, mask)

        with jax.named_scope(GRADS_ACROSS):
            if pair > 0:
                top_diag, end_diag = live.pop("first")
                live["top"], live["end"] = flip(top_diag, X), flip(end_diag, Y)
        if not top:
            with jax.named_scope(GRADS_ALONG):
                live[name] = [flip(live["passed"][0], mask)]
        backward_step(pair, "even" if pair == 0 else "mid")
        weight_step(None if top else "even" if pair == 0 else "mid")
        with jax.named_scope(GRADS_ACROSS):
            if pair == 0:
                to_x, to_y, own = live.pop("odd")
                live["odd"], live["ahead"] = [to_x, own], flip(to_y, Y)
            else:
                even_xy, *live["mid"] = live["mid"]
                live["ahead"] = flip(even_xy, X)
        close("ahead")

        if pair == 0:
            with jax.named_scope(GRADS_ACROSS):
                to_x, own = live.pop("odd")
                to_x = add(to_x, live.pop("o_diag")).astype(BF16)
                live["odd_sum"] = [own, flip(to_x, X), live.pop("ahead")]
                to_x, to_y, own = live.pop("even")
                to_y = add(to_y, live.pop("e_diag")).astype(BF16)
                live["sums"] = [own, flip(to_x, X), flip(to_y, Y)]
        else:
            with jax.named_scope(GRADS_ACROSS):
                odd_y, odd_x = live.pop("mid")
                live["to_y"] = live.pop("ahead")
                odd_y, odd_x = add_diagonals(
                    odd_y, odd_x, live.pop("top"), live.pop("end")
                )
                live["to_odd"] = flip(odd_y, Y)
            with jax.named_scope(GRADS_ALONG):
                live["to_x"] = flip(odd_x, Z)
            backward_step(pair, "last")
        if not top:
            with jax.named_scope(GRADS_ALONG):
                live[name].append(flip(live.pop("passed")[1], mask))
        weight_step("last" if pair else None)
        close(*([] if pair else ["sums"]))

        if pair == 0:
            sums = live["sums"]
            with jax.named_scope(GRADS_ALONG):
                sums.append(flip(add(*live.pop("odd_sum")).astype(BF16), Z))
            with jax.named_scope("activated"):
                live["activated"] = activated_rows(where, *rows, n_rep)
        else:
            to_x, to_y, odd, own = live.pop("last")
            with jax.named_scope(GRADS_ACROSS):
                to_x = add(to_x, live.pop("to_x")).astype(BF16)
                to_y = add(to_y, live.pop("to_y")).astype(BF16)
                sums = [own, flip(to_x, X), flip(to_y, Y)]
            with jax.named_scope(GRADS_ALONG):
                sums.append(flip(add(odd, live.pop("to_odd")).astype(BF16), Z))
            backward_step(pair - 1, "first", *([] if pair > 1 else ["odd"]))
        live["sums"] = sums
        weight_step("first" if pair else None)
        if pair == 1:
            with jax.named_scope(GRADS_ACROSS):
                odd_diag, even_diag = live.pop("first")
                live["o_diag"], live["e_diag"] = flip(odd_diag, Y), flip(even_diag, X)
        close("o_diag", "e_diag")
        sums = live.pop("sums")
        halves = [live.pop(key) for key in list(live) if isinstance(key, tuple) and key[1] == even]
        if pair > 0:
            live["passed"] = [
                add(*tops(sums), *(value[0] for value in halves)).astype(BF16),
                add(*ends(sums), *(value[1] for value in halves)).astype(BF16),
            ]
        if pair > 1:
            (chunk,) = live["first"]
            live["first"] = [chunk[:half], chunk[half:]]
    with jax.named_scope("grads_out"):
        feat_grad, weight_grad = final_sum(where, sums, halves, live["terms"], tuple(z_order))
    return (live["activated"], feat_grad, weight_grad)


def solution(mesh):
    placed = (
        P("section", None),
        P(),
        P("section", "rep", None, None, None),
        P("section", "rep", None),
        P("section", "rep", None),
        P("section", "rep"),
        P(("section", "rep"), None),
    )
    sizes = (mesh.shape["section"], mesh.shape["rep"])
    return jax.shard_map(
        functools.partial(shards, sizes),
        mesh=mesh,
        in_specs=placed,
        out_specs=(P(("section", "rep"), None), P("rep", "section", None), P()),
        check_vma=False,
    )
```

```python
import functools

import jax
import jax.numpy as jnp
from jax import lax
from jax.experimental import pallas as pl
from jax.experimental.pallas import tpu as pltpu
from jax.sharding import PartitionSpec as P

BF16 = jnp.bfloat16
F32 = jnp.float32
BOTH = ("section", "rep")
FEATURES_ACROSS, FEATURES_ALONG = "features_xy", "features_z"
GRADS_ACROSS, GRADS_ALONG = "grads_xy", "grads_z"


def in_hbm(value):
    return pltpu.with_memory_space_constraint(value, pltpu.HBM)


def tile_place(place, row_tiles, per_part):
    row_bits, part_bits = row_tiles.bit_length() - 1, per_part.bit_length() - 1
    tile_col = place & (row_tiles - 1)
    return place >> row_bits, tile_col >> part_bits, tile_col & (per_part - 1)


def dense_kernel(first, where_ref, packed_ref, tiles_ref, *refs):
    out_ref = refs[-1]
    panel = first + pl.program_id(0)
    size, slots = tiles_ref.shape[-1], tiles_ref.shape[1]
    row_tiles, per_part = out_ref.shape[2] // size, out_ref.shape[3] // size
    out_ref[...] = jnp.zeros_like(out_ref)

    def add_tile(slot, carry):
        row, part, col = tile_place(packed_ref[panel, slot], row_tiles, per_part)
        rows = pl.ds(pl.multiple_of(row * size, size), size)
        cols = pl.ds(pl.multiple_of(col * size, size), size)
        out_ref[part, 0, rows, cols] += tiles_ref[0, slot]
        return carry

    lax.fori_loop(0, packed_ref[panel, slots], add_tile, 0)


def make_dense(first, before, where, tiles, packed, block_rows, n_rep):
    panels, slots, size, _ = tiles.shape
    half = panels // 2
    part = block_rows // n_rep
    at = lambda p: first + p
    return pl.pallas_call(
        functools.partial(dense_kernel, first),
        out_shape=pltpu.HBM((n_rep, panels, block_rows, part), BF16),
        grid_spec=pltpu.PrefetchScalarGridSpec(
            num_scalar_prefetch=2,
            grid=(half,),
            in_specs=[pl.BlockSpec((1, slots, size, size), lambda p, *_: (at(p), 0, 0, 0))]
            + [pl.BlockSpec(memory_space=pl.ANY)] * (first > 0),
            out_specs=pl.BlockSpec((n_rep, 1, block_rows, part), lambda p, *_: (0, at(p), 0, 0)),
        ),
        input_output_aliases={3: 0} if first else {},
        compiler_params=pltpu.CompilerParams(vmem_limit_bytes=24 * 2**20),
        cost_estimate=pl.CostEstimate(
            flops=0,
            transcendentals=0,
            bytes_accessed=tiles.size // 8,
        ),
    )(where, packed, in_hbm(tiles), *([in_hbm(before)] if first else []))


def other_kernel(first, where_ref, packed_ref, tiles_ref, out_ref):
    panel = first + pl.program_id(0)
    size, slots = tiles_ref.shape[-1], tiles_ref.shape[1]
    row_tiles, per_part = out_ref.shape[1] // size, out_ref.shape[2] // size
    out_ref[...] = jnp.zeros_like(out_ref)

    def add_tile(slot, carry):
        row, part, col = tile_place(packed_ref[panel, slot], row_tiles, per_part)
        rows = pl.ds(pl.multiple_of(row * size, size), size)
        cols = pl.ds(pl.multiple_of(col * size, size), size)

        @pl.when(part == where_ref[0])
        def _():
            out_ref[0, rows, cols] += tiles_ref[0, slot]

        return carry

    lax.fori_loop(0, packed_ref[panel, slots], add_tile, 0)


def make_other(first, where, tiles, packed, block_rows, n_rep):
    panels, slots, size, _ = tiles.shape
    half = panels // 2
    part = block_rows // n_rep
    return pl.pallas_call(
        functools.partial(other_kernel, first),
        out_shape=pltpu.HBM((half, block_rows, part), BF16),
        grid_spec=pltpu.PrefetchScalarGridSpec(
            num_scalar_prefetch=2,
            grid=(half,),
            in_specs=[pl.BlockSpec((1, slots, size, size), lambda p, *_: (first + p, 0, 0, 0))],
            out_specs=pl.BlockSpec((1, block_rows, part), lambda p, *_: (p, 0, 0)),
        ),
        compiler_params=pltpu.CompilerParams(vmem_limit_bytes=24 * 2**20),
        cost_estimate=pl.CostEstimate(
            flops=0, transcendentals=0, bytes_accessed=tiles.size // 8
        ),
    )(where, packed, tiles)


def forward_kernel(offset, n_pieces, n_others, has_total, where_ref, dense_ref, *refs):
    others, refs = refs[:n_others], refs[n_others:]
    units = []
    for pieces in n_pieces:
        tops, refs = refs[:pieces], refs[pieces:]
        half = tops[0].shape[0] // (2 if pieces == 1 else 1)
        units.append([tops[0].at[pl.ds(0, half)], tops[-1].at[pl.ds(half * (2 - pieces), half)]])
    n_units = len(units)
    total_ref, refs = (refs[0], refs[1:]) if has_total else (None, refs)
    out_ref, sum_ref, a_buf, u_buf, sems, sum_sem = refs
    _, panels, _, part = dense_ref.shape
    some = others[0].shape[0]
    rep = where_ref[0]

    def a_copy(source, slot, side):
        target = a_buf.at[slot, :, pl.ds(side * part, part)]
        return pltpu.make_async_copy(source, target, sems.at[0, slot, side])

    def u_copy(source, slot, side, piece):
        half = part // 2
        target = u_buf.at[slot, pl.ds(side * part + piece * half, half), :]
        return pltpu.make_async_copy(source, target, sems.at[1 + piece, slot, side])

    def fetch(pair, slot):
        for side in range(2):
            place = where_ref[offset + 2 * pair + side]
            owner, panel = place // panels, place % panels
            turn = ((owner ^ rep) - 1) * (panels // some) + panel // some

            @pl.when(owner == rep)
            def _():
                a_copy(dense_ref.at[rep, panel], slot, side).start()

            for number, other_ref in enumerate(others):

                @pl.when((owner != rep) & (turn == number))
                def _():
                    a_copy(other_ref.at[panel % some], slot, side).start()

            for number in range(side, n_units, 2):

                @pl.when(pair == number // 2)
                def _():
                    for piece in range(2):
                        u_copy(units[number][piece], slot, side, piece).start()

    pairs = n_units // 2
    fetch(0, 0)
    if has_total:
        load = pltpu.make_async_copy(total_ref, sum_ref, sum_sem)
        load.start()
        load.wait()
    else:
        sum_ref[...] = jnp.zeros_like(sum_ref)

    def step(pair, carry):
        slot = pair % 2

        @pl.when(pair + 1 < pairs)
        def _():
            fetch(pair + 1, 1 - slot)

        for side in range(2):
            a_copy(dense_ref.at[0, 0], slot, side).wait()
            for piece in range(2):
                u_copy(units[0][piece], slot, side, piece).wait()
        sum_ref[...] += jnp.dot(a_buf[slot], u_buf[slot], preferred_element_type=F32)
        return carry

    lax.fori_loop(0, pairs, step, 0)
    if out_ref.dtype == F32:
        store = pltpu.make_async_copy(sum_ref, out_ref, sum_sem)
        store.start()
        store.wait()
    else:
        out_ref[...] = sum_ref[...].astype(out_ref.dtype)


def forward_part(where, offset, units, total, dense, others, kind):
    _, _, rows, part = dense.shape
    width = units[0].shape[1]
    n_pieces = [len(unit) if isinstance(unit, list) else 1 for unit in units]
    pieces = [piece for unit in units for piece in (unit if isinstance(unit, list) else [unit])]
    near = pl.BlockSpec(memory_space=pl.ANY)
    hbm = pl.BlockSpec(memory_space=pltpu.HBM)
    has_total = total is not None
    n_units, n_others = len(units), len(others)
    return pl.pallas_call(
        functools.partial(forward_kernel, offset, n_pieces, n_others, has_total),
        out_shape=jax.ShapeDtypeStruct((rows, width), kind),
        grid_spec=pltpu.PrefetchScalarGridSpec(
            num_scalar_prefetch=1,
            grid=(1,),
            in_specs=[hbm] * (1 + n_others) + [near] * (len(pieces) + has_total),
            out_specs=near if kind == F32 else pl.BlockSpec((rows, width), lambda i, where: (0, 0)),
            scratch_shapes=[
                pltpu.VMEM((rows, width), F32),
                pltpu.VMEM((2, rows, 2 * part), BF16),
                pltpu.VMEM((2, 2 * part, width), BF16),
                pltpu.SemaphoreType.DMA((3, 2, 2)),
                pltpu.SemaphoreType.DMA,
            ],
        ),
        compiler_params=pltpu.CompilerParams(vmem_limit_bytes=24 * 2**20),
        cost_estimate=pl.CostEstimate(
            flops=2 * n_units * rows * part * width,
            transcendentals=0,
            bytes_accessed=n_units * rows * part * 2 + 8 * rows * width,
        ),
    )(where, in_hbm(dense), *map(in_hbm, others), *pieces, *([total] if has_total else []))


def slopes(mine_ref, other_ref, weight_ref, cot_ref):
    agg = (mine_ref[...].astype(F32) + other_ref[...].astype(F32)).astype(BF16)
    pre = jnp.dot(agg, weight_ref[...], preferred_element_type=F32)
    sigma = 0.5 * jnp.tanh(0.5 * pre) + 0.5
    slope = cot_ref[...].astype(F32) * sigma * (1.0 + pre * (1.0 - sigma))
    return agg, (pre * sigma).astype(BF16), slope.astype(BF16)


def middle_kernel(blocks, where_ref, mine_ref, other_ref, weight_ref, cot_ref, a_ref, *refs):
    grad_ref, top_ref, end_ref, term_ref, sum_ref, full_ref = refs
    step = pl.program_id(0)
    part = mine_ref.shape[0]

    @pl.when(step < blocks)
    def _():
        agg, _, pre_grad = slopes(mine_ref, other_ref, weight_ref, cot_ref)
        grad = lax.dot_general(
            weight_ref[...], pre_grad, (((1,), (1,)), ((), ())), preferred_element_type=F32
        ).astype(BF16)
        grad_ref[...] = grad
        full_ref[:, pl.ds(pl.multiple_of(step * part, part), part)] = grad
        term = lax.dot_general(agg, pre_grad, (((0,), (0,)), ((), ())), preferred_element_type=F32)

        @pl.when(step == 0)
        def _():
            sum_ref[...] = term

        @pl.when(step > 0)
        def _():
            sum_ref[...] += term

    @pl.when(step == blocks)
    def _():
        chunk = jnp.dot(full_ref[...], a_ref[0, 0], preferred_element_type=F32).astype(BF16)
        half = top_ref.shape[0]
        top_ref[...] = chunk[:half]
        end_ref[...] = chunk[half:]
        depth, size, _ = term_ref.shape
        z = where_ref[1] // 4
        for number in range(depth):
            start = (where_ref[0] * depth + (z ^ number)) * size
            rows = sum_ref[pl.ds(pl.multiple_of(start, size), size), :]
            term_ref[number] = rows.astype(BF16)


def middle(where, offset, mine, other, weight, cotangent, dense, depth):
    rows, width = mine.shape
    n_rep, _, _, cols = dense.shape
    blocks = 4
    part = rows // blocks
    size = width // n_rep // depth
    block = pl.BlockSpec((part, width), lambda i, where: (jnp.minimum(i, blocks - 1), 0))
    fixed = lambda *shape: pl.BlockSpec(shape, lambda i, where: (0,) * len(shape))
    half = width // 2
    shapes = [(width, rows), (half, cols), (half, cols), (depth, size, width)]

    def a_block(i, where):
        place = where[offset]
        return (place % n_rep, place // n_rep, 0, 0)

    return pl.pallas_call(
        functools.partial(middle_kernel, blocks),
        out_shape=[jax.ShapeDtypeStruct(shape, BF16) for shape in shapes],
        grid_spec=pltpu.PrefetchScalarGridSpec(
            num_scalar_prefetch=1,
            grid=(blocks + 1,),
            in_specs=[
                block,
                block,
                fixed(width, width),
                block,
                pl.BlockSpec((1, 1, rows, cols), a_block),
            ],
            out_specs=[
                pl.BlockSpec((width, part), lambda i, where: (0, jnp.minimum(i, blocks - 1))),
                *(fixed(*shape) for shape in shapes[1:]),
            ],
            scratch_shapes=[pltpu.VMEM((width, width), F32), pltpu.VMEM((width, rows), BF16)],
        ),
        compiler_params=pltpu.CompilerParams(vmem_limit_bytes=24 * 2**20),
        cost_estimate=pl.CostEstimate(
            flops=6 * rows * width * width + 4 * rows * width * cols,
            transcendentals=rows * width,
            bytes_accessed=rows * width * 12,
        ),
    )(where, mine, other, weight, cotangent, in_hbm(dense))


def activated_kernel(where_ref, mine_ref, other_ref, weight_ref, cot_ref, act_ref):
    act_ref[...] = slopes(mine_ref, other_ref, weight_ref, cot_ref)[1]


def activated_rows(where, mine, other, weight, cotangent, n_rep):
    rows, width = mine.shape
    part = rows // n_rep
    block = pl.BlockSpec((part, width), lambda i, where: (where[0], 0))
    fixed = lambda *shape: pl.BlockSpec(shape, lambda i, where: (0, 0))
    return pl.pallas_call(
        activated_kernel,
        out_shape=jax.ShapeDtypeStruct((part, width), BF16),
        grid_spec=pltpu.PrefetchScalarGridSpec(
            num_scalar_prefetch=1,
            grid=(1,),
            in_specs=[block, block, fixed(width, width), block],
            out_specs=fixed(part, width),
        ),
        compiler_params=pltpu.CompilerParams(vmem_limit_bytes=24 * 2**20),
        cost_estimate=pl.CostEstimate(
            flops=2 * part * width * width,
            transcendentals=part * width,
            bytes_accessed=part * width * 8,
        ),
    )(where, mine, other, weight, cotangent)


def backward_kernel(where_ref, grad_ref, a_ref, *out_refs):
    chunk = jnp.dot(grad_ref[...], a_ref[0, 0], preferred_element_type=F32).astype(BF16)
    for number, out_ref in enumerate(out_refs):

        @pl.when(pl.program_id(0) == number)
        def _():
            out_ref[...] = chunk


def backward_part(where, offset, count, grad, dense):
    width, rows = grad.shape
    n_rep, _, _, cols = dense.shape
    fixed = lambda *shape: pl.BlockSpec(shape, lambda i, where: (0, 0))

    def a_block(i, where):
        place = where[offset + i]
        return (place % n_rep, place // n_rep, 0, 0)

    return pl.pallas_call(
        backward_kernel,
        out_shape=[jax.ShapeDtypeStruct((width, cols), BF16)] * count,
        grid_spec=pltpu.PrefetchScalarGridSpec(
            num_scalar_prefetch=1,
            grid=(count,),
            in_specs=[fixed(width, rows), pl.BlockSpec((1, 1, rows, cols), a_block)],
            out_specs=[fixed(width, cols)] * count,
        ),
        compiler_params=pltpu.CompilerParams(vmem_limit_bytes=24 * 2**20),
        cost_estimate=pl.CostEstimate(
            flops=2 * count * rows * width * cols,
            transcendentals=0,
            bytes_accessed=2 * count * rows * cols + 2 * count * width * cols + 2 * width * rows,
        ),
    )(where, grad, in_hbm(dense))


def diagonals_kernel(y_ref, x_ref, top_ref, end_ref, y_out, x_out):
    half = top_ref.shape[0]
    y_out[:half] = (y_ref[:half].astype(F32) + top_ref[...].astype(F32)).astype(BF16)
    y_out[half:] = y_ref[half:]
    x_out[:half] = x_ref[:half]
    x_out[half:] = (x_ref[half:].astype(F32) + end_ref[...].astype(F32)).astype(BF16)


def add_diagonals(odd_y, odd_x, top, end):
    return pl.pallas_call(
        diagonals_kernel,
        out_shape=[jax.ShapeDtypeStruct(odd_y.shape, BF16)] * 2,
        compiler_params=pltpu.CompilerParams(vmem_limit_bytes=24 * 2**20),
        cost_estimate=pl.CostEstimate(
            flops=odd_y.size, transcendentals=0, bytes_accessed=10 * odd_y.size
        ),
    )(odd_y, odd_x, top, end)


def final_kernel(n_parts, n_halves, z_order, where_ref, *refs):
    parts, terms = refs[:n_parts], refs[n_parts + n_halves : -2]
    halves = refs[n_parts : n_parts + n_halves]
    out_ref, weight_out = refs[-2:]
    values = [part[...].astype(F32) for part in parts]
    for top, end in zip(halves[::2], halves[1::2]):
        values.append(jnp.concatenate([top[...].astype(F32), end[...].astype(F32)]))
    total = functools.reduce(jnp.add, values)
    out_ref[0] = total.T.astype(BF16)
    depth, size, _ = terms[0].shape
    for other, term_ref in enumerate(terms):
        for number, offset in enumerate(z_order):
            place = (where_ref[0] ^ other) * depth + ((where_ref[1] // 4) ^ offset)
            rows = pl.ds(pl.multiple_of(place * size, size), size)
            weight_out[rows, :] = term_ref[number].astype(F32)


def final_sum(where, parts, halves, terms, z_order):
    width, cols = parts[0].shape
    halves = [half for pair in halves for half in pair]
    whole = lambda value: pl.BlockSpec(value.shape, lambda i, where: (0,) * value.ndim)
    outs = [
        jax.ShapeDtypeStruct((1, cols, width), BF16),
        jax.ShapeDtypeStruct((width, width), F32),
    ]
    return pl.pallas_call(
        functools.partial(final_kernel, len(parts), len(halves), z_order),
        out_shape=outs,
        grid_spec=pltpu.PrefetchScalarGridSpec(
            num_scalar_prefetch=1,
            grid=(1,),
            in_specs=[whole(value) for value in [*parts, *halves, *terms]],
            out_specs=[whole(value) for value in outs],
        ),
        compiler_params=pltpu.CompilerParams(vmem_limit_bytes=24 * 2**20),
        cost_estimate=pl.CostEstimate(
            flops=len(parts) * width * cols,
            transcendentals=0,
            bytes_accessed=2 * (len(parts) + 1) * width * cols,
        ),
    )(where, *parts, *halves, *terms)


def shards(sizes, features, weight, tile_values, tile_rows, tile_cols, tile_count, cotangent):
    n_section, n_rep = sizes
    block_rows, width = features.shape
    part = block_rows // n_rep
    section, rep = lax.axis_index("section"), lax.axis_index("rep")

    X, Y, Z = 1, 2, 4
    pair_count = n_section // 8
    low_bit = lambda mask: mask & -mask

    def flip(value, mask, rep_mask=0):
        pairs = [
            (s * n_rep + r, (s ^ mask) * n_rep + (r ^ rep_mask))
            for s in range(n_section)
            for r in range(n_rep)
        ]
        return lax.ppermute(value, BOTH, pairs)

    def gather_rep(value):
        held = [value] + [flip(value, 0, other) for other in range(1, n_rep)]
        order = rep ^ jnp.arange(n_rep)
        if n_rep == 2:
            held = [jnp.where(rep == 0, held[0], held[1]), jnp.where(rep == 0, held[1], held[0])]
            return jnp.concatenate(held)
        return jnp.stack(held)[order].reshape(-1, width)

    live = {}

    def close(*open_names):
        names = [name for name in live if name not in open_names]
        live.update(zip(names, lax.optimization_barrier([live[name] for name in names])))

    masks, offsets = [], {}

    def plan(name, wanted):
        offsets[name] = 2 + len(masks)
        masks.extend(wanted)

    for pair in range(pair_count):
        even, odd = 2 * pair * Z, (2 * pair + 1) * Z
        plan(("early", pair), [even, even + X])
        plan(("more", pair), [even + Y, odd, even + X + Y, odd + Y])
        plan(("late", pair), [odd + X, odd + X + Y])
        if pair == 0:
            plan(("first", pair), [odd + X + Y, even + X + Y])
            plan(("odd", pair), [odd + X, odd + Y, odd])
            plan(("even", pair), [even + X, even + Y, even])
        else:
            plan(("first", pair), [odd + X + Y])
            plan(("mid", pair), [even + X + Y, odd + Y, odd + X])
            plan(("last", pair), [even + X, even + Y, odd, even])
    offsets["joined"] = 2 + len(masks)
    masks += [0, X, Y, Z, Z + X, Z + Y, X + Y, Z + X + Y, 2 * Z, 2 * Z + X]
    where = jnp.concatenate(
        [rep[None], section[None], section ^ jnp.array(masks, jnp.int32)]
    ).astype(jnp.int32)

    def forward_step(names, units, total, kind=F32):
        with jax.named_scope("forward"):
            return forward_part(
                where, offsets[names], units, total, live["dense"], live["others"], kind
            )

    row_tiles = block_rows // tile_values.shape[3]
    packed = jnp.concatenate(
        [tile_rows[0] * row_tiles + tile_cols[0], tile_count[0][:, None]], axis=1
    )
    panels = tile_values.shape[1]
    def build_own(first):
        with jax.named_scope("dense_blocks"):
            live["dense"] = make_dense(
                first, live.get("dense"), where, tile_values[0], packed, block_rows, n_rep
            )

    def build_others(first):
        with jax.named_scope("other_blocks"):
            return [make_other(first, where, *sent, block_rows, n_rep) for sent in live["tiles"]]

    live[0] = lax.dynamic_slice_in_dim(features, rep * part, part, axis=0)
    with jax.named_scope("tiles_exchange"):
        live["tiles"] = [
            (flip(tile_values[0], 0, n), flip(packed, 0, n)) for n in range(1, n_rep)
        ]
    half = part // 2
    for pair in range(pair_count):
        even, odd = 2 * pair * Z, (2 * pair + 1) * Z
        later = even + 2 * Z
        last = pair + 1 == pair_count

        with jax.named_scope(FEATURES_ACROSS):
            live["even_x"], live["even_y"] = flip(live[even], X), flip(live[even], Y)
        with jax.named_scope(FEATURES_ALONG):
            live[odd] = flip(live[even], Z)
        if pair == 0:
            build_own(0)
        if pair == 1:
            two = build_others(panels // 2)
            live["others"] = [side for sides in zip(live.pop("one"), two) for side in sides]
            del live["tiles"]
            with jax.named_scope("cotangents"):
                live["cot"] = gather_rep(cotangent)
        if pair > 1:
            live["total"] = forward_step(("late", pair - 1), live.pop("units"), live["total"])
        close(*(["even_x", "even_y"] if pair == 0 else []))

        if pair == 0:
            with jax.named_scope(FEATURES_ACROSS):
                live["odd_x"], live["odd_y"] = flip(live[odd], X), flip(live[odd], Y)
        else:
            with jax.named_scope(FEATURES_ACROSS):
                live["even_xy"], live["odd_y"] = flip(live["even_y"], X), flip(live[odd], Y)
            with jax.named_scope(FEATURES_ALONG):
                live["odd_x"] = flip(live["even_x"], Z)
            units = [live[even], live["even_x"]]
            if pair == 1:
                live["total"] = forward_step("joined", live.pop("units") + units, None)
            else:
                live["total"] = forward_step(("early", pair), units, live["total"])
        if not last:
            with jax.named_scope(FEATURES_ALONG):
                live[later] = flip(live[later - low_bit(later)], low_bit(later))
        close(*([] if last else [later]))

        if pair == 0:
            units = [live[even], live["even_x"], live["even_y"]]
            units += [live[odd], live["odd_x"], live["odd_y"]]
            with jax.named_scope(FEATURES_ACROSS):
                units += [flip(live["even_x"], Y), flip(live["odd_y"], X)]
            live["units"] = units
            build_own(panels // 2)
            live["one"] = build_others(0)
        else:
            with jax.named_scope(FEATURES_ACROSS):
                odd_xy = [flip(live["odd_y"][:half], X), flip(live["odd_x"][half:], Y)]
            live["units"] = [live["odd_x"], odd_xy]
            units = [live["even_y"], live[odd], live.pop("even_xy"), live["odd_y"]]
            live["total"] = forward_step(("more", pair), units, live["total"])
        for name in ("even_x", "even_y", "odd_x", "odd_y"):
            del live[name]
        close()
    partial = forward_step(
        ("late", pair_count - 1), live.pop("units"), live.get("total"), BF16
    )

    with jax.named_scope("partial_sums"):
        other = flip(partial, 0, 1)
        for bit in range(1, n_rep.bit_length() - 1):
            partial = (partial.astype(F32) + other.astype(F32)).astype(BF16)
            other = flip(partial, 0, 1 << bit)

    with jax.named_scope("middle"):
        depth = n_section // 4
        rows = (partial, other, weight, live["cot"])
        grad, top_diag, end_diag, term = middle(
            where, offsets["first", pair_count - 1], *rows, live["dense"], depth
        )

    live = {"grad": grad, "dense": live["dense"], "term": term}
    add = lambda *values: functools.reduce(jnp.add, [value.astype(F32) for value in values])

    sizes_of = {"mid": 3, "last": 4, "odd": 3, "even": 3}

    def backward_step(pair, *names):
        with jax.named_scope("backward"):
            counts = [sizes_of.get(name, 1 if pair else 2) for name in names]
            chunks = backward_part(
                where, offsets[names[0], pair], sum(counts), live["grad"], live["dense"]
            )
            for name, count in zip(names, counts):
                live[name], chunks = chunks[:count], chunks[count:]

    steps = ["z", X, Y, *(-(Z << bit) for bit in reversed(range(depth.bit_length() - 1)))]
    steps.append("cores")
    z_order = [0]

    def weight_step(after=None):
        if not steps:
            return
        step = steps.pop(0)
        if after:
            live[after], live["term"] = lax.optimization_barrier((live[after], live["term"]))
        term = live["term"]
        with jax.named_scope("weight_grad"):
            if step == "z":
                parts = [term[0], *(flip(term[n], Z * n) for n in range(1, depth))]
                live["term"] = add(*parts).astype(BF16)
            elif step == "cores":
                live["terms"] = [term, *(flip(term, 0, n) for n in range(1, n_rep))]
                del live["term"]
            elif step > 0:
                live["term"] = add(term, flip(term, step)).astype(BF16)
            else:
                term = term[None] if term.ndim == 2 else term
                live["term"] = jnp.concatenate([term, flip(term, -step)])
                z_order.extend([-step // Z ^ other for other in z_order])

    half = width // 2
    tops = lambda values: [value[:half] for value in values]
    ends = lambda values: [value[half:] for value in values]
    live["first"] = [top_diag, end_diag]
    for pair in reversed(range(pair_count)):
        even = 2 * pair * Z
        top = pair + 1 == pair_count
        if not top:
            mask = low_bit(even + 2 * Z)
            name = ("to", even + 2 * Z - mask, mask)

        with jax.named_scope(GRADS_ACROSS):
            if pair > 0:
                top_diag, end_diag = live.pop("first")
                live["top"], live["end"] = flip(top_diag, X), flip(end_diag, Y)
        if not top:
            with jax.named_scope(GRADS_ALONG):
                live[name] = [flip(live["passed"][0], mask)]
        backward_step(pair, "even" if pair == 0 else "mid")
        weight_step(None if top else "even" if pair == 0 else "mid")
        with jax.named_scope(GRADS_ACROSS):
            if pair == 0:
                to_x, to_y, own = live.pop("odd")
                live["odd"], live["ahead"] = [to_x, own], flip(to_y, Y)
            else:
                even_xy, *live["mid"] = live["mid"]
                live["ahead"] = flip(even_xy, X)
        close("ahead")

        if pair == 0:
            with jax.named_scope(GRADS_ACROSS):
                to_x, own = live.pop("odd")
                to_x = add(to_x, live.pop("o_diag")).astype(BF16)
                live["odd_sum"] = [own, flip(to_x, X), live.pop("ahead")]
                to_x, to_y, own = live.pop("even")
                to_y = add(to_y, live.pop("e_diag")).astype(BF16)
                live["sums"] = [own, flip(to_x, X), flip(to_y, Y)]
        else:
            with jax.named_scope(GRADS_ACROSS):
                odd_y, odd_x = live.pop("mid")
                live["to_y"] = live.pop("ahead")
                odd_y, odd_x = add_diagonals(
                    odd_y, odd_x, live.pop("top"), live.pop("end")
                )
                live["to_odd"] = flip(odd_y, Y)
            with jax.named_scope(GRADS_ALONG):
                live["to_x"] = flip(odd_x, Z)
            backward_step(pair, "last")
        if not top:
            with jax.named_scope(GRADS_ALONG):
                live[name].append(flip(live.pop("passed")[1], mask))
        weight_step("last" if pair else None)
        close(*([] if pair else ["sums"]))

        if pair == 0:
            sums = live["sums"]
            with jax.named_scope(GRADS_ALONG):
                sums.append(flip(add(*live.pop("odd_sum")).astype(BF16), Z))
            with jax.named_scope("activated"):
                live["activated"] = activated_rows(where, *rows, n_rep)
        else:
            to_x, to_y, odd, own = live.pop("last")
            with jax.named_scope(GRADS_ACROSS):
                to_x = add(to_x, live.pop("to_x")).astype(BF16)
                to_y = add(to_y, live.pop("to_y")).astype(BF16)
                sums = [own, flip(to_x, X), flip(to_y, Y)]
            with jax.named_scope(GRADS_ALONG):
                sums.append(flip(add(odd, live.pop("to_odd")).astype(BF16), Z))
            backward_step(pair - 1, "first", *([] if pair > 1 else ["odd"]))
        live["sums"] = sums
        weight_step("first" if pair else None)
        if pair == 1:
            with jax.named_scope(GRADS_ACROSS):
                odd_diag, even_diag = live.pop("first")
                live["o_diag"], live["e_diag"] = flip(odd_diag, Y), flip(even_diag, X)
        close("o_diag", "e_diag")
        sums = live.pop("sums")
        halves = [live.pop(key) for key in list(live) if isinstance(key, tuple) and key[1] == even]
        if pair > 0:
            live["passed"] = [
                add(*tops(sums), *(value[0] for value in halves)).astype(BF16),
                add(*ends(sums), *(value[1] for value in halves)).astype(BF16),
            ]
        if pair > 1:
            (chunk,) = live["first"]
            live["first"] = [chunk[:half], chunk[half:]]
    with jax.named_scope("grads_out"):
        feat_grad, weight_grad = final_sum(where, sums, halves, live["terms"], tuple(z_order))
    return (live["activated"], feat_grad, weight_grad)


def solution(mesh):
    placed = (
        P("section", None),
        P(),
        P("section", "rep", None, None, None),
        P("section", "rep", None),
        P("section", "rep", None),
        P("section", "rep"),
        P(("section", "rep"), None),
    )
    sizes = (mesh.shape["section"], mesh.shape["rep"])
    return jax.shard_map(
        functools.partial(shards, sizes),
        mesh=mesh,
        in_specs=placed,
        out_specs=(P(("section", "rep"), None), P("rep", "section", None), P()),
        check_vma=False,
    )
```

```python
import functools

import jax
import jax.numpy as jnp
from jax import lax
from jax.experimental import pallas as pl
from jax.experimental.pallas import tpu as pltpu
from jax.sharding import PartitionSpec as P

BF16 = jnp.bfloat16
F32 = jnp.float32
BOTH = ("section", "rep")
FEATURES_ACROSS, FEATURES_ALONG = "features_xy", "features_z"
GRADS_ACROSS, GRADS_ALONG = "grads_xy", "grads_z"


def in_hbm(value):
    return pltpu.with_memory_space_constraint(value, pltpu.HBM)


def tile_place(place, row_tiles, per_part):
    row_bits, part_bits = row_tiles.bit_length() - 1, per_part.bit_length() - 1
    tile_col = place & (row_tiles - 1)
    return place >> row_bits, tile_col >> part_bits, tile_col & (per_part - 1)


def dense_kernel(first, where_ref, packed_ref, tiles_ref, *refs):
    out_ref = refs[-1]
    panel = first + pl.program_id(0)
    size, slots = tiles_ref.shape[-1], tiles_ref.shape[1]
    row_tiles, per_part = out_ref.shape[2] // size, out_ref.shape[3] // size
    out_ref[...] = jnp.zeros_like(out_ref)

    def add_tile(slot, carry):
        row, part, col = tile_place(packed_ref[panel, slot], row_tiles, per_part)
        rows = pl.ds(pl.multiple_of(row * size, size), size)
        cols = pl.ds(pl.multiple_of(col * size, size), size)
        out_ref[part, 0, rows, cols] += tiles_ref[0, slot]
        return carry

    lax.fori_loop(0, packed_ref[panel, slots], add_tile, 0)


def make_dense(first, before, where, tiles, packed, block_rows, n_rep):
    panels, slots, size, _ = tiles.shape
    half = panels // 2
    part = block_rows // n_rep
    at = lambda p: first + p
    return pl.pallas_call(
        functools.partial(dense_kernel, first),
        out_shape=pltpu.HBM((n_rep, panels, block_rows, part), BF16),
        grid_spec=pltpu.PrefetchScalarGridSpec(
            num_scalar_prefetch=2,
            grid=(half,),
            in_specs=[pl.BlockSpec((1, slots, size, size), lambda p, *_: (at(p), 0, 0, 0))]
            + [pl.BlockSpec(memory_space=pl.ANY)] * (first > 0),
            out_specs=pl.BlockSpec((n_rep, 1, block_rows, part), lambda p, *_: (0, at(p), 0, 0)),
        ),
        input_output_aliases={3: 0} if first else {},
        compiler_params=pltpu.CompilerParams(vmem_limit_bytes=24 * 2**20),
        cost_estimate=pl.CostEstimate(
            flops=0,
            transcendentals=0,
            bytes_accessed=tiles.size // 8,
        ),
    )(where, packed, in_hbm(tiles), *([in_hbm(before)] if first else []))


def other_kernel(first, where_ref, packed_ref, tiles_ref, out_ref):
    panel = first + pl.program_id(0)
    size, slots = tiles_ref.shape[-1], tiles_ref.shape[1]
    row_tiles, per_part = out_ref.shape[1] // size, out_ref.shape[2] // size
    out_ref[...] = jnp.zeros_like(out_ref)

    def add_tile(slot, carry):
        row, part, col = tile_place(packed_ref[panel, slot], row_tiles, per_part)
        rows = pl.ds(pl.multiple_of(row * size, size), size)
        cols = pl.ds(pl.multiple_of(col * size, size), size)

        @pl.when(part == where_ref[0])
        def _():
            out_ref[0, rows, cols] += tiles_ref[0, slot]

        return carry

    lax.fori_loop(0, packed_ref[panel, slots], add_tile, 0)


def make_other(first, where, tiles, packed, block_rows, n_rep):
    panels, slots, size, _ = tiles.shape
    half = panels // 2
    part = block_rows // n_rep
    return pl.pallas_call(
        functools.partial(other_kernel, first),
        out_shape=pltpu.HBM((half, block_rows, part), BF16),
        grid_spec=pltpu.PrefetchScalarGridSpec(
            num_scalar_prefetch=2,
            grid=(half,),
            in_specs=[pl.BlockSpec((1, slots, size, size), lambda p, *_: (first + p, 0, 0, 0))],
            out_specs=pl.BlockSpec((1, block_rows, part), lambda p, *_: (p, 0, 0)),
        ),
        compiler_params=pltpu.CompilerParams(vmem_limit_bytes=24 * 2**20),
        cost_estimate=pl.CostEstimate(
            flops=0, transcendentals=0, bytes_accessed=tiles.size // 8
        ),
    )(where, packed, tiles)


def forward_kernel(offset, n_pieces, n_others, has_total, where_ref, dense_ref, *refs):
    others, refs = refs[:n_others], refs[n_others:]
    units = []
    for pieces in n_pieces:
        tops, refs = refs[:pieces], refs[pieces:]
        half = tops[0].shape[0] // (2 if pieces == 1 else 1)
        units.append([tops[0].at[pl.ds(0, half)], tops[-1].at[pl.ds(half * (2 - pieces), half)]])
    n_units = len(units)
    total_ref, refs = (refs[0], refs[1:]) if has_total else (None, refs)
    out_ref, sum_ref, a_buf, u_buf, sems, sum_sem = refs
    _, panels, _, part = dense_ref.shape
    some = others[0].shape[0]
    rep = where_ref[0]

    def a_copy(source, slot, side):
        target = a_buf.at[slot, :, pl.ds(side * part, part)]
        return pltpu.make_async_copy(source, target, sems.at[0, slot, side])

    def u_copy(source, slot, side, piece):
        half = part // 2
        target = u_buf.at[slot, pl.ds(side * part + piece * half, half), :]
        return pltpu.make_async_copy(source, target, sems.at[1 + piece, slot, side])

    def fetch(pair, slot):
        for side in range(2):
            place = where_ref[offset + 2 * pair + side]
            owner, panel = place // panels, place % panels
            turn = ((owner ^ rep) - 1) * (panels // some) + panel // some

            @pl.when(owner == rep)
            def _():
                a_copy(dense_ref.at[rep, panel], slot, side).start()

            for number, other_ref in enumerate(others):

                @pl.when((owner != rep) & (turn == number))
                def _():
                    a_copy(other_ref.at[panel % some], slot, side).start()

            for number in range(side, n_units, 2):

                @pl.when(pair == number // 2)
                def _():
                    for piece in range(2):
                        u_copy(units[number][piece], slot, side, piece).start()

    pairs = n_units // 2
    fetch(0, 0)
    if has_total:
        load = pltpu.make_async_copy(total_ref, sum_ref, sum_sem)
        load.start()
        load.wait()
    else:
        sum_ref[...] = jnp.zeros_like(sum_ref)

    def step(pair, carry):
        slot = pair % 2

        @pl.when(pair + 1 < pairs)
        def _():
            fetch(pair + 1, 1 - slot)

        for side in range(2):
            a_copy(dense_ref.at[0, 0], slot, side).wait()
            for piece in range(2):
                u_copy(units[0][piece], slot, side, piece).wait()
        sum_ref[...] += jnp.dot(a_buf[slot], u_buf[slot], preferred_element_type=F32)
        return carry

    lax.fori_loop(0, pairs, step, 0)
    if out_ref.dtype == F32:
        store = pltpu.make_async_copy(sum_ref, out_ref, sum_sem)
        store.start()
        store.wait()
    else:
        out_ref[...] = sum_ref[...].astype(out_ref.dtype)


def forward_part(where, offset, units, total, dense, others, kind):
    _, _, rows, part = dense.shape
    width = units[0].shape[1]
    n_pieces = [len(unit) if isinstance(unit, list) else 1 for unit in units]
    pieces = [piece for unit in units for piece in (unit if isinstance(unit, list) else [unit])]
    near = pl.BlockSpec(memory_space=pl.ANY)
    hbm = pl.BlockSpec(memory_space=pltpu.HBM)
    has_total = total is not None
    n_units, n_others = len(units), len(others)
    return pl.pallas_call(
        functools.partial(forward_kernel, offset, n_pieces, n_others, has_total),
        out_shape=jax.ShapeDtypeStruct((rows, width), kind),
        grid_spec=pltpu.PrefetchScalarGridSpec(
            num_scalar_prefetch=1,
            grid=(1,),
            in_specs=[hbm] * (1 + n_others) + [near] * (len(pieces) + has_total),
            out_specs=near if kind == F32 else pl.BlockSpec((rows, width), lambda i, where: (0, 0)),
            scratch_shapes=[
                pltpu.VMEM((rows, width), F32),
                pltpu.VMEM((2, rows, 2 * part), BF16),
                pltpu.VMEM((2, 2 * part, width), BF16),
                pltpu.SemaphoreType.DMA((3, 2, 2)),
                pltpu.SemaphoreType.DMA,
            ],
        ),
        compiler_params=pltpu.CompilerParams(vmem_limit_bytes=24 * 2**20),
        cost_estimate=pl.CostEstimate(
            flops=2 * n_units * rows * part * width,
            transcendentals=0,
            bytes_accessed=n_units * rows * part * 2 + 8 * rows * width,
        ),
    )(where, in_hbm(dense), *map(in_hbm, others), *pieces, *([total] if has_total else []))


def slopes(mine_ref, other_ref, weight_ref, cot_ref):
    agg = (mine_ref[...].astype(F32) + other_ref[...].astype(F32)).astype(BF16)
    pre = jnp.dot(agg, weight_ref[...], preferred_element_type=F32)
    sigma = 0.5 * jnp.tanh(0.5 * pre) + 0.5
    slope = cot_ref[...].astype(F32) * sigma * (1.0 + pre * (1.0 - sigma))
    return agg, (pre * sigma).astype(BF16), slope.astype(BF16)


def middle_kernel(blocks, where_ref, mine_ref, other_ref, weight_ref, cot_ref, a_ref, *refs):
    grad_ref, top_ref, end_ref, term_ref, sum_ref, full_ref = refs
    step = pl.program_id(0)
    part = mine_ref.shape[0]

    @pl.when(step < blocks)
    def _():
        agg, _, pre_grad = slopes(mine_ref, other_ref, weight_ref, cot_ref)
        grad = lax.dot_general(
            weight_ref[...], pre_grad, (((1,), (1,)), ((), ())), preferred_element_type=F32
        ).astype(BF16)
        grad_ref[...] = grad
        full_ref[:, pl.ds(pl.multiple_of(step * part, part), part)] = grad
        term = lax.dot_general(agg, pre_grad, (((0,), (0,)), ((), ())), preferred_element_type=F32)

        @pl.when(step == 0)
        def _():
            sum_ref[...] = term

        @pl.when(step > 0)
        def _():
            sum_ref[...] += term

    @pl.when(step == blocks)
    def _():
        chunk = jnp.dot(full_ref[...], a_ref[0, 0], preferred_element_type=F32).astype(BF16)
        half = top_ref.shape[0]
        top_ref[...] = chunk[:half]
        end_ref[...] = chunk[half:]
        depth, size, _ = term_ref.shape
        z = where_ref[1] // 4
        for number in range(depth):
            start = (where_ref[0] * depth + (z ^ number)) * size
            rows = sum_ref[pl.ds(pl.multiple_of(start, size), size), :]
            term_ref[number] = rows.astype(BF16)


def middle(where, offset, mine, other, weight, cotangent, dense, depth):
    rows, width = mine.shape
    n_rep, _, _, cols = dense.shape
    blocks = 4
    part = rows // blocks
    size = width // n_rep // depth
    block = pl.BlockSpec((part, width), lambda i, where: (jnp.minimum(i, blocks - 1), 0))
    fixed = lambda *shape: pl.BlockSpec(shape, lambda i, where: (0,) * len(shape))
    half = width // 2
    shapes = [(width, rows), (half, cols), (half, cols), (depth, size, width)]

    def a_block(i, where):
        place = where[offset]
        return (place % n_rep, place // n_rep, 0, 0)

    return pl.pallas_call(
        functools.partial(middle_kernel, blocks),
        out_shape=[jax.ShapeDtypeStruct(shape, BF16) for shape in shapes],
        grid_spec=pltpu.PrefetchScalarGridSpec(
            num_scalar_prefetch=1,
            grid=(blocks + 1,),
            in_specs=[
                block,
                block,
                fixed(width, width),
                block,
                pl.BlockSpec((1, 1, rows, cols), a_block),
            ],
            out_specs=[
                pl.BlockSpec((width, part), lambda i, where: (0, jnp.minimum(i, blocks - 1))),
                *(fixed(*shape) for shape in shapes[1:]),
            ],
            scratch_shapes=[pltpu.VMEM((width, width), F32), pltpu.VMEM((width, rows), BF16)],
        ),
        compiler_params=pltpu.CompilerParams(vmem_limit_bytes=24 * 2**20),
        cost_estimate=pl.CostEstimate(
            flops=6 * rows * width * width + 4 * rows * width * cols,
            transcendentals=rows * width,
            bytes_accessed=rows * width * 12,
        ),
    )(where, mine, other, weight, cotangent, in_hbm(dense))


def activated_kernel(where_ref, mine_ref, other_ref, weight_ref, cot_ref, act_ref):
    act_ref[...] = slopes(mine_ref, other_ref, weight_ref, cot_ref)[1]


def activated_rows(where, mine, other, weight, cotangent, n_rep):
    rows, width = mine.shape
    part = rows // n_rep
    block = pl.BlockSpec((part, width), lambda i, where: (where[0], 0))
    fixed = lambda *shape: pl.BlockSpec(shape, lambda i, where: (0, 0))
    return pl.pallas_call(
        activated_kernel,
        out_shape=jax.ShapeDtypeStruct((part, width), BF16),
        grid_spec=pltpu.PrefetchScalarGridSpec(
            num_scalar_prefetch=1,
            grid=(1,),
            in_specs=[block, block, fixed(width, width), block],
            out_specs=fixed(part, width),
        ),
        compiler_params=pltpu.CompilerParams(vmem_limit_bytes=24 * 2**20),
        cost_estimate=pl.CostEstimate(
            flops=2 * part * width * width,
            transcendentals=part * width,
            bytes_accessed=part * width * 8,
        ),
    )(where, mine, other, weight, cotangent)


def backward_kernel(where_ref, grad_ref, a_ref, *out_refs):
    chunk = jnp.dot(grad_ref[...], a_ref[0, 0], preferred_element_type=F32).astype(BF16)
    for number, out_ref in enumerate(out_refs):

        @pl.when(pl.program_id(0) == number)
        def _():
            out_ref[...] = chunk


def backward_part(where, offset, count, grad, dense):
    width, rows = grad.shape
    n_rep, _, _, cols = dense.shape
    fixed = lambda *shape: pl.BlockSpec(shape, lambda i, where: (0, 0))

    def a_block(i, where):
        place = where[offset + i]
        return (place % n_rep, place // n_rep, 0, 0)

    return pl.pallas_call(
        backward_kernel,
        out_shape=[jax.ShapeDtypeStruct((width, cols), BF16)] * count,
        grid_spec=pltpu.PrefetchScalarGridSpec(
            num_scalar_prefetch=1,
            grid=(count,),
            in_specs=[fixed(width, rows), pl.BlockSpec((1, 1, rows, cols), a_block)],
            out_specs=[fixed(width, cols)] * count,
        ),
        compiler_params=pltpu.CompilerParams(vmem_limit_bytes=24 * 2**20),
        cost_estimate=pl.CostEstimate(
            flops=2 * count * rows * width * cols,
            transcendentals=0,
            bytes_accessed=2 * count * rows * cols + 2 * count * width * cols + 2 * width * rows,
        ),
    )(where, grad, in_hbm(dense))


def diagonals_kernel(y_ref, x_ref, top_ref, end_ref, y_out, x_out):
    half = top_ref.shape[0]
    y_out[:half] = (y_ref[:half].astype(F32) + top_ref[...].astype(F32)).astype(BF16)
    y_out[half:] = y_ref[half:]
    x_out[:half] = x_ref[:half]
    x_out[half:] = (x_ref[half:].astype(F32) + end_ref[...].astype(F32)).astype(BF16)


def add_diagonals(odd_y, odd_x, top, end):
    return pl.pallas_call(
        diagonals_kernel,
        out_shape=[jax.ShapeDtypeStruct(odd_y.shape, BF16)] * 2,
        compiler_params=pltpu.CompilerParams(vmem_limit_bytes=24 * 2**20),
        cost_estimate=pl.CostEstimate(
            flops=odd_y.size, transcendentals=0, bytes_accessed=10 * odd_y.size
        ),
    )(odd_y, odd_x, top, end)


def final_kernel(n_parts, n_halves, z_order, where_ref, *refs):
    parts, terms = refs[:n_parts], refs[n_parts + n_halves : -2]
    halves = refs[n_parts : n_parts + n_halves]
    out_ref, weight_out = refs[-2:]
    values = [part[...].astype(F32) for part in parts]
    for top, end in zip(halves[::2], halves[1::2]):
        values.append(jnp.concatenate([top[...].astype(F32), end[...].astype(F32)]))
    total = functools.reduce(jnp.add, values)
    out_ref[0] = total.T.astype(BF16)
    depth, size, _ = terms[0].shape
    for other, term_ref in enumerate(terms):
        for number, offset in enumerate(z_order):
            place = (where_ref[0] ^ other) * depth + ((where_ref[1] // 4) ^ offset)
            rows = pl.ds(pl.multiple_of(place * size, size), size)
            weight_out[rows, :] = term_ref[number].astype(F32)


def final_sum(where, parts, halves, terms, z_order):
    width, cols = parts[0].shape
    halves = [half for pair in halves for half in pair]
    whole = lambda value: pl.BlockSpec(value.shape, lambda i, where: (0,) * value.ndim)
    outs = [
        jax.ShapeDtypeStruct((1, cols, width), BF16),
        jax.ShapeDtypeStruct((width, width), F32),
    ]
    return pl.pallas_call(
        functools.partial(final_kernel, len(parts), len(halves), z_order),
        out_shape=outs,
        grid_spec=pltpu.PrefetchScalarGridSpec(
            num_scalar_prefetch=1,
            grid=(1,),
            in_specs=[whole(value) for value in [*parts, *halves, *terms]],
            out_specs=[whole(value) for value in outs],
        ),
        compiler_params=pltpu.CompilerParams(vmem_limit_bytes=24 * 2**20),
        cost_estimate=pl.CostEstimate(
            flops=len(parts) * width * cols,
            transcendentals=0,
            bytes_accessed=2 * (len(parts) + 1) * width * cols,
        ),
    )(where, *parts, *halves, *terms)


def shards(sizes, features, weight, tile_values, tile_rows, tile_cols, tile_count, cotangent):
    n_section, n_rep = sizes
    block_rows, width = features.shape
    part = block_rows // n_rep
    section, rep = lax.axis_index("section"), lax.axis_index("rep")

    X, Y, Z = 1, 2, 4
    pair_count = n_section // 8
    low_bit = lambda mask: mask & -mask

    def flip(value, mask, rep_mask=0):
        pairs = [
            (s * n_rep + r, (s ^ mask) * n_rep + (r ^ rep_mask))
            for s in range(n_section)
            for r in range(n_rep)
        ]
        return lax.ppermute(value, BOTH, pairs)

    def gather_rep(value):
        held = [value] + [flip(value, 0, other) for other in range(1, n_rep)]
        order = rep ^ jnp.arange(n_rep)
        if n_rep == 2:
            held = [jnp.where(rep == 0, held[0], held[1]), jnp.where(rep == 0, held[1], held[0])]
            return jnp.concatenate(held)
        return jnp.stack(held)[order].reshape(-1, width)

    live = {}

    def close(*open_names):
        names = [name for name in live if name not in open_names]
        live.update(zip(names, lax.optimization_barrier([live[name] for name in names])))

    masks, offsets = [], {}

    def plan(name, wanted):
        offsets[name] = 2 + len(masks)
        masks.extend(wanted)

    for pair in range(pair_count):
        even, odd = 2 * pair * Z, (2 * pair + 1) * Z
        plan(("early", pair), [even, even + X])
        plan(("more", pair), [even + Y, odd, even + X + Y, odd + Y])
        plan(("late", pair), [odd + X, odd + X + Y])
        if pair == 0:
            plan(("first", pair), [odd + X + Y, even + X + Y])
            plan(("odd", pair), [odd + X, odd + Y, odd])
        else:
            plan(("first", pair), [odd + X + Y])
            plan(("mid", pair), [even + X + Y, odd + Y, odd + X])
            more = [X, Y, 0] if pair == 1 else []
            plan(("last", pair), [even + X, even + Y, odd, even, *more])
    offsets["joined"] = 2 + len(masks)
    masks += [0, X, Y, Z, Z + X, Z + Y, X + Y, Z + X + Y, 2 * Z, 2 * Z + X]
    where = jnp.concatenate(
        [rep[None], section[None], section ^ jnp.array(masks, jnp.int32)]
    ).astype(jnp.int32)

    def forward_step(names, units, total, kind=F32):
        with jax.named_scope("forward"):
            return forward_part(
                where, offsets[names], units, total, live["dense"], live["others"], kind
            )

    row_tiles = block_rows // tile_values.shape[3]
    packed = jnp.concatenate(
        [tile_rows[0] * row_tiles + tile_cols[0], tile_count[0][:, None]], axis=1
    )
    panels = tile_values.shape[1]
    def build_own(first):
        with jax.named_scope("dense_blocks"):
            live["dense"] = make_dense(
                first, live.get("dense"), where, tile_values[0], packed, block_rows, n_rep
            )

    def build_others(first):
        with jax.named_scope("other_blocks"):
            return [make_other(first, where, *sent, block_rows, n_rep) for sent in live["tiles"]]

    live[0] = lax.dynamic_slice_in_dim(features, rep * part, part, axis=0)
    with jax.named_scope("tiles_exchange"):
        live["tiles"] = [
            (flip(tile_values[0], 0, n), flip(packed, 0, n)) for n in range(1, n_rep)
        ]
    half = part // 2
    for pair in range(pair_count):
        even, odd = 2 * pair * Z, (2 * pair + 1) * Z
        later = even + 2 * Z
        last = pair + 1 == pair_count

        with jax.named_scope(FEATURES_ACROSS):
            live["even_x"], live["even_y"] = flip(live[even], X), flip(live[even], Y)
        with jax.named_scope(FEATURES_ALONG):
            live[odd] = flip(live[even], Z)
        if pair == 0:
            build_own(0)
        if pair == 1:
            two = build_others(panels // 2)
            live["others"] = [side for sides in zip(live.pop("one"), two) for side in sides]
            del live["tiles"]
            with jax.named_scope("cotangents"):
                live["cot"] = gather_rep(cotangent)
        if pair > 1:
            live["total"] = forward_step(("late", pair - 1), live.pop("units"), live["total"])
        close(*(["even_x", "even_y"] if pair == 0 else []))

        if pair == 0:
            with jax.named_scope(FEATURES_ACROSS):
                live["odd_x"], live["odd_y"] = flip(live[odd], X), flip(live[odd], Y)
        else:
            with jax.named_scope(FEATURES_ACROSS):
                live["even_xy"], live["odd_y"] = flip(live["even_y"], X), flip(live[odd], Y)
            with jax.named_scope(FEATURES_ALONG):
                live["odd_x"] = flip(live["even_x"], Z)
            units = [live[even], live["even_x"]]
            if pair == 1:
                live["total"] = forward_step("joined", live.pop("units") + units, None)
            else:
                live["total"] = forward_step(("early", pair), units, live["total"])
        if not last:
            with jax.named_scope(FEATURES_ALONG):
                live[later] = flip(live[later - low_bit(later)], low_bit(later))
        close(*([] if last else [later]))

        if pair == 0:
            units = [live[even], live["even_x"], live["even_y"]]
            units += [live[odd], live["odd_x"], live["odd_y"]]
            with jax.named_scope(FEATURES_ACROSS):
                units += [flip(live["even_x"], Y), flip(live["odd_y"], X)]
            live["units"] = units
            build_own(panels // 2)
            live["one"] = build_others(0)
        else:
            with jax.named_scope(FEATURES_ACROSS):
                odd_xy = [flip(live["odd_y"][:half], X), flip(live["odd_x"][half:], Y)]
            live["units"] = [live["odd_x"], odd_xy]
            units = [live["even_y"], live[odd], live.pop("even_xy"), live["odd_y"]]
            live["total"] = forward_step(("more", pair), units, live["total"])
        for name in ("even_x", "even_y", "odd_x", "odd_y"):
            del live[name]
        close()
    partial = forward_step(
        ("late", pair_count - 1), live.pop("units"), live.get("total"), BF16
    )

    with jax.named_scope("partial_sums"):
        other = flip(partial, 0, 1)
        for bit in range(1, n_rep.bit_length() - 1):
            partial = (partial.astype(F32) + other.astype(F32)).astype(BF16)
            other = flip(partial, 0, 1 << bit)

    with jax.named_scope("middle"):
        depth = n_section // 4
        rows = (partial, other, weight, live["cot"])
        grad, top_diag, end_diag, term = middle(
            where, offsets["first", pair_count - 1], *rows, live["dense"], depth
        )

    live = {"grad": grad, "dense": live["dense"], "term": term}
    add = lambda *values: functools.reduce(jnp.add, [value.astype(F32) for value in values])

    sizes_of = {"mid": 3, "last": 4, "odd": 3, "even": 3}

    def backward_step(pair, *names):
        with jax.named_scope("backward"):
            counts = [sizes_of.get(name, 1 if pair else 2) for name in names]
            chunks = backward_part(
                where, offsets[names[0], pair], sum(counts), live["grad"], live["dense"]
            )
            for name, count in zip(names, counts):
                live[name], chunks = chunks[:count], chunks[count:]

    back = [-(Z << bit) for bit in reversed(range(depth.bit_length() - 1))]
    steps = [["z"], [X], [], [Y, back[0]], *([step] for step in back[1:]), ["cores"]]
    z_order = [0]

    def weight_step(after=None):
        todo = steps.pop(0) if steps else []
        if after and todo:
            live[after], live["term"] = lax.optimization_barrier((live[after], live["term"]))
        for step in todo:
            with jax.named_scope("weight_grad"):
                one_step(step, live["term"])

    def one_step(step, term):
        if step == "z":
            parts = [term[0], *(flip(term[n], Z * n) for n in range(1, depth))]
            live["term"] = add(*parts).astype(BF16)
        elif step == "cores":
            live["terms"] = [term, *(flip(term, 0, n) for n in range(1, n_rep))]
            del live["term"]
        elif step > 0:
            live["term"] = add(term, flip(term, step)).astype(BF16)
        else:
            term = term[None] if term.ndim == 2 else term
            live["term"] = jnp.concatenate([term, flip(term, -step)])
            z_order.extend([-step // Z ^ other for other in z_order])

    half = width // 2
    tops = lambda values: [value[:half] for value in values]
    ends = lambda values: [value[half:] for value in values]
    live["first"] = [top_diag, end_diag]
    for pair in reversed(range(pair_count)):
        even = 2 * pair * Z
        top = pair + 1 == pair_count
        if not top:
            mask = low_bit(even + 2 * Z)
            name = ("to", even + 2 * Z - mask, mask)

        with jax.named_scope(GRADS_ACROSS):
            if pair > 0:
                top_diag, end_diag = live.pop("first")
                live["top"], live["end"] = flip(top_diag, X), flip(end_diag, Y)
        if not top:
            with jax.named_scope(GRADS_ALONG):
                live[name] = [flip(live["passed"][0], mask)]
        if pair > 0:
            backward_step(pair, "mid")
        weight_step(None if top or pair == 0 else "mid")
        with jax.named_scope(GRADS_ACROSS):
            if pair == 0:
                to_x, to_y, own = live.pop("odd")
                live["odd"], live["ahead"] = [to_x, own], flip(to_y, Y)
            else:
                even_xy, *live["mid"] = live["mid"]
                live["ahead"] = flip(even_xy, X)
        close("ahead")

        if pair == 0:
            with jax.named_scope(GRADS_ACROSS):
                to_x, own = live.pop("odd")
                to_x = add(to_x, live.pop("o_diag")).astype(BF16)
                live["odd_sum"] = [own, flip(to_x, X), live.pop("ahead")]
                to_x, to_y, own = live.pop("even")
                to_y = add(to_y, live.pop("e_diag")).astype(BF16)
                live["sums"] = [own, flip(to_x, X), flip(to_y, Y)]
        else:
            with jax.named_scope(GRADS_ACROSS):
                odd_y, odd_x = live.pop("mid")
                live["to_y"] = live.pop("ahead")
                odd_y, odd_x = add_diagonals(
                    odd_y, odd_x, live.pop("top"), live.pop("end")
                )
                live["to_odd"] = flip(odd_y, Y)
            with jax.named_scope(GRADS_ALONG):
                live["to_x"] = flip(odd_x, Z)
            backward_step(pair, "last", *(["even"] if pair == 1 else []))
        if not top:
            with jax.named_scope(GRADS_ALONG):
                live[name].append(flip(live.pop("passed")[1], mask))
        weight_step("last" if pair else None)
        close(*([] if pair else ["sums"]))

        if pair == 0:
            sums = live["sums"]
            with jax.named_scope(GRADS_ALONG):
                sums.append(flip(add(*live.pop("odd_sum")).astype(BF16), Z))
            with jax.named_scope("activated"):
                live["activated"] = activated_rows(where, *rows, n_rep)
        else:
            to_x, to_y, odd, own = live.pop("last")
            with jax.named_scope(GRADS_ACROSS):
                to_x = add(to_x, live.pop("to_x")).astype(BF16)
                to_y = add(to_y, live.pop("to_y")).astype(BF16)
                sums = [own, flip(to_x, X), flip(to_y, Y)]
            with jax.named_scope(GRADS_ALONG):
                sums.append(flip(add(odd, live.pop("to_odd")).astype(BF16), Z))
            backward_step(pair - 1, "first", *([] if pair > 1 else ["odd"]))
        live["sums"] = sums
        weight_step("first" if pair else None)
        if pair == 1:
            with jax.named_scope(GRADS_ACROSS):
                odd_diag, even_diag = live.pop("first")
                live["o_diag"], live["e_diag"] = flip(odd_diag, Y), flip(even_diag, X)
        close("o_diag", "e_diag")
        sums = live.pop("sums")
        halves = [live.pop(key) for key in list(live) if isinstance(key, tuple) and key[1] == even]
        if pair > 0:
            live["passed"] = [
                add(*tops(sums), *(value[0] for value in halves)).astype(BF16),
                add(*ends(sums), *(value[1] for value in halves)).astype(BF16),
            ]
        if pair > 1:
            (chunk,) = live["first"]
            live["first"] = [chunk[:half], chunk[half:]]
    with jax.named_scope("grads_out"):
        feat_grad, weight_grad = final_sum(where, sums, halves, live["terms"], tuple(z_order))
    return (live["activated"], feat_grad, weight_grad)


def solution(mesh):
    placed = (
        P("section", None),
        P(),
        P("section", "rep", None, None, None),
        P("section", "rep", None),
        P("section", "rep", None),
        P("section", "rep"),
        P(("section", "rep"), None),
    )
    sizes = (mesh.shape["section"], mesh.shape["rep"])
    return jax.shard_map(
        functools.partial(shards, sizes),
        mesh=mesh,
        in_specs=placed,
        out_specs=(P(("section", "rep"), None), P("rep", "section", None), P()),
        check_vma=False,
    )
```

```python
import functools

import jax
import jax.numpy as jnp
from jax import lax
from jax.experimental import pallas as pl
from jax.experimental.pallas import tpu as pltpu
from jax.sharding import PartitionSpec as P

BF16 = jnp.bfloat16
F32 = jnp.float32
BOTH = ("section", "rep")
FEATURES_ACROSS, FEATURES_ALONG = "features_xy", "features_z"
GRADS_ACROSS, GRADS_ALONG = "grads_xy", "grads_z"


def in_hbm(value):
    return pltpu.with_memory_space_constraint(value, pltpu.HBM)


def tile_place(place, row_tiles, per_part):
    row_bits, part_bits = row_tiles.bit_length() - 1, per_part.bit_length() - 1
    tile_col = place & (row_tiles - 1)
    return place >> row_bits, tile_col >> part_bits, tile_col & (per_part - 1)


def dense_kernel(first, where_ref, packed_ref, tiles_ref, *refs):
    out_ref = refs[-1]
    panel = first + pl.program_id(0)
    size, slots = tiles_ref.shape[-1], tiles_ref.shape[1]
    row_tiles, per_part = out_ref.shape[2] // size, out_ref.shape[3] // size
    out_ref[...] = jnp.zeros_like(out_ref)

    def add_tile(slot, carry):
        row, part, col = tile_place(packed_ref[panel, slot], row_tiles, per_part)
        rows = pl.ds(pl.multiple_of(row * size, size), size)
        cols = pl.ds(pl.multiple_of(col * size, size), size)
        out_ref[part, 0, rows, cols] += tiles_ref[0, slot]
        return carry

    lax.fori_loop(0, packed_ref[panel, slots], add_tile, 0)


def make_dense(first, before, where, tiles, packed, block_rows, n_rep):
    panels, slots, size, _ = tiles.shape
    half = panels // 2
    part = block_rows // n_rep
    at = lambda p: first + p
    return pl.pallas_call(
        functools.partial(dense_kernel, first),
        out_shape=pltpu.HBM((n_rep, panels, block_rows, part), BF16),
        grid_spec=pltpu.PrefetchScalarGridSpec(
            num_scalar_prefetch=2,
            grid=(half,),
            in_specs=[pl.BlockSpec((1, slots, size, size), lambda p, *_: (at(p), 0, 0, 0))]
            + [pl.BlockSpec(memory_space=pl.ANY)] * (first > 0),
            out_specs=pl.BlockSpec((n_rep, 1, block_rows, part), lambda p, *_: (0, at(p), 0, 0)),
        ),
        input_output_aliases={3: 0} if first else {},
        compiler_params=pltpu.CompilerParams(vmem_limit_bytes=24 * 2**20),
        cost_estimate=pl.CostEstimate(
            flops=0,
            transcendentals=0,
            bytes_accessed=tiles.size // 8,
        ),
    )(where, packed, in_hbm(tiles), *([in_hbm(before)] if first else []))


def other_kernel(first, where_ref, packed_ref, tiles_ref, out_ref):
    panel = first + pl.program_id(0)
    size, slots = tiles_ref.shape[-1], tiles_ref.shape[1]
    row_tiles, per_part = out_ref.shape[1] // size, out_ref.shape[2] // size
    out_ref[...] = jnp.zeros_like(out_ref)

    def add_tile(slot, carry):
        row, part, col = tile_place(packed_ref[panel, slot], row_tiles, per_part)
        rows = pl.ds(pl.multiple_of(row * size, size), size)
        cols = pl.ds(pl.multiple_of(col * size, size), size)

        @pl.when(part == where_ref[0])
        def _():
            out_ref[0, rows, cols] += tiles_ref[0, slot]

        return carry

    lax.fori_loop(0, packed_ref[panel, slots], add_tile, 0)


def make_other(first, where, tiles, packed, block_rows, n_rep):
    panels, slots, size, _ = tiles.shape
    half = panels // 2
    part = block_rows // n_rep
    return pl.pallas_call(
        functools.partial(other_kernel, first),
        out_shape=pltpu.HBM((half, block_rows, part), BF16),
        grid_spec=pltpu.PrefetchScalarGridSpec(
            num_scalar_prefetch=2,
            grid=(half,),
            in_specs=[pl.BlockSpec((1, slots, size, size), lambda p, *_: (first + p, 0, 0, 0))],
            out_specs=pl.BlockSpec((1, block_rows, part), lambda p, *_: (p, 0, 0)),
        ),
        compiler_params=pltpu.CompilerParams(vmem_limit_bytes=24 * 2**20),
        cost_estimate=pl.CostEstimate(
            flops=0, transcendentals=0, bytes_accessed=tiles.size // 8
        ),
    )(where, packed, tiles)


def forward_kernel(offset, n_pieces, n_others, has_total, where_ref, dense_ref, *refs):
    others, refs = refs[:n_others], refs[n_others:]
    units = []
    for pieces in n_pieces:
        tops, refs = refs[:pieces], refs[pieces:]
        half = tops[0].shape[0] // (2 if pieces == 1 else 1)
        units.append([tops[0].at[pl.ds(0, half)], tops[-1].at[pl.ds(half * (2 - pieces), half)]])
    n_units = len(units)
    total_ref, refs = (refs[0], refs[1:]) if has_total else (None, refs)
    out_ref, sum_ref, a_buf, u_buf, sems, sum_sem = refs
    _, panels, _, part = dense_ref.shape
    some = others[0].shape[0]
    rep = where_ref[0]

    def a_copy(source, slot, side):
        target = a_buf.at[slot, :, pl.ds(side * part, part)]
        return pltpu.make_async_copy(source, target, sems.at[0, slot, side])

    def u_copy(source, slot, side, piece):
        half = part // 2
        target = u_buf.at[slot, pl.ds(side * part + piece * half, half), :]
        return pltpu.make_async_copy(source, target, sems.at[1 + piece, slot, side])

    def fetch(pair, slot):
        for side in range(2):
            place = where_ref[offset + 2 * pair + side]
            owner, panel = place // panels, place % panels
            turn = ((owner ^ rep) - 1) * (panels // some) + panel // some

            @pl.when(owner == rep)
            def _():
                a_copy(dense_ref.at[rep, panel], slot, side).start()

            for number, other_ref in enumerate(others):

                @pl.when((owner != rep) & (turn == number))
                def _():
                    a_copy(other_ref.at[panel % some], slot, side).start()

            for number in range(side, n_units, 2):

                @pl.when(pair == number // 2)
                def _():
                    for piece in range(2):
                        u_copy(units[number][piece], slot, side, piece).start()

    pairs = n_units // 2
    fetch(0, 0)
    if has_total:
        load = pltpu.make_async_copy(total_ref, sum_ref, sum_sem)
        load.start()
        load.wait()
    else:
        sum_ref[...] = jnp.zeros_like(sum_ref)

    def step(pair, carry):
        slot = pair % 2

        @pl.when(pair + 1 < pairs)
        def _():
            fetch(pair + 1, 1 - slot)

        for side in range(2):
            a_copy(dense_ref.at[0, 0], slot, side).wait()
            for piece in range(2):
                u_copy(units[0][piece], slot, side, piece).wait()
        sum_ref[...] += jnp.dot(a_buf[slot], u_buf[slot], preferred_element_type=F32)
        return carry

    lax.fori_loop(0, pairs, step, 0)
    if out_ref.dtype == F32:
        store = pltpu.make_async_copy(sum_ref, out_ref, sum_sem)
        store.start()
        store.wait()
    else:
        out_ref[...] = sum_ref[...].astype(out_ref.dtype)


def forward_part(where, offset, units, total, dense, others, kind):
    _, _, rows, part = dense.shape
    width = units[0].shape[1]
    n_pieces = [len(unit) if isinstance(unit, list) else 1 for unit in units]
    pieces = [piece for unit in units for piece in (unit if isinstance(unit, list) else [unit])]
    near = pl.BlockSpec(memory_space=pl.ANY)
    hbm = pl.BlockSpec(memory_space=pltpu.HBM)
    has_total = total is not None
    n_units, n_others = len(units), len(others)
    return pl.pallas_call(
        functools.partial(forward_kernel, offset, n_pieces, n_others, has_total),
        out_shape=jax.ShapeDtypeStruct((rows, width), kind),
        grid_spec=pltpu.PrefetchScalarGridSpec(
            num_scalar_prefetch=1,
            grid=(1,),
            in_specs=[hbm] * (1 + n_others) + [near] * (len(pieces) + has_total),
            out_specs=near if kind == F32 else pl.BlockSpec((rows, width), lambda i, where: (0, 0)),
            scratch_shapes=[
                pltpu.VMEM((rows, width), F32),
                pltpu.VMEM((2, rows, 2 * part), BF16),
                pltpu.VMEM((2, 2 * part, width), BF16),
                pltpu.SemaphoreType.DMA((3, 2, 2)),
                pltpu.SemaphoreType.DMA,
            ],
        ),
        compiler_params=pltpu.CompilerParams(vmem_limit_bytes=24 * 2**20),
        cost_estimate=pl.CostEstimate(
            flops=2 * n_units * rows * part * width,
            transcendentals=0,
            bytes_accessed=n_units * rows * part * 2 + 8 * rows * width,
        ),
    )(where, in_hbm(dense), *map(in_hbm, others), *pieces, *([total] if has_total else []))


def slopes(mine_ref, other_ref, weight_ref, cot_ref):
    agg = (mine_ref[...].astype(F32) + other_ref[...].astype(F32)).astype(BF16)
    pre = jnp.dot(agg, weight_ref[...], preferred_element_type=F32)
    sigma = 0.5 * jnp.tanh(0.5 * pre) + 0.5
    slope = cot_ref[...].astype(F32) * sigma * (1.0 + pre * (1.0 - sigma))
    return agg, (pre * sigma).astype(BF16), slope.astype(BF16)


def middle_kernel(blocks, where_ref, mine_ref, other_ref, weight_ref, cot_ref, a_ref, *refs):
    grad_ref, top_ref, end_ref, term_ref, sum_ref, full_ref = refs
    step = pl.program_id(0)
    part = mine_ref.shape[0]

    @pl.when(step < blocks)
    def _():
        agg, _, pre_grad = slopes(mine_ref, other_ref, weight_ref, cot_ref)
        grad = lax.dot_general(
            weight_ref[...], pre_grad, (((1,), (1,)), ((), ())), preferred_element_type=F32
        ).astype(BF16)
        grad_ref[...] = grad
        full_ref[:, pl.ds(pl.multiple_of(step * part, part), part)] = grad
        term = lax.dot_general(agg, pre_grad, (((0,), (0,)), ((), ())), preferred_element_type=F32)

        @pl.when(step == 0)
        def _():
            sum_ref[...] = term

        @pl.when(step > 0)
        def _():
            sum_ref[...] += term

    @pl.when(step == blocks)
    def _():
        chunk = jnp.dot(full_ref[...], a_ref[0, 0], preferred_element_type=F32).astype(BF16)
        half = top_ref.shape[0]
        top_ref[...] = chunk[:half]
        end_ref[...] = chunk[half:]
        depth, size, _ = term_ref.shape
        z = where_ref[1] // 4
        for number in range(depth):
            start = (where_ref[0] * depth + (z ^ number)) * size
            rows = sum_ref[pl.ds(pl.multiple_of(start, size), size), :]
            term_ref[number] = rows.astype(BF16)


def middle(where, offset, mine, other, weight, cotangent, dense, depth):
    rows, width = mine.shape
    n_rep, _, _, cols = dense.shape
    blocks = 4
    part = rows // blocks
    size = width // n_rep // depth
    block = pl.BlockSpec((part, width), lambda i, where: (jnp.minimum(i, blocks - 1), 0))
    fixed = lambda *shape: pl.BlockSpec(shape, lambda i, where: (0,) * len(shape))
    half = width // 2
    shapes = [(width, rows), (half, cols), (half, cols), (depth, size, width)]

    def a_block(i, where):
        place = where[offset]
        return (place % n_rep, place // n_rep, 0, 0)

    return pl.pallas_call(
        functools.partial(middle_kernel, blocks),
        out_shape=[jax.ShapeDtypeStruct(shape, BF16) for shape in shapes],
        grid_spec=pltpu.PrefetchScalarGridSpec(
            num_scalar_prefetch=1,
            grid=(blocks + 1,),
            in_specs=[
                block,
                block,
                fixed(width, width),
                block,
                pl.BlockSpec((1, 1, rows, cols), a_block),
            ],
            out_specs=[
                pl.BlockSpec((width, part), lambda i, where: (0, jnp.minimum(i, blocks - 1))),
                *(fixed(*shape) for shape in shapes[1:]),
            ],
            scratch_shapes=[pltpu.VMEM((width, width), F32), pltpu.VMEM((width, rows), BF16)],
        ),
        compiler_params=pltpu.CompilerParams(vmem_limit_bytes=24 * 2**20),
        cost_estimate=pl.CostEstimate(
            flops=6 * rows * width * width + 4 * rows * width * cols,
            transcendentals=rows * width,
            bytes_accessed=rows * width * 12,
        ),
    )(where, mine, other, weight, cotangent, in_hbm(dense))


def activated_kernel(where_ref, mine_ref, other_ref, weight_ref, cot_ref, act_ref):
    act_ref[...] = slopes(mine_ref, other_ref, weight_ref, cot_ref)[1]


def activated_rows(where, mine, other, weight, cotangent, n_rep):
    rows, width = mine.shape
    part = rows // n_rep
    block = pl.BlockSpec((part, width), lambda i, where: (where[0], 0))
    fixed = lambda *shape: pl.BlockSpec(shape, lambda i, where: (0, 0))
    return pl.pallas_call(
        activated_kernel,
        out_shape=jax.ShapeDtypeStruct((part, width), BF16),
        grid_spec=pltpu.PrefetchScalarGridSpec(
            num_scalar_prefetch=1,
            grid=(1,),
            in_specs=[block, block, fixed(width, width), block],
            out_specs=fixed(part, width),
        ),
        compiler_params=pltpu.CompilerParams(vmem_limit_bytes=24 * 2**20),
        cost_estimate=pl.CostEstimate(
            flops=2 * part * width * width,
            transcendentals=part * width,
            bytes_accessed=part * width * 8,
        ),
    )(where, mine, other, weight, cotangent)


def backward_kernel(where_ref, grad_ref, a_ref, *out_refs):
    chunk = jnp.dot(grad_ref[...], a_ref[0, 0], preferred_element_type=F32).astype(BF16)
    for number, out_ref in enumerate(out_refs):

        @pl.when(pl.program_id(0) == number)
        def _():
            out_ref[...] = chunk


def backward_part(where, offset, count, grad, dense):
    width, rows = grad.shape
    n_rep, _, _, cols = dense.shape
    fixed = lambda *shape: pl.BlockSpec(shape, lambda i, where: (0, 0))

    def a_block(i, where):
        place = where[offset + i]
        return (place % n_rep, place // n_rep, 0, 0)

    return pl.pallas_call(
        backward_kernel,
        out_shape=[jax.ShapeDtypeStruct((width, cols), BF16)] * count,
        grid_spec=pltpu.PrefetchScalarGridSpec(
            num_scalar_prefetch=1,
            grid=(count,),
            in_specs=[fixed(width, rows), pl.BlockSpec((1, 1, rows, cols), a_block)],
            out_specs=[fixed(width, cols)] * count,
        ),
        compiler_params=pltpu.CompilerParams(vmem_limit_bytes=24 * 2**20),
        cost_estimate=pl.CostEstimate(
            flops=2 * count * rows * width * cols,
            transcendentals=0,
            bytes_accessed=2 * count * rows * cols + 2 * count * width * cols + 2 * width * rows,
        ),
    )(where, grad, in_hbm(dense))


def diagonals_kernel(y_ref, x_ref, top_ref, end_ref, y_out, x_out):
    half = top_ref.shape[0]
    y_out[:half] = (y_ref[:half].astype(F32) + top_ref[...].astype(F32)).astype(BF16)
    y_out[half:] = y_ref[half:]
    x_out[:half] = x_ref[:half]
    x_out[half:] = (x_ref[half:].astype(F32) + end_ref[...].astype(F32)).astype(BF16)


def add_diagonals(odd_y, odd_x, top, end):
    return pl.pallas_call(
        diagonals_kernel,
        out_shape=[jax.ShapeDtypeStruct(odd_y.shape, BF16)] * 2,
        compiler_params=pltpu.CompilerParams(vmem_limit_bytes=24 * 2**20),
        cost_estimate=pl.CostEstimate(
            flops=odd_y.size, transcendentals=0, bytes_accessed=10 * odd_y.size
        ),
    )(odd_y, odd_x, top, end)


def final_kernel(n_parts, n_halves, z_order, where_ref, *refs):
    parts, terms = refs[:n_parts], refs[n_parts + n_halves : -2]
    halves = refs[n_parts : n_parts + n_halves]
    out_ref, weight_out = refs[-2:]
    values = [part[...].astype(F32) for part in parts]
    for top, end in zip(halves[::2], halves[1::2]):
        values.append(jnp.concatenate([top[...].astype(F32), end[...].astype(F32)]))
    total = functools.reduce(jnp.add, values)
    out_ref[0] = total.T.astype(BF16)
    depth, size, _ = terms[0].shape
    for other, term_ref in enumerate(terms):
        for number, offset in enumerate(z_order):
            place = (where_ref[0] ^ other) * depth + ((where_ref[1] // 4) ^ offset)
            rows = pl.ds(pl.multiple_of(place * size, size), size)
            weight_out[rows, :] = term_ref[number].astype(F32)


def final_sum(where, parts, halves, terms, z_order):
    width, cols = parts[0].shape
    halves = [half for pair in halves for half in pair]
    whole = lambda value: pl.BlockSpec(value.shape, lambda i, where: (0,) * value.ndim)
    outs = [
        jax.ShapeDtypeStruct((1, cols, width), BF16),
        jax.ShapeDtypeStruct((width, width), F32),
    ]
    return pl.pallas_call(
        functools.partial(final_kernel, len(parts), len(halves), z_order),
        out_shape=outs,
        grid_spec=pltpu.PrefetchScalarGridSpec(
            num_scalar_prefetch=1,
            grid=(1,),
            in_specs=[whole(value) for value in [*parts, *halves, *terms]],
            out_specs=[whole(value) for value in outs],
        ),
        compiler_params=pltpu.CompilerParams(vmem_limit_bytes=24 * 2**20),
        cost_estimate=pl.CostEstimate(
            flops=len(parts) * width * cols,
            transcendentals=0,
            bytes_accessed=2 * (len(parts) + 1) * width * cols,
        ),
    )(where, *parts, *halves, *terms)


def shards(sizes, features, weight, tile_values, tile_rows, tile_cols, tile_count, cotangent):
    n_section, n_rep = sizes
    block_rows, width = features.shape
    part = block_rows // n_rep
    section, rep = lax.axis_index("section"), lax.axis_index("rep")

    X, Y, Z = 1, 2, 4
    pair_count = n_section // 8
    low_bit = lambda mask: mask & -mask

    def flip(value, mask, rep_mask=0):
        pairs = [
            (s * n_rep + r, (s ^ mask) * n_rep + (r ^ rep_mask))
            for s in range(n_section)
            for r in range(n_rep)
        ]
        return lax.ppermute(value, BOTH, pairs)

    def gather_rep(value):
        held = [value] + [flip(value, 0, other) for other in range(1, n_rep)]
        order = rep ^ jnp.arange(n_rep)
        if n_rep == 2:
            held = [jnp.where(rep == 0, held[0], held[1]), jnp.where(rep == 0, held[1], held[0])]
            return jnp.concatenate(held)
        return jnp.stack(held)[order].reshape(-1, width)

    live = {}

    def close(*open_names):
        names = [name for name in live if name not in open_names]
        live.update(zip(names, lax.optimization_barrier([live[name] for name in names])))

    masks, offsets = [], {}

    def plan(name, wanted):
        offsets[name] = 2 + len(masks)
        masks.extend(wanted)

    for pair in range(pair_count):
        even, odd = 2 * pair * Z, (2 * pair + 1) * Z
        plan(("early", pair), [even, even + X])
        plan(("more", pair), [even + Y, odd, even + X + Y, odd + Y])
        plan(("late", pair), [odd + X, odd + X + Y])
        if pair == 0:
            plan(("first", pair), [odd + X + Y, even + X + Y])
            plan(("odd", pair), [odd + X, odd + Y, odd])
            plan(("even", pair), [even + X, even + Y, even])
        else:
            plan(("first", pair), [odd + X + Y])
            plan(("mid", pair), [even + X + Y, odd + Y, odd + X])
            plan(("last", pair), [even + X, even + Y, odd, even])
    offsets["joined"] = 2 + len(masks)
    masks += [0, X, Y, Z, Z + X, Z + Y, X + Y, Z + X + Y, 2 * Z, 2 * Z + X]
    where = jnp.concatenate(
        [rep[None], section[None], section ^ jnp.array(masks, jnp.int32)]
    ).astype(jnp.int32)

    def forward_step(names, units, total, kind=F32):
        with jax.named_scope("forward"):
            return forward_part(
                where, offsets[names], units, total, live["dense"], live["others"], kind
            )

    row_tiles = block_rows // tile_values.shape[3]
    packed = jnp.concatenate(
        [tile_rows[0] * row_tiles + tile_cols[0], tile_count[0][:, None]], axis=1
    )
    panels = tile_values.shape[1]
    def build_own(first):
        with jax.named_scope("dense_blocks"):
            live["dense"] = make_dense(
                first, live.get("dense"), where, tile_values[0], packed, block_rows, n_rep
            )

    def build_others(first):
        with jax.named_scope("other_blocks"):
            return [make_other(first, where, *sent, block_rows, n_rep) for sent in live["tiles"]]

    live["cot"] = cotangent
    live[0] = lax.dynamic_slice_in_dim(features, rep * part, part, axis=0)
    with jax.named_scope("tiles_exchange"):
        live["tiles"] = [
            (flip(tile_values[0], 0, n), flip(packed, 0, n)) for n in range(1, n_rep)
        ]
    half = part // 2
    for pair in range(pair_count):
        even, odd = 2 * pair * Z, (2 * pair + 1) * Z
        later = even + 2 * Z
        last = pair + 1 == pair_count

        with jax.named_scope(FEATURES_ACROSS):
            live["even_x"], live["even_y"] = flip(live[even], X), flip(live[even], Y)
        with jax.named_scope(FEATURES_ALONG):
            live[odd] = flip(live[even], Z)
        if pair == 0:
            build_own(0)
        if pair == 1:
            one, two = build_others(0), build_others(panels // 2)
            live["others"] = [side for sides in zip(one, two) for side in sides]
            del live["tiles"]
        if pair > 1:
            live["total"] = forward_step(("late", pair - 1), live.pop("units"), live["total"])
        close(*(["even_x", "even_y"] if pair == 0 else []))

        if pair == 0:
            with jax.named_scope(FEATURES_ACROSS):
                live["odd_x"], live["odd_y"] = flip(live[odd], X), flip(live[odd], Y)
        else:
            with jax.named_scope(FEATURES_ACROSS):
                live["even_xy"], live["odd_y"] = flip(live["even_y"], X), flip(live[odd], Y)
            with jax.named_scope(FEATURES_ALONG):
                live["odd_x"] = flip(live["even_x"], Z)
            units = [live[even], live["even_x"]]
            if pair == 1:
                live["total"] = forward_step("joined", live.pop("units") + units, None)
            else:
                live["total"] = forward_step(("early", pair), units, live["total"])
        if not last:
            with jax.named_scope(FEATURES_ALONG):
                live[later] = flip(live[later - low_bit(later)], low_bit(later))
        close(*([] if last else [later]))

        if pair == 0:
            units = [live[even], live["even_x"], live["even_y"]]
            units += [live[odd], live["odd_x"], live["odd_y"]]
            with jax.named_scope(FEATURES_ACROSS):
                units += [flip(live["even_x"], Y), flip(live["odd_y"], X)]
            live["units"] = units
            build_own(panels // 2)
            with jax.named_scope("cotangents"):
                live["cot"] = gather_rep(live["cot"])
        else:
            with jax.named_scope(FEATURES_ACROSS):
                odd_xy = [flip(live["odd_y"][:half], X), flip(live["odd_x"][half:], Y)]
            live["units"] = [live["odd_x"], odd_xy]
            units = [live["even_y"], live[odd], live.pop("even_xy"), live["odd_y"]]
            live["total"] = forward_step(("more", pair), units, live["total"])
        for name in ("even_x", "even_y", "odd_x", "odd_y"):
            del live[name]
        close()
    partial = forward_step(
        ("late", pair_count - 1), live.pop("units"), live.get("total"), BF16
    )

    with jax.named_scope("partial_sums"):
        other = flip(partial, 0, 1)
        for bit in range(1, n_rep.bit_length() - 1):
            partial = (partial.astype(F32) + other.astype(F32)).astype(BF16)
            other = flip(partial, 0, 1 << bit)

    with jax.named_scope("middle"):
        depth = n_section // 4
        rows = (partial, other, weight, live["cot"])
        grad, top_diag, end_diag, term = middle(
            where, offsets["first", pair_count - 1], *rows, live["dense"], depth
        )

    live = {"grad": grad, "dense": live["dense"], "term": term}
    add = lambda *values: functools.reduce(jnp.add, [value.astype(F32) for value in values])

    sizes_of = {"mid": 3, "last": 4, "odd": 3, "even": 3}

    def backward_step(pair, *names):
        with jax.named_scope("backward"):
            counts = [sizes_of.get(name, 1 if pair else 2) for name in names]
            chunks = backward_part(
                where, offsets[names[0], pair], sum(counts), live["grad"], live["dense"]
            )
            for name, count in zip(names, counts):
                live[name], chunks = chunks[:count], chunks[count:]

    steps = ["z", X, Y, *(-(Z << bit) for bit in reversed(range(depth.bit_length() - 1)))]
    steps.append("cores")
    z_order = [0]

    def weight_step(after=None):
        if not steps:
            return
        step = steps.pop(0)
        if after:
            live[after], live["term"] = lax.optimization_barrier((live[after], live["term"]))
        term = live["term"]
        with jax.named_scope("weight_grad"):
            if step == "z":
                parts = [term[0], *(flip(term[n], Z * n) for n in range(1, depth))]
                live["term"] = add(*parts).astype(BF16)
            elif step == "cores":
                live["terms"] = [term, *(flip(term, 0, n) for n in range(1, n_rep))]
                del live["term"]
            elif step > 0:
                live["term"] = add(term, flip(term, step)).astype(BF16)
            else:
                term = term[None] if term.ndim == 2 else term
                live["term"] = jnp.concatenate([term, flip(term, -step)])
                z_order.extend([-step // Z ^ other for other in z_order])

    half = width // 2
    tops = lambda values: [value[:half] for value in values]
    ends = lambda values: [value[half:] for value in values]
    live["first"] = [top_diag, end_diag]
    for pair in reversed(range(pair_count)):
        even = 2 * pair * Z
        top = pair + 1 == pair_count
        if not top:
            mask = low_bit(even + 2 * Z)
            name = ("to", even + 2 * Z - mask, mask)

        with jax.named_scope(GRADS_ACROSS):
            if pair > 0:
                top_diag, end_diag = live.pop("first")
                live["top"], live["end"] = flip(top_diag, X), flip(end_diag, Y)
        if not top:
            with jax.named_scope(GRADS_ALONG):
                live[name] = [flip(live["passed"][0], mask)]
        backward_step(pair, "even" if pair == 0 else "mid")
        weight_step(None if top else "even" if pair == 0 else "mid")
        with jax.named_scope(GRADS_ACROSS):
            if pair == 0:
                to_x, to_y, own = live.pop("odd")
                live["odd"], live["ahead"] = [to_x, own], flip(to_y, Y)
            else:
                even_xy, *live["mid"] = live["mid"]
                live["ahead"] = flip(even_xy, X)
        close("ahead")

        if pair == 0:
            with jax.named_scope(GRADS_ACROSS):
                to_x, own = live.pop("odd")
                to_x = add(to_x, live.pop("o_diag")).astype(BF16)
                live["odd_sum"] = [own, flip(to_x, X), live.pop("ahead")]
                to_x, to_y, own = live.pop("even")
                to_y = add(to_y, live.pop("e_diag")).astype(BF16)
                live["sums"] = [own, flip(to_x, X), flip(to_y, Y)]
        else:
            with jax.named_scope(GRADS_ACROSS):
                odd_y, odd_x = live.pop("mid")
                live["to_y"] = live.pop("ahead")
                odd_y, odd_x = add_diagonals(
                    odd_y, odd_x, live.pop("top"), live.pop("end")
                )
                live["to_odd"] = flip(odd_y, Y)
            with jax.named_scope(GRADS_ALONG):
                live["to_x"] = flip(odd_x, Z)
            backward_step(pair, "last")
        if not top:
            with jax.named_scope(GRADS_ALONG):
                live[name].append(flip(live.pop("passed")[1], mask))
        weight_step("last" if pair else None)
        close(*([] if pair else ["sums"]))

        if pair == 0:
            sums = live["sums"]
            with jax.named_scope(GRADS_ALONG):
                sums.append(flip(add(*live.pop("odd_sum")).astype(BF16), Z))
            with jax.named_scope("activated"):
                live["activated"] = activated_rows(where, *rows, n_rep)
        else:
            to_x, to_y, odd, own = live.pop("last")
            with jax.named_scope(GRADS_ACROSS):
                to_x = add(to_x, live.pop("to_x")).astype(BF16)
                to_y = add(to_y, live.pop("to_y")).astype(BF16)
                sums = [own, flip(to_x, X), flip(to_y, Y)]
            with jax.named_scope(GRADS_ALONG):
                sums.append(flip(add(odd, live.pop("to_odd")).astype(BF16), Z))
            backward_step(pair - 1, "first", *([] if pair > 1 else ["odd"]))
        live["sums"] = sums
        weight_step("first" if pair else None)
        if pair == 1:
            with jax.named_scope(GRADS_ACROSS):
                odd_diag, even_diag = live.pop("first")
                live["o_diag"], live["e_diag"] = flip(odd_diag, Y), flip(even_diag, X)
        close("o_diag", "e_diag")
        sums = live.pop("sums")
        halves = [live.pop(key) for key in list(live) if isinstance(key, tuple) and key[1] == even]
        if pair > 0:
            live["passed"] = [
                add(*tops(sums), *(value[0] for value in halves)).astype(BF16),
                add(*ends(sums), *(value[1] for value in halves)).astype(BF16),
            ]
        if pair > 1:
            (chunk,) = live["first"]
            live["first"] = [chunk[:half], chunk[half:]]
    with jax.named_scope("grads_out"):
        feat_grad, weight_grad = final_sum(where, sums, halves, live["terms"], tuple(z_order))
    return (live["activated"], feat_grad, weight_grad)


def solution(mesh):
    placed = (
        P("section", None),
        P(),
        P("section", "rep", None, None, None),
        P("section", "rep", None),
        P("section", "rep", None),
        P("section", "rep"),
        P(("section", "rep"), None),
    )
    sizes = (mesh.shape["section"], mesh.shape["rep"])
    return jax.shard_map(
        functools.partial(shards, sizes),
        mesh=mesh,
        in_specs=placed,
        out_specs=(P(("section", "rep"), None), P("rep", "section", None), P()),
        check_vma=False,
    )
```

```python
import functools

import jax
import jax.numpy as jnp
from jax import lax
from jax.experimental import pallas as pl
from jax.experimental.pallas import tpu as pltpu
from jax.sharding import PartitionSpec as P

BF16 = jnp.bfloat16
F32 = jnp.float32
BOTH = ("section", "rep")
FEATURES_ACROSS, FEATURES_ALONG = "features_xy", "features_z"
GRADS_ACROSS, GRADS_ALONG = "grads_xy", "grads_z"


def in_hbm(value):
    return pltpu.with_memory_space_constraint(value, pltpu.HBM)


def tile_place(place, row_tiles, per_part):
    row_bits, part_bits = row_tiles.bit_length() - 1, per_part.bit_length() - 1
    tile_col = place & (row_tiles - 1)
    return place >> row_bits, tile_col >> part_bits, tile_col & (per_part - 1)


def dense_kernel(first, where_ref, packed_ref, tiles_ref, *refs):
    out_ref = refs[-1]
    panel = first + pl.program_id(0)
    size, slots = tiles_ref.shape[-1], tiles_ref.shape[1]
    row_tiles, per_part = out_ref.shape[2] // size, out_ref.shape[3] // size
    out_ref[...] = jnp.zeros_like(out_ref)

    def add_tile(slot, carry):
        row, part, col = tile_place(packed_ref[panel, slot], row_tiles, per_part)
        rows = pl.ds(pl.multiple_of(row * size, size), size)
        cols = pl.ds(pl.multiple_of(col * size, size), size)
        out_ref[part, 0, rows, cols] += tiles_ref[0, slot]
        return carry

    lax.fori_loop(0, packed_ref[panel, slots], add_tile, 0)


def make_dense(first, before, where, tiles, packed, block_rows, n_rep):
    panels, slots, size, _ = tiles.shape
    half = panels // 2
    part = block_rows // n_rep
    at = lambda p: first + p
    return pl.pallas_call(
        functools.partial(dense_kernel, first),
        out_shape=pltpu.HBM((n_rep, panels, block_rows, part), BF16),
        grid_spec=pltpu.PrefetchScalarGridSpec(
            num_scalar_prefetch=2,
            grid=(half,),
            in_specs=[pl.BlockSpec((1, slots, size, size), lambda p, *_: (at(p), 0, 0, 0))]
            + [pl.BlockSpec(memory_space=pl.ANY)] * (first > 0),
            out_specs=pl.BlockSpec((n_rep, 1, block_rows, part), lambda p, *_: (0, at(p), 0, 0)),
        ),
        input_output_aliases={3: 0} if first else {},
        compiler_params=pltpu.CompilerParams(vmem_limit_bytes=24 * 2**20),
        cost_estimate=pl.CostEstimate(
            flops=0,
            transcendentals=0,
            bytes_accessed=tiles.size // 8,
        ),
    )(where, packed, in_hbm(tiles), *([in_hbm(before)] if first else []))


def other_kernel(first, where_ref, packed_ref, tiles_ref, out_ref):
    panel = first + pl.program_id(0)
    size, slots = tiles_ref.shape[-1], tiles_ref.shape[1]
    row_tiles, per_part = out_ref.shape[1] // size, out_ref.shape[2] // size
    out_ref[...] = jnp.zeros_like(out_ref)

    def add_tile(slot, carry):
        row, part, col = tile_place(packed_ref[panel, slot], row_tiles, per_part)
        rows = pl.ds(pl.multiple_of(row * size, size), size)
        cols = pl.ds(pl.multiple_of(col * size, size), size)

        @pl.when(part == where_ref[0])
        def _():
            out_ref[0, rows, cols] += tiles_ref[0, slot]

        return carry

    lax.fori_loop(0, packed_ref[panel, slots], add_tile, 0)


def make_other(first, where, tiles, packed, block_rows, n_rep):
    panels, slots, size, _ = tiles.shape
    half = panels // 2
    part = block_rows // n_rep
    return pl.pallas_call(
        functools.partial(other_kernel, first),
        out_shape=pltpu.HBM((half, block_rows, part), BF16),
        grid_spec=pltpu.PrefetchScalarGridSpec(
            num_scalar_prefetch=2,
            grid=(half,),
            in_specs=[pl.BlockSpec((1, slots, size, size), lambda p, *_: (first + p, 0, 0, 0))],
            out_specs=pl.BlockSpec((1, block_rows, part), lambda p, *_: (p, 0, 0)),
        ),
        compiler_params=pltpu.CompilerParams(vmem_limit_bytes=24 * 2**20),
        cost_estimate=pl.CostEstimate(
            flops=0, transcendentals=0, bytes_accessed=tiles.size // 8
        ),
    )(where, packed, tiles)


def forward_kernel(offset, n_pieces, n_others, has_total, where_ref, dense_ref, *refs):
    others, refs = refs[:n_others], refs[n_others:]
    units = []
    for pieces in n_pieces:
        tops, refs = refs[:pieces], refs[pieces:]
        half = tops[0].shape[0] // (2 if pieces == 1 else 1)
        units.append([tops[0].at[pl.ds(0, half)], tops[-1].at[pl.ds(half * (2 - pieces), half)]])
    n_units = len(units)
    total_ref, refs = (refs[0], refs[1:]) if has_total else (None, refs)
    out_ref, sum_ref, a_buf, u_buf, sems, sum_sem = refs
    _, panels, _, part = dense_ref.shape
    some = others[0].shape[0]
    rep = where_ref[0]

    def a_copy(source, slot, side):
        target = a_buf.at[slot, :, pl.ds(side * part, part)]
        return pltpu.make_async_copy(source, target, sems.at[0, slot, side])

    def u_copy(source, slot, side, piece):
        half = part // 2
        target = u_buf.at[slot, pl.ds(side * part + piece * half, half), :]
        return pltpu.make_async_copy(source, target, sems.at[1 + piece, slot, side])

    def fetch(pair, slot):
        for side in range(2):
            place = where_ref[offset + 2 * pair + side]
            owner, panel = place // panels, place % panels
            turn = ((owner ^ rep) - 1) * (panels // some) + panel // some

            @pl.when(owner == rep)
            def _():
                a_copy(dense_ref.at[rep, panel], slot, side).start()

            for number, other_ref in enumerate(others):

                @pl.when((owner != rep) & (turn == number))
                def _():
                    a_copy(other_ref.at[panel % some], slot, side).start()

            for number in range(side, n_units, 2):

                @pl.when(pair == number // 2)
                def _():
                    for piece in range(2):
                        u_copy(units[number][piece], slot, side, piece).start()

    pairs = n_units // 2
    fetch(0, 0)
    if has_total:
        load = pltpu.make_async_copy(total_ref, sum_ref, sum_sem)
        load.start()
        load.wait()
    else:
        sum_ref[...] = jnp.zeros_like(sum_ref)

    def step(pair, carry):
        slot = pair % 2

        @pl.when(pair + 1 < pairs)
        def _():
            fetch(pair + 1, 1 - slot)

        for side in range(2):
            a_copy(dense_ref.at[0, 0], slot, side).wait()
            for piece in range(2):
                u_copy(units[0][piece], slot, side, piece).wait()
        sum_ref[...] += jnp.dot(a_buf[slot], u_buf[slot], preferred_element_type=F32)
        return carry

    lax.fori_loop(0, pairs, step, 0)
    if out_ref.dtype == F32:
        store = pltpu.make_async_copy(sum_ref, out_ref, sum_sem)
        store.start()
        store.wait()
    else:
        out_ref[...] = sum_ref[...].astype(out_ref.dtype)


def forward_part(where, offset, units, total, dense, others, kind):
    _, _, rows, part = dense.shape
    width = units[0].shape[1]
    n_pieces = [len(unit) if isinstance(unit, list) else 1 for unit in units]
    pieces = [piece for unit in units for piece in (unit if isinstance(unit, list) else [unit])]
    near = pl.BlockSpec(memory_space=pl.ANY)
    hbm = pl.BlockSpec(memory_space=pltpu.HBM)
    has_total = total is not None
    n_units, n_others = len(units), len(others)
    return pl.pallas_call(
        functools.partial(forward_kernel, offset, n_pieces, n_others, has_total),
        out_shape=jax.ShapeDtypeStruct((rows, width), kind),
        grid_spec=pltpu.PrefetchScalarGridSpec(
            num_scalar_prefetch=1,
            grid=(1,),
            in_specs=[hbm] * (1 + n_others) + [near] * (len(pieces) + has_total),
            out_specs=near if kind == F32 else pl.BlockSpec((rows, width), lambda i, where: (0, 0)),
            scratch_shapes=[
                pltpu.VMEM((rows, width), F32),
                pltpu.VMEM((2, rows, 2 * part), BF16),
                pltpu.VMEM((2, 2 * part, width), BF16),
                pltpu.SemaphoreType.DMA((3, 2, 2)),
                pltpu.SemaphoreType.DMA,
            ],
        ),
        compiler_params=pltpu.CompilerParams(vmem_limit_bytes=24 * 2**20),
        cost_estimate=pl.CostEstimate(
            flops=2 * n_units * rows * part * width,
            transcendentals=0,
            bytes_accessed=n_units * rows * part * 2 + 8 * rows * width,
        ),
    )(where, in_hbm(dense), *map(in_hbm, others), *pieces, *([total] if has_total else []))


def slopes(mine_ref, other_ref, weight_ref, cot_ref):
    agg = (mine_ref[...].astype(F32) + other_ref[...].astype(F32)).astype(BF16)
    pre = jnp.dot(agg, weight_ref[...], preferred_element_type=F32)
    sigma = 0.5 * jnp.tanh(0.5 * pre) + 0.5
    slope = cot_ref[...].astype(F32) * sigma * (1.0 + pre * (1.0 - sigma))
    return agg, (pre * sigma).astype(BF16), slope.astype(BF16)


def middle_kernel(blocks, where_ref, mine_ref, other_ref, weight_ref, cot_ref, a_ref, *refs):
    grad_ref, top_ref, end_ref, term_ref, sum_ref, full_ref = refs
    step = pl.program_id(0)
    part = mine_ref.shape[0]

    @pl.when(step < blocks)
    def _():
        agg, _, pre_grad = slopes(mine_ref, other_ref, weight_ref, cot_ref)
        grad = lax.dot_general(
            weight_ref[...], pre_grad, (((1,), (1,)), ((), ())), preferred_element_type=F32
        ).astype(BF16)
        grad_ref[...] = grad
        full_ref[:, pl.ds(pl.multiple_of(step * part, part), part)] = grad
        term = lax.dot_general(agg, pre_grad, (((0,), (0,)), ((), ())), preferred_element_type=F32)

        @pl.when(step == 0)
        def _():
            sum_ref[...] = term

        @pl.when(step > 0)
        def _():
            sum_ref[...] += term

    @pl.when(step == blocks)
    def _():
        chunk = jnp.dot(full_ref[...], a_ref[0, 0], preferred_element_type=F32).astype(BF16)
        half = top_ref.shape[0]
        top_ref[...] = chunk[:half]
        end_ref[...] = chunk[half:]
        depth, size, _ = term_ref.shape
        z = where_ref[1] // 4
        for number in range(depth):
            start = (where_ref[0] * depth + (z ^ number)) * size
            rows = sum_ref[pl.ds(pl.multiple_of(start, size), size), :]
            term_ref[number] = rows.astype(BF16)


def middle(where, offset, mine, other, weight, cotangent, dense, depth):
    rows, width = mine.shape
    n_rep, _, _, cols = dense.shape
    blocks = 4
    part = rows // blocks
    size = width // n_rep // depth
    block = pl.BlockSpec((part, width), lambda i, where: (jnp.minimum(i, blocks - 1), 0))
    fixed = lambda *shape: pl.BlockSpec(shape, lambda i, where: (0,) * len(shape))
    half = width // 2
    shapes = [(width, rows), (half, cols), (half, cols), (depth, size, width)]

    def a_block(i, where):
        place = where[offset]
        return (place % n_rep, place // n_rep, 0, 0)

    return pl.pallas_call(
        functools.partial(middle_kernel, blocks),
        out_shape=[jax.ShapeDtypeStruct(shape, BF16) for shape in shapes],
        grid_spec=pltpu.PrefetchScalarGridSpec(
            num_scalar_prefetch=1,
            grid=(blocks + 1,),
            in_specs=[
                block,
                block,
                fixed(width, width),
                block,
                pl.BlockSpec((1, 1, rows, cols), a_block),
            ],
            out_specs=[
                pl.BlockSpec((width, part), lambda i, where: (0, jnp.minimum(i, blocks - 1))),
                *(fixed(*shape) for shape in shapes[1:]),
            ],
            scratch_shapes=[pltpu.VMEM((width, width), F32), pltpu.VMEM((width, rows), BF16)],
        ),
        compiler_params=pltpu.CompilerParams(vmem_limit_bytes=24 * 2**20),
        cost_estimate=pl.CostEstimate(
            flops=6 * rows * width * width + 4 * rows * width * cols,
            transcendentals=rows * width,
            bytes_accessed=rows * width * 12,
        ),
    )(where, mine, other, weight, cotangent, in_hbm(dense))


def activated_kernel(where_ref, mine_ref, other_ref, weight_ref, cot_ref, act_ref):
    act_ref[...] = slopes(mine_ref, other_ref, weight_ref, cot_ref)[1]


def activated_rows(where, mine, other, weight, cotangent, n_rep):
    rows, width = mine.shape
    part = rows // n_rep
    block = pl.BlockSpec((part, width), lambda i, where: (where[0], 0))
    fixed = lambda *shape: pl.BlockSpec(shape, lambda i, where: (0, 0))
    return pl.pallas_call(
        activated_kernel,
        out_shape=jax.ShapeDtypeStruct((part, width), BF16),
        grid_spec=pltpu.PrefetchScalarGridSpec(
            num_scalar_prefetch=1,
            grid=(1,),
            in_specs=[block, block, fixed(width, width), block],
            out_specs=fixed(part, width),
        ),
        compiler_params=pltpu.CompilerParams(vmem_limit_bytes=24 * 2**20),
        cost_estimate=pl.CostEstimate(
            flops=2 * part * width * width,
            transcendentals=part * width,
            bytes_accessed=part * width * 8,
        ),
    )(where, mine, other, weight, cotangent)


def backward_kernel(where_ref, grad_ref, a_ref, *out_refs):
    chunk = jnp.dot(grad_ref[...], a_ref[0, 0], preferred_element_type=F32).astype(BF16)
    for number, out_ref in enumerate(out_refs):

        @pl.when(pl.program_id(0) == number)
        def _():
            out_ref[...] = chunk


def backward_part(where, offset, count, grad, dense):
    width, rows = grad.shape
    n_rep, _, _, cols = dense.shape
    fixed = lambda *shape: pl.BlockSpec(shape, lambda i, where: (0, 0))

    def a_block(i, where):
        place = where[offset + i]
        return (place % n_rep, place // n_rep, 0, 0)

    return pl.pallas_call(
        backward_kernel,
        out_shape=[jax.ShapeDtypeStruct((width, cols), BF16)] * count,
        grid_spec=pltpu.PrefetchScalarGridSpec(
            num_scalar_prefetch=1,
            grid=(count,),
            in_specs=[fixed(width, rows), pl.BlockSpec((1, 1, rows, cols), a_block)],
            out_specs=[fixed(width, cols)] * count,
        ),
        compiler_params=pltpu.CompilerParams(vmem_limit_bytes=24 * 2**20),
        cost_estimate=pl.CostEstimate(
            flops=2 * count * rows * width * cols,
            transcendentals=0,
            bytes_accessed=2 * count * rows * cols + 2 * count * width * cols + 2 * width * rows,
        ),
    )(where, grad, in_hbm(dense))


def diagonals_kernel(y_ref, x_ref, top_ref, end_ref, y_out, x_out):
    half = top_ref.shape[0]
    y_out[:half] = (y_ref[:half].astype(F32) + top_ref[...].astype(F32)).astype(BF16)
    y_out[half:] = y_ref[half:]
    x_out[:half] = x_ref[:half]
    x_out[half:] = (x_ref[half:].astype(F32) + end_ref[...].astype(F32)).astype(BF16)


def add_diagonals(odd_y, odd_x, top, end):
    return pl.pallas_call(
        diagonals_kernel,
        out_shape=[jax.ShapeDtypeStruct(odd_y.shape, BF16)] * 2,
        compiler_params=pltpu.CompilerParams(vmem_limit_bytes=24 * 2**20),
        cost_estimate=pl.CostEstimate(
            flops=odd_y.size, transcendentals=0, bytes_accessed=10 * odd_y.size
        ),
    )(odd_y, odd_x, top, end)


def final_kernel(n_parts, n_halves, z_order, where_ref, *refs):
    parts, terms = refs[:n_parts], refs[n_parts + n_halves : -2]
    halves = refs[n_parts : n_parts + n_halves]
    out_ref, weight_out = refs[-2:]
    values = [part[...].astype(F32) for part in parts]
    for top, end in zip(halves[::2], halves[1::2]):
        values.append(jnp.concatenate([top[...].astype(F32), end[...].astype(F32)]))
    total = functools.reduce(jnp.add, values)
    out_ref[0] = total.T.astype(BF16)
    depth, size, _ = terms[0].shape
    for other, term_ref in enumerate(terms):
        for number, offset in enumerate(z_order):
            place = (where_ref[0] ^ other) * depth + ((where_ref[1] // 4) ^ offset)
            rows = pl.ds(pl.multiple_of(place * size, size), size)
            weight_out[rows, :] = term_ref[number].astype(F32)


def final_sum(where, parts, halves, terms, z_order):
    width, cols = parts[0].shape
    halves = [half for pair in halves for half in pair]
    whole = lambda value: pl.BlockSpec(value.shape, lambda i, where: (0,) * value.ndim)
    outs = [
        jax.ShapeDtypeStruct((1, cols, width), BF16),
        jax.ShapeDtypeStruct((width, width), F32),
    ]
    return pl.pallas_call(
        functools.partial(final_kernel, len(parts), len(halves), z_order),
        out_shape=outs,
        grid_spec=pltpu.PrefetchScalarGridSpec(
            num_scalar_prefetch=1,
            grid=(1,),
            in_specs=[whole(value) for value in [*parts, *halves, *terms]],
            out_specs=[whole(value) for value in outs],
        ),
        compiler_params=pltpu.CompilerParams(vmem_limit_bytes=24 * 2**20),
        cost_estimate=pl.CostEstimate(
            flops=len(parts) * width * cols,
            transcendentals=0,
            bytes_accessed=2 * (len(parts) + 1) * width * cols,
        ),
    )(where, *parts, *halves, *terms)


def shards(sizes, features, weight, tile_values, tile_rows, tile_cols, tile_count, cotangent):
    n_section, n_rep = sizes
    block_rows, width = features.shape
    part = block_rows // n_rep
    section, rep = lax.axis_index("section"), lax.axis_index("rep")

    X, Y, Z = 1, 2, 4
    pair_count = n_section // 8
    low_bit = lambda mask: mask & -mask

    def flip(value, mask, rep_mask=0):
        pairs = [
            (s * n_rep + r, (s ^ mask) * n_rep + (r ^ rep_mask))
            for s in range(n_section)
            for r in range(n_rep)
        ]
        return lax.ppermute(value, BOTH, pairs)

    def gather_rep(value):
        held = [value] + [flip(value, 0, other) for other in range(1, n_rep)]
        order = rep ^ jnp.arange(n_rep)
        if n_rep == 2:
            held = [jnp.where(rep == 0, held[0], held[1]), jnp.where(rep == 0, held[1], held[0])]
            return jnp.concatenate(held)
        return jnp.stack(held)[order].reshape(-1, width)

    live = {}

    def close(*open_names):
        names = [name for name in live if name not in open_names]
        live.update(zip(names, lax.optimization_barrier([live[name] for name in names])))

    masks, offsets = [], {}

    def plan(name, wanted):
        offsets[name] = 2 + len(masks)
        masks.extend(wanted)

    for pair in range(pair_count):
        even, odd = 2 * pair * Z, (2 * pair + 1) * Z
        plan(("early", pair), [even, even + X])
        plan(("more", pair), [even + Y, odd, even + X + Y, odd + Y])
        plan(("late", pair), [odd + X, odd + X + Y])
        if pair == 0:
            plan(("first", pair), [odd + X + Y, even + X + Y])
            plan(("odd", pair), [odd + X, odd + Y, odd])
            plan(("even", pair), [even + X, even + Y, even])
        else:
            plan(("first", pair), [odd + X + Y])
            plan(("mid", pair), [even + X + Y, odd + Y, odd + X])
            plan(("last", pair), [even + X, even + Y, odd, even])
    offsets["joined"] = 2 + len(masks)
    masks += [0, X, Y, Z, Z + X, Z + Y, X + Y, Z + X + Y, 2 * Z, 2 * Z + X]
    where = jnp.concatenate(
        [rep[None], section[None], section ^ jnp.array(masks, jnp.int32)]
    ).astype(jnp.int32)

    def forward_step(names, units, total, kind=F32):
        with jax.named_scope("forward"):
            return forward_part(
                where, offsets[names], units, total, live["dense"], live["others"], kind
            )

    row_tiles = block_rows // tile_values.shape[3]
    packed = jnp.concatenate(
        [tile_rows[0] * row_tiles + tile_cols[0], tile_count[0][:, None]], axis=1
    )
    panels = tile_values.shape[1]
    def build_own(first):
        with jax.named_scope("dense_blocks"):
            live["dense"] = make_dense(
                first, live.get("dense"), where, tile_values[0], packed, block_rows, n_rep
            )

    def build_others(first):
        with jax.named_scope("other_blocks"):
            return [make_other(first, where, *sent, block_rows, n_rep) for sent in live["tiles"]]

    live[0] = lax.dynamic_slice_in_dim(features, rep * part, part, axis=0)
    with jax.named_scope("tiles_exchange"):
        live["tiles"] = [
            (flip(tile_values[0], 0, n), flip(packed, 0, n)) for n in range(1, n_rep)
        ]
    half = part // 2
    for pair in range(pair_count):
        even, odd = 2 * pair * Z, (2 * pair + 1) * Z
        later = even + 2 * Z
        last = pair + 1 == pair_count

        with jax.named_scope(FEATURES_ACROSS):
            live["even_x"], live["even_y"] = flip(live[even], X), flip(live[even], Y)
        with jax.named_scope(FEATURES_ALONG):
            live[odd] = flip(live[even], Z)
        if pair == 0:
            build_own(0)
        if pair == 1:
            one, two = build_others(0), build_others(panels // 2)
            live["others"] = [side for sides in zip(one, two) for side in sides]
            del live["tiles"]
        if pair > 1:
            live["total"] = forward_step(("late", pair - 1), live.pop("units"), live["total"])
        close(*(["even_x", "even_y"] if pair == 0 else []))

        if pair == 0:
            with jax.named_scope(FEATURES_ACROSS):
                live["odd_x"], live["odd_y"] = flip(live[odd], X), flip(live[odd], Y)
        else:
            with jax.named_scope(FEATURES_ACROSS):
                live["even_xy"], live["odd_y"] = flip(live["even_y"], X), flip(live[odd], Y)
            with jax.named_scope(FEATURES_ALONG):
                live["odd_x"] = flip(live["even_x"], Z)
            units = [live[even], live["even_x"]]
            if pair == 1:
                live["total"] = forward_step("joined", live.pop("units") + units, None)
            else:
                live["total"] = forward_step(("early", pair), units, live["total"])
        if not last:
            with jax.named_scope(FEATURES_ALONG):
                live[later] = flip(live[later - low_bit(later)], low_bit(later))
        close(*([] if last else [later]))

        if pair == 0:
            units = [live[even], live["even_x"], live["even_y"]]
            units += [live[odd], live["odd_x"], live["odd_y"]]
            with jax.named_scope(FEATURES_ACROSS):
                units += [flip(live["even_x"], Y), flip(live["odd_y"], X)]
            live["units"] = units
            build_own(panels // 2)
            with jax.named_scope("cotangents"):
                live["cot"] = gather_rep(cotangent)
        else:
            with jax.named_scope(FEATURES_ACROSS):
                odd_xy = [flip(live["odd_y"][:half], X), flip(live["odd_x"][half:], Y)]
            live["units"] = [live["odd_x"], odd_xy]
            units = [live["even_y"], live[odd], live.pop("even_xy"), live["odd_y"]]
            live["total"] = forward_step(("more", pair), units, live["total"])
        for name in ("even_x", "even_y", "odd_x", "odd_y"):
            del live[name]
        close()
    partial = forward_step(
        ("late", pair_count - 1), live.pop("units"), live.get("total"), BF16
    )

    with jax.named_scope("partial_sums"):
        other = flip(partial, 0, 1)
        for bit in range(1, n_rep.bit_length() - 1):
            partial = (partial.astype(F32) + other.astype(F32)).astype(BF16)
            other = flip(partial, 0, 1 << bit)

    with jax.named_scope("middle"):
        depth = n_section // 4
        rows = (partial, other, weight, live["cot"])
        grad, top_diag, end_diag, term = middle(
            where, offsets["first", pair_count - 1], *rows, live["dense"], depth
        )

    live = {"grad": grad, "dense": live["dense"], "term": term}
    add = lambda *values: functools.reduce(jnp.add, [value.astype(F32) for value in values])

    sizes_of = {"mid": 3, "last": 4, "odd": 3, "even": 3}

    def backward_step(pair, *names):
        with jax.named_scope("backward"):
            counts = [sizes_of.get(name, 1 if pair else 2) for name in names]
            chunks = backward_part(
                where, offsets[names[0], pair], sum(counts), live["grad"], live["dense"]
            )
            for name, count in zip(names, counts):
                live[name], chunks = chunks[:count], chunks[count:]

    steps = ["z", X, Y, *(-(Z << bit) for bit in reversed(range(depth.bit_length() - 1)))]
    steps.append("cores")
    z_order = [0]

    def weight_step(after=None):
        if not steps:
            return
        step = steps.pop(0)
        if after:
            live[after], live["term"] = lax.optimization_barrier((live[after], live["term"]))
        term = live["term"]
        with jax.named_scope("weight_grad"):
            if step == "z":
                parts = [term[0], *(flip(term[n], Z * n) for n in range(1, depth))]
                live["term"] = add(*parts).astype(BF16)
            elif step == "cores":
                live["terms"] = [term, *(flip(term, 0, n) for n in range(1, n_rep))]
                del live["term"]
            elif step > 0:
                live["term"] = add(term, flip(term, step)).astype(BF16)
            else:
                term = term[None] if term.ndim == 2 else term
                live["term"] = jnp.concatenate([term, flip(term, -step)])
                z_order.extend([-step // Z ^ other for other in z_order])

    half = width // 2
    tops = lambda values: [value[:half] for value in values]
    ends = lambda values: [value[half:] for value in values]
    live["first"] = [top_diag, end_diag]
    for pair in reversed(range(pair_count)):
        even = 2 * pair * Z
        top = pair + 1 == pair_count
        if not top:
            mask = low_bit(even + 2 * Z)
            name = ("to", even + 2 * Z - mask, mask)

        with jax.named_scope(GRADS_ACROSS):
            if pair > 0:
                top_diag, end_diag = live.pop("first")
                live["top"], live["end"] = flip(top_diag, X), flip(end_diag, Y)
        if not top:
            with jax.named_scope(GRADS_ALONG):
                live[name] = [flip(live["passed"][0], mask)]
        backward_step(pair, "even" if pair == 0 else "mid")
        weight_step(None if top else "even" if pair == 0 else "mid")
        with jax.named_scope(GRADS_ACROSS):
            if pair == 0:
                to_x, to_y, own = live.pop("odd")
                live["odd"], live["ahead"] = [to_x, own], flip(to_y, Y)
            else:
                even_xy, *live["mid"] = live["mid"]
                live["ahead"] = flip(even_xy, X)
        close("ahead")

        if pair == 0:
            with jax.named_scope(GRADS_ACROSS):
                to_x, own = live.pop("odd")
                to_x = add(to_x, live.pop("o_diag")).astype(BF16)
                live["odd_sum"] = [own, flip(to_x, X), live.pop("ahead")]
                to_x, to_y, own = live.pop("even")
                to_y = add(to_y, live.pop("e_diag")).astype(BF16)
                live["sums"] = [own, flip(to_x, X), flip(to_y, Y)]
        else:
            with jax.named_scope(GRADS_ACROSS):
                odd_y, odd_x = live.pop("mid")
                live["to_y"] = live.pop("ahead")
                odd_y, odd_x = add_diagonals(
                    odd_y, odd_x, live.pop("top"), live.pop("end")
                )
                live["to_odd"] = flip(odd_y, Y)
            with jax.named_scope(GRADS_ALONG):
                live["to_x"] = flip(odd_x, Z)
            backward_step(pair, "last")
        if not top:
            with jax.named_scope(GRADS_ALONG):
                live[name].append(flip(live.pop("passed")[1], mask))
        weight_step("last" if pair else None)
        close(*([] if pair else ["sums"]))

        if pair == 0:
            sums = live["sums"]
            with jax.named_scope(GRADS_ALONG):
                sums.append(flip(add(*live.pop("odd_sum")).astype(BF16), Z))
            with jax.named_scope("activated"):
                live["activated"] = activated_rows(where, *rows, n_rep)
        else:
            to_x, to_y, odd, own = live.pop("last")
            with jax.named_scope(GRADS_ACROSS):
                to_x = add(to_x, live.pop("to_x")).astype(BF16)
                to_y = add(to_y, live.pop("to_y")).astype(BF16)
                sums = [own, flip(to_x, X), flip(to_y, Y)]
            with jax.named_scope(GRADS_ALONG):
                sums.append(flip(add(odd, live.pop("to_odd")).astype(BF16), Z))
            backward_step(pair - 1, "first", *([] if pair > 1 else ["odd"]))
        live["sums"] = sums
        weight_step("first" if pair else None)
        if pair == 1:
            with jax.named_scope(GRADS_ACROSS):
                odd_diag, even_diag = live.pop("first")
                live["o_diag"], live["e_diag"] = flip(odd_diag, Y), flip(even_diag, X)
        close("o_diag", "e_diag")
        sums = live.pop("sums")
        halves = [live.pop(key) for key in list(live) if isinstance(key, tuple) and key[1] == even]
        if pair > 0:
            live["passed"] = [
                add(*tops(sums), *(value[0] for value in halves)).astype(BF16),
                add(*ends(sums), *(value[1] for value in halves)).astype(BF16),
            ]
        if pair > 1:
            (chunk,) = live["first"]
            live["first"] = [chunk[:half], chunk[half:]]
    with jax.named_scope("grads_out"):
        feat_grad, weight_grad = final_sum(where, sums, halves, live["terms"], tuple(z_order))
    return (live["activated"], feat_grad, weight_grad)


def solution(mesh):
    placed = (
        P("section", None),
        P(),
        P("section", "rep", None, None, None),
        P("section", "rep", None),
        P("section", "rep", None),
        P("section", "rep"),
        P(("section", "rep"), None),
    )
    sizes = (mesh.shape["section"], mesh.shape["rep"])
    return jax.shard_map(
        functools.partial(shards, sizes),
        mesh=mesh,
        in_specs=placed,
        out_specs=(P(("section", "rep"), None), P("rep", "section", None), P()),
        check_vma=False,
    )
```
